128 devices in a mesh: dp: 16 (over z, x_hi, core), ctx: 8 (over x_lo, y).
Axes of the slice: x: 4 (x_hi: 2, x_lo: 2; x = x_hi * 2 + x_lo), y: 4, z: 4, core: 2. Of those that a mesh axis runs over, the one named last changes fastest.
Arguments:
- tokens: bfloat16 [16384, 2048], P(('dp', 'ctx')), may hold values from -6 to 6
- positions: int32 [16384], P(('dp', 'ctx')), may hold values from 0 to 1023, as said below
- attn_in: bfloat16 [2048, 2560], P(('dp', 'ctx')), may hold values from -0.125 to 0.125
- attn_out: bfloat16 [2048, 2048], P(('dp', 'ctx')), may hold values from -0.5 to 0.5
- attn_gain: bfloat16 [2048], P(('dp', 'ctx')), may hold values from 0.5 to 1.5
- mlp_in: bfloat16 [2048, 11264], P(('dp', 'ctx')), may hold values from -0.125 to 0.125
- mlp_down: bfloat16 [2048, 5632], P(('dp', 'ctx')), may hold values from -0.078125 to 0.078125
- mlp_gain: bfloat16 [2048], P(('dp', 'ctx')), may hold values from 0.5 to 1.5
- cotangent: bfloat16 [16384, 2048], P(('dp', 'ctx')), may hold values from -6 to 6
Outputs:
- activations: bfloat16 [16384, 2048], P(('dp', 'ctx'))
- input_grad: float32 [16384, 2048], P(('dp', 'ctx'))
- grad_attn_in: float32 [2048, 2560], P(('dp', 'ctx'))
- grad_attn_out: float32 [2048, 2048], P(('dp', 'ctx'))
- grad_attn_gain: float32 [2048], P(('dp', 'ctx'))
- grad_mlp_in: float32 [2048, 11264], P(('dp', 'ctx'))
- grad_mlp_down: float32 [2048, 5632], P(('dp', 'ctx'))
- grad_mlp_gain: float32 [2048], P(('dp', 'ctx'))
The draws below stay inside these ranges and needn't reach their ends.
Inputs may be any that keep to these rules, and one draw needn't show every extreme that they name: Within each sequence positions rise by one from token to token and restart at 0 where a document begins; the first document of a sequence may continue one begun earlier. One document of every sequence begins within its first 128 tokens and ends within its last 128.
All inputs are finite; a program needn't handle non-finite values.
Results may differ from the reference program's by a relative error of at most 0.019.
Values may be sent and summed in bfloat16 or wider, within the bound.
A program may use at most 192 MiB of HBM per device.

```python
import jax
import jax.numpy as jnp
from jax import lax

D = 2048
HEADS = 32
KV_HEADS = 4
HEAD_DIM = 64
FF = 5632
SEQ_LEN = 1024
TOKENS = 16384
QKV = 2560


def draw_positions(key, part):
    key = jax.random.fold_in(key, 11)
    seq_count = TOKENS // SEQ_LEN
    key_start, key_end = jax.random.split(key)
    doc_starts = jax.random.randint(key_start, (seq_count, 1), 1, SEQ_LEN // 8)
    doc_ends = jax.random.randint(key_end, (seq_count, 1), SEQ_LEN - SEQ_LEN // 8 + 1, SEQ_LEN + 1)
    token_index = jnp.arange(SEQ_LEN, dtype=jnp.int32)[None, :]
    placed = jnp.where(token_index < doc_starts, token_index + SEQ_LEN - doc_starts, jnp.where(token_index < doc_ends, token_index - doc_starts, token_index - doc_ends))
    return placed.reshape(TOKENS).astype(jnp.int32)


def level_of(rng, extent, cuts, least, high):
    def one(dim, shards_of):
        steps = jax.random.uniform(jax.random.fold_in(jax.random.fold_in(rng, 6), dim), (shards_of,), jnp.float32, least / len(cuts), high / len(cuts))
        return jnp.repeat(jnp.exp(steps), extent[dim] // shards_of).reshape((-1,) + (1,) * (len(extent) - dim - 1))

    factor_of = one(*cuts[0])
    for cut in cuts[1:]:
        factor_of = factor_of * one(*cut)
    return factor_of


def noise(stream_key, shape, width, most, pieces=(), kind=jnp.bfloat16):
    entries = width * jax.random.normal(stream_key, shape, jnp.float32)
    if pieces:
        entries = entries * level_of(stream_key, shape, pieces, -0.22, 0.18)
    return jnp.clip(entries, -most, most).astype(kind)


def setup_inputs(seed: int = 0) -> dict:
    streams_of = jax.random.split(jax.random.key(seed), 10)
    return {
        "tokens": noise(streams_of[0], (TOKENS, D), 1.0, 6.0, ((0, 128),)),
        "positions": draw_positions(jax.random.fold_in(streams_of[9], 71), 0),
        "attn_in": noise(streams_of[2], (D, QKV), D ** -0.5, 0.125, ((0, 128),)),
        "attn_out": noise(streams_of[3], (D, D), (D // 16) ** -0.5, 0.5, ((0, 128),)),
        "attn_gain": jnp.clip(1.0 + 0.1 * jax.random.normal(streams_of[4], (D,), jnp.float32), 0.5, 1.5).astype(jnp.bfloat16),
        "mlp_in": noise(streams_of[5], (D, 2 * FF), D ** -0.5, 0.125, ((0, 128),)),
        "mlp_down": noise(streams_of[6], (D, FF), FF ** -0.5, 0.078125, ((0, 128),)),
        "mlp_gain": jnp.clip(1.0 + 0.1 * jax.random.normal(streams_of[7], (D,), jnp.float32), 0.5, 1.5).astype(jnp.bfloat16),
        "cotangent": noise(streams_of[8], (TOKENS, D), 1.0, 6.0, ((0, 128),)),
    }


EPS = 1e-05
ROPE_BASE = 10000.0
NEG_FILL = -1e+30
HIGH = lax.Precision.HIGHEST

@jax.custom_vjp
def low(v):
    return lax.optimization_barrier(v.astype(jnp.bfloat16)).astype(jnp.float32)

@jax.custom_vjp
def low_back(v):
    return v

def low_keep(v):
    return (low(v), None)

def low_pass(kept, grad):
    return (grad,)

def back_keep(v):
    return (v, None)

def back_low(kept, grad):
    return (low(grad),)
low.defvjp(low_keep, low_pass)
low_back.defvjp(back_keep, back_low)

def normalize(values, gain_vec):
    inv_root = lax.rsqrt(lax.optimization_barrier(jnp.mean(values * values, -1, keepdims=True)) + EPS)
    return values * inv_root * gain_vec

def angles(positions):
    inv_freq = ROPE_BASE ** (-jnp.arange(0, HEAD_DIM, 2, dtype=jnp.float32) / HEAD_DIM)
    phase_angle = positions.astype(jnp.float32)[:, None] * inv_freq[None, :]
    return (jnp.cos(phase_angle)[:, None, :], jnp.sin(phase_angle)[:, None, :])

def rotary(values, cosines, sines):
    half_dim = values.shape[-1] // 2
    first_half = values[..., :half_dim]
    second = values[..., half_dim:]
    return jnp.concatenate([first_half * cosines - second * sines, second * cosines + first_half * sines], axis=-1)

def one_sequence(inputs, positions, attn_in, attn_out, attn_gain, mlp_in, mlp_down, mlp_gain):
    seq_len = inputs.shape[0]
    repeat = HEADS // KV_HEADS
    kv_width = KV_HEADS * HEAD_DIM
    score_scale = HEAD_DIM ** (-0.5)
    scaled_one = low(normalize(inputs, attn_gain))
    projected = low_back(jnp.dot(scaled_one, attn_in, precision=HIGH))
    cosines, sines = angles(positions)
    queries = low(rotary(projected[:, :D].reshape(seq_len, HEADS, HEAD_DIM), cosines, sines))
    queries = queries.reshape(seq_len, KV_HEADS, repeat, HEAD_DIM)
    keys = low(rotary(projected[:, D:D + kv_width].reshape(seq_len, KV_HEADS, HEAD_DIM), cosines, sines))
    values = low(projected[:, D + kv_width:]).reshape(seq_len, KV_HEADS, HEAD_DIM)
    token_index = jnp.arange(seq_len, dtype=jnp.int32)
    visible = (token_index[None, :] <= token_index[:, None]) & (token_index[:, None] - token_index[None, :] <= positions[:, None])
    scores = low_back(jnp.einsum('qgrd,kgd->grqk', queries, keys, precision=HIGH) * score_scale)
    scores = jnp.where(visible[None, None], scores, NEG_FILL)
    probs = low(jax.nn.softmax(scores, axis=-1))
    attended = jnp.einsum('grqk,kgd->qgrd', probs, values, precision=HIGH).reshape(seq_len, D)
    attended = low(low_back(attended))
    middle = inputs + low_back(jnp.dot(attended, attn_out, precision=HIGH))
    scaled_two = low(normalize(middle, mlp_gain))
    gate_up = low_back(jnp.dot(scaled_two, mlp_in, precision=HIGH))
    hidden_act = low(jax.nn.silu(gate_up[:, :FF]) * gate_up[:, FF:])
    return middle + low_back(jnp.dot(hidden_act, mlp_down.T, precision=HIGH))

def reference(tokens, positions, attn_in, attn_out, attn_gain, mlp_in, mlp_down, mlp_gain, cotangent):
    seq_count = tokens.shape[0] // SEQ_LEN
    pos_rows = positions.reshape(seq_count, SEQ_LEN)
    checked = jax.checkpoint(one_sequence)

    def forward(inputs, weight_in, weight_out, gain_one, weight_gu, weight_down, gain_two):

        def apply_one(sequence_pair):
            return checked(sequence_pair[0], sequence_pair[1], weight_in, weight_out, gain_one, weight_gu, weight_down, gain_two)
        result = lax.map(apply_one, (inputs.reshape(seq_count, SEQ_LEN, D), pos_rows))
        return result.reshape(seq_count * SEQ_LEN, D)
    outputs, pullback = jax.vjp(forward, tokens.astype(jnp.float32), attn_in.astype(jnp.float32), attn_out.astype(jnp.float32), attn_gain.astype(jnp.float32), mlp_in.astype(jnp.float32), mlp_down.astype(jnp.float32), mlp_gain.astype(jnp.float32))
    grads = pullback(cotangent.astype(jnp.float32))
    return (outputs.astype(jnp.bfloat16), grads[0], grads[1], grads[2], grads[3], grads[4], grads[5], grads[6])
```

```python
import jax
import jax.numpy as jnp
from jax import lax
from jax.experimental import pallas as pl
from jax.experimental.pallas import tpu as pltpu
from jax.sharding import PartitionSpec as P


D = 2048
HEADS = 32
KV_HEADS = 4
HEAD_DIM = 64
FF = 5632
REPEAT = HEADS // KV_HEADS
TP = 4
Q_COLS = D // TP
PROJ = Q_COLS + 2 * HEAD_DIM
HID = FF // TP

EPS = 1e-05
ROPE_BASE = 10000.0
NEG_FILL = -1e30

MESH = pl.DeviceIdType.MESH
BF16 = jnp.bfloat16
F32 = jnp.float32

SPLITS = ((PROJ, 384), (2 * HID, HID), (HID, 640))
OUT_SPLIT = 1024


def place():
    dp, ctx = lax.axis_index("dp"), lax.axis_index("ctx")
    return (dp // 2) % 2, ctx // 4, ctx % 4, dp // 4, dp % 2


def device(xh, xl, y, z, c):
    return (z * 4 + xh * 2 + c, xl * 4 + y)


def along_y(d):
    def to(xh, xl, y, z, c):
        return xh, xl, (y + d) % 4, z, c

    return to


def along_x(d):
    def to(xh, xl, y, z, c):
        x = (xh * 2 + xl + d) % 4
        return x // 2, x % 2, y, z, c

    return to


def along_z(d):
    def to(xh, xl, y, z, c):
        return xh, xl, y, (z + d) % 4, c

    return to


def sibling(xh, xl, y, z, c):
    return xh, xl, y, z, 1 - c


def half_partner(xh, xl, y, z, c):
    return xh, 1 - xl, y, z, c


def crossed(xh, xl, y, z, c):
    return xh, xl, z, y, c


def greet(routes, cross):
    here = place()
    barrier = pltpu.get_barrier_semaphore()
    for back in routes:
        pl.semaphore_signal(barrier, inc=1, device_id=device(*back(*here)), device_id_type=MESH)
    if not cross:
        pl.semaphore_wait(barrier, len(routes))
        return
    away = here[2] != here[3]

    @pl.when(away)
    def _():
        pl.semaphore_signal(barrier, inc=1, device_id=device(*crossed(*here)), device_id_type=MESH)
        pl.semaphore_wait(barrier, len(routes) + 1)

    @pl.when(jnp.logical_not(away))
    def _():
        pl.semaphore_wait(barrier, len(routes))


class Copies:
    def __init__(self, send, recv):
        self.send, self.recv, self.count = send, recv, 0

    def __call__(self, src, dst, to):
        k, self.count = self.count, self.count + 1
        return pltpu.make_async_remote_copy(
            src_ref=src,
            dst_ref=dst,
            send_sem=self.send.at[k],
            recv_sem=self.recv.at[k],
            device_id=device(*to(*place())),
            device_id_type=MESH,
        )


def comm_call(kernel, name, ident, ins, outs, copies, locals_=0):
    return pl.pallas_call(
        kernel,
        out_shape=outs,
        in_specs=[pl.BlockSpec(memory_space=pl.ANY)] * len(ins),
        out_specs=[pl.BlockSpec(memory_space=pl.ANY)] * len(outs),
        scratch_shapes=[
            pltpu.SemaphoreType.DMA((copies,)),
            pltpu.SemaphoreType.DMA((copies,)),
            pltpu.SemaphoreType.DMA((max(locals_, 1),)),
        ],
        name=name,
        compiler_params=pltpu.CompilerParams(collective_id=ident, has_side_effects=True),
    )(*ins)


def struct(shape, dtype=BF16):
    return jax.ShapeDtypeStruct(shape, dtype)


def ring_gather(parts, ident, name):
    n = len(parts)

    def kernel(*refs):
        ins, outs, (send, recv, local) = refs[:n], refs[n : 2 * n], refs[2 * n :]
        xh, xl, y, z, c = place()
        greet([along_y(d) for d in (1, 2, 3)], False)
        copy = Copies(send, recv)
        going = []
        for i, o in zip(ins, outs):
            for d in (1, 3, 2):
                going.append(copy(i, o.at[y], along_y(d)))
                going[-1].start()
        own = [pltpu.make_async_copy(i, o.at[y], local.at[k]) for k, (i, o) in enumerate(zip(ins, outs))]
        for cp in own:
            cp.start()
        for cp in going:
            cp.wait()
        for cp in own:
            cp.wait()

    return comm_call(
        kernel, name, ident, parts, [struct((4,) + p.shape, p.dtype) for p in parts], 3 * n, n
    )


def ring_scatter(part, ident, name):
    def kernel(src, dst, send, recv, local):
        xh, xl, y, z, c = place()
        greet([along_y(d) for d in (1, 2, 3)], False)
        copy = Copies(send, recv)
        going = []
        for d in (1, 3, 2):
            going.append(copy(src.at[(y + d) % 4], dst.at[d - 1], along_y(d)))
            going[-1].start()
        for cp in going:
            cp.wait()

    (out,) = comm_call(kernel, name, ident, [part], [struct((3,) + part.shape[1:])], 3)
    return out


def ring_sum(part, ident, name):
    part = part.reshape(4, part.shape[0] // 4, part.shape[1])
    own = lax.dynamic_index_in_dim(part, lax.axis_index("ctx") % 4, 0, keepdims=False)
    others = ring_scatter(part, ident, name)
    return own.astype(F32) + jnp.sum(others.astype(F32), 0)


def swap(part, to, ident, name):
    def kernel(src, dst, send, recv, local):
        greet([to], False)
        cp = Copies(send, recv)(src, dst, to)
        cp.start()
        cp.wait()

    (out,) = comm_call(kernel, name, ident, [part], [struct(part.shape, part.dtype)], 1)
    return out


def gather_weights(blocks, out_rows, ident):
    n = len(blocks)

    def kernel(*refs):
        ins, rows_in = refs[:n], refs[n]
        outs, rows_out = refs[n + 1 : 2 * n + 1], refs[2 * n + 1]
        send, recv, local = refs[2 * n + 2 :]
        xh, xl, y, z, c = place()
        greet(
            [along_y(d) for d in (1, 2, 3)]
            + [along_x(d) for d in (1, 2, 3)]
            + [along_z(d) for d in (1, 2, 3)]
            + [sibling],
            True,
        )
        copy = Copies(send, recv)
        mine = pl.ds(xl * 64, 64)
        slot = pl.ds(xl * 64 + y * 16, 16)
        started = []

        def go(src, dst, to):
            cp = copy(src, dst, to)
            cp.start()
            started.append(cp)
            return cp

        first = []
        for i, o in zip(ins, outs):
            for d in (1, 3, 2):
                first.append(go(i.at[(y + d) % 4], o.at[z, xh, c, slot], along_y(d)))
        over = copy(rows_in, rows_out.at[xh, c, xl, y], crossed)
        away = y != z

        @pl.when(away)
        def _():
            over.start()

        own = [
            pltpu.make_async_copy(i.at[y], o.at[z, xh, c, slot], local.at[k])
            for k, (i, o) in enumerate(zip(ins, outs))
        ]
        for cp in own:
            cp.start()
        stay = pltpu.make_async_copy(rows_in, rows_out.at[xh, c, xl, z], local.at[n])

        @pl.when(jnp.logical_not(away))
        def _():
            stay.start()
            stay.wait()

        for cp in own:
            cp.wait()
        for cp in first:
            cp.wait_recv()

        @pl.when(away)
        def _():
            over.wait()

        a_first, b_first = [], []
        for o, (cols, a) in zip(outs, SPLITS):
            left, right = pl.ds(0, a), pl.ds(a, cols - a)
            for d in (1, 3, 2):
                a_first.append(go(o.at[z, xh, c, mine, left], o.at[z, xh, c, mine, left], along_x(d)))
                b_first.append(go(o.at[z, xh, c, mine, right], o.at[z, xh, c, mine, right], along_z(d)))
        left, right = pl.ds(0, OUT_SPLIT), pl.ds(OUT_SPLIT, D - OUT_SPLIT)
        for d in (1, 3, 2):
            at = rows_out.at[xh, c, xl, z, :, left]
            a_first.append(go(at, at, along_x(d)))
            at = rows_out.at[xh, c, xl, z, :, right]
            b_first.append(go(at, at, along_z(d)))
        cores = []
        for o in outs:
            cores.append(go(o.at[z, xh, c, mine], o.at[z, xh, c, mine], sibling))
        at = rows_out.at[xh, c, xl, z]
        cores.append(go(at, at, sibling))
        for cp in a_first + b_first:
            cp.wait_recv()

        a_second, b_second = [], []
        for d in (1, 3, 2):
            for o, (cols, a) in zip(outs, SPLITS):
                left, right = pl.ds(0, a), pl.ds(a, cols - a)
                at = o.at[z, :, c, :, left]
                a_second.append(go(at, at, along_z(d)))
                at = o.at[:, xh, c, mine, right]
                b_second.append(go(at, at, along_x(d)))
            left, right = pl.ds(0, OUT_SPLIT), pl.ds(OUT_SPLIT, D - OUT_SPLIT)
            at = rows_out.at[:, c, :, z, :, left]
            a_second.append(go(at, at, along_z(d)))
            at = rows_out.at[xh, c, xl, :, :, right]
            b_second.append(go(at, at, along_x(d)))

        for d in (1, 3, 2):
            fx, fxl, _, _, _ = along_x(4 - d)(xh, xl, y, z, c)
            fz = (z + 4 - d) % 4
            theirs = pl.ds(fxl * 64, 64)
            for o, (cols, a) in zip(outs, SPLITS):
                left, right = pl.ds(0, a), pl.ds(a, cols - a)
                at = o.at[z, fx, c, theirs, left]
                cores.append(go(at, at, sibling))
                at = o.at[fz, xh, c, mine, right]
                cores.append(go(at, at, sibling))
            left, right = pl.ds(0, OUT_SPLIT), pl.ds(OUT_SPLIT, D - OUT_SPLIT)
            at = rows_out.at[fx, c, fxl, z, :, left]
            cores.append(go(at, at, sibling))
            at = rows_out.at[xh, c, xl, fz, :, right]
            cores.append(go(at, at, sibling))

        at_a, at_b = iter(a_second), iter(b_second)
        for d in (1, 3, 2):
            fx, fxl, _, _, _ = along_x(4 - d)(xh, xl, y, z, c)
            fz = (z + 4 - d) % 4
            theirs = pl.ds(fxl * 64, 64)
            for o, (cols, a) in zip(outs, SPLITS):
                left, right = pl.ds(0, a), pl.ds(a, cols - a)
                next(at_a).wait_recv()
                at = o.at[fz, :, c, :, left]
                cores.append(go(at, at, sibling))
                next(at_b).wait_recv()
                at = o.at[:, fx, c, theirs, right]
                cores.append(go(at, at, sibling))
            left, right = pl.ds(0, OUT_SPLIT), pl.ds(OUT_SPLIT, D - OUT_SPLIT)
            next(at_a).wait_recv()
            at = rows_out.at[:, c, :, fz, :, left]
            cores.append(go(at, at, sibling))
            next(at_b).wait_recv()
            at = rows_out.at[fx, c, fxl, :, :, right]
            cores.append(go(at, at, sibling))
        for cp in cores:
            cp.wait_recv()
        for cp in started:
            cp.wait_send()

    outs = [struct((4, 2, 2, 128, b.shape[2])) for b in blocks] + [struct((2, 2, 2, 4, 16, D))]
    copies = 3 * n + 1 + 7 * 3 * (n + 1) * 2
    got = comm_call(kernel, "gather_weights", ident, [*blocks, out_rows], outs, copies, n + 1)
    return [g.reshape(D, g.shape[-1]) for g in got[:-1]] + [got[-1].reshape(Q_COLS, D)]


def across(parts, rows_part, ident, name, stage):
    n = len(SPLITS)
    everything = [*parts, rows_part]
    if stage == "core":
        routes = [sibling]
    elif stage == "y":
        routes = [along_y(d) for d in (1, 2, 3)]
    else:
        routes = [along_x(d) for d in (1, 2, 3)] + [along_z(d) for d in (1, 2, 3)]

    if stage == "core":
        outs = [struct(p.shape[:2] + p.shape[3:]) for p in parts] + [struct((2, 2, 4, 16, D))]
    elif stage == "first":
        outs = []
        for cols, a in SPLITS:
            outs += [struct((3, 2, 128, a)), struct((3, 4, 64, cols - a))]
        outs += [struct((3, 2, 2, 16, OUT_SPLIT)), struct((3, 4, 16, D - OUT_SPLIT))]
    elif stage == "second":
        outs = []
        for cols, a in SPLITS:
            outs += [struct((3, 64, a)), struct((3, 64, cols - a))]
        outs += [struct((3, 16, OUT_SPLIT)), struct((3, 16, D - OUT_SPLIT))]
    else:
        outs = [struct(p.shape) for p in parts] + [struct(rows_part.shape)]

    def kernel(*refs):
        ins, dsts = refs[: len(everything)], refs[len(everything) : len(everything) + len(outs)]
        send, recv, local = refs[len(everything) + len(outs) :]
        xh, xl, y, z, c = place()
        greet(routes, stage == "y")
        copy = Copies(send, recv)
        going = []
        if stage == "core":
            for i, o in zip(ins[:n], dsts[:n]):
                going.append(copy(i.at[:, :, 1 - c], o, sibling))
            going.append(copy(ins[n].at[:, 1 - c], dsts[n], sibling))
        elif stage == "first":
            for d in (1, 3, 2):
                tx, txl, _, _, _ = along_x(d)(xh, xl, y, z, c)
                tz = (z + d) % 4
                theirs = pl.ds(txl * 64, 64)
                for k, (cols, a) in enumerate(SPLITS):
                    left, right = pl.ds(0, a), pl.ds(a, cols - a)
                    going.append(copy(ins[k].at[tz, :, :, left], dsts[2 * k].at[d - 1], along_z(d)))
                    going.append(
                        copy(ins[k].at[:, tx, theirs, right], dsts[2 * k + 1].at[d - 1], along_x(d))
                    )
                left, right = pl.ds(0, OUT_SPLIT), pl.ds(OUT_SPLIT, D - OUT_SPLIT)
                going.append(copy(ins[n].at[:, :, tz, :, left], dsts[2 * n].at[d - 1], along_z(d)))
                going.append(
                    copy(ins[n].at[tx, txl, :, :, right], dsts[2 * n + 1].at[d - 1], along_x(d))
                )
        elif stage == "second":
            for d in (1, 3, 2):
                tx, txl, _, _, _ = along_x(d)(xh, xl, y, z, c)
                tz = (z + d) % 4
                theirs = pl.ds(txl * 64, 64)
                for k in range(n):
                    going.append(copy(ins[2 * k].at[tx, theirs], dsts[2 * k].at[d - 1], along_x(d)))
                    going.append(copy(ins[2 * k + 1].at[tz], dsts[2 * k + 1].at[d - 1], along_z(d)))
                going.append(copy(ins[2 * n].at[tx, txl], dsts[2 * n].at[d - 1], along_x(d)))
                going.append(copy(ins[2 * n + 1].at[tz], dsts[2 * n + 1].at[d - 1], along_z(d)))
        else:
            for i, o in zip(ins[:n], dsts[:n]):
                for d in (1, 3, 2):
                    going.append(copy(i.at[(y + d) % 4], o.at[y], along_y(d)))
            over = copy(ins[n], dsts[n], crossed)
        for cp in going:
            cp.start()
        if stage == "y":
            away = y != z
            stay = pltpu.make_async_copy(ins[n], dsts[n], local.at[n])

            @pl.when(away)
            def _():
                over.start()

            @pl.when(jnp.logical_not(away))
            def _():
                stay.start()
                stay.wait()

            own = [
                pltpu.make_async_copy(i.at[y], o.at[y], local.at[k])
                for k, (i, o) in enumerate(zip(ins[:n], dsts[:n]))
            ]
            for cp in own:
                cp.start()
            for cp in own:
                cp.wait()

            @pl.when(away)
            def _():
                over.wait()

        for cp in going:
            cp.wait()

    return comm_call(kernel, name, ident, everything, outs, 6 * (n + 1) + 1, n + 1)


def total(own, others):
    return (own.astype(F32) + jnp.sum(others.astype(F32), 0)).astype(BF16)


def scatter_grads(blocks, rows_block, idents):
    xh, xl, y, z, c = place()
    n = len(blocks)
    pick = lax.dynamic_index_in_dim
    parts = [b.reshape(4, 2, 2, 128, b.shape[1]) for b in blocks]
    rows_part = rows_block.reshape(2, 2, 2, 4, 16, D)
    got = across(parts, rows_part, idents[0], "grads_core", "core")
    parts = [total(pick(p, c, 2, False), g[None]) for p, g in zip(parts, got)]
    rows_part = total(pick(rows_part, c, 1, False), got[n][None])
    got = across(parts, rows_part, idents[1], "grads_first", "first")
    second = []
    for k, (cols, a) in enumerate(SPLITS):
        mine = pick(parts[k], z, 0, False)[..., :a]
        second.append(total(mine, got[2 * k]))
        mine = lax.dynamic_slice_in_dim(pick(parts[k], xh, 1, False), xl * 64, 64, 1)[..., a:]
        second.append(total(mine, got[2 * k + 1]))
    second.append(total(pick(rows_part, z, 2, False)[..., :OUT_SPLIT], got[2 * n]))
    second_rows = total(pick(pick(rows_part, xh, 0, False), xl, 0, False)[..., OUT_SPLIT:], got[2 * n + 1])
    got = across(second, second_rows, idents[2], "grads_second", "second")
    last = []
    for k in range(n):
        left = lax.dynamic_slice_in_dim(pick(second[2 * k], xh, 0, False), xl * 64, 64, 0)
        left = total(left, got[2 * k])
        right = total(pick(second[2 * k + 1], z, 0, False), got[2 * k + 1])
        last.append(jnp.concatenate([left, right], -1).reshape(4, 16, -1))
    left = total(pick(pick(second[2 * n], xh, 0, False), xl, 0, False), got[2 * n])
    right = total(pick(second_rows, z, 0, False), got[2 * n + 1])
    return across(last, jnp.concatenate([left, right], -1), idents[3], "grads_y", "y")


def angles(positions):
    inv_freq = ROPE_BASE ** (-jnp.arange(0, HEAD_DIM, 2, dtype=F32) / HEAD_DIM)
    phase = positions.astype(F32)[:, None] * inv_freq[None, :]
    return jnp.cos(phase)[:, None, :], jnp.sin(phase)[:, None, :]


def rotary(values, cosines, sines):
    half = values.shape[-1] // 2
    first, second = values[..., :half], values[..., half:]
    return jnp.concatenate([first * cosines - second * sines, second * cosines + first * sines], -1)


def inv_norm(values):
    return lax.rsqrt(jnp.mean(values * values, -1, keepdims=True) + EPS)


def norm_back(grad_normed, inv_root, normed):
    return inv_root * (grad_normed - normed * jnp.mean(grad_normed * normed, -1, keepdims=True))


def mm(left, right, dims, out=F32):
    return lax.dot_general(left, right, (dims, ((), ())), preferred_element_type=F32).astype(out)


NN = ((1,), (0,))
NT = ((1,), (1,))
TN = ((0,), (0,))


def shards(tokens, positions, attn_in, attn_out, attn_gain, mlp_in, mlp_down, mlp_gain, cotangent):
    xh, xl, y, z, c = place()
    rows = tokens.shape[0]
    count = 4 * rows
    scale = HEAD_DIM ** (-0.5)
    gain_one = attn_gain.astype(F32)[:, None]
    gain_two = mlp_gain.astype(F32)[:, None]

    in_f = attn_in.astype(F32)
    mlp_f = mlp_in.astype(F32)
    kv = HEAD_DIM * KV_HEADS
    by_y = lambda a: a.reshape(16, TP, -1)
    w_proj = jnp.concatenate(
        [by_y(in_f[:, :D]), by_y(in_f[:, D : D + kv]), by_y(in_f[:, D + kv :])], -1
    )
    w_proj = (w_proj * gain_one[:, :, None]).astype(BF16).transpose(1, 0, 2)
    w_gu = jnp.concatenate([by_y(mlp_f[:, :FF]), by_y(mlp_f[:, FF:])], -1)
    w_gu = (w_gu * gain_two[:, :, None]).astype(BF16).transpose(1, 0, 2)
    w_down = by_y(mlp_down).transpose(1, 0, 2)
    proj_w, gu_w, down_w, out_w = gather_weights([w_proj, w_gu, w_down], attn_out, 0)

    spots = jnp.broadcast_to(positions[None, :], (8, rows))
    tokens_all, cot_all, spots_all = ring_gather([tokens, cotangent, spots], 1, "gather_tokens")
    seq_tokens = tokens_all.reshape(count, D).astype(F32)
    seq_cot = cot_all.reshape(count, D)
    seq_pos = spots_all[:, 0].reshape(count)

    normed_one_all = (seq_tokens * inv_norm(seq_tokens)).astype(BF16)
    projected = mm(normed_one_all, proj_w, NN)
    cosines, sines = angles(seq_pos)
    queries = rotary(projected[:, :Q_COLS].reshape(count, REPEAT, HEAD_DIM), cosines, sines).astype(BF16)
    keys = rotary(projected[:, None, Q_COLS : Q_COLS + HEAD_DIM], cosines, sines)[:, 0].astype(BF16)
    keys_values = jnp.concatenate([keys, projected[:, Q_COLS + HEAD_DIM :].astype(BF16)], -1)
    theirs = swap(keys_values, half_partner, 2, "swap_keys")
    low_half = xl == 0
    kv_all = jnp.concatenate(
        [jnp.where(low_half, keys_values, theirs), jnp.where(low_half, theirs, keys_values)], 0
    )
    keys_all, values_all = kv_all[:, :HEAD_DIM], kv_all[:, HEAD_DIM:]
    query_index = xl * count + jnp.arange(count, dtype=jnp.int32)
    key_index = jnp.arange(2 * count, dtype=jnp.int32)
    visible = (key_index[None, :] <= query_index[:, None]) & (
        query_index[:, None] - key_index[None, :] <= seq_pos[:, None]
    )

    def masked_scores():
        raw = jnp.einsum("qhd,kd->hqk", queries, keys_all, preferred_element_type=F32)
        return jnp.where(visible[None], raw * scale, NEG_FILL)

    scores = masked_scores()
    peak = jnp.max(scores, -1, keepdims=True)
    exps = jnp.exp(scores - peak)
    row_total = jnp.sum(exps, -1, keepdims=True)
    probs_low = (exps / row_total).astype(BF16)
    log_total = peak + jnp.log(row_total)
    attended = jnp.einsum("hqk,kd->qhd", probs_low, values_all, preferred_element_type=F32)
    attended_low = attended.reshape(count, Q_COLS).astype(BF16)
    branch = ring_sum(mm(attended_low, out_w, NN, BF16), 3, "sum_branch")
    inputs = tokens.astype(F32)
    middle = inputs + branch
    inv_two = inv_norm(middle)
    normed_two = middle * inv_two
    (seq_two,) = ring_gather([normed_two.astype(BF16)], 4, "gather_two")
    seq_two = seq_two.reshape(count, D)

    gate_up = mm(seq_two, gu_w, NN)
    gate, up = gate_up[:, :HID], gate_up[:, HID:]
    gate_sigmoid = jax.nn.sigmoid(gate)
    gate_silu = gate * gate_sigmoid
    hidden_act = (gate_silu * up).astype(BF16)
    outputs = middle + ring_sum(mm(hidden_act, down_w, NT, BF16), 5, "sum_outputs")

    grad_hidden = mm(seq_cot, down_w, NN)
    grad_gate = grad_hidden * up * gate_sigmoid * (1.0 + gate * (1.0 - gate_sigmoid))
    grad_gu = jnp.concatenate([grad_gate, grad_hidden * gate_silu], -1).astype(BF16)
    grad_two = ring_sum(mm(grad_gu, gu_w, NT, BF16), 6, "sum_grad_two")
    grad_middle = cotangent.astype(F32) + norm_back(grad_two, inv_two, normed_two)
    term_gu = mm(seq_two, grad_gu, TN, BF16)
    term_down = mm(seq_cot, hidden_act, TN, BF16)

    (seq_branch,) = ring_gather([grad_middle.astype(BF16)], 7, "gather_branch")
    seq_branch = seq_branch.reshape(count, D)
    grad_att = mm(seq_branch, out_w, NT, BF16).reshape(count, REPEAT, HEAD_DIM)
    probs = jnp.exp(masked_scores() - log_total)
    grad_probs = jnp.einsum("qhd,kd->hqk", grad_att, values_all, preferred_element_type=F32)
    row_delta = jnp.sum(probs * grad_probs, -1, keepdims=True)
    grad_scores = (probs * (grad_probs - row_delta)).astype(BF16)
    grad_q = jnp.einsum("hqk,kd->qhd", grad_scores, keys_all, preferred_element_type=F32) * scale
    grad_k = jnp.einsum("hqk,qhd->kd", grad_scores, queries, preferred_element_type=F32) * scale
    grad_v = jnp.einsum("hqk,qhd->kd", probs.astype(BF16), grad_att, preferred_element_type=F32)
    grad_kv = jnp.concatenate([grad_k, grad_v], -1).reshape(2, count, 2 * HEAD_DIM)
    away = lax.dynamic_index_in_dim(grad_kv, 1 - xl, 0, False).astype(BF16)
    grad_kv = lax.dynamic_index_in_dim(grad_kv, xl, 0, False)
    grad_kv = grad_kv + swap(away, half_partner, 8, "swap_grad_keys").astype(F32)
    grad_q = rotary(grad_q, cosines, -sines).reshape(count, Q_COLS)
    grad_k = rotary(grad_kv[:, None, :HEAD_DIM], cosines, -sines)[:, 0]
    grad_proj = jnp.concatenate([grad_q, grad_k, grad_kv[:, HEAD_DIM:]], -1).astype(BF16)
    grad_one = ring_sum(mm(grad_proj, proj_w, NT, BF16), 9, "sum_grad_one")
    inv_one = inv_norm(inputs)
    input_grad = grad_middle + norm_back(grad_one, inv_one, inputs * inv_one)
    term_proj = mm(normed_one_all, grad_proj, TN, BF16)
    term_out = mm(attended_low, seq_branch, TN, BF16)

    own_proj, own_gu, own_down, own_out = scatter_grads(
        [term_proj, term_gu, term_down], term_out, (10, 11, 12, 13)
    )
    own_proj = own_proj.astype(F32).transpose(1, 0, 2)
    cut = lambda a, start, stop: a[:, :, start:stop].reshape(16, -1)
    own_proj = jnp.concatenate(
        [
            cut(own_proj, 0, Q_COLS),
            cut(own_proj, Q_COLS, Q_COLS + HEAD_DIM),
            cut(own_proj, Q_COLS + HEAD_DIM, PROJ),
        ],
        -1,
    )
    own_gu = own_gu.astype(F32).transpose(1, 0, 2)
    own_gu = jnp.concatenate([cut(own_gu, 0, HID), cut(own_gu, HID, 2 * HID)], -1)
    own_down = own_down.astype(F32).transpose(1, 0, 2).reshape(16, FF)
    return (
        outputs.astype(BF16),
        input_grad,
        own_proj * gain_one,
        own_out.astype(F32),
        jnp.sum(own_proj * in_f, -1),
        own_gu * gain_two,
        own_down,
        jnp.sum(own_gu * mlp_f, -1),
    )


def solution(mesh):
    both = ("dp", "ctx")
    wide, flat = P(both, None), P(both)
    in_specs = (wide, flat, wide, wide, flat, wide, wide, flat, wide)
    out_specs = (wide, wide, wide, wide, flat, wide, wide, flat)
    return jax.shard_map(shards, mesh=mesh, in_specs=in_specs, out_specs=out_specs, check_vma=False)
```

```python
import jax
import jax.numpy as jnp
from jax import lax
from jax.experimental import pallas as pl
from jax.experimental.pallas import tpu as pltpu
from jax.sharding import PartitionSpec as P


D = 2048
HEADS = 32
KV_HEADS = 4
HEAD_DIM = 64
FF = 5632
REPEAT = HEADS // KV_HEADS
TP = 4
Q_COLS = D // TP
PROJ = Q_COLS + 2 * HEAD_DIM
HID = FF // TP

EPS = 1e-05
ROPE_BASE = 10000.0
NEG_FILL = -1e30

MESH = pl.DeviceIdType.MESH
BF16 = jnp.bfloat16
F32 = jnp.float32

SPLITS = ((PROJ, 384), (2 * HID, HID), (HID, 640))
OUT_SPLIT = 1024
VMEM_LIMIT = 60 << 20

NN = ((1,), (0,))
NT = ((1,), (1,))
TN = ((0,), (0,))


def place():
    dp, ctx = lax.axis_index("dp"), lax.axis_index("ctx")
    return (dp // 2) % 2, ctx // 4, ctx % 4, dp // 4, dp % 2


def device(xh, xl, y, z, c):
    return (z * 4 + xh * 2 + c, xl * 4 + y)


def along_y(d):
    def to(xh, xl, y, z, c):
        return xh, xl, (y + d) % 4, z, c

    return to


def along_x(d):
    def to(xh, xl, y, z, c):
        x = (xh * 2 + xl + d) % 4
        return x // 2, x % 2, y, z, c

    return to


def along_z(d):
    def to(xh, xl, y, z, c):
        return xh, xl, y, (z + d) % 4, c

    return to


def sibling(xh, xl, y, z, c):
    return xh, xl, y, z, 1 - c


def half_partner(xh, xl, y, z, c):
    return xh, 1 - xl, y, z, c


def crossed(xh, xl, y, z, c):
    return xh, xl, z, y, c


def greet(routes, cross):
    here = place()
    barrier = pltpu.get_barrier_semaphore()
    for back in routes:
        pl.semaphore_signal(barrier, inc=1, device_id=device(*back(*here)), device_id_type=MESH)
    if not cross:
        pl.semaphore_wait(barrier, len(routes))
        return
    away = here[2] != here[3]

    @pl.when(away)
    def _():
        pl.semaphore_signal(barrier, inc=1, device_id=device(*crossed(*here)), device_id_type=MESH)
        pl.semaphore_wait(barrier, len(routes) + 1)

    @pl.when(jnp.logical_not(away))
    def _():
        pl.semaphore_wait(barrier, len(routes))


class Copies:
    def __init__(self, send, recv):
        self.send, self.recv, self.count = send, recv, 0

    def __call__(self, src, dst, to):
        k, self.count = self.count, self.count + 1
        return pltpu.make_async_remote_copy(
            src_ref=src,
            dst_ref=dst,
            send_sem=self.send.at[k],
            recv_sem=self.recv.at[k],
            device_id=device(*to(*place())),
            device_id_type=MESH,
        )


def comm_call(kernel, name, ident, ins, outs, copies, locals_=0):
    return pl.pallas_call(
        kernel,
        out_shape=outs,
        in_specs=[pl.BlockSpec(memory_space=pl.ANY)] * len(ins),
        out_specs=[pl.BlockSpec(memory_space=pl.ANY)] * len(outs),
        scratch_shapes=[
            pltpu.SemaphoreType.DMA((copies,)),
            pltpu.SemaphoreType.DMA((copies,)),
            pltpu.SemaphoreType.DMA((max(locals_, 1),)),
        ],
        name=name,
        compiler_params=pltpu.CompilerParams(collective_id=ident, has_side_effects=True),
    )(*ins)


def struct(shape, dtype=BF16):
    return jax.ShapeDtypeStruct(shape, dtype)


class RingGather:
    def __init__(self, copy, own, dst, y):
        half = dst.shape[2] // 2
        lo, hi = pl.ds(0, half), pl.ds(half, half)
        back, on = (y + 3) % 4, (y + 1) % 4

        def first(cols, to):
            return copy(own.at[:, cols], dst.at[y, :, cols], to)

        def one(slot, cols, to):
            at = dst.at[slot, :, cols]
            return copy(at, at, to)

        self.first = [first(lo, along_y(1)), first(hi, along_y(3)), first(hi, along_y(1)), first(lo, along_y(3))]
        self.second = [one(back, lo, along_y(1)), one(on, hi, along_y(3))]

    def start(self):
        for cp in self.first:
            cp.start()

    def turn(self):
        for got, cp in zip(self.first, self.second):
            got.wait_recv()
            cp.start()

    def near(self):
        for cp in self.first[2:]:
            cp.wait_recv()

    def far(self):
        for cp in self.second:
            cp.wait_recv()

    def sent(self):
        for cp in self.first + self.second:
            cp.wait_send()


class RingSum:
    def __init__(self, copy, part, halves, whole, y):
        half = part.shape[2] // 2
        lo, hi = pl.ds(0, half), pl.ds(half, half)
        self.part, self.halves, self.whole, self.y = part, halves, whole, y
        self.cols = (lo, hi)
        far, on, back = (y + 2) % 4, (y + 1) % 4, (y + 3) % 4
        self.far = [
            copy(part.at[far, :, lo], halves.at[0], along_y(1)),
            copy(part.at[far, :, hi], halves.at[1], along_y(3)),
        ]
        self.near = [
            copy(part.at[on, :, hi], whole.at[0, :, hi], along_y(1)),
            copy(part.at[back, :, lo], whole.at[1, :, lo], along_y(3)),
        ]
        self.last = [
            copy(part.at[on, :, lo], whole.at[0, :, lo], along_y(1)),
            copy(part.at[back, :, hi], whole.at[1, :, hi], along_y(3)),
        ]
        self.slots = (on, back)

    def start(self):
        for cp in self.far + self.near:
            cp.start()

    def turn(self):
        for k in range(2):
            self.far[k].wait_recv()
            slot, cols = self.slots[k], self.cols[k]

            def body(r, _, slot=slot, cols=cols, k=k):
                rows = pl.ds(r * 32, 32)
                both = self.part[slot, rows, cols].astype(F32) + self.halves[k, rows].astype(F32)
                self.part[slot, rows, cols] = both.astype(BF16)
                return 0

            lax.fori_loop(0, self.part.shape[1] // 32, body, 0)
            self.last[k].start()

    def finish(self):
        for cp in self.near + self.last:
            cp.wait_recv()

    def rows(self, rows):
        own = self.part[self.y, rows].astype(F32)
        return own + self.whole[0, rows].astype(F32) + self.whole[1, rows].astype(F32)

    def sent(self):
        for cp in self.far + self.near + self.last:
            cp.wait_send()


def ring_sum(part, ident, name):
    rows, cols = part.shape[0] // 4, part.shape[1]

    def kernel(src, dst, work, halves, whole, send, recv, local):
        y = place()[2]
        load = pltpu.make_async_copy(src, work, local.at[0])
        load.start()
        greet([along_y(1), along_y(3)], False)
        load.wait()
        ring = RingSum(Copies(send, recv), work, halves, whole, y)
        ring.start()
        ring.turn()
        ring.finish()

        def body(r, _):
            at = pl.ds(r * 32, 32)
            dst[at] = ring.rows(at)
            return 0

        lax.fori_loop(0, rows // 32, body, 0)
        ring.sent()

    return pl.pallas_call(
        kernel,
        out_shape=struct((rows, cols), F32),
        in_specs=[pl.BlockSpec(memory_space=pl.ANY)],
        out_specs=pl.BlockSpec(memory_space=pltpu.VMEM),
        scratch_shapes=[
            pltpu.VMEM((4, rows, cols), BF16),
            pltpu.VMEM((2, rows, cols // 2), BF16),
            pltpu.VMEM((2, rows, cols), BF16),
            pltpu.SemaphoreType.DMA((6,)),
            pltpu.SemaphoreType.DMA((6,)),
            pltpu.SemaphoreType.DMA((1,)),
        ],
        name=name,
        compiler_params=pltpu.CompilerParams(
            collective_id=ident, has_side_effects=True, vmem_limit_bytes=VMEM_LIMIT
        ),
    )(part.reshape(4, rows, cols))


def ring_gather(part, ident, name):
    def kernel(src, dst, send, recv, local):
        y = place()[2]
        own = pltpu.make_async_copy(src, dst.at[y], local.at[0])
        own.start()
        greet([along_y(1), along_y(3)], False)
        ring = RingGather(Copies(send, recv), src, dst, y)
        ring.start()
        ring.turn()
        ring.near()
        ring.far()
        ring.sent()
        own.wait()

    return pl.pallas_call(
        kernel,
        out_shape=struct((4,) + part.shape, part.dtype),
        in_specs=[pl.BlockSpec(memory_space=pltpu.VMEM)],
        out_specs=pl.BlockSpec(memory_space=pl.ANY),
        scratch_shapes=[
            pltpu.SemaphoreType.DMA((6,)),
            pltpu.SemaphoreType.DMA((6,)),
            pltpu.SemaphoreType.DMA((1,)),
        ],
        name=name,
        compiler_params=pltpu.CompilerParams(collective_id=ident, has_side_effects=True),
    )(part)


class Gather:
    def __init__(self, copy, out, a, at, rows_only=False):
        xh, xl, y, z, c = at
        cols = out.shape[-1]
        left, right = pl.ds(0, a), pl.ds(a, cols - a)
        def cut(half, n):
            return slice(None) if half is None else pl.ds(half * (n // 2), n // 2)

        if rows_only:
            block = lambda z, x, c, cols: out.at[x[0], c, x[1], z, :, cols]
            z_line = lambda x, c, cols, half: out.at[x[0], c, x[1], cut(half, 4), :, cols]
            x_line = lambda z, c, cols, half: out.at[cut(half, 2), c, :, z, :, cols]
        else:
            block = lambda z, x, c, cols: out.at[z, x[0], c, pl.ds(x[1] * 64, 64), cols]
            z_line = lambda x, c, cols, half: out.at[cut(half, 4), x[0], c, pl.ds(x[1] * 64, 64), cols]
            x_line = lambda z, c, cols, half: out.at[z, cut(half, 2), c, :, cols]

        def same(ref, to):
            return copy(ref, ref, to)

        here = (xh, xl)
        self.first = []
        for d in (1, 3, 2):
            self.first.append(same(block(z, here, c, left), along_x(d)))
            self.first.append(same(block(z, here, c, right), along_z(d)))
        a_lo, a_hi = lambda z: x_line(z, c, left, 0), lambda z: x_line(z, c, left, 1)
        b_lo, b_hi = lambda x: z_line(x, c, right, 0), lambda x: z_line(x, c, right, 1)
        z_at = [(z + d) % 4 for d in range(4)]
        x_at = [along_x(d)(*at)[:2] for d in range(4)]
        self.lines = []
        for lo, hi, spots, along in ((a_lo, a_hi, z_at, along_z), (b_lo, b_hi, x_at, along_x)):
            going = [
                same(lo(spots[0]), along(1)),
                same(hi(spots[0]), along(3)),
                same(hi(spots[0]), along(1)),
                same(lo(spots[0]), along(3)),
            ]
            on = [same(lo(spots[3]), along(1)), same(hi(spots[1]), along(3))]
            self.lines.append((going, on))
        self.core = [same(block(z, here, c, pl.ds(0, cols)), sibling)]
        for d in (1, 3, 2):
            self.core.append(same(block(z, x_at[d], c, left), sibling))
            self.core.append(same(block(z_at[d], here, c, right), sibling))
        self.core_lines = []
        for d in (3, 1, 2):
            self.core_lines.append(
                (same(x_line(z_at[d], c, left, None), sibling), same(z_line(x_at[d], c, right, None), sibling))
            )

    def start(self):
        for cp in self.first:
            cp.start()
        self.core[0].start()

    def turn(self):
        for cp in self.first:
            cp.wait_recv()
        for going, _ in self.lines:
            for cp in going:
                cp.start()
        for cp in self.core[1:]:
            cp.start()

    def pass_on(self):
        for going, on in self.lines:
            for got, cp in zip(going[:2], on):
                got.wait_recv()
                cp.start()

    def near(self):
        for k, (going, _) in enumerate(self.lines):
            for side in range(2):
                going[2 + side].wait_recv()
                self.core_lines[side][k].start()

    def far(self):
        for k, (_, on) in enumerate(self.lines):
            for cp in on:
                cp.wait_recv()
            self.core_lines[2][k].start()

    def finish(self):
        for cp in self.core + [cp for pair in self.core_lines for cp in pair]:
            cp.wait_recv()

    def sent(self):
        for going, on in self.lines:
            for cp in going + on:
                cp.wait_send()
        for cp in self.first + self.core + [cp for pair in self.core_lines for cp in pair]:
            cp.wait_send()


def dot(left, right, dims=((1,), (0,))):
    return lax.dot_general(left, right, (dims, ((), ())), preferred_element_type=F32)


def swap_halves(v):
    lane = lax.broadcasted_iota(jnp.int32, v.shape, 1)
    return jnp.where(lane % 64 < 32, pltpu.roll(v, 96, 1), pltpu.roll(v, 32, 1))


def forward_attention(tokens, cotangent, spots, freqs, w_proj, w_gu, w_down, out_rows, ident):
    rows = tokens.shape[0]
    count = 4 * rows
    groups = [w_proj, w_gu, w_down]

    def kernel(
        tok_ref, cot_ref, spot_ref, freq_ref, wp, wg, wd, wo,
        normed_out, cot_all, gp, gg, gd, go, q_out, kv_out, att_out, lse_out, spot_out, middle_out, two_all,
        tok, normed, wp_v, wo_v, q_s, kv, vx, bias, att, part, halves, whole, spot_all, own_two, send, recv, local,
    ):
        at = place()
        xh, xl, y, z, c = at
        copy = Copies(send, recv)
        slot = pl.ds(xl * 64 + y * 16, 16)
        nlocal = [0]

        def near(src, dst):
            cp = pltpu.make_async_copy(src, dst, local.at[nlocal[0]])
            nlocal[0] += 1
            return cp

        to_y = []
        stay = []
        for i, o in ((wp, gp), (wg, gg), (wd, gd)):
            to_y.append([copy(i.at[(y + d) % 4], o.at[z, xh, c, slot], along_y(d)) for d in (1, 3, 2)])
            stay.append(near(i.at[y], o.at[z, xh, c, slot]))
        over = copy(wo, go.at[xh, c, xl, y], crossed)
        keep = near(wo, go.at[xh, c, xl, z])
        spot_copies = [copy(spot_all.at[y], spot_all.at[y], along_y(d)) for d in (1, 3, 2)]
        tok_ring = RingGather(copy, tok_ref, tok, y)
        cot_ring = RingGather(copy, cot_ref, cot_all, y)
        two_ring = RingGather(copy, own_two, two_all, y)
        branch = RingSum(copy, part, halves, whole, y)
        kv_copy = copy(kv.at[1], kv.at[0], half_partner)
        g_proj = Gather(copy, gp, SPLITS[0][1], at)
        g_gu = Gather(copy, gg, SPLITS[1][1], at)
        g_down = Gather(copy, gd, SPLITS[2][1], at)
        g_out = Gather(copy, go, OUT_SPLIT, at, True)

        cot_own = near(cot_ref, cot_all.at[y])
        tok_own = near(tok_ref, tok.at[y])
        tok_own.start()
        cot_own.start()
        spot_all[y] = spot_ref[...]
        for cp in stay:
            cp.start()
        greet(
            [along_y(d) for d in (1, 2, 3)]
            + [along_x(d) for d in (1, 2, 3)]
            + [along_z(d) for d in (1, 2, 3)]
            + [sibling],
            True,
        )
        away = y != z
        for cp in to_y[0]:
            cp.start()

        @pl.when(away)
        def _():
            over.start()

        @pl.when(jnp.logical_not(away))
        def _():
            keep.start()

        tok_ring.start()
        for cp in spot_copies + to_y[1] + to_y[2]:
            cp.start()

        def norm_block(k):
            def body(r, _):
                rs = pl.ds(r * 32, 32)
                v = tok[k, rs].astype(F32)
                inv = lax.rsqrt(jnp.mean(v * v, -1, keepdims=True) + EPS)
                normed[k, rs] = (v * inv).astype(BF16)
                return 0

            lax.fori_loop(0, rows // 32, body, 0)

        stay[0].wait()
        for cp in to_y[0]:
            cp.wait_recv()
        g_proj.start()

        @pl.when(away)
        def _():
            over.wait()

        @pl.when(jnp.logical_not(away))
        def _():
            keep.wait()

        g_out.start()
        tok_own.wait()
        norm_block(y)
        g_proj.turn()
        tok_ring.turn()
        g_proj.pass_on()
        g_out.turn()
        for cp in spot_copies:
            cp.wait_recv()

        cos, sin = [], []
        freq, sign = freq_ref[0:1, :], freq_ref[1:2, :]
        spot_cols = []
        for k in range(4):
            col = jnp.transpose(jnp.broadcast_to(spot_all[k, 0:1, :], (128, 128)))
            spot_out[k] = col
            spot_cols.append(col)
            cos.append(jnp.cos(col * freq))
            sin.append(jnp.sin(col * freq) * sign)
        cos, sin = jnp.concatenate(cos, 0), jnp.concatenate(sin, 0)
        low_half = xl == 0
        reach = jnp.where(low_half, -1.0, 2048.0)
        for k in range(4):
            for j in range(8):
                row = lax.broadcasted_iota(jnp.int32, (128, 128), 0) + k * 128
                col = lax.broadcasted_iota(jnp.int32, (128, 128), 1) + j * 128
                apart = (row - col + 512).astype(F32)
                seen = apart <= spot_cols[k]
                if j < 4:
                    seen = seen & (apart <= reach)
                else:
                    seen = seen & (col - 512 <= row)
                bias[pl.ds(k * 128, 128), pl.ds(j * 128, 128)] = jnp.where(seen, 0.0, NEG_FILL)

        g_proj.near()
        stay[1].wait()
        stay[2].wait()
        for cp in to_y[1] + to_y[2]:
            cp.wait_recv()
        g_gu.start()
        g_down.start()
        g_proj.far()
        g_out.pass_on()
        tok_ring.near()
        norm_block((y + 3) % 4)
        norm_block((y + 1) % 4)
        g_proj.finish()
        wp_load = near(gp, wp_v)
        wp_load.start()
        g_out.near()
        tok_ring.far()
        cot_ring.start()
        norm_block((y + 2) % 4)
        normed_save = near(normed, normed_out)
        normed_save.start()

        wp_load.wait()
        left = normed[...].reshape(count, D)
        lane = lax.broadcasted_iota(jnp.int32, (count, 128), 1)
        upper = lane >= 64
        raw = dot(left, wp_v[:, :, :, :, pl.ds(Q_COLS, 128)].reshape(D, 128))
        turned = raw * jnp.where(upper, 1.0, cos) + swap_halves(raw) * jnp.where(upper, 0.0, sin)
        kv[1] = turned.astype(BF16)
        kv_copy.start()
        g_out.far()
        g_gu.turn()
        g_down.turn()
        for j in range(2):
            raw2 = dot(left, wp_v[:, :, :, :, pl.ds(j * 256, 256)].reshape(D, 256))
            for e in range(2):
                raw = raw2[:, e * 128 : e * 128 + 128]
                turned = (raw * cos + swap_halves(raw) * sin).astype(BF16).astype(F32) * (HEAD_DIM ** (-0.5))
                pair = j * 2 + e
                q_s[2 * pair] = jnp.where(upper, 0.0, turned).astype(BF16)
                q_s[2 * pair + 1] = jnp.where(upper, 0.0, pltpu.roll(turned, 64, 1)).astype(BF16)
        kv_copy.wait_recv()
        for k in range(2):
            vx[k] = jnp.where(upper, kv[k].astype(F32), 1.0).astype(BF16)
        q_save = near(q_s, q_out)
        q_save.start()
        kv_save = near(kv, kv_out)
        kv_save.start()
        g_out.finish()
        wo_load = near(go, wo_v)
        wo_load.start()
        cot_ring.turn()

        def attend(pair):
            for b in range(2):
                rs = pl.ds(b * 256, 256)
                seen = 256 * (b + 1)
                lane = lax.broadcasted_iota(jnp.int32, (256, 128), 1) < 64
                found = []
                for e in range(2):
                    q = q_s[2 * pair + e, rs]
                    s0 = dot(q, kv[0], NT) + bias[rs, pl.ds(0, 512)]
                    s1 = dot(q, kv[1, pl.ds(0, seen)], NT) + bias[rs, pl.ds(512, seen)]
                    m = jnp.maximum(jnp.max(s0, -1, keepdims=True), jnp.max(s1, -1, keepdims=True))
                    p0 = jnp.exp(s0 - m).astype(BF16)
                    p1 = jnp.exp(s1 - m).astype(BF16)
                    o = dot(p0, vx[0]) + dot(p1, vx[1, pl.ds(0, seen)])
                    r = pltpu.roll(o, 64, 1)
                    found.append((o, r))
                    log_total = m + jnp.log(jnp.where(lane, o, r))
                    lse_out[2 * pair + e, :, rs] = jnp.transpose(log_total)[0:8]
                (o, r), (o2, r2) = found
                both = jnp.where(lane, r / o, o2 / r2)
                att[rs, pl.ds(pl.multiple_of(pair * 128, 128), 128)] = both.astype(BF16)

        def two_pairs(k):
            def body(i, _):
                attend(2 * k + i)
                return 0

            lax.fori_loop(0, 2, body, 0)

        two_pairs(0)
        g_gu.pass_on()
        g_down.pass_on()
        two_pairs(1)
        att_save = near(att, att_out)
        att_save.start()
        wo_load.wait()

        for j in range(4):
            cols = pl.ds(j * 512, 512)
            w = wo_v[:, :, :, :, :, cols].reshape(Q_COLS, 512)
            part[:, :, cols] = dot(att[...], w).astype(BF16).reshape(4, rows, 512)
        branch.start()
        g_gu.near()
        g_down.near()
        branch.turn()
        cot_ring.near()
        cot_ring.far()
        branch.finish()

        def mid(r, _):
            rs = pl.ds(r * 32, 32)
            v = tok_ref[rs].astype(F32) + branch.rows(rs)
            middle_out[rs] = v
            inv = lax.rsqrt(jnp.mean(v * v, -1, keepdims=True) + EPS)
            own_two[rs] = (v * inv).astype(BF16)
            return 0

        lax.fori_loop(0, rows // 32, mid, 0)
        two_own = near(own_two, two_all.at[y])
        two_own.start()
        two_ring.start()
        g_gu.far()
        g_down.far()
        two_ring.turn()
        two_ring.near()
        two_ring.far()
        g_gu.finish()
        g_down.finish()
        for cp in (cot_own, normed_save, q_save, kv_save, att_save, two_own):
            cp.wait()
        for group in to_y:
            for cp in group:
                cp.wait_send()
        for cp in spot_copies + [kv_copy]:
            cp.wait_send()
        for thing in (g_proj, g_out, g_gu, g_down, tok_ring, cot_ring, two_ring, branch):
            thing.sent()

    anywhere, vmem = pl.BlockSpec(memory_space=pl.ANY), pl.BlockSpec(memory_space=pltpu.VMEM)
    outs = [
        (struct((4, rows, D)), anywhere),
        (struct((4, rows, D)), anywhere),
        (struct((4, 2, 2, 128, PROJ)), anywhere),
        (struct((4, 2, 2, 128, 2 * HID)), anywhere),
        (struct((4, 2, 2, 128, HID)), anywhere),
        (struct((2, 2, 2, 4, 16, D)), anywhere),
        (struct((REPEAT, count, 128)), anywhere),
        (struct((2, count, 128)), anywhere),
        (struct((count, Q_COLS)), anywhere),
        (struct((REPEAT, 8, count), F32), vmem),
        (struct((4, 128, 128), F32), vmem),
        (struct((rows, D), F32), vmem),
        (struct((4, rows, D)), anywhere),
    ]
    copies = 9 + 1 + 3 + 6 * 3 + 6 + 1 + 31 * 4
    return pl.pallas_call(
        kernel,
        out_shape=[o[0] for o in outs],
        in_specs=[vmem] * 8,
        out_specs=[o[1] for o in outs],
        scratch_shapes=[
            pltpu.VMEM((4, rows, D), BF16),
            pltpu.VMEM((4, rows, D), BF16),
            pltpu.VMEM((4, 2, 2, 128, PROJ), BF16),
            pltpu.VMEM((2, 2, 2, 4, 16, D), BF16),
            pltpu.VMEM((REPEAT, count, 128), BF16),
            pltpu.VMEM((2, count, 128), BF16),
            pltpu.VMEM((2, count, 128), BF16),
            pltpu.VMEM((count, 2 * count), F32),
            pltpu.VMEM((count, Q_COLS), BF16),
            pltpu.VMEM((4, rows, D), BF16),
            pltpu.VMEM((2, rows, D // 2), BF16),
            pltpu.VMEM((2, rows, D), BF16),
            pltpu.VMEM((4, 8, 128), F32),
            pltpu.VMEM((rows, D), BF16),
            pltpu.SemaphoreType.DMA((copies,)),
            pltpu.SemaphoreType.DMA((copies,)),
            pltpu.SemaphoreType.DMA((16,)),
        ],
        name="forward_attention",
        compiler_params=pltpu.CompilerParams(
            collective_id=ident, has_side_effects=True, vmem_limit_bytes=VMEM_LIMIT
        ),
    )(tokens, cotangent, spots, freqs, w_proj, w_gu, w_down, out_rows)


def swap(part, to, ident, name):
    def kernel(src, dst, send, recv, local):
        greet([to], False)
        cp = Copies(send, recv)(src, dst, to)
        cp.start()
        cp.wait()

    (out,) = comm_call(kernel, name, ident, [part], [struct(part.shape, part.dtype)], 1)
    return out


def across(parts, rows_part, ident, name, stage):
    n = len(SPLITS)
    everything = [*parts, rows_part]
    if stage == "core":
        routes = [sibling]
    elif stage == "y":
        routes = [along_y(d) for d in (1, 2, 3)]
    else:
        routes = [along_x(d) for d in (1, 2, 3)] + [along_z(d) for d in (1, 2, 3)]

    if stage == "core":
        outs = [struct(p.shape[:2] + p.shape[3:]) for p in parts] + [struct((2, 2, 4, 16, D))]
    elif stage == "first":
        outs = []
        for cols, a in SPLITS:
            outs += [struct((3, 2, 128, a)), struct((3, 4, 64, cols - a))]
        outs += [struct((3, 2, 2, 16, OUT_SPLIT)), struct((3, 4, 16, D - OUT_SPLIT))]
    elif stage == "second":
        outs = []
        for cols, a in SPLITS:
            outs += [struct((3, 64, a)), struct((3, 64, cols - a))]
        outs += [struct((3, 16, OUT_SPLIT)), struct((3, 16, D - OUT_SPLIT))]
    else:
        outs = [struct(p.shape) for p in parts] + [struct(rows_part.shape)]

    def kernel(*refs):
        ins, dsts = refs[: len(everything)], refs[len(everything) : len(everything) + len(outs)]
        send, recv, local = refs[len(everything) + len(outs) :]
        xh, xl, y, z, c = place()
        greet(routes, stage == "y")
        copy = Copies(send, recv)
        going = []
        if stage == "core":
            for i, o in zip(ins[:n], dsts[:n]):
                going.append(copy(i.at[:, :, 1 - c], o, sibling))
            going.append(copy(ins[n].at[:, 1 - c], dsts[n], sibling))
        elif stage == "first":
            for d in (1, 3, 2):
                tx, txl, _, _, _ = along_x(d)(xh, xl, y, z, c)
                tz = (z + d) % 4
                theirs = pl.ds(txl * 64, 64)
                for k, (cols, a) in enumerate(SPLITS):
                    left, right = pl.ds(0, a), pl.ds(a, cols - a)
                    going.append(copy(ins[k].at[tz, :, :, left], dsts[2 * k].at[d - 1], along_z(d)))
                    going.append(
                        copy(ins[k].at[:, tx, theirs, right], dsts[2 * k + 1].at[d - 1], along_x(d))
                    )
                left, right = pl.ds(0, OUT_SPLIT), pl.ds(OUT_SPLIT, D - OUT_SPLIT)
                going.append(copy(ins[n].at[:, :, tz, :, left], dsts[2 * n].at[d - 1], along_z(d)))
                going.append(
                    copy(ins[n].at[tx, txl, :, :, right], dsts[2 * n + 1].at[d - 1], along_x(d))
                )
        elif stage == "second":
            for d in (1, 3, 2):
                tx, txl, _, _, _ = along_x(d)(xh, xl, y, z, c)
                tz = (z + d) % 4
                theirs = pl.ds(txl * 64, 64)
                for k in range(n):
                    going.append(copy(ins[2 * k].at[tx, theirs], dsts[2 * k].at[d - 1], along_x(d)))
                    going.append(copy(ins[2 * k + 1].at[tz], dsts[2 * k + 1].at[d - 1], along_z(d)))
                going.append(copy(ins[2 * n].at[tx, txl], dsts[2 * n].at[d - 1], along_x(d)))
                going.append(copy(ins[2 * n + 1].at[tz], dsts[2 * n + 1].at[d - 1], along_z(d)))
        else:
            for i, o in zip(ins[:n], dsts[:n]):
                for d in (1, 3, 2):
                    going.append(copy(i.at[(y + d) % 4], o.at[y], along_y(d)))
            over = copy(ins[n], dsts[n], crossed)
        for cp in going:
            cp.start()
        if stage == "y":
            away = y != z
            stay = pltpu.make_async_copy(ins[n], dsts[n], local.at[n])

            @pl.when(away)
            def _():
                over.start()

            @pl.when(jnp.logical_not(away))
            def _():
                stay.start()
                stay.wait()

            own = [
                pltpu.make_async_copy(i.at[y], o.at[y], local.at[k])
                for k, (i, o) in enumerate(zip(ins[:n], dsts[:n]))
            ]
            for cp in own:
                cp.start()
            for cp in own:
                cp.wait()

            @pl.when(away)
            def _():
                over.wait()

        for cp in going:
            cp.wait()

    return comm_call(kernel, name, ident, everything, outs, 6 * (n + 1) + 1, n + 1)


def total(own, others):
    return (own.astype(F32) + jnp.sum(others.astype(F32), 0)).astype(BF16)


def scatter_grads(blocks, rows_block, idents):
    xh, xl, y, z, c = place()
    n = len(blocks)
    pick = lax.dynamic_index_in_dim
    parts = [b.reshape(4, 2, 2, 128, b.shape[1]) for b in blocks]
    rows_part = rows_block.reshape(2, 2, 2, 4, 16, D)
    got = across(parts, rows_part, idents[0], "grads_core", "core")
    parts = [total(pick(p, c, 2, False), g[None]) for p, g in zip(parts, got)]
    rows_part = total(pick(rows_part, c, 1, False), got[n][None])
    got = across(parts, rows_part, idents[1], "grads_first", "first")
    second = []
    for k, (cols, a) in enumerate(SPLITS):
        mine = pick(parts[k], z, 0, False)[..., :a]
        second.append(total(mine, got[2 * k]))
        mine = lax.dynamic_slice_in_dim(pick(parts[k], xh, 1, False), xl * 64, 64, 1)[..., a:]
        second.append(total(mine, got[2 * k + 1]))
    second.append(total(pick(rows_part, z, 2, False)[..., :OUT_SPLIT], got[2 * n]))
    second_rows = total(pick(pick(rows_part, xh, 0, False), xl, 0, False)[..., OUT_SPLIT:], got[2 * n + 1])
    got = across(second, second_rows, idents[2], "grads_second", "second")
    last = []
    for k in range(n):
        left = lax.dynamic_slice_in_dim(pick(second[2 * k], xh, 0, False), xl * 64, 64, 0)
        left = total(left, got[2 * k])
        right = total(pick(second[2 * k + 1], z, 0, False), got[2 * k + 1])
        last.append(jnp.concatenate([left, right], -1).reshape(4, 16, -1))
    left = total(pick(pick(second[2 * n], xh, 0, False), xl, 0, False), got[2 * n])
    right = total(pick(second_rows, z, 0, False), got[2 * n + 1])
    return across(last, jnp.concatenate([left, right], -1), idents[3], "grads_y", "y")


def angles(positions):
    inv_freq = ROPE_BASE ** (-jnp.arange(0, HEAD_DIM, 2, dtype=F32) / HEAD_DIM)
    phase = positions.astype(F32)[:, None] * inv_freq[None, :]
    return jnp.cos(phase)[:, None, :], jnp.sin(phase)[:, None, :]


def rotary(values, cosines, sines):
    half = values.shape[-1] // 2
    first, second = values[..., :half], values[..., half:]
    return jnp.concatenate([first * cosines - second * sines, second * cosines + first * sines], -1)


def inv_norm(values):
    return lax.rsqrt(jnp.mean(values * values, -1, keepdims=True) + EPS)


def norm_back(grad_normed, inv_root, normed):
    return inv_root * (grad_normed - normed * jnp.mean(grad_normed * normed, -1, keepdims=True))


def mm(left, right, dims, out=F32):
    return lax.dot_general(left, right, (dims, ((), ())), preferred_element_type=F32).astype(out)


def shards(tokens, positions, attn_in, attn_out, attn_gain, mlp_in, mlp_down, mlp_gain, cotangent):
    xh, xl, y, z, c = place()
    rows = tokens.shape[0]
    count = 4 * rows
    scale = HEAD_DIM ** (-0.5)
    gain_one = attn_gain.astype(F32)[:, None]
    gain_two = mlp_gain.astype(F32)[:, None]

    in_f = attn_in.astype(F32)
    mlp_f = mlp_in.astype(F32)
    kv = HEAD_DIM * KV_HEADS
    by_y = lambda a: a.reshape(16, TP, -1)
    w_proj = jnp.concatenate(
        [by_y(in_f[:, :D]), by_y(in_f[:, D : D + kv]), by_y(in_f[:, D + kv :])], -1
    )
    w_proj = (w_proj * gain_one[:, :, None]).astype(BF16).transpose(1, 0, 2)
    w_gu = jnp.concatenate([by_y(mlp_f[:, :FF]), by_y(mlp_f[:, FF:])], -1)
    w_gu = (w_gu * gain_two[:, :, None]).astype(BF16).transpose(1, 0, 2)
    w_down = by_y(mlp_down).transpose(1, 0, 2)
    spots = jnp.broadcast_to(positions.astype(F32)[None, :], (8, rows))
    lanes = jnp.arange(128)
    inv_freq = ROPE_BASE ** (-2.0 * (lanes % 32).astype(F32) / HEAD_DIM)
    signs = jnp.where(lanes % 64 < 32, -1.0, 1.0)
    freqs = jnp.zeros((8, 128), F32).at[0].set(inv_freq).at[1].set(signs)
    (normed_one_all, cot_all, proj_w, gu_w, down_w, out_w, q_all, kv_all, attended_low, lse, spots_all, middle, seq_two) = (
        forward_attention(tokens, cotangent, spots, freqs, w_proj, w_gu, w_down, attn_out, 0)
    )
    normed_one_all = normed_one_all.reshape(count, D)
    seq_cot, seq_two = cot_all.reshape(count, D), seq_two.reshape(count, D)
    proj_w, gu_w, down_w = (w.reshape(D, w.shape[-1]) for w in (proj_w, gu_w, down_w))
    out_w = out_w.reshape(Q_COLS, D)
    seq_pos = spots_all.reshape(count, 128)[:, 0]
    cosines, sines = angles(seq_pos)
    queries = q_all[:, :, :HEAD_DIM].transpose(1, 0, 2)
    kv_all = kv_all.reshape(2 * count, 2 * HEAD_DIM)
    keys_all, values_all = kv_all[:, :HEAD_DIM], kv_all[:, HEAD_DIM:]
    row = jnp.arange(count, dtype=jnp.int32)[:, None]
    col = jnp.arange(2 * count, dtype=jnp.int32)[None, :]
    apart = row + count - col
    visible = (apart.astype(F32) <= seq_pos[:, None]) & jnp.where(col < count, xl == 1, apart >= 0)
    log_total = lse[:, 0, :, None]

    def masked_scores():
        raw = jnp.einsum("qhd,kd->hqk", queries, keys_all, preferred_element_type=F32)
        return jnp.where(visible[None], raw, NEG_FILL)

    inputs = tokens.astype(F32)
    inv_two = inv_norm(middle)
    normed_two = middle * inv_two

    gate_up = mm(seq_two, gu_w, NN)
    gate, up = gate_up[:, :HID], gate_up[:, HID:]
    gate_sigmoid = jax.nn.sigmoid(gate)
    gate_silu = gate * gate_sigmoid
    hidden_act = (gate_silu * up).astype(BF16)
    outputs = middle + ring_sum(mm(hidden_act, down_w, NT, BF16), 5, "sum_outputs")

    grad_hidden = mm(seq_cot, down_w, NN)
    grad_gate = grad_hidden * up * gate_sigmoid * (1.0 + gate * (1.0 - gate_sigmoid))
    grad_gu = jnp.concatenate([grad_gate, grad_hidden * gate_silu], -1).astype(BF16)
    grad_two = ring_sum(mm(grad_gu, gu_w, NT, BF16), 6, "sum_grad_two")
    grad_middle = cotangent.astype(F32) + norm_back(grad_two, inv_two, normed_two)
    term_gu = mm(seq_two, grad_gu, TN, BF16)
    term_down = mm(seq_cot, hidden_act, TN, BF16)

    seq_branch = ring_gather(grad_middle.astype(BF16), 7, "gather_branch").reshape(count, D)
    grad_att = mm(seq_branch, out_w, NT, BF16).reshape(count, REPEAT, HEAD_DIM)
    probs = jnp.exp(masked_scores() - log_total)
    grad_probs = jnp.einsum("qhd,kd->hqk", grad_att, values_all, preferred_element_type=F32)
    row_delta = jnp.sum(probs * grad_probs, -1, keepdims=True)
    grad_scores = (probs * (grad_probs - row_delta)).astype(BF16)
    grad_q = jnp.einsum("hqk,kd->qhd", grad_scores, keys_all, preferred_element_type=F32) * scale
    grad_k = jnp.einsum("hqk,qhd->kd", grad_scores, queries, preferred_element_type=F32)
    grad_v = jnp.einsum("hqk,qhd->kd", probs.astype(BF16), grad_att, preferred_element_type=F32)
    grad_kv = jnp.concatenate([grad_k, grad_v], -1).reshape(2, count, 2 * HEAD_DIM)
    away = grad_kv[0].astype(BF16)
    grad_kv = grad_kv[1]
    grad_kv = grad_kv + swap(away, half_partner, 8, "swap_grad_keys").astype(F32)
    grad_q = rotary(grad_q, cosines, -sines).reshape(count, Q_COLS)
    grad_k = rotary(grad_kv[:, None, :HEAD_DIM], cosines, -sines)[:, 0]
    grad_proj = jnp.concatenate([grad_q, grad_k, grad_kv[:, HEAD_DIM:]], -1).astype(BF16)
    grad_one = ring_sum(mm(grad_proj, proj_w, NT, BF16), 9, "sum_grad_one")
    inv_one = inv_norm(inputs)
    input_grad = grad_middle + norm_back(grad_one, inv_one, inputs * inv_one)
    term_proj = mm(normed_one_all, grad_proj, TN, BF16)
    term_out = mm(attended_low, seq_branch, TN, BF16)

    own_proj, own_gu, own_down, own_out = scatter_grads(
        [term_proj, term_gu, term_down], term_out, (10, 11, 12, 13)
    )
    own_proj = own_proj.astype(F32).transpose(1, 0, 2)
    cut = lambda a, start, stop: a[:, :, start:stop].reshape(16, -1)
    own_proj = jnp.concatenate(
        [
            cut(own_proj, 0, Q_COLS),
            cut(own_proj, Q_COLS, Q_COLS + HEAD_DIM),
            cut(own_proj, Q_COLS + HEAD_DIM, PROJ),
        ],
        -1,
    )
    own_gu = own_gu.astype(F32).transpose(1, 0, 2)
    own_gu = jnp.concatenate([cut(own_gu, 0, HID), cut(own_gu, HID, 2 * HID)], -1)
    own_down = own_down.astype(F32).transpose(1, 0, 2).reshape(16, FF)
    return (
        outputs.astype(BF16),
        input_grad,
        own_proj * gain_one,
        own_out.astype(F32),
        jnp.sum(own_proj * in_f, -1),
        own_gu * gain_two,
        own_down,
        jnp.sum(own_gu * mlp_f, -1),
    )


def solution(mesh):
    both = ("dp", "ctx")
    wide, flat = P(both, None), P(both)
    in_specs = (wide, flat, wide, wide, flat, wide, wide, flat, wide)
    out_specs = (wide, wide, wide, wide, flat, wide, wide, flat)
    return jax.shard_map(shards, mesh=mesh, in_specs=in_specs, out_specs=out_specs, check_vma=False)
```

```python
import jax
import jax.numpy as jnp
from jax import lax
from jax.experimental import pallas as pl
from jax.experimental.pallas import tpu as pltpu
from jax.sharding import PartitionSpec as P


D = 2048
HEADS = 32
KV_HEADS = 4
HEAD_DIM = 64
FF = 5632
REPEAT = HEADS // KV_HEADS
TP = 4
Q_COLS = D // TP
PROJ = Q_COLS + 2 * HEAD_DIM
HID = FF // TP

EPS = 1e-05
ROPE_BASE = 10000.0
NEG_FILL = -1e30

MESH = pl.DeviceIdType.MESH
BF16 = jnp.bfloat16
F32 = jnp.float32

SPLITS = ((PROJ, 384), (2 * HID, HID), (HID, 640))
OUT_SPLIT = 1024
VMEM_LIMIT = 60 << 20

NN = ((1,), (0,))
NT = ((1,), (1,))
TN = ((0,), (0,))


def place():
    dp, ctx = lax.axis_index("dp"), lax.axis_index("ctx")
    return (dp // 2) % 2, ctx // 4, ctx % 4, dp // 4, dp % 2


def device(xh, xl, y, z, c):
    return (z * 4 + xh * 2 + c, xl * 4 + y)


def along_y(d):
    def to(xh, xl, y, z, c):
        return xh, xl, (y + d) % 4, z, c

    return to


def along_x(d):
    def to(xh, xl, y, z, c):
        x = (xh * 2 + xl + d) % 4
        return x // 2, x % 2, y, z, c

    return to


def along_z(d):
    def to(xh, xl, y, z, c):
        return xh, xl, y, (z + d) % 4, c

    return to


def sibling(xh, xl, y, z, c):
    return xh, xl, y, z, 1 - c


def half_partner(xh, xl, y, z, c):
    return xh, 1 - xl, y, z, c


def crossed(xh, xl, y, z, c):
    return xh, xl, z, y, c


def greet(routes, cross):
    here = place()
    barrier = pltpu.get_barrier_semaphore()
    for back in routes:
        pl.semaphore_signal(barrier, inc=1, device_id=device(*back(*here)), device_id_type=MESH)
    if not cross:
        pl.semaphore_wait(barrier, len(routes))
        return
    away = here[2] != here[3]

    @pl.when(away)
    def _():
        pl.semaphore_signal(barrier, inc=1, device_id=device(*crossed(*here)), device_id_type=MESH)
        pl.semaphore_wait(barrier, len(routes) + 1)

    @pl.when(jnp.logical_not(away))
    def _():
        pl.semaphore_wait(barrier, len(routes))


class Copies:
    def __init__(self, send, recv):
        self.send, self.recv, self.count = send, recv, 0

    def __call__(self, src, dst, to):
        k, self.count = self.count, self.count + 1
        return pltpu.make_async_remote_copy(
            src_ref=src,
            dst_ref=dst,
            send_sem=self.send.at[k],
            recv_sem=self.recv.at[k],
            device_id=device(*to(*place())),
            device_id_type=MESH,
        )


def comm_call(kernel, name, ident, ins, outs, copies, locals_=0):
    return pl.pallas_call(
        kernel,
        out_shape=outs,
        in_specs=[pl.BlockSpec(memory_space=pl.ANY)] * len(ins),
        out_specs=[pl.BlockSpec(memory_space=pl.ANY)] * len(outs),
        scratch_shapes=[
            pltpu.SemaphoreType.DMA((copies,)),
            pltpu.SemaphoreType.DMA((copies,)),
            pltpu.SemaphoreType.DMA((max(locals_, 1),)),
        ],
        name=name,
        compiler_params=pltpu.CompilerParams(collective_id=ident, has_side_effects=True),
    )(*ins)


def struct(shape, dtype=BF16):
    return jax.ShapeDtypeStruct(shape, dtype)


class RingGather:
    def __init__(self, copy, own, dst, y):
        half = dst.shape[2] // 2
        lo, hi = pl.ds(0, half), pl.ds(half, half)
        back, on = (y + 3) % 4, (y + 1) % 4

        def first(cols, to):
            return copy(own.at[:, cols], dst.at[y, :, cols], to)

        def one(slot, cols, to):
            at = dst.at[slot, :, cols]
            return copy(at, at, to)

        self.first = [first(lo, along_y(1)), first(hi, along_y(3)), first(hi, along_y(1)), first(lo, along_y(3))]
        self.second = [one(back, lo, along_y(1)), one(on, hi, along_y(3))]

    def start(self):
        for cp in self.first:
            cp.start()

    def turn(self):
        for got, cp in zip(self.first, self.second):
            got.wait_recv()
            cp.start()

    def near(self):
        for cp in self.first[2:]:
            cp.wait_recv()

    def far(self):
        for cp in self.second:
            cp.wait_recv()

    def sent(self):
        for cp in self.first + self.second:
            cp.wait_send()


class RingSum:
    def __init__(self, copy, part, halves, whole, y):
        half = part.shape[2] // 2
        lo, hi = pl.ds(0, half), pl.ds(half, half)
        self.part, self.halves, self.whole, self.y = part, halves, whole, y
        self.cols = (lo, hi)
        far, on, back = (y + 2) % 4, (y + 1) % 4, (y + 3) % 4
        self.far = [
            copy(part.at[far, :, lo], halves.at[0], along_y(1)),
            copy(part.at[far, :, hi], halves.at[1], along_y(3)),
        ]
        self.near = [
            copy(part.at[on, :, hi], whole.at[0, :, hi], along_y(1)),
            copy(part.at[back, :, lo], whole.at[1, :, lo], along_y(3)),
        ]
        self.last = [
            copy(part.at[on, :, lo], whole.at[0, :, lo], along_y(1)),
            copy(part.at[back, :, hi], whole.at[1, :, hi], along_y(3)),
        ]
        self.slots = (on, back)

    def start(self):
        for cp in self.far + self.near:
            cp.start()

    def turn(self):
        for k in range(2):
            self.far[k].wait_recv()
            slot, cols = self.slots[k], self.cols[k]

            def body(r, _, slot=slot, cols=cols, k=k):
                rows = pl.ds(r * 32, 32)
                both = self.part[slot, rows, cols].astype(F32) + self.halves[k, rows].astype(F32)
                self.part[slot, rows, cols] = both.astype(BF16)
                return 0

            lax.fori_loop(0, self.part.shape[1] // 32, body, 0)
            self.last[k].start()

    def finish(self):
        for cp in self.near + self.last:
            cp.wait_recv()

    def rows(self, rows):
        own = self.part[self.y, rows].astype(F32)
        return own + self.whole[0, rows].astype(F32) + self.whole[1, rows].astype(F32)

    def sent(self):
        for cp in self.far + self.near + self.last:
            cp.wait_send()


def ring_sum(part, ident, name):
    rows, cols = part.shape[0] // 4, part.shape[1]

    def kernel(src, dst, work, halves, whole, send, recv, local):
        y = place()[2]
        load = pltpu.make_async_copy(src, work, local.at[0])
        load.start()
        greet([along_y(1), along_y(3)], False)
        load.wait()
        ring = RingSum(Copies(send, recv), work, halves, whole, y)
        ring.start()
        ring.turn()
        ring.finish()

        def body(r, _):
            at = pl.ds(r * 32, 32)
            dst[at] = ring.rows(at)
            return 0

        lax.fori_loop(0, rows // 32, body, 0)
        ring.sent()

    return pl.pallas_call(
        kernel,
        out_shape=struct((rows, cols), F32),
        in_specs=[pl.BlockSpec(memory_space=pl.ANY)],
        out_specs=pl.BlockSpec(memory_space=pltpu.VMEM),
        scratch_shapes=[
            pltpu.VMEM((4, rows, cols), BF16),
            pltpu.VMEM((2, rows, cols // 2), BF16),
            pltpu.VMEM((2, rows, cols), BF16),
            pltpu.SemaphoreType.DMA((6,)),
            pltpu.SemaphoreType.DMA((6,)),
            pltpu.SemaphoreType.DMA((1,)),
        ],
        name=name,
        compiler_params=pltpu.CompilerParams(
            collective_id=ident, has_side_effects=True, vmem_limit_bytes=VMEM_LIMIT
        ),
    )(part.reshape(4, rows, cols))


def ring_gather(part, ident, name):
    def kernel(src, dst, send, recv, local):
        y = place()[2]
        own = pltpu.make_async_copy(src, dst.at[y], local.at[0])
        own.start()
        greet([along_y(1), along_y(3)], False)
        ring = RingGather(Copies(send, recv), src, dst, y)
        ring.start()
        ring.turn()
        ring.near()
        ring.far()
        ring.sent()
        own.wait()

    return pl.pallas_call(
        kernel,
        out_shape=struct((4,) + part.shape, part.dtype),
        in_specs=[pl.BlockSpec(memory_space=pltpu.VMEM)],
        out_specs=pl.BlockSpec(memory_space=pl.ANY),
        scratch_shapes=[
            pltpu.SemaphoreType.DMA((6,)),
            pltpu.SemaphoreType.DMA((6,)),
            pltpu.SemaphoreType.DMA((1,)),
        ],
        name=name,
        compiler_params=pltpu.CompilerParams(collective_id=ident, has_side_effects=True),
    )(part)


class Gather:
    def __init__(self, copy, out, a, at, rows_only=False):
        xh, xl, y, z, c = at
        cols = out.shape[-1]
        left, right = pl.ds(0, a), pl.ds(a, cols - a)
        def cut(half, n):
            return slice(None) if half is None else pl.ds(half * (n // 2), n // 2)

        if rows_only:
            block = lambda z, x, c, cols: out.at[x[0], c, x[1], z, :, cols]
            z_line = lambda x, c, cols, half: out.at[x[0], c, x[1], cut(half, 4), :, cols]
            x_line = lambda z, c, cols, half: out.at[cut(half, 2), c, :, z, :, cols]
        else:
            block = lambda z, x, c, cols: out.at[z, x[0], c, pl.ds(x[1] * 64, 64), cols]
            z_line = lambda x, c, cols, half: out.at[cut(half, 4), x[0], c, pl.ds(x[1] * 64, 64), cols]
            x_line = lambda z, c, cols, half: out.at[z, cut(half, 2), c, :, cols]

        def same(ref, to):
            return copy(ref, ref, to)

        here = (xh, xl)
        self.first = []
        for d in (1, 3, 2):
            self.first.append(same(block(z, here, c, left), along_x(d)))
            self.first.append(same(block(z, here, c, right), along_z(d)))
        a_lo, a_hi = lambda z: x_line(z, c, left, 0), lambda z: x_line(z, c, left, 1)
        b_lo, b_hi = lambda x: z_line(x, c, right, 0), lambda x: z_line(x, c, right, 1)
        z_at = [(z + d) % 4 for d in range(4)]
        x_at = [along_x(d)(*at)[:2] for d in range(4)]
        self.lines = []
        for lo, hi, spots, along in ((a_lo, a_hi, z_at, along_z), (b_lo, b_hi, x_at, along_x)):
            going = [
                same(lo(spots[0]), along(1)),
                same(hi(spots[0]), along(3)),
                same(hi(spots[0]), along(1)),
                same(lo(spots[0]), along(3)),
            ]
            on = [same(lo(spots[3]), along(1)), same(hi(spots[1]), along(3))]
            self.lines.append((going, on))
        self.core = [same(block(z, here, c, pl.ds(0, cols)), sibling)]
        for d in (1, 3, 2):
            self.core.append(same(block(z, x_at[d], c, left), sibling))
            self.core.append(same(block(z_at[d], here, c, right), sibling))
        self.core_lines = []
        for d in (3, 1, 2):
            self.core_lines.append(
                (same(x_line(z_at[d], c, left, None), sibling), same(z_line(x_at[d], c, right, None), sibling))
            )

    def start(self):
        for cp in self.first:
            cp.start()
        self.core[0].start()

    def turn(self):
        for cp in self.first:
            cp.wait_recv()
        for going, _ in self.lines:
            for cp in going:
                cp.start()
        for cp in self.core[1:]:
            cp.start()

    def pass_on(self):
        for going, on in self.lines:
            for got, cp in zip(going[:2], on):
                got.wait_recv()
                cp.start()

    def near(self):
        for k, (going, _) in enumerate(self.lines):
            for side in range(2):
                going[2 + side].wait_recv()
                self.core_lines[side][k].start()

    def far(self):
        for k, (_, on) in enumerate(self.lines):
            for cp in on:
                cp.wait_recv()
            self.core_lines[2][k].start()

    def finish(self):
        for cp in self.core + [cp for pair in self.core_lines for cp in pair]:
            cp.wait_recv()

    def sent(self):
        for going, on in self.lines:
            for cp in going + on:
                cp.wait_send()
        for cp in self.first + self.core + [cp for pair in self.core_lines for cp in pair]:
            cp.wait_send()


def dot(left, right, dims=((1,), (0,))):
    return lax.dot_general(left, right, (dims, ((), ())), preferred_element_type=F32)


def swap_halves(v):
    lane = lax.broadcasted_iota(jnp.int32, v.shape, 1)
    return jnp.where(lane % 64 < 32, pltpu.roll(v, 96, 1), pltpu.roll(v, 32, 1))


def forward_attention(tokens, cotangent, spots, freqs, w_proj, w_gu, w_down, out_rows, ident):
    rows = tokens.shape[0]
    count = 4 * rows
    groups = [w_proj, w_gu, w_down]

    def kernel(
        tok_ref, cot_ref, spot_ref, freq_ref, wp, wg, wd, wo,
        normed_out, cot_all, gp, gg, gd, go, q_out, kv_out, att_out, lse_out, spot_out, middle_out, two_all,
        tok, normed, wp_v, wo_v, q_s, kv, vx, bias, att, part, halves, whole, spot_all, own_two, send, recv, local,
    ):
        at = place()
        xh, xl, y, z, c = at
        copy = Copies(send, recv)
        slot = pl.ds(xl * 64 + y * 16, 16)
        nlocal = [0]

        def near(src, dst):
            cp = pltpu.make_async_copy(src, dst, local.at[nlocal[0]])
            nlocal[0] += 1
            return cp

        to_y = []
        stay = []
        for i, o in ((wp, gp), (wg, gg), (wd, gd)):
            to_y.append([copy(i.at[(y + d) % 4], o.at[z, xh, c, slot], along_y(d)) for d in (1, 3, 2)])
            stay.append(near(i.at[y], o.at[z, xh, c, slot]))
        over = copy(wo, go.at[xh, c, xl, y], crossed)
        keep = near(wo, go.at[xh, c, xl, z])
        spot_copies = [copy(spot_all.at[y], spot_all.at[y], along_y(d)) for d in (1, 3, 2)]
        tok_ring = RingGather(copy, tok_ref, tok, y)
        cot_ring = RingGather(copy, cot_ref, cot_all, y)
        two_ring = RingGather(copy, own_two, two_all, y)
        branch = RingSum(copy, part, halves, whole, y)
        kv_copy = copy(kv.at[1], kv.at[0], half_partner)
        g_proj = Gather(copy, gp, SPLITS[0][1], at)
        g_gu = Gather(copy, gg, SPLITS[1][1], at)
        g_down = Gather(copy, gd, SPLITS[2][1], at)
        g_out = Gather(copy, go, OUT_SPLIT, at, True)

        cot_own = near(cot_ref, cot_all.at[y])
        tok_own = near(tok_ref, tok.at[y])
        tok_own.start()
        cot_own.start()
        spot_all[y] = spot_ref[...]
        for cp in stay:
            cp.start()
        greet(
            [along_y(d) for d in (1, 2, 3)]
            + [along_x(d) for d in (1, 2, 3)]
            + [along_z(d) for d in (1, 2, 3)]
            + [sibling],
            True,
        )
        away = y != z
        for cp in to_y[0]:
            cp.start()

        @pl.when(away)
        def _():
            over.start()

        @pl.when(jnp.logical_not(away))
        def _():
            keep.start()

        tok_ring.start()
        for cp in spot_copies + to_y[1] + to_y[2]:
            cp.start()

        def norm_block(k):
            def body(r, _):
                rs = pl.ds(r * 32, 32)
                v = tok[k, rs].astype(F32)
                inv = lax.rsqrt(jnp.mean(v * v, -1, keepdims=True) + EPS)
                normed[k, rs] = (v * inv).astype(BF16)
                return 0

            lax.fori_loop(0, rows // 32, body, 0)

        stay[0].wait()
        for cp in to_y[0]:
            cp.wait_recv()
        g_proj.start()

        @pl.when(away)
        def _():
            over.wait()

        @pl.when(jnp.logical_not(away))
        def _():
            keep.wait()

        g_out.start()
        tok_own.wait()
        norm_block(y)
        g_proj.turn()
        tok_ring.turn()
        g_proj.pass_on()
        g_out.turn()
        for cp in spot_copies:
            cp.wait_recv()

        cos, sin = [], []
        freq, sign = freq_ref[0:1, :], freq_ref[1:2, :]
        spot_cols = []
        for k in range(4):
            col = jnp.transpose(jnp.broadcast_to(spot_all[k, 0:1, :], (128, 128)))
            spot_out[k] = spot_all[k]
            spot_cols.append(col)
            cos.append(jnp.cos(col * freq))
            sin.append(jnp.sin(col * freq) * sign)
        cos, sin = jnp.concatenate(cos, 0), jnp.concatenate(sin, 0)
        low_half = xl == 0
        reach = jnp.where(low_half, -1.0, 2048.0)
        for k in range(4):
            for j in range(8):
                row = lax.broadcasted_iota(jnp.int32, (128, 128), 0) + k * 128
                col = lax.broadcasted_iota(jnp.int32, (128, 128), 1) + j * 128
                apart = (row - col + 512).astype(F32)
                seen = apart <= spot_cols[k]
                if j < 4:
                    seen = seen & (apart <= reach)
                else:
                    seen = seen & (col - 512 <= row)
                bias[pl.ds(k * 128, 128), pl.ds(j * 128, 128)] = jnp.where(seen, 0.0, NEG_FILL)

        g_proj.near()
        stay[1].wait()
        stay[2].wait()
        for cp in to_y[1] + to_y[2]:
            cp.wait_recv()
        g_gu.start()
        g_down.start()
        g_proj.far()
        g_out.pass_on()
        tok_ring.near()
        norm_block((y + 3) % 4)
        norm_block((y + 1) % 4)
        g_proj.finish()
        wp_load = near(gp, wp_v)
        wp_load.start()
        g_out.near()
        tok_ring.far()
        cot_ring.start()
        norm_block((y + 2) % 4)
        normed_save = near(normed, normed_out)
        normed_save.start()

        wp_load.wait()
        left = normed[...].reshape(count, D)
        lane = lax.broadcasted_iota(jnp.int32, (count, 128), 1)
        upper = lane >= 64
        raw = dot(left, wp_v[:, :, :, :, pl.ds(Q_COLS, 128)].reshape(D, 128))
        turned = raw * jnp.where(upper, 1.0, cos) + swap_halves(raw) * jnp.where(upper, 0.0, sin)
        kv[1] = turned.astype(BF16)
        kv_copy.start()
        g_out.far()
        g_gu.turn()
        g_down.turn()
        for j in range(2):
            raw2 = dot(left, wp_v[:, :, :, :, pl.ds(j * 256, 256)].reshape(D, 256))
            for e in range(2):
                raw = raw2[:, e * 128 : e * 128 + 128]
                turned = (raw * cos + swap_halves(raw) * sin).astype(BF16).astype(F32) * (HEAD_DIM ** (-0.5))
                pair = j * 2 + e
                q_s[2 * pair] = jnp.where(upper, 0.0, turned).astype(BF16)
                q_s[2 * pair + 1] = jnp.where(upper, 0.0, pltpu.roll(turned, 64, 1)).astype(BF16)
        kv_copy.wait_recv()
        for k in range(2):
            vx[k] = jnp.where(upper, kv[k].astype(F32), 1.0).astype(BF16)
        q_save = near(q_s, q_out)
        q_save.start()
        kv_save = near(kv, kv_out)
        kv_save.start()
        g_out.finish()
        wo_load = near(go, wo_v)
        wo_load.start()
        cot_ring.turn()

        def attend(pair):
            for b in range(2):
                rs = pl.ds(b * 256, 256)
                seen = 256 * (b + 1)
                lane = lax.broadcasted_iota(jnp.int32, (256, 128), 1) < 64
                found = []
                for e in range(2):
                    q = q_s[2 * pair + e, rs]
                    s0 = dot(q, kv[0], NT) + bias[rs, pl.ds(0, 512)]
                    s1 = dot(q, kv[1, pl.ds(0, seen)], NT) + bias[rs, pl.ds(512, seen)]
                    m = jnp.maximum(jnp.max(s0, -1, keepdims=True), jnp.max(s1, -1, keepdims=True))
                    p0 = jnp.exp(s0 - m).astype(BF16)
                    p1 = jnp.exp(s1 - m).astype(BF16)
                    o = dot(p0, vx[0]) + dot(p1, vx[1, pl.ds(0, seen)])
                    r = pltpu.roll(o, 64, 1)
                    found.append((o, r))
                    log_total = m + jnp.log(jnp.where(lane, o, r))
                    lse_out[2 * pair + e, :, rs] = jnp.transpose(log_total)[0:8]
                (o, r), (o2, r2) = found
                both = jnp.where(lane, r / o, o2 / r2)
                att[rs, pl.ds(pl.multiple_of(pair * 128, 128), 128)] = both.astype(BF16)

        def two_pairs(k):
            def body(i, _):
                attend(2 * k + i)
                return 0

            lax.fori_loop(0, 2, body, 0)

        two_pairs(0)
        g_gu.pass_on()
        g_down.pass_on()
        two_pairs(1)
        att_save = near(att, att_out)
        att_save.start()
        wo_load.wait()

        for j in range(4):
            cols = pl.ds(j * 512, 512)
            w = wo_v[:, :, :, :, :, cols].reshape(Q_COLS, 512)
            part[:, :, cols] = dot(att[...], w).astype(BF16).reshape(4, rows, 512)
        branch.start()
        g_gu.near()
        g_down.near()
        branch.turn()
        cot_ring.near()
        cot_ring.far()
        branch.finish()

        def mid(r, _):
            rs = pl.ds(r * 32, 32)
            v = tok_ref[rs].astype(F32) + branch.rows(rs)
            middle_out[rs] = v
            inv = lax.rsqrt(jnp.mean(v * v, -1, keepdims=True) + EPS)
            own_two[rs] = (v * inv).astype(BF16)
            return 0

        lax.fori_loop(0, rows // 32, mid, 0)
        two_own = near(own_two, two_all.at[y])
        two_own.start()
        two_ring.start()
        g_gu.far()
        g_down.far()
        two_ring.turn()
        two_ring.near()
        two_ring.far()
        g_gu.finish()
        g_down.finish()
        for cp in (cot_own, normed_save, q_save, kv_save, att_save, two_own):
            cp.wait()
        for group in to_y:
            for cp in group:
                cp.wait_send()
        for cp in spot_copies + [kv_copy]:
            cp.wait_send()
        for thing in (g_proj, g_out, g_gu, g_down, tok_ring, cot_ring, two_ring, branch):
            thing.sent()

    anywhere, vmem = pl.BlockSpec(memory_space=pl.ANY), pl.BlockSpec(memory_space=pltpu.VMEM)
    outs = [
        (struct((4, rows, D)), anywhere),
        (struct((4, rows, D)), anywhere),
        (struct((4, 2, 2, 128, PROJ)), anywhere),
        (struct((4, 2, 2, 128, 2 * HID)), anywhere),
        (struct((4, 2, 2, 128, HID)), anywhere),
        (struct((2, 2, 2, 4, 16, D)), anywhere),
        (struct((REPEAT, count, 128)), anywhere),
        (struct((2, count, 128)), anywhere),
        (struct((count, Q_COLS)), anywhere),
        (struct((REPEAT, 8, count), F32), vmem),
        (struct((4, 8, 128), F32), vmem),
        (struct((rows, D), F32), vmem),
        (struct((4, rows, D)), anywhere),
    ]
    copies = 9 + 1 + 3 + 6 * 3 + 6 + 1 + 31 * 4
    return pl.pallas_call(
        kernel,
        out_shape=[o[0] for o in outs],
        in_specs=[vmem] * 8,
        out_specs=[o[1] for o in outs],
        scratch_shapes=[
            pltpu.VMEM((4, rows, D), BF16),
            pltpu.VMEM((4, rows, D), BF16),
            pltpu.VMEM((4, 2, 2, 128, PROJ), BF16),
            pltpu.VMEM((2, 2, 2, 4, 16, D), BF16),
            pltpu.VMEM((REPEAT, count, 128), BF16),
            pltpu.VMEM((2, count, 128), BF16),
            pltpu.VMEM((2, count, 128), BF16),
            pltpu.VMEM((count, 2 * count), F32),
            pltpu.VMEM((count, Q_COLS), BF16),
            pltpu.VMEM((4, rows, D), BF16),
            pltpu.VMEM((2, rows, D // 2), BF16),
            pltpu.VMEM((2, rows, D), BF16),
            pltpu.VMEM((4, 8, 128), F32),
            pltpu.VMEM((rows, D), BF16),
            pltpu.SemaphoreType.DMA((copies,)),
            pltpu.SemaphoreType.DMA((copies,)),
            pltpu.SemaphoreType.DMA((16,)),
        ],
        name="forward_attention",
        compiler_params=pltpu.CompilerParams(
            collective_id=ident, has_side_effects=True, vmem_limit_bytes=VMEM_LIMIT
        ),
    )(tokens, cotangent, spots, freqs, w_proj, w_gu, w_down, out_rows)


def tiles(ref):
    if len(ref.shape) == 2:
        return [ref]
    return [t for k in range(ref.shape[0]) for t in tiles(ref.at[k])]


def add_up(dst, *others):
    for out, *terms in zip(tiles(dst), *[tiles(o) for o in others]):
        rows = out.shape[0]
        step = min(rows, 32)

        def body(r, _, out=out, terms=terms, step=step):
            rs = pl.ds(r * step, step)
            value = out[rs].astype(F32)
            for t in terms:
                value = value + t[rs].astype(F32)
            out[rs] = value.astype(BF16)
            return 0

        lax.fori_loop(0, rows // step, body, 0)


class LineSum:
    def __init__(self, copy, lo, hi, along, far, near):
        self.lo, self.hi, self.far_in, self.near_in = lo, hi, far, near
        self.far = [copy(lo(2), far.at[0], along(1)), copy(hi(2), far.at[1], along(3))]
        self.near = [copy(hi(1), near.at[0, 1], along(1)), copy(lo(3), near.at[1, 0], along(3))]
        self.last = [copy(lo(1), near.at[0, 0], along(1)), copy(hi(3), near.at[1, 1], along(3))]

    def start(self):
        for cp in self.far + self.near:
            cp.start()

    def turn(self):
        self.far[0].wait_recv()
        add_up(self.lo(1), self.far_in.at[0])
        self.last[0].start()
        self.far[1].wait_recv()
        add_up(self.hi(3), self.far_in.at[1])
        self.last[1].start()

    def finish(self):
        for cp in self.near + self.last:
            cp.wait_recv()
        add_up(self.lo(0), self.near_in.at[0, 0], self.near_in.at[1, 0])
        add_up(self.hi(0), self.near_in.at[0, 1], self.near_in.at[1, 1])

    def sent(self):
        for cp in self.far + self.near + self.last:
            cp.wait_send()


class GradSum:
    def __init__(self, copy, local_copy, terms, out, a, at, buffers, rows_only=False):
        xh, xl, y, z, c = at
        self.at, self.rows_only = at, rows_only
        far_a, near_a, far_b, near_b, got_a, got_b, own = buffers
        cols = terms.shape[-1]
        left, right = pl.ds(0, a), pl.ds(a, cols - a)
        x_at = [along_x(d)(*at)[:2] for d in range(4)]
        z_at = [(z + d) % 4 for d in range(4)]
        if rows_only:
            spot = lambda x, z, cols: terms.at[x[0], c, x[1], z, :, cols]
            a_half = lambda h: lambda d: terms.at[h, c, :, z_at[d], :, left]
            b_half = lambda h: lambda d: terms.at[x_at[d][0], c, x_at[d][1], pl.ds(2 * h, 2), :, right]
        else:
            base = (lambda z, xh: (z, xh, c)) if len(terms.shape) == 5 else (lambda z, xh: (z, xh))
            spot = lambda x, z, cols: terms.at[base(z, x[0]) + (pl.ds(x[1] * 64, 64), cols)]
            a_half = lambda h: lambda d: terms.at[base(z_at[d], h) + (slice(None), left)]
            b_half = lambda h: lambda d: terms.at[
                base(pl.ds(2 * h, 2), x_at[d][0]) + (pl.ds(x_at[d][1] * 64, 64), right)
            ]
        self.lines = [
            LineSum(copy, a_half(0), a_half(1), along_z, far_a, near_a),
            LineSum(copy, b_half(0), b_half(1), along_x, far_b, near_b),
        ]
        here = x_at[0]
        self.second = []
        for d in (1, 3, 2):
            self.second.append(copy(spot(x_at[d], z, left), got_a.at[d - 1], along_x(d)))
            self.second.append(copy(spot(here, z_at[d], right), got_b.at[d - 1], along_z(d)))
        self.mine = (spot(here, z, left), spot(here, z, right))
        self.got = (got_a, got_b)
        self.own, self.cuts = own, (left, right)
        if rows_only:
            self.over = copy(own, out, crossed)
            self.keep = local_copy(own, out)
        else:
            self.to_y = [copy(own.at[(y + d) % 4], out.at[y], along_y(d)) for d in (1, 3, 2)]
            self.keep = local_copy(own.at[y], out.at[y])

    def start(self):
        for line in self.lines:
            line.start()

    def turn(self):
        for line in self.lines:
            line.turn()

    def cross(self):
        for line in self.lines:
            line.finish()
        for cp in self.second:
            cp.start()

    def deliver(self):
        for cp in self.second:
            cp.wait_recv()
        for mine, got, cut in zip(self.mine, self.got, self.cuts):
            value = mine[...].astype(F32)
            for d in range(3):
                value = value + got[d].astype(F32)
            own = self.own
            if self.rows_only:
                own[:, cut] = value.astype(BF16)
            else:
                own[:, :, cut] = value.astype(BF16).reshape(4, 16, value.shape[-1])
        if self.rows_only:
            y, z = self.at[2], self.at[3]

            @pl.when(y != z)
            def _():
                self.over.start()

            @pl.when(y == z)
            def _():
                self.keep.start()

        else:
            for cp in self.to_y:
                cp.start()
            self.keep.start()

    def finish(self):
        if self.rows_only:
            y, z = self.at[2], self.at[3]

            @pl.when(y != z)
            def _():
                self.over.wait()

            @pl.when(y == z)
            def _():
                self.keep.wait()

        else:
            for cp in self.to_y:
                cp.wait()
            self.keep.wait()
        for line in self.lines:
            line.sent()
        for cp in self.second:
            cp.wait_send()


def grad_buffers(cols, a, rows_only=False):
    b = cols - a
    if rows_only:
        a_half, b_half, spot, own = (2, 16), (2, 16), 16, (16, cols)
    else:
        a_half, b_half, spot, own = (128,), (2, 64), 64, (4, 16, cols)
    return [
        pltpu.VMEM((2,) + a_half + (a,), BF16),
        pltpu.VMEM((2, 2) + a_half + (a,), BF16),
        pltpu.VMEM((2,) + b_half + (b,), BF16),
        pltpu.VMEM((2, 2) + b_half + (b,), BF16),
        pltpu.VMEM((3, spot, a), BF16),
        pltpu.VMEM((3, spot, b), BF16),
        pltpu.VMEM(own, BF16),
    ]


def rotation(spot_rows, freq_ref):
    cos, sin = [], []
    for k in range(4):
        col = jnp.transpose(jnp.broadcast_to(spot_rows[k, 0:1, :], (128, 128)))
        cos.append(jnp.cos(col * freq_ref[0:1, :]))
        sin.append(jnp.sin(col * freq_ref[0:1, :]) * freq_ref[1:2, :])
    return jnp.concatenate(cos, 0), jnp.concatenate(sin, 0)


def backward_attention(
    sum_gu, sum_down, out_part, branch_all, grad_middle, middle, tokens, freqs,
    spots, q_all, kv_all, attended, lse, normed_all, proj_w, out_w, ident,
):
    rows = tokens.shape[0]
    count = 4 * rows
    scale = HEAD_DIM ** (-0.5)

    def kernel(
        s_gu, s_down, op_ref, br_ref, gm_ref, mid_ref, tok_ref, freq_ref,
        spot_ref, q_ref, kv_ref, att_ref, lse_ref, nm_ref, wp_ref, wo_ref,
        out_ref, ig_ref, o_proj, o_gu, o_down, o_out,
        v_gu, v_down, part, halves, whole, halves2, whole2, br, q_s, do_s, kv, kvt, att, delta, bias, cos_s, sin_s,
        dkv, kv_send, kv_in, gp, normed, wp, wo, t_proj, rc_proj, t_out, rc_out, *rest,
    ):
        bufs, (send, recv, local) = rest[:28], rest[28:]
        at = place()
        xh, xl, y, z, c = at
        copy = Copies(send, recv)
        nlocal = [0]

        def near(src, dst):
            cp = pltpu.make_async_copy(src, dst, local.at[nlocal[0]])
            nlocal[0] += 1
            return cp

        load_gu, load_down = near(s_gu, v_gu), near(s_down, v_down)
        load_op, load_br, load_wo = near(op_ref, part), near(br_ref, br), near(wo_ref, wo)
        load_att, load_q = near(att_ref, att), near(q_ref, q_s)
        load_kv = near(kv_ref, kv)
        load_nm, load_wp = near(nm_ref, normed), near(wp_ref, wp)
        for cp in (load_gu, load_op, load_down, load_br, load_wo, load_att, load_q, load_kv, load_nm, load_wp):
            cp.start()
        outs = RingSum(copy, part, halves, whole, y)
        ones = RingSum(copy, part, halves2, whole2, y)
        kv_copy = copy(kv_send, kv_in, half_partner)
        core_proj = copy(t_proj.at[:, :, 1 - c], rc_proj, sibling)
        core_out = copy(t_out.at[:, 1 - c], rc_out, sibling)
        g_gu = GradSum(copy, near, v_gu, o_gu, SPLITS[1][1], at, bufs[0:7])
        g_down = GradSum(copy, near, v_down, o_down, SPLITS[2][1], at, bufs[7:14])
        g_proj = GradSum(copy, near, t_proj, o_proj, SPLITS[0][1], at, bufs[14:21])
        g_out = GradSum(copy, near, t_out, o_out, OUT_SPLIT, at, bufs[21:28], True)
        greet(
            [along_y(d) for d in (1, 2, 3)]
            + [along_x(d) for d in (1, 2, 3)]
            + [along_z(d) for d in (1, 2, 3)]
            + [sibling],
            True,
        )
        load_gu.wait()
        g_gu.start()
        load_op.wait()
        outs.start()
        load_down.wait()
        g_down.start()

        cos, sin = rotation(spot_ref, freq_ref)
        cos_s[...] = cos
        sin_s[...] = sin
        reach = jnp.where(xl == 0, -1.0, 2048.0)
        for k in range(4):
            spots_row = spot_ref[k, 0:1, :]
            for j in range(8):
                key = lax.broadcasted_iota(jnp.int32, (128, 128), 0) + j * 128
                row = lax.broadcasted_iota(jnp.int32, (128, 128), 1) + k * 128
                apart = (row - key + 512).astype(F32)
                seen = apart <= spots_row
                if j < 4:
                    seen = seen & (apart <= reach)
                else:
                    seen = seen & (key - 512 <= row)
                bias[pl.ds(j * 128, 128), pl.ds(k * 128, 128)] = jnp.where(seen, 0.0, NEG_FILL)
        dkv[...] = jnp.zeros_like(dkv)

        load_br.wait()
        load_wo.wait()
        load_att.wait()
        lane = lax.broadcasted_iota(jnp.int32, (count, 128), 1)
        for p in range(4):
            w = wo[p // 2, p % 2].reshape(128, D)
            low = dot(br[...].reshape(count, D), w, NT).astype(BF16).astype(F32)
            do_s[2 * p] = jnp.where(lane < 64, 0.0, pltpu.roll(low, 64, 1)).astype(BF16)
            do_s[2 * p + 1] = jnp.where(lane < 64, 0.0, low).astype(BF16)
            prod = jnp.transpose(low * att[:, pl.ds(p * 128, 128)].astype(F32))
            for e in range(2):
                total_row = jnp.sum(prod[e * 64 : e * 64 + 64], 0, keepdims=True)
                delta[2 * p + e] = jnp.broadcast_to(total_row, (8, count))
        outs.turn()

        for k in range(4):
            term = dot(att[:, pl.ds(k * 128, 128)], br[...].reshape(count, D), TN)
            t_out[k // 2, k % 2] = term.astype(BF16).reshape(2, 4, 16, D)
        core_out.start()
        load_q.wait()
        load_kv.wait()
        for k in range(2):
            turned = jnp.transpose(kv[pl.ds(k * count, count)].astype(F32)).astype(BF16)
            kvt[:, pl.ds(k * count, count)] = turned

        def backward(pair):
            for b in range(2):
                rs = pl.ds(b * 256, 256)
                seen = pl.ds(0, 512 + 256 * (b + 1))
                found = []
                for e in range(2):
                    h = 2 * pair + e
                    q, do = q_s[h, rs], do_s[h, rs]
                    st = dot(kv[seen], q, NT) + bias[seen, rs] - lse_ref[h, 0:1, rs]
                    p = jnp.exp(st)
                    dp = dot(kv[seen], do, NT)
                    ds = (p * (dp - delta[h, 0:1, rs])).astype(BF16)
                    dkv[seen] += dot(ds, q) + dot(p.astype(BF16), do)
                    found.append(dot(kvt[:, seen], ds)[0:64])
                both = jnp.transpose(jnp.concatenate(found, 0)) * scale
                both = both * cos_s[rs] - swap_halves(both) * sin_s[rs]
                gp[rs, pl.ds(pl.multiple_of(pair * 128, 128), 128)] = both.astype(BF16)

        def two_pairs(k):
            def body(i, _):
                backward(2 * k + i)
                return 0

            lax.fori_loop(0, 2, body, 0)

        two_pairs(0)
        g_gu.turn()
        g_down.turn()
        two_pairs(1)
        kv_send[...] = dkv[pl.ds(0, count)].astype(BF16)
        kv_copy.start()
        core_out.wait_recv()
        add_up(t_out.at[:, c], rc_out)
        g_out.start()
        outs.finish()

        def finish_out(r, _):
            rs = pl.ds(r * 32, 32)
            out_ref[rs] = (mid_ref[rs] + outs.rows(rs)).astype(BF16)
            return 0

        lax.fori_loop(0, rows // 32, finish_out, 0)
        outs.sent()
        kv_copy.wait_recv()
        got = dkv[pl.ds(count, count)] + kv_in[...].astype(F32)
        back = got * cos_s[...] - swap_halves(got) * sin_s[...]
        gp[:, pl.ds(Q_COLS, 128)] = jnp.where(lane < 64, back, got).astype(BF16)

        load_wp.wait()
        for j in range(4):
            w = wp[j].reshape(512, PROJ)
            part[:, :, pl.ds(j * 512, 512)] = dot(gp[...], w, NT).astype(BF16).reshape(4, rows, 512)
        ones.start()
        load_nm.wait()
        for k in range(4):
            left = normed[:, :, pl.ds(k * 512, 512)].reshape(count, 512)
            t_proj[k] = dot(left, gp[...], TN).astype(BF16).reshape(2, 2, 128, PROJ)
        core_proj.start()
        g_gu.cross()
        g_down.cross()
        ones.turn()
        g_out.turn()
        core_proj.wait_recv()
        for k in range(4):
            add_up(t_proj.at[k, :, c], rc_proj.at[k])
        g_proj.start()
        g_gu.deliver()
        g_down.deliver()
        g_proj.turn()
        g_out.cross()
        ones.finish()

        def finish_in(r, _):
            rs = pl.ds(r * 32, 32)
            v = tok_ref[rs].astype(F32)
            inv = lax.rsqrt(jnp.mean(v * v, -1, keepdims=True) + EPS)
            v = v * inv
            g = ones.rows(rs)
            ig_ref[rs] = gm_ref[rs] + inv * (g - v * jnp.mean(g * v, -1, keepdims=True))
            return 0

        lax.fori_loop(0, rows // 32, finish_in, 0)
        g_proj.cross()
        g_out.deliver()
        g_proj.deliver()
        ones.sent()
        for cp in (kv_copy, core_proj, core_out):
            cp.wait_send()
        for g in (g_gu, g_down, g_out, g_proj):
            g.finish()

    anywhere, vmem = pl.BlockSpec(memory_space=pl.ANY), pl.BlockSpec(memory_space=pltpu.VMEM)
    in_specs = [anywhere] * 4 + [vmem] * 5 + [anywhere] * 3 + [vmem] + [anywhere] * 3
    outs = [
        (struct((rows, D)), vmem),
        (struct((rows, D), F32), vmem),
        (struct((4, 16, PROJ)), anywhere),
        (struct((4, 16, 2 * HID)), anywhere),
        (struct((4, 16, HID)), anywhere),
        (struct((16, D)), anywhere),
    ]
    whole = lambda: [pltpu.VMEM((2, rows, D // 2), BF16), pltpu.VMEM((2, rows, D), BF16)]
    copies = 12 + 3 + 21 * 3 + 19
    return pl.pallas_call(
        kernel,
        out_shape=[o[0] for o in outs],
        in_specs=in_specs,
        out_specs=[o[1] for o in outs],
        scratch_shapes=[
            pltpu.VMEM((4, 2, 128, 2 * HID), BF16),
            pltpu.VMEM((4, 2, 128, HID), BF16),
            pltpu.VMEM((4, rows, D), BF16),
            *whole(),
            *whole(),
            pltpu.VMEM((4, rows, D), BF16),
            pltpu.VMEM((REPEAT, count, 128), BF16),
            pltpu.VMEM((REPEAT, count, 128), BF16),
            pltpu.VMEM((2 * count, 128), BF16),
            pltpu.VMEM((128, 2 * count), BF16),
            pltpu.VMEM((count, Q_COLS), BF16),
            pltpu.VMEM((REPEAT, 8, count), F32),
            pltpu.VMEM((2 * count, count), F32),
            pltpu.VMEM((count, 128), F32),
            pltpu.VMEM((count, 128), F32),
            pltpu.VMEM((2 * count, 128), F32),
            pltpu.VMEM((count, 128), BF16),
            pltpu.VMEM((count, 128), BF16),
            pltpu.VMEM((count, PROJ), BF16),
            pltpu.VMEM((4, rows, D), BF16),
            pltpu.VMEM((4, 2, 2, 128, PROJ), BF16),
            pltpu.VMEM((2, 2, 2, 4, 16, D), BF16),
            pltpu.VMEM((4, 2, 2, 128, PROJ), BF16),
            pltpu.VMEM((4, 2, 128, PROJ), BF16),
            pltpu.VMEM((2, 2, 2, 4, 16, D), BF16),
            pltpu.VMEM((2, 2, 4, 16, D), BF16),
            *grad_buffers(2 * HID, SPLITS[1][1]),
            *grad_buffers(HID, SPLITS[2][1]),
            *grad_buffers(PROJ, SPLITS[0][1]),
            *grad_buffers(D, OUT_SPLIT, True),
            pltpu.SemaphoreType.DMA((copies,)),
            pltpu.SemaphoreType.DMA((copies,)),
            pltpu.SemaphoreType.DMA((16,)),
        ],
        name="backward_attention",
        compiler_params=pltpu.CompilerParams(
            collective_id=ident, has_side_effects=True, vmem_limit_bytes=VMEM_LIMIT
        ),
    )(
        sum_gu, sum_down, out_part, branch_all, grad_middle, middle, tokens, freqs,
        spots, q_all, kv_all, attended, lse, normed_all, proj_w, out_w,
    )


def core_sum(parts, ident):
    c = place()[4]
    parts = [p.reshape(4, 2, 2, 128, p.shape[-1]) for p in parts]
    n = len(parts)

    def kernel(*refs):
        send, recv, local = refs[2 * n :]
        copy = Copies(send, recv)
        greet([sibling], False)
        going = [copy(i.at[:, :, 1 - c_of()], o, sibling) for i, o in zip(refs[:n], refs[n : 2 * n])]
        for cp in going:
            cp.start()
        for cp in going:
            cp.wait()

    def c_of():
        return place()[4]

    outs = [struct((4, 2, 128, p.shape[-1])) for p in parts]
    got = comm_call(kernel, "grads_core", ident, parts, outs, n)
    own = [lax.dynamic_index_in_dim(p, c, 2, False) for p in parts]
    return [(o.astype(F32) + g.astype(F32)).astype(BF16) for o, g in zip(own, got)]


def inv_norm(values):
    return lax.rsqrt(jnp.mean(values * values, -1, keepdims=True) + EPS)


def norm_back(grad_normed, inv_root, normed):
    return inv_root * (grad_normed - normed * jnp.mean(grad_normed * normed, -1, keepdims=True))


def mm(left, right, dims, out=F32):
    return lax.dot_general(left, right, (dims, ((), ())), preferred_element_type=F32).astype(out)


def shards(tokens, positions, attn_in, attn_out, attn_gain, mlp_in, mlp_down, mlp_gain, cotangent):
    xh, xl, y, z, c = place()
    rows = tokens.shape[0]
    count = 4 * rows
    scale = HEAD_DIM ** (-0.5)
    gain_one = attn_gain.astype(F32)[:, None]
    gain_two = mlp_gain.astype(F32)[:, None]

    in_f = attn_in.astype(F32)
    mlp_f = mlp_in.astype(F32)
    kv = HEAD_DIM * KV_HEADS
    by_y = lambda a: a.reshape(16, TP, -1)
    w_proj = jnp.concatenate(
        [by_y(in_f[:, :D]), by_y(in_f[:, D : D + kv]), by_y(in_f[:, D + kv :])], -1
    )
    w_proj = (w_proj * gain_one[:, :, None]).astype(BF16).transpose(1, 0, 2)
    w_gu = jnp.concatenate([by_y(mlp_f[:, :FF]), by_y(mlp_f[:, FF:])], -1)
    w_gu = (w_gu * gain_two[:, :, None]).astype(BF16).transpose(1, 0, 2)
    w_down = by_y(mlp_down).transpose(1, 0, 2)
    spots = jnp.broadcast_to(positions.astype(F32)[None, :], (8, rows))
    lanes = jnp.arange(128)
    inv_freq = ROPE_BASE ** (-2.0 * (lanes % 32).astype(F32) / HEAD_DIM)
    signs = jnp.where(lanes % 64 < 32, -1.0, 1.0)
    freqs = jnp.zeros((8, 128), F32).at[0].set(inv_freq).at[1].set(signs)
    (normed_one_all, cot_all, proj_w, gu_w, down_w, out_w, q_all, kv_all, attended_low, lse, spots_all, middle, seq_two) = (
        forward_attention(tokens, cotangent, spots, freqs, w_proj, w_gu, w_down, attn_out, 0)
    )
    seq_cot, seq_two = cot_all.reshape(count, D), seq_two.reshape(count, D)
    gu_w, down_w = gu_w.reshape(D, 2 * HID), down_w.reshape(D, HID)
    inv_two = inv_norm(middle)
    normed_two = middle * inv_two

    gate_up = mm(seq_two, gu_w, NN)
    gate, up = gate_up[:, :HID], gate_up[:, HID:]
    gate_sigmoid = jax.nn.sigmoid(gate)
    gate_silu = gate * gate_sigmoid
    hidden_act = (gate_silu * up).astype(BF16)
    out_part = mm(hidden_act, down_w, NT, BF16).reshape(4, rows, D)

    grad_hidden = mm(seq_cot, down_w, NN)
    grad_gate = grad_hidden * up * gate_sigmoid * (1.0 + gate * (1.0 - gate_sigmoid))
    grad_gu = jnp.concatenate([grad_gate, grad_hidden * gate_silu], -1).astype(BF16)
    grad_two = ring_sum(mm(grad_gu, gu_w, NT, BF16), 6, "sum_grad_two")
    grad_middle = cotangent.astype(F32) + norm_back(grad_two, inv_two, normed_two)
    term_gu = mm(seq_two, grad_gu, TN, BF16)
    term_down = mm(seq_cot, hidden_act, TN, BF16)

    sum_gu, sum_down = core_sum([term_gu, term_down], 8)
    branch_all = ring_gather(grad_middle.astype(BF16), 7, "gather_branch")
    outputs, input_grad, own_proj, own_gu, own_down, own_out = backward_attention(
        sum_gu, sum_down, out_part, branch_all, grad_middle, middle, tokens, freqs,
        spots_all, q_all, kv_all.reshape(2 * count, 128), attended_low, lse, normed_one_all, proj_w, out_w, 9,
    )
    own_proj = own_proj.astype(F32).transpose(1, 0, 2)
    cut = lambda a, start, stop: a[:, :, start:stop].reshape(16, -1)
    own_proj = jnp.concatenate(
        [
            cut(own_proj, 0, Q_COLS),
            cut(own_proj, Q_COLS, Q_COLS + HEAD_DIM),
            cut(own_proj, Q_COLS + HEAD_DIM, PROJ),
        ],
        -1,
    )
    own_gu = own_gu.astype(F32).transpose(1, 0, 2)
    own_gu = jnp.concatenate([cut(own_gu, 0, HID), cut(own_gu, HID, 2 * HID)], -1)
    own_down = own_down.astype(F32).transpose(1, 0, 2).reshape(16, FF)
    return (
        outputs,
        input_grad,
        own_proj * gain_one,
        own_out.astype(F32),
        jnp.sum(own_proj * in_f, -1),
        own_gu * gain_two,
        own_down,
        jnp.sum(own_gu * mlp_f, -1),
    )


def solution(mesh):
    both = ("dp", "ctx")
    wide, flat = P(both, None), P(both)
    in_specs = (wide, flat, wide, wide, flat, wide, wide, flat, wide)
    out_specs = (wide, wide, wide, wide, flat, wide, wide, flat)
    return jax.shard_map(shards, mesh=mesh, in_specs=in_specs, out_specs=out_specs, check_vma=False)
```

```python
import jax
import jax.numpy as jnp
from jax import lax
from jax.experimental import pallas as pl
from jax.experimental.pallas import tpu as pltpu
from jax.sharding import PartitionSpec as P


D = 2048
HEADS = 32
KV_HEADS = 4
HEAD_DIM = 64
FF = 5632
REPEAT = HEADS // KV_HEADS
TP = 4
Q_COLS = D // TP
PROJ = Q_COLS + 2 * HEAD_DIM
HID = FF // TP

EPS = 1e-05
ROPE_BASE = 10000.0
NEG_FILL = -1e30

MESH = pl.DeviceIdType.MESH
BF16 = jnp.bfloat16
F32 = jnp.float32

SPLITS = ((PROJ, 384), (2 * HID, HID), (HID, 640))
OUT_SPLIT = 1024
VMEM_LIMIT = 60 << 20

NN = ((1,), (0,))
NT = ((1,), (1,))
TN = ((0,), (0,))


def place():
    dp, ctx = lax.axis_index("dp"), lax.axis_index("ctx")
    return (dp // 2) % 2, ctx // 4, ctx % 4, dp // 4, dp % 2


def device(xh, xl, y, z, c):
    return (z * 4 + xh * 2 + c, xl * 4 + y)


def along_y(d):
    def to(xh, xl, y, z, c):
        return xh, xl, (y + d) % 4, z, c

    return to


def along_x(d):
    def to(xh, xl, y, z, c):
        x = (xh * 2 + xl + d) % 4
        return x // 2, x % 2, y, z, c

    return to


def along_z(d):
    def to(xh, xl, y, z, c):
        return xh, xl, y, (z + d) % 4, c

    return to


def sibling(xh, xl, y, z, c):
    return xh, xl, y, z, 1 - c


def half_partner(xh, xl, y, z, c):
    return xh, 1 - xl, y, z, c


def crossed(xh, xl, y, z, c):
    return xh, xl, z, y, c


def greet(routes, cross):
    here = place()
    barrier = pltpu.get_barrier_semaphore()
    for back in routes:
        pl.semaphore_signal(barrier, inc=1, device_id=device(*back(*here)), device_id_type=MESH)
    if not cross:
        pl.semaphore_wait(barrier, len(routes))
        return
    away = here[2] != here[3]

    @pl.when(away)
    def _():
        pl.semaphore_signal(barrier, inc=1, device_id=device(*crossed(*here)), device_id_type=MESH)
        pl.semaphore_wait(barrier, len(routes) + 1)

    @pl.when(jnp.logical_not(away))
    def _():
        pl.semaphore_wait(barrier, len(routes))


class Copies:
    def __init__(self, send, recv):
        self.send, self.recv, self.count = send, recv, 0

    def __call__(self, src, dst, to):
        k, self.count = self.count, self.count + 1
        return pltpu.make_async_remote_copy(
            src_ref=src,
            dst_ref=dst,
            send_sem=self.send.at[k],
            recv_sem=self.recv.at[k],
            device_id=device(*to(*place())),
            device_id_type=MESH,
        )


def comm_call(kernel, name, ident, ins, outs, copies, locals_=0):
    return pl.pallas_call(
        kernel,
        out_shape=outs,
        in_specs=[pl.BlockSpec(memory_space=pl.ANY)] * len(ins),
        out_specs=[pl.BlockSpec(memory_space=pl.ANY)] * len(outs),
        scratch_shapes=[
            pltpu.SemaphoreType.DMA((copies,)),
            pltpu.SemaphoreType.DMA((copies,)),
            pltpu.SemaphoreType.DMA((max(locals_, 1),)),
        ],
        name=name,
        compiler_params=pltpu.CompilerParams(collective_id=ident, has_side_effects=True),
    )(*ins)


def struct(shape, dtype=BF16):
    return jax.ShapeDtypeStruct(shape, dtype)


class RingGather:
    def __init__(self, copy, own, dst, y):
        half = dst.shape[2] // 2
        lo, hi = pl.ds(0, half), pl.ds(half, half)
        back, on = (y + 3) % 4, (y + 1) % 4

        def first(cols, to):
            return copy(own.at[:, cols], dst.at[y, :, cols], to)

        def one(slot, cols, to):
            at = dst.at[slot, :, cols]
            return copy(at, at, to)

        self.first = [first(lo, along_y(1)), first(hi, along_y(3)), first(hi, along_y(1)), first(lo, along_y(3))]
        self.second = [one(back, lo, along_y(1)), one(on, hi, along_y(3))]

    def start(self):
        for cp in self.first:
            cp.start()

    def turn(self):
        for got, cp in zip(self.first, self.second):
            got.wait_recv()
            cp.start()

    def near(self):
        for cp in self.first[2:]:
            cp.wait_recv()

    def far(self):
        for cp in self.second:
            cp.wait_recv()

    def sent(self):
        for cp in self.first + self.second:
            cp.wait_send()


class RingSum:
    def __init__(self, copy, part, halves, whole, y):
        half = part.shape[2] // 2
        lo, hi = pl.ds(0, half), pl.ds(half, half)
        self.part, self.halves, self.whole, self.y = part, halves, whole, y
        self.cols = (lo, hi)
        far, on, back = (y + 2) % 4, (y + 1) % 4, (y + 3) % 4
        self.far = [
            copy(part.at[far, :, lo], halves.at[0], along_y(1)),
            copy(part.at[far, :, hi], halves.at[1], along_y(3)),
        ]
        self.near = [
            copy(part.at[on, :, hi], whole.at[0, :, hi], along_y(1)),
            copy(part.at[back, :, lo], whole.at[1, :, lo], along_y(3)),
        ]
        self.last = [
            copy(part.at[on, :, lo], whole.at[0, :, lo], along_y(1)),
            copy(part.at[back, :, hi], whole.at[1, :, hi], along_y(3)),
        ]
        self.slots = (on, back)

    def start(self):
        for cp in self.far + self.near:
            cp.start()

    def turn(self):
        for k in range(2):
            self.far[k].wait_recv()
            slot, cols = self.slots[k], self.cols[k]

            def body(r, _, slot=slot, cols=cols, k=k):
                rows = pl.ds(r * 32, 32)
                both = self.part[slot, rows, cols].astype(F32) + self.halves[k, rows].astype(F32)
                self.part[slot, rows, cols] = both.astype(BF16)
                return 0

            lax.fori_loop(0, self.part.shape[1] // 32, body, 0)
            self.last[k].start()

    def finish(self):
        for cp in self.near + self.last:
            cp.wait_recv()

    def rows(self, rows):
        own = self.part[self.y, rows].astype(F32)
        return own + self.whole[0, rows].astype(F32) + self.whole[1, rows].astype(F32)

    def sent(self):
        for cp in self.far + self.near + self.last:
            cp.wait_send()


class Gather:
    def __init__(self, copy, out, a, at, rows_only=False):
        xh, xl, y, z, c = at
        cols = out.shape[-1]
        left, right = pl.ds(0, a), pl.ds(a, cols - a)
        def cut(half, n):
            return slice(None) if half is None else pl.ds(half * (n // 2), n // 2)

        if rows_only:
            block = lambda z, x, c, cols: out.at[x[0], c, x[1], z, :, cols]
            z_line = lambda x, c, cols, half: out.at[x[0], c, x[1], cut(half, 4), :, cols]
            x_line = lambda z, c, cols, half: out.at[cut(half, 2), c, :, z, :, cols]
        else:
            block = lambda z, x, c, cols: out.at[z, x[0], c, pl.ds(x[1] * 64, 64), cols]
            z_line = lambda x, c, cols, half: out.at[cut(half, 4), x[0], c, pl.ds(x[1] * 64, 64), cols]
            x_line = lambda z, c, cols, half: out.at[z, cut(half, 2), c, :, cols]

        def same(ref, to):
            return copy(ref, ref, to)

        here = (xh, xl)
        self.first = []
        for d in (1, 3, 2):
            self.first.append(same(block(z, here, c, left), along_x(d)))
            self.first.append(same(block(z, here, c, right), along_z(d)))
        a_lo, a_hi = lambda z: x_line(z, c, left, 0), lambda z: x_line(z, c, left, 1)
        b_lo, b_hi = lambda x: z_line(x, c, right, 0), lambda x: z_line(x, c, right, 1)
        z_at = [(z + d) % 4 for d in range(4)]
        x_at = [along_x(d)(*at)[:2] for d in range(4)]
        self.lines = []
        for lo, hi, spots, along in ((a_lo, a_hi, z_at, along_z), (b_lo, b_hi, x_at, along_x)):
            going = [
                same(lo(spots[0]), along(1)),
                same(hi(spots[0]), along(3)),
                same(hi(spots[0]), along(1)),
                same(lo(spots[0]), along(3)),
            ]
            on = [same(lo(spots[3]), along(1)), same(hi(spots[1]), along(3))]
            self.lines.append((going, on))
        self.core = [same(block(z, here, c, pl.ds(0, cols)), sibling)]
        for d in (1, 3, 2):
            self.core.append(same(block(z, x_at[d], c, left), sibling))
            self.core.append(same(block(z_at[d], here, c, right), sibling))
        self.core_lines = []
        for d in (3, 1, 2):
            self.core_lines.append(
                (same(x_line(z_at[d], c, left, None), sibling), same(z_line(x_at[d], c, right, None), sibling))
            )

    def start(self):
        for cp in self.first:
            cp.start()
        self.core[0].start()

    def turn(self):
        for cp in self.first:
            cp.wait_recv()
        for going, _ in self.lines:
            for cp in going:
                cp.start()
        for cp in self.core[1:]:
            cp.start()

    def pass_on(self):
        for going, on in self.lines:
            for got, cp in zip(going[:2], on):
                got.wait_recv()
                cp.start()

    def near(self):
        for k, (going, _) in enumerate(self.lines):
            for side in range(2):
                going[2 + side].wait_recv()
                self.core_lines[side][k].start()

    def far(self):
        for k, (_, on) in enumerate(self.lines):
            for cp in on:
                cp.wait_recv()
            self.core_lines[2][k].start()

    def finish(self):
        for cp in self.core + [cp for pair in self.core_lines for cp in pair]:
            cp.wait_recv()

    def sent(self):
        for going, on in self.lines:
            for cp in going + on:
                cp.wait_send()
        for cp in self.first + self.core + [cp for pair in self.core_lines for cp in pair]:
            cp.wait_send()


def dot(left, right, dims=((1,), (0,))):
    return lax.dot_general(left, right, (dims, ((), ())), preferred_element_type=F32)


def swap_halves(v):
    lane = lax.broadcasted_iota(jnp.int32, v.shape, 1)
    return jnp.where(lane % 64 < 32, pltpu.roll(v, 96, 1), pltpu.roll(v, 32, 1))


def forward_attention(tokens, cotangent, spots, freqs, w_proj, w_gu, w_down, out_rows, ident):
    rows = tokens.shape[0]
    count = 4 * rows
    groups = [w_proj, w_gu, w_down]

    def kernel(
        tok_ref, cot_ref, spot_ref, freq_ref, wp, wg, wd, wo,
        normed_out, cot_all, gp, gg, gd, go, q_out, kv_out, att_out, lse_out, spot_out, middle_out, two_all,
        tok, normed, wp_v, wo_v, q_s, kv, vx, bias, att, part, halves, whole, spot_all, own_two, send, recv, local,
    ):
        at = place()
        xh, xl, y, z, c = at
        copy = Copies(send, recv)
        slot = pl.ds(xl * 64 + y * 16, 16)
        nlocal = [0]

        def near(src, dst):
            cp = pltpu.make_async_copy(src, dst, local.at[nlocal[0]])
            nlocal[0] += 1
            return cp

        to_y = []
        stay = []
        for i, o in ((wp, gp), (wg, gg), (wd, gd)):
            to_y.append([copy(i.at[(y + d) % 4], o.at[z, xh, c, slot], along_y(d)) for d in (1, 3, 2)])
            stay.append(near(i.at[y], o.at[z, xh, c, slot]))
        over = copy(wo, go.at[xh, c, xl, y], crossed)
        keep = near(wo, go.at[xh, c, xl, z])
        spot_copies = [copy(spot_all.at[y], spot_all.at[y], along_y(d)) for d in (1, 3, 2)]
        tok_ring = RingGather(copy, tok_ref, tok, y)
        cot_ring = RingGather(copy, cot_ref, cot_all, y)
        two_ring = RingGather(copy, own_two, two_all, y)
        branch = RingSum(copy, part, halves, whole, y)
        kv_copy = copy(kv.at[1], kv.at[0], half_partner)
        g_proj = Gather(copy, gp, SPLITS[0][1], at)
        g_gu = Gather(copy, gg, SPLITS[1][1], at)
        g_down = Gather(copy, gd, SPLITS[2][1], at)
        g_out = Gather(copy, go, OUT_SPLIT, at, True)

        cot_own = near(cot_ref, cot_all.at[y])
        tok_own = near(tok_ref, tok.at[y])
        tok_own.start()
        cot_own.start()
        spot_all[y] = spot_ref[...]
        for cp in stay:
            cp.start()
        greet(
            [along_y(d) for d in (1, 2, 3)]
            + [along_x(d) for d in (1, 2, 3)]
            + [along_z(d) for d in (1, 2, 3)]
            + [sibling],
            True,
        )
        away = y != z
        for cp in to_y[0]:
            cp.start()

        @pl.when(away)
        def _():
            over.start()

        @pl.when(jnp.logical_not(away))
        def _():
            keep.start()

        tok_ring.start()
        for cp in spot_copies + to_y[1] + to_y[2]:
            cp.start()

        def norm_block(k):
            def body(r, _):
                rs = pl.ds(r * 32, 32)
                v = tok[k, rs].astype(F32)
                inv = lax.rsqrt(jnp.mean(v * v, -1, keepdims=True) + EPS)
                normed[k, rs] = (v * inv).astype(BF16)
                return 0

            lax.fori_loop(0, rows // 32, body, 0)

        stay[0].wait()
        for cp in to_y[0]:
            cp.wait_recv()
        g_proj.start()

        @pl.when(away)
        def _():
            over.wait()

        @pl.when(jnp.logical_not(away))
        def _():
            keep.wait()

        g_out.start()
        tok_own.wait()
        norm_block(y)
        g_proj.turn()
        tok_ring.turn()
        g_proj.pass_on()
        g_out.turn()
        for cp in spot_copies:
            cp.wait_recv()

        cos, sin = [], []
        freq, sign = freq_ref[0:1, :], freq_ref[1:2, :]
        spot_cols = []
        for k in range(4):
            col = jnp.transpose(jnp.broadcast_to(spot_all[k, 0:1, :], (128, 128)))
            spot_out[k] = spot_all[k]
            spot_cols.append(col)
            cos.append(jnp.cos(col * freq))
            sin.append(jnp.sin(col * freq) * sign)
        cos, sin = jnp.concatenate(cos, 0), jnp.concatenate(sin, 0)
        low_half = xl == 0
        reach = jnp.where(low_half, -1.0, 2048.0)
        for k in range(4):
            for j in range(8):
                row = lax.broadcasted_iota(jnp.int32, (128, 128), 0) + k * 128
                col = lax.broadcasted_iota(jnp.int32, (128, 128), 1) + j * 128
                apart = (row - col + 512).astype(F32)
                seen = apart <= spot_cols[k]
                if j < 4:
                    seen = seen & (apart <= reach)
                else:
                    seen = seen & (col - 512 <= row)
                bias[pl.ds(k * 128, 128), pl.ds(j * 128, 128)] = jnp.where(seen, 0.0, NEG_FILL)

        g_proj.near()
        stay[1].wait()
        stay[2].wait()
        for cp in to_y[1] + to_y[2]:
            cp.wait_recv()
        g_gu.start()
        g_down.start()
        g_proj.far()
        g_out.pass_on()
        tok_ring.near()
        norm_block((y + 3) % 4)
        norm_block((y + 1) % 4)
        g_proj.finish()
        wp_load = near(gp, wp_v)
        wp_load.start()
        g_out.near()
        tok_ring.far()
        cot_ring.start()
        norm_block((y + 2) % 4)
        normed_save = near(normed, normed_out)
        normed_save.start()

        wp_load.wait()
        left = normed[...].reshape(count, D)
        lane = lax.broadcasted_iota(jnp.int32, (count, 128), 1)
        upper = lane >= 64
        raw = dot(left, wp_v[:, :, :, :, pl.ds(Q_COLS, 128)].reshape(D, 128))
        turned = raw * jnp.where(upper, 1.0, cos) + swap_halves(raw) * jnp.where(upper, 0.0, sin)
        kv[1] = turned.astype(BF16)
        kv_copy.start()
        g_out.far()
        g_gu.turn()
        g_down.turn()
        for j in range(2):
            raw2 = dot(left, wp_v[:, :, :, :, pl.ds(j * 256, 256)].reshape(D, 256))
            for e in range(2):
                raw = raw2[:, e * 128 : e * 128 + 128]
                turned = (raw * cos + swap_halves(raw) * sin).astype(BF16).astype(F32) * (HEAD_DIM ** (-0.5))
                pair = j * 2 + e
                q_s[2 * pair] = jnp.where(upper, 0.0, turned).astype(BF16)
                q_s[2 * pair + 1] = jnp.where(upper, 0.0, pltpu.roll(turned, 64, 1)).astype(BF16)
        kv_copy.wait_recv()
        for k in range(2):
            vx[k] = jnp.where(upper, kv[k].astype(F32), 1.0).astype(BF16)
        q_save = near(q_s, q_out)
        q_save.start()
        kv_save = near(kv, kv_out)
        kv_save.start()
        g_out.finish()
        wo_load = near(go, wo_v)
        wo_load.start()
        cot_ring.turn()

        def attend(pair):
            for b in range(2):
                rs = pl.ds(b * 256, 256)
                seen = 256 * (b + 1)
                lane = lax.broadcasted_iota(jnp.int32, (256, 128), 1) < 64
                found = []
                for e in range(2):
                    q = q_s[2 * pair + e, rs]
                    s0 = dot(q, kv[0], NT) + bias[rs, pl.ds(0, 512)]
                    s1 = dot(q, kv[1, pl.ds(0, seen)], NT) + bias[rs, pl.ds(512, seen)]
                    m = jnp.maximum(jnp.max(s0, -1, keepdims=True), jnp.max(s1, -1, keepdims=True))
                    p0 = jnp.exp(s0 - m).astype(BF16)
                    p1 = jnp.exp(s1 - m).astype(BF16)
                    o = dot(p0, vx[0]) + dot(p1, vx[1, pl.ds(0, seen)])
                    r = pltpu.roll(o, 64, 1)
                    found.append((o, r))
                    log_total = m + jnp.log(jnp.where(lane, o, r))
                    lse_out[2 * pair + e, :, rs] = jnp.transpose(log_total)[0:8]
                (o, r), (o2, r2) = found
                both = jnp.where(lane, r / o, o2 / r2)
                att[rs, pl.ds(pl.multiple_of(pair * 128, 128), 128)] = both.astype(BF16)

        def two_pairs(k):
            def body(i, _):
                attend(2 * k + i)
                return 0

            lax.fori_loop(0, 2, body, 0)

        two_pairs(0)
        g_gu.pass_on()
        g_down.pass_on()
        two_pairs(1)
        att_save = near(att, att_out)
        att_save.start()
        wo_load.wait()

        for j in range(4):
            cols = pl.ds(j * 512, 512)
            w = wo_v[:, :, :, :, :, cols].reshape(Q_COLS, 512)
            part[:, :, cols] = dot(att[...], w).astype(BF16).reshape(4, rows, 512)
        branch.start()
        g_gu.near()
        g_down.near()
        branch.turn()
        cot_ring.near()
        cot_ring.far()
        branch.finish()

        def mid(r, _):
            rs = pl.ds(r * 32, 32)
            v = tok_ref[rs].astype(F32) + branch.rows(rs)
            middle_out[rs] = v
            inv = lax.rsqrt(jnp.mean(v * v, -1, keepdims=True) + EPS)
            own_two[rs] = (v * inv).astype(BF16)
            return 0

        lax.fori_loop(0, rows // 32, mid, 0)
        two_own = near(own_two, two_all.at[y])
        two_own.start()
        two_ring.start()
        g_gu.far()
        g_down.far()
        two_ring.turn()
        two_ring.near()
        two_ring.far()
        g_gu.finish()
        g_down.finish()
        for cp in (cot_own, normed_save, q_save, kv_save, att_save, two_own):
            cp.wait()
        for group in to_y:
            for cp in group:
                cp.wait_send()
        for cp in spot_copies + [kv_copy]:
            cp.wait_send()
        for thing in (g_proj, g_out, g_gu, g_down, tok_ring, cot_ring, two_ring, branch):
            thing.sent()

    anywhere, vmem = pl.BlockSpec(memory_space=pl.ANY), pl.BlockSpec(memory_space=pltpu.VMEM)
    outs = [
        (struct((4, rows, D)), anywhere),
        (struct((4, rows, D)), anywhere),
        (struct((4, 2, 2, 128, PROJ)), anywhere),
        (struct((4, 2, 2, 128, 2 * HID)), anywhere),
        (struct((4, 2, 2, 128, HID)), anywhere),
        (struct((2, 2, 2, 4, 16, D)), anywhere),
        (struct((REPEAT, count, 128)), anywhere),
        (struct((2, count, 128)), anywhere),
        (struct((count, Q_COLS)), anywhere),
        (struct((REPEAT, 8, count), F32), vmem),
        (struct((4, 8, 128), F32), vmem),
        (struct((rows, D), F32), vmem),
        (struct((4, rows, D)), anywhere),
    ]
    copies = 9 + 1 + 3 + 6 * 3 + 6 + 1 + 31 * 4
    return pl.pallas_call(
        kernel,
        out_shape=[o[0] for o in outs],
        in_specs=[vmem] * 8,
        out_specs=[o[1] for o in outs],
        scratch_shapes=[
            pltpu.VMEM((4, rows, D), BF16),
            pltpu.VMEM((4, rows, D), BF16),
            pltpu.VMEM((4, 2, 2, 128, PROJ), BF16),
            pltpu.VMEM((2, 2, 2, 4, 16, D), BF16),
            pltpu.VMEM((REPEAT, count, 128), BF16),
            pltpu.VMEM((2, count, 128), BF16),
            pltpu.VMEM((2, count, 128), BF16),
            pltpu.VMEM((count, 2 * count), F32),
            pltpu.VMEM((count, Q_COLS), BF16),
            pltpu.VMEM((4, rows, D), BF16),
            pltpu.VMEM((2, rows, D // 2), BF16),
            pltpu.VMEM((2, rows, D), BF16),
            pltpu.VMEM((4, 8, 128), F32),
            pltpu.VMEM((rows, D), BF16),
            pltpu.SemaphoreType.DMA((copies,)),
            pltpu.SemaphoreType.DMA((copies,)),
            pltpu.SemaphoreType.DMA((16,)),
        ],
        name="forward_attention",
        compiler_params=pltpu.CompilerParams(
            collective_id=ident, has_side_effects=True, vmem_limit_bytes=VMEM_LIMIT
        ),
    )(tokens, cotangent, spots, freqs, w_proj, w_gu, w_down, out_rows)


def tiles(ref):
    if len(ref.shape) == 2:
        return [ref]
    return [t for k in range(ref.shape[0]) for t in tiles(ref.at[k])]


def add_up(dst, *others):
    for out, *terms in zip(tiles(dst), *[tiles(o) for o in others]):
        rows = out.shape[0]
        step = min(rows, 32)

        def body(r, _, out=out, terms=terms, step=step):
            rs = pl.ds(r * step, step)
            value = out[rs].astype(F32)
            for t in terms:
                value = value + t[rs].astype(F32)
            out[rs] = value.astype(BF16)
            return 0

        lax.fori_loop(0, rows // step, body, 0)


class LineSum:
    def __init__(self, copy, lo, hi, along, far, near):
        self.lo, self.hi, self.far_in, self.near_in = lo, hi, far, near
        self.far = [copy(lo(2), far.at[0], along(1)), copy(hi(2), far.at[1], along(3))]
        self.near = [copy(hi(1), near.at[0, 1], along(1)), copy(lo(3), near.at[1, 0], along(3))]
        self.last = [copy(lo(1), near.at[0, 0], along(1)), copy(hi(3), near.at[1, 1], along(3))]

    def start(self):
        for cp in self.far + self.near:
            cp.start()

    def turn(self):
        self.far[0].wait_recv()
        add_up(self.lo(1), self.far_in.at[0])
        self.last[0].start()
        self.far[1].wait_recv()
        add_up(self.hi(3), self.far_in.at[1])
        self.last[1].start()

    def finish(self):
        for cp in self.near + self.last:
            cp.wait_recv()
        add_up(self.lo(0), self.near_in.at[0, 0], self.near_in.at[1, 0])
        add_up(self.hi(0), self.near_in.at[0, 1], self.near_in.at[1, 1])

    def sent(self):
        for cp in self.far + self.near + self.last:
            cp.wait_send()


class GradSum:
    def __init__(self, copy, local_copy, terms, out, a, at, buffers, rows_only=False):
        xh, xl, y, z, c = at
        self.at, self.rows_only = at, rows_only
        far_a, near_a, far_b, near_b, got_a, got_b, own = buffers
        cols = terms.shape[-1]
        left, right = pl.ds(0, a), pl.ds(a, cols - a)
        x_at = [along_x(d)(*at)[:2] for d in range(4)]
        z_at = [(z + d) % 4 for d in range(4)]
        if rows_only:
            spot = lambda x, z, cols: terms.at[x[0], c, x[1], z, :, cols]
            a_half = lambda h: lambda d: terms.at[h, c, :, z_at[d], :, left]
            b_half = lambda h: lambda d: terms.at[x_at[d][0], c, x_at[d][1], pl.ds(2 * h, 2), :, right]
        else:
            base = (lambda z, xh: (z, xh, c)) if len(terms.shape) == 5 else (lambda z, xh: (z, xh))
            spot = lambda x, z, cols: terms.at[base(z, x[0]) + (pl.ds(x[1] * 64, 64), cols)]
            a_half = lambda h: lambda d: terms.at[base(z_at[d], h) + (slice(None), left)]
            b_half = lambda h: lambda d: terms.at[
                base(pl.ds(2 * h, 2), x_at[d][0]) + (pl.ds(x_at[d][1] * 64, 64), right)
            ]
        self.lines = [
            LineSum(copy, a_half(0), a_half(1), along_z, far_a, near_a),
            LineSum(copy, b_half(0), b_half(1), along_x, far_b, near_b),
        ]
        here = x_at[0]
        self.second = []
        for d in (1, 3, 2):
            self.second.append(copy(spot(x_at[d], z, left), got_a.at[d - 1], along_x(d)))
            self.second.append(copy(spot(here, z_at[d], right), got_b.at[d - 1], along_z(d)))
        self.mine = (spot(here, z, left), spot(here, z, right))
        self.got = (got_a, got_b)
        self.own, self.cuts = own, (left, right)
        if rows_only:
            self.over = copy(own, out, crossed)
            self.keep = local_copy(own, out)
        else:
            self.to_y = [copy(own.at[(y + d) % 4], out.at[y], along_y(d)) for d in (1, 3, 2)]
            self.keep = local_copy(own.at[y], out.at[y])

    def start(self):
        for line in self.lines:
            line.start()

    def turn(self):
        for line in self.lines:
            line.turn()

    def cross(self):
        for line in self.lines:
            line.finish()
        for cp in self.second:
            cp.start()

    def deliver(self):
        for cp in self.second:
            cp.wait_recv()
        for mine, got, cut in zip(self.mine, self.got, self.cuts):
            value = mine[...].astype(F32)
            for d in range(3):
                value = value + got[d].astype(F32)
            own = self.own
            if self.rows_only:
                own[:, cut] = value.astype(BF16)
            else:
                own[:, :, cut] = value.astype(BF16).reshape(4, 16, value.shape[-1])
        if self.rows_only:
            y, z = self.at[2], self.at[3]

            @pl.when(y != z)
            def _():
                self.over.start()

            @pl.when(y == z)
            def _():
                self.keep.start()

        else:
            for cp in self.to_y:
                cp.start()
            self.keep.start()

    def finish(self):
        if self.rows_only:
            y, z = self.at[2], self.at[3]

            @pl.when(y != z)
            def _():
                self.over.wait()

            @pl.when(y == z)
            def _():
                self.keep.wait()

        else:
            for cp in self.to_y:
                cp.wait()
            self.keep.wait()
        for line in self.lines:
            line.sent()
        for cp in self.second:
            cp.wait_send()


def grad_buffers(cols, a, rows_only=False):
    b = cols - a
    if rows_only:
        a_half, b_half, spot, own = (2, 16), (2, 16), 16, (16, cols)
    else:
        a_half, b_half, spot, own = (128,), (2, 64), 64, (4, 16, cols)
    return [
        pltpu.VMEM((2,) + a_half + (a,), BF16),
        pltpu.VMEM((2, 2) + a_half + (a,), BF16),
        pltpu.VMEM((2,) + b_half + (b,), BF16),
        pltpu.VMEM((2, 2) + b_half + (b,), BF16),
        pltpu.VMEM((3, spot, a), BF16),
        pltpu.VMEM((3, spot, b), BF16),
        pltpu.VMEM(own, BF16),
    ]


def rotation(spot_rows, freq_ref):
    cos, sin = [], []
    for k in range(4):
        col = jnp.transpose(jnp.broadcast_to(spot_rows[k, 0:1, :], (128, 128)))
        cos.append(jnp.cos(col * freq_ref[0:1, :]))
        sin.append(jnp.sin(col * freq_ref[0:1, :]) * freq_ref[1:2, :])
    return jnp.concatenate(cos, 0), jnp.concatenate(sin, 0)


def backward_attention(
    sum_gu, sum_down, out_part, branch_all, grad_middle, middle, tokens, freqs,
    spots, q_all, kv_all, attended, lse, normed_all, proj_w, out_w, ident,
):
    rows = tokens.shape[0]
    count = 4 * rows
    scale = HEAD_DIM ** (-0.5)

    def kernel(
        s_gu, s_down, op_ref, br_ref, gm_ref, mid_ref, tok_ref, freq_ref,
        spot_ref, q_ref, kv_ref, att_ref, lse_ref, nm_ref, wp_ref, wo_ref,
        out_ref, ig_ref, o_proj, o_gu, o_down, o_out,
        v_gu, v_down, part, halves, whole, halves2, whole2, br, q_s, do_s, kv, kvt, att, delta, bias, cos_s, sin_s,
        dkv, kv_send, kv_in, gp, normed, wp, wo, t_proj, rc_proj, t_out, rc_out, *rest,
    ):
        bufs, (send, recv, local) = rest[:28], rest[28:]
        at = place()
        xh, xl, y, z, c = at
        copy = Copies(send, recv)
        nlocal = [0]

        def near(src, dst):
            cp = pltpu.make_async_copy(src, dst, local.at[nlocal[0]])
            nlocal[0] += 1
            return cp

        load_gu, load_down = near(s_gu, v_gu), near(s_down, v_down)
        load_op, load_br, load_wo = near(op_ref, part), near(br_ref, br), near(wo_ref, wo)
        load_att, load_q = near(att_ref, att), near(q_ref, q_s)
        load_kv = near(kv_ref, kv)
        load_nm, load_wp = near(nm_ref, normed), near(wp_ref, wp)
        for cp in (load_gu, load_op, load_down, load_br, load_wo, load_att, load_q, load_kv, load_nm, load_wp):
            cp.start()
        outs = RingSum(copy, part, halves, whole, y)
        ones = RingSum(copy, part, halves2, whole2, y)
        kv_copy = copy(kv_send, kv_in, half_partner)
        core_proj = copy(t_proj.at[:, :, 1 - c], rc_proj, sibling)
        core_out = copy(t_out.at[:, 1 - c], rc_out, sibling)
        g_gu = GradSum(copy, near, v_gu, o_gu, SPLITS[1][1], at, bufs[0:7])
        g_down = GradSum(copy, near, v_down, o_down, SPLITS[2][1], at, bufs[7:14])
        g_proj = GradSum(copy, near, t_proj, o_proj, SPLITS[0][1], at, bufs[14:21])
        g_out = GradSum(copy, near, t_out, o_out, OUT_SPLIT, at, bufs[21:28], True)
        greet(
            [along_y(d) for d in (1, 2, 3)]
            + [along_x(d) for d in (1, 2, 3)]
            + [along_z(d) for d in (1, 2, 3)]
            + [sibling],
            True,
        )
        load_gu.wait()
        g_gu.start()
        load_op.wait()
        outs.start()
        load_down.wait()
        g_down.start()

        cos, sin = rotation(spot_ref, freq_ref)
        cos_s[...] = cos
        sin_s[...] = sin
        reach = jnp.where(xl == 0, -1.0, 2048.0)
        for k in range(4):
            spots_row = spot_ref[k, 0:1, :]
            for j in range(8):
                key = lax.broadcasted_iota(jnp.int32, (128, 128), 0) + j * 128
                row = lax.broadcasted_iota(jnp.int32, (128, 128), 1) + k * 128
                apart = (row - key + 512).astype(F32)
                seen = apart <= spots_row
                if j < 4:
                    seen = seen & (apart <= reach)
                else:
                    seen = seen & (key - 512 <= row)
                bias[pl.ds(j * 128, 128), pl.ds(k * 128, 128)] = jnp.where(seen, 0.0, NEG_FILL)
        dkv[...] = jnp.zeros_like(dkv)

        load_br.wait()
        load_wo.wait()
        load_att.wait()
        lane = lax.broadcasted_iota(jnp.int32, (count, 128), 1)
        for p in range(4):
            w = wo[p // 2, p % 2].reshape(128, D)
            low = dot(br[...].reshape(count, D), w, NT).astype(BF16).astype(F32)
            do_s[2 * p] = jnp.where(lane < 64, 0.0, pltpu.roll(low, 64, 1)).astype(BF16)
            do_s[2 * p + 1] = jnp.where(lane < 64, 0.0, low).astype(BF16)
            prod = jnp.transpose(low * att[:, pl.ds(p * 128, 128)].astype(F32))
            for e in range(2):
                total_row = jnp.sum(prod[e * 64 : e * 64 + 64], 0, keepdims=True)
                delta[2 * p + e] = jnp.broadcast_to(total_row, (8, count))
        outs.turn()

        for k in range(4):
            term = dot(att[:, pl.ds(k * 128, 128)], br[...].reshape(count, D), TN)
            t_out[k // 2, k % 2] = term.astype(BF16).reshape(2, 4, 16, D)
        core_out.start()
        load_q.wait()
        load_kv.wait()
        for k in range(2):
            turned = jnp.transpose(kv[pl.ds(k * count, count)].astype(F32)).astype(BF16)
            kvt[:, pl.ds(k * count, count)] = turned

        def backward(pair):
            for b in range(2):
                rs = pl.ds(b * 256, 256)
                seen = pl.ds(0, 512 + 256 * (b + 1))
                found = []
                for e in range(2):
                    h = 2 * pair + e
                    q, do = q_s[h, rs], do_s[h, rs]
                    st = dot(kv[seen], q, NT) + bias[seen, rs] - lse_ref[h, 0:1, rs]
                    p = jnp.exp(st)
                    dp = dot(kv[seen], do, NT)
                    ds = (p * (dp - delta[h, 0:1, rs])).astype(BF16)
                    dkv[seen] += dot(ds, q) + dot(p.astype(BF16), do)
                    found.append(dot(kvt[:, seen], ds)[0:64])
                both = jnp.transpose(jnp.concatenate(found, 0)) * scale
                both = both * cos_s[rs] - swap_halves(both) * sin_s[rs]
                gp[rs, pl.ds(pl.multiple_of(pair * 128, 128), 128)] = both.astype(BF16)

        def two_pairs(k):
            def body(i, _):
                backward(2 * k + i)
                return 0

            lax.fori_loop(0, 2, body, 0)

        two_pairs(0)
        g_gu.turn()
        g_down.turn()
        two_pairs(1)
        kv_send[...] = dkv[pl.ds(0, count)].astype(BF16)
        kv_copy.start()
        core_out.wait_recv()
        add_up(t_out.at[:, c], rc_out)
        g_out.start()
        outs.finish()

        def finish_out(r, _):
            rs = pl.ds(r * 32, 32)
            out_ref[rs] = (mid_ref[rs] + outs.rows(rs)).astype(BF16)
            return 0

        lax.fori_loop(0, rows // 32, finish_out, 0)
        outs.sent()
        kv_copy.wait_recv()
        got = dkv[pl.ds(count, count)] + kv_in[...].astype(F32)
        back = got * cos_s[...] - swap_halves(got) * sin_s[...]
        gp[:, pl.ds(Q_COLS, 128)] = jnp.where(lane < 64, back, got).astype(BF16)

        load_wp.wait()
        for j in range(4):
            w = wp[j].reshape(512, PROJ)
            part[:, :, pl.ds(j * 512, 512)] = dot(gp[...], w, NT).astype(BF16).reshape(4, rows, 512)
        ones.start()
        load_nm.wait()
        for k in range(4):
            left = normed[:, :, pl.ds(k * 512, 512)].reshape(count, 512)
            t_proj[k] = dot(left, gp[...], TN).astype(BF16).reshape(2, 2, 128, PROJ)
        core_proj.start()
        g_gu.cross()
        g_down.cross()
        ones.turn()
        g_out.turn()
        core_proj.wait_recv()
        for k in range(4):
            add_up(t_proj.at[k, :, c], rc_proj.at[k])
        g_proj.start()
        g_gu.deliver()
        g_down.deliver()
        g_proj.turn()
        g_out.cross()
        ones.finish()

        def finish_in(r, _):
            rs = pl.ds(r * 32, 32)
            v = tok_ref[rs].astype(F32)
            inv = lax.rsqrt(jnp.mean(v * v, -1, keepdims=True) + EPS)
            v = v * inv
            g = ones.rows(rs)
            ig_ref[rs] = gm_ref[rs] + inv * (g - v * jnp.mean(g * v, -1, keepdims=True))
            return 0

        lax.fori_loop(0, rows // 32, finish_in, 0)
        g_proj.cross()
        g_out.deliver()
        g_proj.deliver()
        ones.sent()
        for cp in (kv_copy, core_proj, core_out):
            cp.wait_send()
        for g in (g_gu, g_down, g_out, g_proj):
            g.finish()

    anywhere, vmem = pl.BlockSpec(memory_space=pl.ANY), pl.BlockSpec(memory_space=pltpu.VMEM)
    in_specs = [anywhere] * 4 + [vmem] * 5 + [anywhere] * 3 + [vmem] + [anywhere] * 3
    outs = [
        (struct((rows, D)), vmem),
        (struct((rows, D), F32), vmem),
        (struct((4, 16, PROJ)), anywhere),
        (struct((4, 16, 2 * HID)), anywhere),
        (struct((4, 16, HID)), anywhere),
        (struct((16, D)), anywhere),
    ]
    whole = lambda: [pltpu.VMEM((2, rows, D // 2), BF16), pltpu.VMEM((2, rows, D), BF16)]
    copies = 12 + 3 + 21 * 3 + 19
    return pl.pallas_call(
        kernel,
        out_shape=[o[0] for o in outs],
        in_specs=in_specs,
        out_specs=[o[1] for o in outs],
        scratch_shapes=[
            pltpu.VMEM((4, 2, 128, 2 * HID), BF16),
            pltpu.VMEM((4, 2, 128, HID), BF16),
            pltpu.VMEM((4, rows, D), BF16),
            *whole(),
            *whole(),
            pltpu.VMEM((4, rows, D), BF16),
            pltpu.VMEM((REPEAT, count, 128), BF16),
            pltpu.VMEM((REPEAT, count, 128), BF16),
            pltpu.VMEM((2 * count, 128), BF16),
            pltpu.VMEM((128, 2 * count), BF16),
            pltpu.VMEM((count, Q_COLS), BF16),
            pltpu.VMEM((REPEAT, 8, count), F32),
            pltpu.VMEM((2 * count, count), F32),
            pltpu.VMEM((count, 128), F32),
            pltpu.VMEM((count, 128), F32),
            pltpu.VMEM((2 * count, 128), F32),
            pltpu.VMEM((count, 128), BF16),
            pltpu.VMEM((count, 128), BF16),
            pltpu.VMEM((count, PROJ), BF16),
            pltpu.VMEM((4, rows, D), BF16),
            pltpu.VMEM((4, 2, 2, 128, PROJ), BF16),
            pltpu.VMEM((2, 2, 2, 4, 16, D), BF16),
            pltpu.VMEM((4, 2, 2, 128, PROJ), BF16),
            pltpu.VMEM((4, 2, 128, PROJ), BF16),
            pltpu.VMEM((2, 2, 2, 4, 16, D), BF16),
            pltpu.VMEM((2, 2, 4, 16, D), BF16),
            *grad_buffers(2 * HID, SPLITS[1][1]),
            *grad_buffers(HID, SPLITS[2][1]),
            *grad_buffers(PROJ, SPLITS[0][1]),
            *grad_buffers(D, OUT_SPLIT, True),
            pltpu.SemaphoreType.DMA((copies,)),
            pltpu.SemaphoreType.DMA((copies,)),
            pltpu.SemaphoreType.DMA((16,)),
        ],
        name="backward_attention",
        compiler_params=pltpu.CompilerParams(
            collective_id=ident, has_side_effects=True, vmem_limit_bytes=VMEM_LIMIT
        ),
    )(
        sum_gu, sum_down, out_part, branch_all, grad_middle, middle, tokens, freqs,
        spots, q_all, kv_all, attended, lse, normed_all, proj_w, out_w,
    )


def feed_forward(seq_two, seq_cot, gu_w, down_w, middle, cotangent, ident):
    rows = middle.shape[0]
    count = 4 * rows
    tiles_gu, pairs = HID // 128, HID // 256

    def kernel(
        two_ref, cot_ref, wg_ref, wd_ref, mid_ref, own_cot,
        branch_all, gm_ref, s_gu, s_down, op_out,
        part, halves, whole, two, gu, cot, hid, gh, turned, t_gu, t_down, rc_gu, rc_down, branch, op,
        send, recv, local, weights,
    ):
        at = place()
        xh, xl, y, z, c = at
        copy = Copies(send, recv)
        nlocal = [0]

        def near(src, dst):
            cp = pltpu.make_async_copy(src, dst, local.at[nlocal[0]])
            nlocal[0] += 1
            return cp

        def load_gu(j):
            tile = pl.ds(pl.multiple_of(j * 256, 256), 256)
            return pltpu.make_async_copy(wg_ref.at[:, :, :, :, tile], t_gu.at[:, :, :, :, tile], weights.at[j])

        def load_down(j, width=256):
            tile = pl.ds(pl.multiple_of(j * 256, 256), width)
            return pltpu.make_async_copy(
                wd_ref.at[:, :, :, :, tile], t_down.at[:, :, :, :, tile], weights.at[tiles_gu + j]
            )

        load_cot, load_two = near(cot_ref, cot), near(two_ref, two)
        load_cot.start()
        last_down = load_down(pairs, HID - 256 * pairs)

        def begin_down(j, _):
            load_down(j).start()
            return 0

        def begin_gu(j, _):
            load_gu(j).start()
            return 0

        lax.fori_loop(0, pairs, begin_down, 0)
        last_down.start()
        load_two.start()
        lax.fori_loop(0, tiles_gu, begin_gu, 0)
        ring = RingSum(copy, part, halves, whole, y)
        gather = RingGather(copy, branch, branch_all, y)
        own = near(branch, branch_all.at[y])
        cores = [
            (copy(t_gu.at[k, :, 1 - c], rc_gu.at[k], sibling), copy(t_down.at[k, :, 1 - c], rc_down.at[k], sibling))
            for k in range(4)
        ]
        saves = [(near(t_gu.at[k, :, c], s_gu.at[k]), near(t_down.at[k, :, c], s_down.at[k])) for k in range(4)]
        save_op = near(op, op_out)
        greet([along_y(1), along_y(3), sibling], False)
        load_cot.wait()

        def hidden_back(j, _):
            load_down(j).wait()
            tile = pl.ds(pl.multiple_of(j * 256, 256), 256)
            gh[:, tile] = dot(cot[...].reshape(count, D), t_down[:, :, :, :, tile].reshape(D, 256))
            return 0

        lax.fori_loop(0, pairs, hidden_back, 0)
        last_down.wait()
        tile = pl.ds(256 * pairs, HID - 256 * pairs)
        gh[:, tile] = dot(cot[...].reshape(count, D), t_down[:, :, :, :, tile].reshape(D, HID - 256 * pairs))
        load_two.wait()

        def hidden(j, _):
            load_gu(j).wait()
            both = pl.ds(pl.multiple_of(j * 256, 256), 256)
            one = pl.ds(pl.multiple_of(j * 128, 128), 128)
            gate_up = dot(two[...].reshape(count, D), t_gu[:, :, :, :, both].reshape(D, 256))
            gate, up = gate_up[:, :128], gate_up[:, 128:]
            back = gh[:, one]
            sigmoid = jax.nn.sigmoid(gate)
            silu = gate * sigmoid
            hid[:, one] = (silu * up).astype(BF16)
            grad_gate = back * up * sigmoid * (1.0 + gate * (1.0 - sigmoid))
            gu[:, both] = jnp.concatenate([grad_gate, back * silu], 1).astype(BF16)
            return 0

        lax.fori_loop(0, tiles_gu, hidden, 0)

        def part_two(k, _):
            cols = pl.ds(pl.multiple_of(k * 512, 512), 512)
            part[:, :, cols] = dot(gu[...], t_gu[k].reshape(512, 2 * HID), NT).astype(BF16).reshape(4, rows, 512)
            return 0

        lax.fori_loop(0, 4, part_two, 0)
        ring.start()

        def part_out(k, _):
            cols = pl.ds(pl.multiple_of(k * 512, 512), 512)
            op[:, :, cols] = dot(hid[...], t_down[k].reshape(512, HID), NT).astype(BF16).reshape(4, rows, 512)
            return 0

        lax.fori_loop(0, 4, part_out, 0)
        save_op.start()

        def terms(k):
            cols = pl.ds(k * 512, 512)
            turned[...] = jnp.transpose(two[:, :, cols].reshape(count, 512))

            def some(j, _):
                tile = pl.ds(pl.multiple_of(j * 256, 256), 256)
                t_gu[k, :, :, :, tile] = dot(turned[...], gu[:, tile]).astype(BF16).reshape(2, 2, 128, 256)
                return 0

            lax.fori_loop(0, 2 * HID // 256, some, 0)
            cores[k][0].start()
            turned[...] = jnp.transpose(cot[:, :, cols].reshape(count, 512))

            def more(j, width=256):
                tile = pl.ds(pl.multiple_of(j * 256, 256), width)
                t_down[k, :, :, :, tile] = dot(turned[...], hid[:, tile]).astype(BF16).reshape(2, 2, 128, width)
                return 0

            lax.fori_loop(0, pairs, lambda j, _: more(j), 0)
            more(pairs, HID - 256 * pairs)
            cores[k][1].start()

        def add_core(k):
            for cp in cores[k]:
                cp.wait_recv()
            add_up(t_gu.at[k, :, c], rc_gu.at[k])
            add_up(t_down.at[k, :, c], rc_down.at[k])
            for cp in saves[k]:
                cp.start()

        ring.turn()
        terms(0)
        terms(1)
        terms(2)
        ring.finish()

        def back(r, _):
            rs = pl.ds(r * 32, 32)
            v = mid_ref[rs]
            inv = lax.rsqrt(jnp.mean(v * v, -1, keepdims=True) + EPS)
            v = v * inv
            g = ring.rows(rs)
            value = own_cot[rs].astype(F32) + inv * (g - v * jnp.mean(g * v, -1, keepdims=True))
            gm_ref[rs] = value
            branch[rs] = value.astype(BF16)
            return 0

        lax.fori_loop(0, rows // 32, back, 0)
        gather.start()
        own.start()
        terms(3)
        add_core(0)
        gather.turn()
        for k in (1, 2, 3):
            add_core(k)
        gather.near()
        gather.far()
        own.wait()
        save_op.wait()
        for pair in saves:
            for cp in pair:
                cp.wait()
        for pair in cores:
            for cp in pair:
                cp.wait_send()
        ring.sent()
        gather.sent()

    anywhere, vmem = pl.BlockSpec(memory_space=pl.ANY), pl.BlockSpec(memory_space=pltpu.VMEM)
    copies = 12 + 8
    return pl.pallas_call(
        kernel,
        out_shape=[
            struct((4, rows, D)),
            struct((rows, D), F32),
            struct((4, 2, 128, 2 * HID)),
            struct((4, 2, 128, HID)),
            struct((4, rows, D)),
        ],
        in_specs=[anywhere] * 4 + [vmem] * 2,
        out_specs=[anywhere, vmem, anywhere, anywhere, anywhere],
        scratch_shapes=[
            pltpu.VMEM((4, rows, D), BF16),
            pltpu.VMEM((2, rows, D // 2), BF16),
            pltpu.VMEM((2, rows, D), BF16),
            pltpu.VMEM((4, rows, D), BF16),
            pltpu.VMEM((count, 2 * HID), BF16),
            pltpu.VMEM((4, rows, D), BF16),
            pltpu.VMEM((count, HID), BF16),
            pltpu.VMEM((count, HID), F32),
            pltpu.VMEM((512, count), BF16),
            pltpu.VMEM((4, 2, 2, 128, 2 * HID), BF16),
            pltpu.VMEM((4, 2, 2, 128, HID), BF16),
            pltpu.VMEM((4, 2, 128, 2 * HID), BF16),
            pltpu.VMEM((4, 2, 128, HID), BF16),
            pltpu.VMEM((rows, D), BF16),
            pltpu.VMEM((4, rows, D), BF16),
            pltpu.SemaphoreType.DMA((copies,)),
            pltpu.SemaphoreType.DMA((copies,)),
            pltpu.SemaphoreType.DMA((14,)),
            pltpu.SemaphoreType.DMA((tiles_gu + pairs + 1,)),
        ],
        name="feed_forward",
        compiler_params=pltpu.CompilerParams(
            collective_id=ident, has_side_effects=True, vmem_limit_bytes=VMEM_LIMIT
        ),
    )(seq_two, seq_cot, gu_w, down_w, middle, cotangent)


def shards(tokens, positions, attn_in, attn_out, attn_gain, mlp_in, mlp_down, mlp_gain, cotangent):
    xh, xl, y, z, c = place()
    rows = tokens.shape[0]
    count = 4 * rows
    gain_one = attn_gain.astype(F32)[:, None]
    gain_two = mlp_gain.astype(F32)[:, None]

    in_f = attn_in.astype(F32)
    mlp_f = mlp_in.astype(F32)
    kv = HEAD_DIM * KV_HEADS
    by_y = lambda a: a.reshape(16, TP, -1)
    w_proj = jnp.concatenate(
        [by_y(in_f[:, :D]), by_y(in_f[:, D : D + kv]), by_y(in_f[:, D + kv :])], -1
    )
    w_proj = (w_proj * gain_one[:, :, None]).astype(BF16).transpose(1, 0, 2)
    by_tile = lambda a: a.reshape(16, TP, HID // 128, 1, 128)
    w_gu = jnp.concatenate([by_tile(mlp_f[:, :FF]), by_tile(mlp_f[:, FF:])], 3).reshape(16, TP, 2 * HID)
    w_gu = (w_gu * gain_two[:, :, None]).astype(BF16).transpose(1, 0, 2)
    w_down = by_y(mlp_down).transpose(1, 0, 2)
    spots = jnp.broadcast_to(positions.astype(F32)[None, :], (8, rows))
    lanes = jnp.arange(128)
    inv_freq = ROPE_BASE ** (-2.0 * (lanes % 32).astype(F32) / HEAD_DIM)
    signs = jnp.where(lanes % 64 < 32, -1.0, 1.0)
    freqs = jnp.zeros((8, 128), F32).at[0].set(inv_freq).at[1].set(signs)
    (normed_one_all, cot_all, proj_w, gu_w, down_w, out_w, q_all, kv_all, attended_low, lse, spots_all, middle, two_all) = (
        forward_attention(tokens, cotangent, spots, freqs, w_proj, w_gu, w_down, attn_out, 0)
    )
    branch_all, grad_middle, sum_gu, sum_down, out_part = feed_forward(
        two_all, cot_all, gu_w, down_w, middle, cotangent, 1
    )
    outputs, input_grad, own_proj, own_gu, own_down, own_out = backward_attention(
        sum_gu, sum_down, out_part, branch_all, grad_middle, middle, tokens, freqs,
        spots_all, q_all, kv_all.reshape(2 * count, 128), attended_low, lse, normed_one_all, proj_w, out_w, 2,
    )
    own_proj = own_proj.astype(F32).transpose(1, 0, 2)
    cut = lambda a, start, stop: a[:, :, start:stop].reshape(16, -1)
    own_proj = jnp.concatenate(
        [
            cut(own_proj, 0, Q_COLS),
            cut(own_proj, Q_COLS, Q_COLS + HEAD_DIM),
            cut(own_proj, Q_COLS + HEAD_DIM, PROJ),
        ],
        -1,
    )
    own_gu = own_gu.reshape(TP, 16, HID // 128, 2, 128).transpose(1, 3, 0, 2, 4).reshape(16, 2 * FF).astype(F32)
    own_down = own_down.astype(F32).transpose(1, 0, 2).reshape(16, FF)
    return (
        outputs,
        input_grad,
        own_proj * gain_one,
        own_out.astype(F32),
        jnp.sum(own_proj * in_f, -1),
        own_gu * gain_two,
        own_down,
        jnp.sum(own_gu * mlp_f, -1),
    )


def solution(mesh):
    both = ("dp", "ctx")
    wide, flat = P(both, None), P(both)
    in_specs = (wide, flat, wide, wide, flat, wide, wide, flat, wide)
    out_specs = (wide, wide, wide, wide, flat, wide, wide, flat)
    return jax.shard_map(shards, mesh=mesh, in_specs=in_specs, out_specs=out_specs, check_vma=False)
```

```python
import jax
import jax.numpy as jnp
from jax import lax
from jax.experimental import pallas as pl
from jax.experimental.pallas import tpu as pltpu
from jax.sharding import PartitionSpec as P


D = 2048
HEADS = 32
KV_HEADS = 4
HEAD_DIM = 64
FF = 5632
REPEAT = HEADS // KV_HEADS
TP = 4
Q_COLS = D // TP
PROJ = Q_COLS + 2 * HEAD_DIM
HID = FF // TP

EPS = 1e-05
ROPE_BASE = 10000.0
NEG_FILL = -1e30

MESH = pl.DeviceIdType.MESH
BF16 = jnp.bfloat16
F32 = jnp.float32

SPLITS = ((PROJ, 384), (2 * HID, HID), (HID, 640))
OUT_SPLIT = 1024
VMEM_LIMIT = 60 << 20

NN = ((1,), (0,))
NT = ((1,), (1,))
TN = ((0,), (0,))


def place():
    dp, ctx = lax.axis_index("dp"), lax.axis_index("ctx")
    return (dp // 2) % 2, ctx // 4, ctx % 4, dp // 4, dp % 2


def device(xh, xl, y, z, c):
    return (z * 4 + xh * 2 + c, xl * 4 + y)


def along_y(d):
    def to(xh, xl, y, z, c):
        return xh, xl, (y + d) % 4, z, c

    return to


def along_x(d):
    def to(xh, xl, y, z, c):
        x = (xh * 2 + xl + d) % 4
        return x // 2, x % 2, y, z, c

    return to


def along_z(d):
    def to(xh, xl, y, z, c):
        return xh, xl, y, (z + d) % 4, c

    return to


def sibling(xh, xl, y, z, c):
    return xh, xl, y, z, 1 - c


def half_partner(xh, xl, y, z, c):
    return xh, 1 - xl, y, z, c


def crossed(xh, xl, y, z, c):
    return xh, xl, z, y, c


def say_hello(routes, cross=False):
    here = place()
    barrier = pltpu.get_barrier_semaphore()
    for back in routes:
        pl.semaphore_signal(barrier, inc=1, device_id=device(*back(*here)), device_id_type=MESH)
    if cross:

        @pl.when(here[2] != here[3])
        def _():
            pl.semaphore_signal(barrier, inc=1, device_id=device(*crossed(*here)), device_id_type=MESH)


def meet(routes, cross=False):
    here = place()
    barrier = pltpu.get_barrier_semaphore()
    if not cross:
        pl.semaphore_wait(barrier, len(routes))
        return
    away = here[2] != here[3]

    @pl.when(away)
    def _():
        pl.semaphore_wait(barrier, len(routes) + 1)

    @pl.when(jnp.logical_not(away))
    def _():
        pl.semaphore_wait(barrier, len(routes))


ALL_LINES = [along(d) for along in (along_y, along_x, along_z) for d in (1, 2, 3)] + [sibling]


class Copies:
    def __init__(self, send, recv):
        self.send, self.recv, self.count = send, recv, 0

    def __call__(self, src, dst, to):
        k, self.count = self.count, self.count + 1
        return pltpu.make_async_remote_copy(
            src_ref=src,
            dst_ref=dst,
            send_sem=self.send.at[k],
            recv_sem=self.recv.at[k],
            device_id=device(*to(*place())),
            device_id_type=MESH,
        )


def comm_call(kernel, name, ident, ins, outs, copies, locals_=0):
    return pl.pallas_call(
        kernel,
        out_shape=outs,
        in_specs=[pl.BlockSpec(memory_space=pl.ANY)] * len(ins),
        out_specs=[pl.BlockSpec(memory_space=pl.ANY)] * len(outs),
        scratch_shapes=[
            pltpu.SemaphoreType.DMA((copies,)),
            pltpu.SemaphoreType.DMA((copies,)),
            pltpu.SemaphoreType.DMA((max(locals_, 1),)),
        ],
        name=name,
        compiler_params=pltpu.CompilerParams(collective_id=ident, has_side_effects=True),
    )(*ins)


def struct(shape, dtype=BF16):
    return jax.ShapeDtypeStruct(shape, dtype)


class RingGather:
    def __init__(self, copy, own, dst, y):
        half = dst.shape[2] // 2
        lo, hi = pl.ds(0, half), pl.ds(half, half)
        back, on = (y + 3) % 4, (y + 1) % 4

        def first(cols, to):
            return copy(own.at[:, cols], dst.at[y, :, cols], to)

        def one(slot, cols, to):
            at = dst.at[slot, :, cols]
            return copy(at, at, to)

        self.first = [first(lo, along_y(1)), first(hi, along_y(3)), first(hi, along_y(1)), first(lo, along_y(3))]
        self.second = [one(back, lo, along_y(1)), one(on, hi, along_y(3))]

    def start(self):
        for cp in self.first:
            cp.start()

    def turn(self):
        for got, cp in zip(self.first, self.second):
            got.wait_recv()
            cp.start()

    def near(self):
        for cp in self.first[2:]:
            cp.wait_recv()

    def far(self):
        for cp in self.second:
            cp.wait_recv()

    def sent(self):
        for cp in self.first + self.second:
            cp.wait_send()


class RingSum:
    def __init__(self, copy, part, halves, whole, y):
        half = part.shape[2] // 2
        lo, hi = pl.ds(0, half), pl.ds(half, half)
        self.part, self.halves, self.whole, self.y = part, halves, whole, y
        self.cols = (lo, hi)
        far, on, back = (y + 2) % 4, (y + 1) % 4, (y + 3) % 4
        self.far = [
            copy(part.at[far, :, lo], halves.at[0], along_y(1)),
            copy(part.at[far, :, hi], halves.at[1], along_y(3)),
        ]
        self.near = [
            copy(part.at[on, :, hi], whole.at[0, :, hi], along_y(1)),
            copy(part.at[back, :, lo], whole.at[1, :, lo], along_y(3)),
        ]
        self.last = [
            copy(part.at[on, :, lo], whole.at[0, :, lo], along_y(1)),
            copy(part.at[back, :, hi], whole.at[1, :, hi], along_y(3)),
        ]
        self.slots = (on, back)

    def start(self):
        for cp in self.far + self.near:
            cp.start()

    def turn(self):
        for k in range(2):
            self.far[k].wait_recv()
            slot, cols = self.slots[k], self.cols[k]

            def body(r, _, slot=slot, cols=cols, k=k):
                rows = pl.ds(r * 32, 32)
                both = self.part[slot, rows, cols].astype(F32) + self.halves[k, rows].astype(F32)
                self.part[slot, rows, cols] = both.astype(BF16)
                return 0

            lax.fori_loop(0, self.part.shape[1] // 32, body, 0)
            self.last[k].start()

    def finish(self):
        for cp in self.near + self.last:
            cp.wait_recv()

    def rows(self, rows):
        own = self.part[self.y, rows].astype(F32)
        return own + self.whole[0, rows].astype(F32) + self.whole[1, rows].astype(F32)

    def sent(self):
        for cp in self.far + self.near + self.last:
            cp.wait_send()


class Gather:
    def __init__(self, copy, out, a, at, rows_only=False):
        xh, xl, y, z, c = at
        cols = out.shape[-1]
        left, right = pl.ds(0, a), pl.ds(a, cols - a)
        def cut(half, n):
            return slice(None) if half is None else pl.ds(half * (n // 2), n // 2)

        if rows_only:
            block = lambda z, x, c, cols: out.at[x[0], c, x[1], z, :, cols]
            z_line = lambda x, c, cols, half: out.at[x[0], c, x[1], cut(half, 4), :, cols]
            x_line = lambda z, c, cols, half: out.at[cut(half, 2), c, :, z, :, cols]
        else:
            block = lambda z, x, c, cols: out.at[z, x[0], c, pl.ds(x[1] * 64, 64), cols]
            z_line = lambda x, c, cols, half: out.at[cut(half, 4), x[0], c, pl.ds(x[1] * 64, 64), cols]
            x_line = lambda z, c, cols, half: out.at[z, cut(half, 2), c, :, cols]

        def same(ref, to):
            return copy(ref, ref, to)

        here = (xh, xl)
        self.first = []
        for d in (1, 3, 2):
            self.first.append(same(block(z, here, c, left), along_x(d)))
            self.first.append(same(block(z, here, c, right), along_z(d)))
        a_lo, a_hi = lambda z: x_line(z, c, left, 0), lambda z: x_line(z, c, left, 1)
        b_lo, b_hi = lambda x: z_line(x, c, right, 0), lambda x: z_line(x, c, right, 1)
        z_at = [(z + d) % 4 for d in range(4)]
        x_at = [along_x(d)(*at)[:2] for d in range(4)]
        self.lines = []
        for lo, hi, spots, along in ((a_lo, a_hi, z_at, along_z), (b_lo, b_hi, x_at, along_x)):
            going = [
                same(lo(spots[0]), along(1)),
                same(hi(spots[0]), along(3)),
                same(hi(spots[0]), along(1)),
                same(lo(spots[0]), along(3)),
            ]
            on = [same(lo(spots[3]), along(1)), same(hi(spots[1]), along(3))]
            self.lines.append((going, on))
        self.core = [same(block(z, here, c, pl.ds(0, cols)), sibling)]
        for d in (1, 3, 2):
            self.core.append(same(block(z, x_at[d], c, left), sibling))
            self.core.append(same(block(z_at[d], here, c, right), sibling))
        self.core_lines = []
        for d in (3, 1, 2):
            self.core_lines.append(
                (same(x_line(z_at[d], c, left, None), sibling), same(z_line(x_at[d], c, right, None), sibling))
            )

    def start(self):
        for cp in self.first:
            cp.start()
        self.core[0].start()

    def turn(self):
        for cp in self.first:
            cp.wait_recv()
        for going, _ in self.lines:
            for cp in going:
                cp.start()
        for cp in self.core[1:]:
            cp.start()

    def pass_on(self):
        for going, on in self.lines:
            for got, cp in zip(going[:2], on):
                got.wait_recv()
                cp.start()

    def near(self):
        for k, (going, _) in enumerate(self.lines):
            for side in range(2):
                going[2 + side].wait_recv()
                self.core_lines[side][k].start()

    def far(self):
        for k, (_, on) in enumerate(self.lines):
            for cp in on:
                cp.wait_recv()
            self.core_lines[2][k].start()

    def finish(self):
        for cp in self.core + [cp for pair in self.core_lines for cp in pair]:
            cp.wait_recv()

    def sent(self):
        for going, on in self.lines:
            for cp in going + on:
                cp.wait_send()
        for cp in self.first + self.core + [cp for pair in self.core_lines for cp in pair]:
            cp.wait_send()


def dot(left, right, dims=((1,), (0,))):
    return lax.dot_general(left, right, (dims, ((), ())), preferred_element_type=F32)


def swap_halves(v):
    lane = lax.broadcasted_iota(jnp.int32, v.shape, 1)
    return jnp.where(lane % 64 < 32, pltpu.roll(v, 96, 1), pltpu.roll(v, 32, 1))


def forward_attention(tokens, cotangent, spots, freqs, w_proj, w_gu, w_down, out_rows, ident):
    rows = tokens.shape[0]
    count = 4 * rows
    groups = [w_proj, w_gu, w_down]

    def kernel(
        tok_ref, cot_ref, spot_ref, freq_ref, wp, wg, wd, wo,
        normed_out, cot_all, gp, gg, gd, go, q_out, kv_out, att_out, lse_out, spot_out, middle_out, two_all,
        tok, normed, wp_v, wo_v, q_s, kv, vx, bias, att, part, halves, whole, spot_all, own_two, send, recv, local,
    ):
        say_hello(ALL_LINES, True)
        at = place()
        xh, xl, y, z, c = at
        copy = Copies(send, recv)
        slot = pl.ds(xl * 64 + y * 16, 16)
        nlocal = [0]

        def near(src, dst):
            cp = pltpu.make_async_copy(src, dst, local.at[nlocal[0]])
            nlocal[0] += 1
            return cp

        to_y = []
        stay = []
        for i, o in ((wp, gp), (wg, gg), (wd, gd)):
            to_y.append([copy(i.at[(y + d) % 4], o.at[z, xh, c, slot], along_y(d)) for d in (1, 3, 2)])
            stay.append(near(i.at[y], o.at[z, xh, c, slot]))
        over = copy(wo, go.at[xh, c, xl, y], crossed)
        keep = near(wo, go.at[xh, c, xl, z])
        spot_copies = [copy(spot_all.at[y], spot_all.at[y], along_y(d)) for d in (1, 3, 2)]
        tok_ring = RingGather(copy, tok_ref, tok, y)
        cot_ring = RingGather(copy, cot_ref, cot_all, y)
        two_ring = RingGather(copy, own_two, two_all, y)
        branch = RingSum(copy, part, halves, whole, y)
        kv_copy = copy(kv.at[1], kv.at[0], half_partner)
        g_proj = Gather(copy, gp, SPLITS[0][1], at)
        g_gu = Gather(copy, gg, SPLITS[1][1], at)
        g_down = Gather(copy, gd, SPLITS[2][1], at)
        g_out = Gather(copy, go, OUT_SPLIT, at, True)

        cot_own = near(cot_ref, cot_all.at[y])
        tok_own = near(tok_ref, tok.at[y])
        tok_own.start()
        cot_own.start()
        spot_all[y] = spot_ref[...]
        for cp in stay:
            cp.start()
        meet(ALL_LINES, True)
        away = y != z
        for cp in to_y[0]:
            cp.start()

        @pl.when(away)
        def _():
            over.start()

        @pl.when(jnp.logical_not(away))
        def _():
            keep.start()

        for cp in spot_copies + to_y[1] + to_y[2] + tok_ring.first:
            cp.start()

        def norm_block(k):
            def body(r, _):
                rs = pl.ds(r * 32, 32)
                v = tok[k, rs].astype(F32)
                inv = lax.rsqrt(jnp.mean(v * v, -1, keepdims=True) + EPS)
                normed[k, rs] = (v * inv).astype(BF16)
                return 0

            lax.fori_loop(0, rows // 32, body, 0)

        stay[0].wait()
        for cp in to_y[0]:
            cp.wait_recv()
        g_proj.start()

        @pl.when(away)
        def _():
            over.wait()

        @pl.when(jnp.logical_not(away))
        def _():
            keep.wait()

        g_out.start()
        tok_own.wait()
        norm_block(y)
        g_proj.turn()
        stay[1].wait()
        stay[2].wait()
        for cp in to_y[1] + to_y[2]:
            cp.wait_recv()
        g_gu.start()
        g_down.start()
        g_proj.pass_on()
        g_out.turn()
        for cp in spot_copies:
            cp.wait_recv()
        tok_ring.turn()
        g_proj.near()
        g_proj.far()

        cos, sin = [], []
        freq, sign = freq_ref[0:1, :], freq_ref[1:2, :]
        spot_cols = []
        for k in range(4):
            col = jnp.transpose(jnp.broadcast_to(spot_all[k, 0:1, :], (128, 128)))
            spot_out[k] = spot_all[k]
            spot_cols.append(col)
            cos.append(jnp.cos(col * freq))
            sin.append(jnp.sin(col * freq) * sign)
        cos, sin = jnp.concatenate(cos, 0), jnp.concatenate(sin, 0)
        low_half = xl == 0
        reach = jnp.where(low_half, -1.0, 2048.0)
        for k in range(4):
            for j in range(8):
                row = lax.broadcasted_iota(jnp.int32, (128, 128), 0) + k * 128
                col = lax.broadcasted_iota(jnp.int32, (128, 128), 1) + j * 128
                apart = (row - col + 512).astype(F32)
                seen = apart <= spot_cols[k]
                if j < 4:
                    seen = seen & (apart <= reach)
                else:
                    seen = seen & (col - 512 <= row)
                bias[pl.ds(k * 128, 128), pl.ds(j * 128, 128)] = jnp.where(seen, 0.0, NEG_FILL)

        g_proj.finish()
        wp_load = near(gp, wp_v)
        wp_load.start()
        g_out.pass_on()
        tok_ring.near()
        norm_block((y + 3) % 4)
        norm_block((y + 1) % 4)
        g_out.near()
        tok_ring.far()
        cot_ring.start()
        norm_block((y + 2) % 4)
        normed_save = near(normed, normed_out)
        normed_save.start()

        wp_load.wait()
        left = normed[...].reshape(count, D)
        lane = lax.broadcasted_iota(jnp.int32, (count, 128), 1)
        upper = lane >= 64
        raw = dot(left, wp_v[:, :, :, :, pl.ds(Q_COLS, 128)].reshape(D, 128))
        turned = raw * jnp.where(upper, 1.0, cos) + swap_halves(raw) * jnp.where(upper, 0.0, sin)
        kv[1] = turned.astype(BF16)
        kv_copy.start()
        g_out.far()
        g_gu.turn()
        g_down.turn()
        for j in range(2):
            raw2 = dot(left, wp_v[:, :, :, :, pl.ds(j * 256, 256)].reshape(D, 256))
            for e in range(2):
                raw = raw2[:, e * 128 : e * 128 + 128]
                turned = (raw * cos + swap_halves(raw) * sin).astype(BF16).astype(F32) * (HEAD_DIM ** (-0.5))
                pair = j * 2 + e
                q_s[2 * pair] = jnp.where(upper, 0.0, turned).astype(BF16)
                q_s[2 * pair + 1] = jnp.where(upper, 0.0, pltpu.roll(turned, 64, 1)).astype(BF16)
        kv_copy.wait_recv()
        for k in range(2):
            vx[k] = jnp.where(upper, kv[k].astype(F32), 1.0).astype(BF16)
        q_save = near(q_s, q_out)
        q_save.start()
        kv_save = near(kv, kv_out)
        kv_save.start()
        g_out.finish()
        wo_load = near(go, wo_v)
        wo_load.start()

        def attend(pair):
            for b in range(2):
                rs = pl.ds(b * 256, 256)
                seen = 256 * (b + 1)
                lane = lax.broadcasted_iota(jnp.int32, (256, 128), 1) < 64
                found = []
                for e in range(2):
                    q = q_s[2 * pair + e, rs]
                    s0 = dot(q, kv[0], NT) + bias[rs, pl.ds(0, 512)]
                    s1 = dot(q, kv[1, pl.ds(0, seen)], NT) + bias[rs, pl.ds(512, seen)]
                    m = jnp.maximum(jnp.max(s0, -1, keepdims=True), jnp.max(s1, -1, keepdims=True))
                    p0 = jnp.exp(s0 - m).astype(BF16)
                    p1 = jnp.exp(s1 - m).astype(BF16)
                    o = dot(p0, vx[0]) + dot(p1, vx[1, pl.ds(0, seen)])
                    r = pltpu.roll(o, 64, 1)
                    found.append((o, r))
                    log_total = m + jnp.log(jnp.where(lane, o, r))
                    lse_out[2 * pair + e, :, rs] = jnp.transpose(log_total)[0:8]
                (o, r), (o2, r2) = found
                both = jnp.where(lane, r / o, o2 / r2)
                att[rs, pl.ds(pl.multiple_of(pair * 128, 128), 128)] = both.astype(BF16)

        def two_pairs(k):
            def body(i, _):
                attend(2 * k + i)
                return 0

            lax.fori_loop(0, 2, body, 0)

        two_pairs(0)
        cot_ring.turn()
        two_pairs(1)
        att_save = near(att, att_out)
        att_save.start()
        wo_load.wait()

        for j in range(4):
            cols = pl.ds(j * 512, 512)
            w = wo_v[:, :, :, :, :, cols].reshape(Q_COLS, 512)
            part[:, :, cols] = dot(att[...], w).astype(BF16).reshape(4, rows, 512)
        branch.start()
        g_gu.pass_on()
        g_down.pass_on()
        branch.turn()
        g_gu.near()
        g_down.near()
        cot_ring.near()
        cot_ring.far()
        branch.finish()

        def mid(r, _):
            rs = pl.ds(r * 32, 32)
            v = tok_ref[rs].astype(F32) + branch.rows(rs)
            middle_out[rs] = v
            inv = lax.rsqrt(jnp.mean(v * v, -1, keepdims=True) + EPS)
            own_two[rs] = (v * inv).astype(BF16)
            return 0

        lax.fori_loop(0, rows // 32, mid, 0)
        two_own = near(own_two, two_all.at[y])
        two_own.start()
        two_ring.start()
        two_ring.turn()
        g_gu.far()
        g_down.far()
        two_ring.near()
        two_ring.far()
        g_gu.finish()
        g_down.finish()
        for cp in (cot_own, normed_save, q_save, kv_save, att_save, two_own):
            cp.wait()
        for group in to_y:
            for cp in group:
                cp.wait_send()
        for cp in spot_copies + [kv_copy]:
            cp.wait_send()
        for thing in (g_proj, g_out, g_gu, g_down, tok_ring, cot_ring, two_ring, branch):
            thing.sent()

    anywhere, vmem = pl.BlockSpec(memory_space=pl.ANY), pl.BlockSpec(memory_space=pltpu.VMEM)
    outs = [
        (struct((4, rows, D)), anywhere),
        (struct((4, rows, D)), anywhere),
        (struct((4, 2, 2, 128, PROJ)), anywhere),
        (struct((4, 2, 2, 128, 2 * HID)), anywhere),
        (struct((4, 2, 2, 128, HID)), anywhere),
        (struct((2, 2, 2, 4, 16, D)), anywhere),
        (struct((REPEAT, count, 128)), anywhere),
        (struct((2, count, 128)), anywhere),
        (struct((count, Q_COLS)), anywhere),
        (struct((REPEAT, 8, count), F32), vmem),
        (struct((4, 8, 128), F32), vmem),
        (struct((rows, D), F32), vmem),
        (struct((4, rows, D)), anywhere),
    ]
    copies = 9 + 1 + 3 + 6 * 3 + 6 + 1 + 31 * 4
    return pl.pallas_call(
        kernel,
        out_shape=[o[0] for o in outs],
        in_specs=[vmem] * 8,
        out_specs=[o[1] for o in outs],
        scratch_shapes=[
            pltpu.VMEM((4, rows, D), BF16),
            pltpu.VMEM((4, rows, D), BF16),
            pltpu.VMEM((4, 2, 2, 128, PROJ), BF16),
            pltpu.VMEM((2, 2, 2, 4, 16, D), BF16),
            pltpu.VMEM((REPEAT, count, 128), BF16),
            pltpu.VMEM((2, count, 128), BF16),
            pltpu.VMEM((2, count, 128), BF16),
            pltpu.VMEM((count, 2 * count), F32),
            pltpu.VMEM((count, Q_COLS), BF16),
            pltpu.VMEM((4, rows, D), BF16),
            pltpu.VMEM((2, rows, D // 2), BF16),
            pltpu.VMEM((2, rows, D), BF16),
            pltpu.VMEM((4, 8, 128), F32),
            pltpu.VMEM((rows, D), BF16),
            pltpu.SemaphoreType.DMA((copies,)),
            pltpu.SemaphoreType.DMA((copies,)),
            pltpu.SemaphoreType.DMA((16,)),
        ],
        name="forward_attention",
        compiler_params=pltpu.CompilerParams(
            collective_id=ident, has_side_effects=True, vmem_limit_bytes=VMEM_LIMIT
        ),
    )(tokens, cotangent, spots, freqs, w_proj, w_gu, w_down, out_rows)


def tiles(ref):
    if len(ref.shape) == 2:
        return [ref]
    return [t for k in range(ref.shape[0]) for t in tiles(ref.at[k])]


def add_up(dst, *others):
    for out, *terms in zip(tiles(dst), *[tiles(o) for o in others]):
        rows = out.shape[0]
        step = min(rows, 32)

        def body(r, _, out=out, terms=terms, step=step):
            rs = pl.ds(r * step, step)
            value = out[rs].astype(F32)
            for t in terms:
                value = value + t[rs].astype(F32)
            out[rs] = value.astype(BF16)
            return 0

        lax.fori_loop(0, rows // step, body, 0)


class LineSum:
    def __init__(self, copy, lo, hi, along, far, near):
        self.lo, self.hi, self.far_in, self.near_in = lo, hi, far, near
        self.far = [copy(lo(2), far.at[0], along(1)), copy(hi(2), far.at[1], along(3))]
        self.near = [copy(hi(1), near.at[0, 1], along(1)), copy(lo(3), near.at[1, 0], along(3))]
        self.last = [copy(lo(1), near.at[0, 0], along(1)), copy(hi(3), near.at[1, 1], along(3))]

    def start(self):
        for cp in self.far + self.near:
            cp.start()

    def turn(self):
        self.far[0].wait_recv()
        add_up(self.lo(1), self.far_in.at[0])
        self.last[0].start()
        self.far[1].wait_recv()
        add_up(self.hi(3), self.far_in.at[1])
        self.last[1].start()

    def finish(self):
        for cp in self.near + self.last:
            cp.wait_recv()
        add_up(self.lo(0), self.near_in.at[0, 0], self.near_in.at[1, 0])
        add_up(self.hi(0), self.near_in.at[0, 1], self.near_in.at[1, 1])

    def sent(self):
        for cp in self.far + self.near + self.last:
            cp.wait_send()


class GradLines:
    def __init__(self, copy, terms, a, at, buffers, rows_only=False):
        xh, xl, y, z, c = at
        far_a, near_a, far_b, near_b = buffers
        cols = terms.shape[-1]
        left, right = pl.ds(0, a), pl.ds(a, cols - a)
        x_at = [along_x(d)(*at)[:2] for d in range(4)]
        z_at = [(z + d) % 4 for d in range(4)]
        if rows_only:
            spot = lambda x, z, cols: terms.at[x[0], c, x[1], z, :, cols]
            a_half = lambda h: lambda d: terms.at[h, c, :, z_at[d], :, left]
            b_half = lambda h: lambda d: terms.at[x_at[d][0], c, x_at[d][1], pl.ds(2 * h, 2), :, right]
        else:
            base = (lambda z, xh: (z, xh, c)) if len(terms.shape) == 5 else (lambda z, xh: (z, xh))
            spot = lambda x, z, cols: terms.at[base(z, x[0]) + (pl.ds(x[1] * 64, 64), cols)]
            a_half = lambda h: lambda d: terms.at[base(z_at[d], h) + (slice(None), left)]
            b_half = lambda h: lambda d: terms.at[
                base(pl.ds(2 * h, 2), x_at[d][0]) + (pl.ds(x_at[d][1] * 64, 64), right)
            ]
        self.lines = [
            LineSum(copy, a_half(0), a_half(1), along_z, far_a, near_a),
            LineSum(copy, b_half(0), b_half(1), along_x, far_b, near_b),
        ]
        self.spot_a = lambda x: spot(x, z, left)
        self.spot_b = lambda z: spot(x_at[0], z, right)

    def start(self):
        for line in self.lines:
            line.start()

    def turn(self):
        for line in self.lines:
            line.turn()

    def finish(self):
        for line in self.lines:
            line.finish()

    def sent(self):
        for line in self.lines:
            line.sent()


class GradOwners:
    def __init__(self, copy, local_copy, spot_a, spot_b, out, at, buffers, rows_only=False):
        xh, xl, y, z, c = at
        self.at, self.rows_only = at, rows_only
        got_a, got_b, own = buffers
        a, cols = got_a.shape[-1], own.shape[-1]
        self.second = []
        for d in (1, 3, 2):
            self.second.append(copy(spot_a(along_x(d)(*at)[:2]), got_a.at[d - 1], along_x(d)))
            self.second.append(copy(spot_b((z + d) % 4), got_b.at[d - 1], along_z(d)))
        self.mine = (spot_a((xh, xl)), spot_b(z))
        self.got = (got_a, got_b)
        self.own, self.cuts = own, (pl.ds(0, a), pl.ds(a, cols - a))
        if rows_only:
            self.over = copy(own, out, crossed)
            self.keep = local_copy(own, out)
        else:
            self.to_y = [copy(own.at[(y + d) % 4], out.at[y], along_y(d)) for d in (1, 3, 2)]
            self.keep = local_copy(own.at[y], out.at[y])

    def start(self):
        for cp in self.second:
            cp.start()

    def deliver(self):
        for cp in self.second:
            cp.wait_recv()
        for mine, got, cut in zip(self.mine, self.got, self.cuts):
            value = mine[...].astype(F32)
            for d in range(3):
                value = value + got[d].astype(F32)
            own = self.own
            if self.rows_only:
                own[:, cut] = value.astype(BF16)
            else:
                own[:, :, cut] = value.astype(BF16).reshape(4, 16, value.shape[-1])
        if self.rows_only:
            y, z = self.at[2], self.at[3]

            @pl.when(y != z)
            def _():
                self.over.start()

            @pl.when(y == z)
            def _():
                self.keep.start()

        else:
            for cp in self.to_y:
                cp.start()
            self.keep.start()

    def finish(self):
        if self.rows_only:
            y, z = self.at[2], self.at[3]

            @pl.when(y != z)
            def _():
                self.over.wait()

            @pl.when(y == z)
            def _():
                self.keep.wait()

        else:
            for cp in self.to_y:
                cp.wait()
            self.keep.wait()
        for cp in self.second:
            cp.wait_send()


def line_buffers(cols, a, rows_only=False):
    b = cols - a
    a_half, b_half = ((2, 16), (2, 16)) if rows_only else ((128,), (2, 64))
    return [
        pltpu.VMEM((2,) + a_half + (a,), BF16),
        pltpu.VMEM((2, 2) + a_half + (a,), BF16),
        pltpu.VMEM((2,) + b_half + (b,), BF16),
        pltpu.VMEM((2, 2) + b_half + (b,), BF16),
    ]


def owner_buffers(cols, a, rows_only=False):
    spot, own = (16, (16, cols)) if rows_only else (64, (4, 16, cols))
    return [pltpu.VMEM((3, spot, a), BF16), pltpu.VMEM((3, spot, cols - a), BF16), pltpu.VMEM(own, BF16)]


def rotation(spot_rows, freq_ref):
    cos, sin = [], []
    for k in range(4):
        col = jnp.transpose(jnp.broadcast_to(spot_rows[k, 0:1, :], (128, 128)))
        cos.append(jnp.cos(col * freq_ref[0:1, :]))
        sin.append(jnp.sin(col * freq_ref[0:1, :]) * freq_ref[1:2, :])
    return jnp.concatenate(cos, 0), jnp.concatenate(sin, 0)


def backward_attention(
    gu_a, gu_b, sum_down, out_part, branch_all, grad_middle, middle, tokens, freqs,
    spots, q_all, kv_all, attended, lse, normed_all, proj_w, out_w, ident,
):
    rows = tokens.shape[0]
    count = 4 * rows
    scale = HEAD_DIM ** (-0.5)

    def kernel(
        gu_a_ref, gu_b_ref, s_down, op_ref, br_ref, gm_ref, mid_ref, tok_ref, freq_ref,
        spot_ref, q_ref, kv_ref, att_ref, lse_ref, nm_ref, wp_ref, wo_ref,
        out_ref, ig_ref, o_proj, o_gu, o_down, o_out,
        v_gu_a, v_gu_b, v_down, part, halves, whole, halves2, whole2, br, q_s, do_s, kv, kvt, att, delta, bias, cos_s, sin_s,
        dkv, kv_send, kv_in, gp, normed, wp, wo, t_proj, rc_proj, t_out, rc_out, *rest,
    ):
        bufs, (send, recv, local) = rest[:24], rest[24:]
        say_hello(ALL_LINES, True)
        at = place()
        xh, xl, y, z, c = at
        copy = Copies(send, recv)
        nlocal = [0]

        def near(src, dst):
            cp = pltpu.make_async_copy(src, dst, local.at[nlocal[0]])
            nlocal[0] += 1
            return cp

        load_gu, load_gu_b, load_down = near(gu_a_ref, v_gu_a), near(gu_b_ref, v_gu_b), near(s_down, v_down)
        load_op, load_br, load_wo = near(op_ref, part), near(br_ref, br), near(wo_ref, wo)
        load_att, load_q = near(att_ref, att), near(q_ref, q_s)
        load_kv = near(kv_ref, kv)
        load_nm, load_wp = near(nm_ref, normed), near(wp_ref, wp)
        for cp in (load_br, load_wo, load_gu, load_gu_b, load_op, load_down, load_att, load_q, load_kv, load_nm, load_wp):
            cp.start()
        outs = RingSum(copy, part, halves, whole, y)
        ones = RingSum(copy, part, halves2, whole2, y)
        kv_copy = copy(kv_send, kv_in, half_partner)
        core_proj = copy(t_proj.at[:, :, 1 - c], rc_proj, sibling)
        core_out = copy(t_out.at[:, 1 - c], rc_out, sibling)
        gu_owners = GradOwners(
            copy,
            near,
            lambda x: v_gu_a.at[x[0], pl.ds(x[1] * 64, 64)],
            lambda z: v_gu_b.at[z],
            o_gu,
            at,
            bufs[0:3],
        )
        down_lines = GradLines(copy, v_down, SPLITS[2][1], at, bufs[3:7])
        down_owners = GradOwners(copy, near, down_lines.spot_a, down_lines.spot_b, o_down, at, bufs[7:10])
        proj_lines = GradLines(copy, t_proj, SPLITS[0][1], at, bufs[10:14])
        proj_owners = GradOwners(copy, near, proj_lines.spot_a, proj_lines.spot_b, o_proj, at, bufs[14:17])
        out_lines = GradLines(copy, t_out, OUT_SPLIT, at, bufs[17:21], True)
        out_owners = GradOwners(copy, near, out_lines.spot_a, out_lines.spot_b, o_out, at, bufs[21:24], True)

        cos, sin = rotation(spot_ref, freq_ref)
        cos_s[...] = cos
        sin_s[...] = sin
        reach = jnp.where(xl == 0, -1.0, 2048.0)
        for k in range(4):
            spots_row = spot_ref[k, 0:1, :]
            for j in range(8):
                key = lax.broadcasted_iota(jnp.int32, (128, 128), 0) + j * 128
                row = lax.broadcasted_iota(jnp.int32, (128, 128), 1) + k * 128
                apart = (row - key + 512).astype(F32)
                seen = apart <= spots_row
                if j < 4:
                    seen = seen & (apart <= reach)
                else:
                    seen = seen & (key - 512 <= row)
                bias[pl.ds(j * 128, 128), pl.ds(k * 128, 128)] = jnp.where(seen, 0.0, NEG_FILL)
        dkv[...] = jnp.zeros_like(dkv)

        meet(ALL_LINES, True)
        load_op.wait()
        outs.start()
        load_gu.wait()
        load_gu_b.wait()
        gu_owners.start()
        load_down.wait()
        down_lines.start()

        load_br.wait()
        load_wo.wait()
        load_att.wait()
        lane = lax.broadcasted_iota(jnp.int32, (count, 128), 1)
        for p in range(4):
            w = wo[p // 2, p % 2].reshape(128, D)
            low = dot(br[...].reshape(count, D), w, NT).astype(BF16).astype(F32)
            do_s[2 * p] = jnp.where(lane < 64, 0.0, pltpu.roll(low, 64, 1)).astype(BF16)
            do_s[2 * p + 1] = jnp.where(lane < 64, 0.0, low).astype(BF16)
            prod = jnp.transpose(low * att[:, pl.ds(p * 128, 128)].astype(F32))
            for e in range(2):
                total_row = jnp.sum(prod[e * 64 : e * 64 + 64], 0, keepdims=True)
                delta[2 * p + e] = jnp.broadcast_to(total_row, (8, count))
        outs.turn()

        for k in range(4):
            term = dot(att[:, pl.ds(k * 128, 128)], br[...].reshape(count, D), TN)
            t_out[k // 2, k % 2] = term.astype(BF16).reshape(2, 4, 16, D)
        core_out.start()
        load_q.wait()
        load_kv.wait()
        for k in range(2):
            turned = jnp.transpose(kv[pl.ds(k * count, count)].astype(F32)).astype(BF16)
            kvt[:, pl.ds(k * count, count)] = turned

        def backward(pair):
            for b in range(2):
                rs = pl.ds(b * 256, 256)
                seen = pl.ds(0, 512 + 256 * (b + 1))
                found = []
                for e in range(2):
                    h = 2 * pair + e
                    q, do = q_s[h, rs], do_s[h, rs]
                    st = dot(kv[seen], q, NT) + bias[seen, rs] - lse_ref[h, 0:1, rs]
                    p = jnp.exp(st)
                    dp = dot(kv[seen], do, NT)
                    ds = (p * (dp - delta[h, 0:1, rs])).astype(BF16)
                    dkv[seen] += dot(ds, q) + dot(p.astype(BF16), do)
                    found.append(dot(kvt[:, seen], ds)[0:64])
                both = jnp.transpose(jnp.concatenate(found, 0)) * scale
                both = both * cos_s[rs] - swap_halves(both) * sin_s[rs]
                gp[rs, pl.ds(pl.multiple_of(pair * 128, 128), 128)] = both.astype(BF16)

        def two_pairs(k):
            def body(i, _):
                backward(2 * k + i)
                return 0

            lax.fori_loop(0, 2, body, 0)

        two_pairs(0)
        down_lines.turn()
        gu_owners.deliver()
        two_pairs(1)
        kv_send[...] = dkv[pl.ds(0, count)].astype(BF16)
        kv_copy.start()
        core_out.wait_recv()
        add_up(t_out.at[:, c], rc_out)
        out_lines.start()
        down_lines.finish()
        down_owners.start()
        outs.finish()

        def finish_out(r, _):
            rs = pl.ds(r * 32, 32)
            out_ref[rs] = (mid_ref[rs] + outs.rows(rs)).astype(BF16)
            return 0

        lax.fori_loop(0, rows // 32, finish_out, 0)
        outs.sent()
        kv_copy.wait_recv()
        got = dkv[pl.ds(count, count)] + kv_in[...].astype(F32)
        back = got * cos_s[...] - swap_halves(got) * sin_s[...]
        gp[:, pl.ds(Q_COLS, 128)] = jnp.where(lane < 64, back, got).astype(BF16)

        load_wp.wait()
        for j in range(4):
            w = wp[j].reshape(512, PROJ)
            part[:, :, pl.ds(j * 512, 512)] = dot(gp[...], w, NT).astype(BF16).reshape(4, rows, 512)
        ones.start()
        load_nm.wait()
        for k in range(4):
            left = normed[:, :, pl.ds(k * 512, 512)].reshape(count, 512)
            t_proj[k] = dot(left, gp[...], TN).astype(BF16).reshape(2, 2, 128, PROJ)
        core_proj.start()
        out_lines.turn()
        ones.turn()
        down_owners.deliver()
        core_proj.wait_recv()
        for k in range(4):
            add_up(t_proj.at[k, :, c], rc_proj.at[k])
        proj_lines.start()
        out_lines.finish()
        out_owners.start()
        proj_lines.turn()
        ones.finish()

        def finish_in(r, _):
            rs = pl.ds(r * 32, 32)
            v = tok_ref[rs].astype(F32)
            inv = lax.rsqrt(jnp.mean(v * v, -1, keepdims=True) + EPS)
            v = v * inv
            g = ones.rows(rs)
            ig_ref[rs] = gm_ref[rs] + inv * (g - v * jnp.mean(g * v, -1, keepdims=True))
            return 0

        lax.fori_loop(0, rows // 32, finish_in, 0)
        proj_lines.finish()
        proj_owners.start()
        out_owners.deliver()
        proj_owners.deliver()
        ones.sent()
        for cp in (kv_copy, core_proj, core_out):
            cp.wait_send()
        for owners in (gu_owners, down_owners, out_owners, proj_owners):
            owners.finish()
        for lines in (down_lines, out_lines, proj_lines):
            lines.sent()

    anywhere, vmem = pl.BlockSpec(memory_space=pl.ANY), pl.BlockSpec(memory_space=pltpu.VMEM)
    in_specs = [anywhere] * 5 + [vmem] * 5 + [anywhere] * 3 + [vmem] + [anywhere] * 3
    outs = [
        (struct((rows, D)), vmem),
        (struct((rows, D), F32), vmem),
        (struct((4, 16, PROJ)), anywhere),
        (struct((4, 16, 2 * HID)), anywhere),
        (struct((4, 16, HID)), anywhere),
        (struct((16, D)), anywhere),
    ]
    whole = lambda: [pltpu.VMEM((2, rows, D // 2), BF16), pltpu.VMEM((2, rows, D), BF16)]
    copies = 12 + 3 + 9 + 21 * 2 + 19
    return pl.pallas_call(
        kernel,
        out_shape=[o[0] for o in outs],
        in_specs=in_specs,
        out_specs=[o[1] for o in outs],
        scratch_shapes=[
            pltpu.VMEM((2, 128, SPLITS[1][1]), BF16),
            pltpu.VMEM((4, 64, 2 * HID - SPLITS[1][1]), BF16),
            pltpu.VMEM((4, 2, 128, HID), BF16),
            pltpu.VMEM((4, rows, D), BF16),
            *whole(),
            *whole(),
            pltpu.VMEM((4, rows, D), BF16),
            pltpu.VMEM((REPEAT, count, 128), BF16),
            pltpu.VMEM((REPEAT, count, 128), BF16),
            pltpu.VMEM((2 * count, 128), BF16),
            pltpu.VMEM((128, 2 * count), BF16),
            pltpu.VMEM((count, Q_COLS), BF16),
            pltpu.VMEM((REPEAT, 8, count), F32),
            pltpu.VMEM((2 * count, count), F32),
            pltpu.VMEM((count, 128), F32),
            pltpu.VMEM((count, 128), F32),
            pltpu.VMEM((2 * count, 128), F32),
            pltpu.VMEM((count, 128), BF16),
            pltpu.VMEM((count, 128), BF16),
            pltpu.VMEM((count, PROJ), BF16),
            pltpu.VMEM((4, rows, D), BF16),
            pltpu.VMEM((4, 2, 2, 128, PROJ), BF16),
            pltpu.VMEM((2, 2, 2, 4, 16, D), BF16),
            pltpu.VMEM((4, 2, 2, 128, PROJ), BF16),
            pltpu.VMEM((4, 2, 128, PROJ), BF16),
            pltpu.VMEM((2, 2, 2, 4, 16, D), BF16),
            pltpu.VMEM((2, 2, 4, 16, D), BF16),
            *owner_buffers(2 * HID, SPLITS[1][1]),
            *line_buffers(HID, SPLITS[2][1]),
            *owner_buffers(HID, SPLITS[2][1]),
            *line_buffers(PROJ, SPLITS[0][1]),
            *owner_buffers(PROJ, SPLITS[0][1]),
            *line_buffers(D, OUT_SPLIT, True),
            *owner_buffers(D, OUT_SPLIT, True),
            pltpu.SemaphoreType.DMA((copies,)),
            pltpu.SemaphoreType.DMA((copies,)),
            pltpu.SemaphoreType.DMA((16,)),
        ],
        name="backward_attention",
        compiler_params=pltpu.CompilerParams(
            collective_id=ident, has_side_effects=True, vmem_limit_bytes=VMEM_LIMIT
        ),
    )(
        gu_a, gu_b, sum_down, out_part, branch_all, grad_middle, middle, tokens, freqs,
        spots, q_all, kv_all, attended, lse, normed_all, proj_w, out_w,
    )


def feed_forward(seq_two, seq_cot, gu_w, down_w, middle, cotangent, ident):
    rows = middle.shape[0]
    count = 4 * rows
    tiles_gu, pairs = HID // 128, HID // 256

    def kernel(
        two_ref, cot_ref, wg_ref, wd_ref, mid_ref, own_cot,
        branch_all, gm_ref, gu_a, gu_b, s_down, op_out,
        part, halves, whole, two, gu, cot, hid, gh, turned, t_gu, t_down, rc_gu, rc_down, branch, op,
        far_a, near_a, far_b, near_b, send, recv, local, weights,
    ):
        partners = [along_y(1), along_y(3), along_x(1), along_x(3), along_z(1), along_z(3), sibling]
        say_hello(partners)
        at = place()
        xh, xl, y, z, c = at
        copy = Copies(send, recv)
        nlocal = [0]

        def near(src, dst):
            cp = pltpu.make_async_copy(src, dst, local.at[nlocal[0]])
            nlocal[0] += 1
            return cp

        def load_gu(j):
            tile = pl.ds(pl.multiple_of(j * 256, 256), 256)
            return pltpu.make_async_copy(wg_ref.at[:, :, :, :, tile], t_gu.at[:, :, :, :, tile], weights.at[j])

        def load_down(j, width=256):
            tile = pl.ds(pl.multiple_of(j * 256, 256), width)
            return pltpu.make_async_copy(
                wd_ref.at[:, :, :, :, tile], t_down.at[:, :, :, :, tile], weights.at[tiles_gu + j]
            )

        load_cot, load_two = near(cot_ref, cot), near(two_ref, two)
        load_cot.start()
        last_down = load_down(pairs, HID - 256 * pairs)

        def begin_down(j, _):
            load_down(j).start()
            return 0

        def begin_gu(j, _):
            load_gu(j).start()
            return 0

        lax.fori_loop(0, pairs, begin_down, 0)
        last_down.start()
        load_two.start()
        lax.fori_loop(0, tiles_gu, begin_gu, 0)
        ring = RingSum(copy, part, halves, whole, y)
        gather = RingGather(copy, branch, branch_all, y)
        own = near(branch, branch_all.at[y])
        cores = [
            (copy(t_gu.at[k, :, 1 - c], rc_gu.at[k], sibling), copy(t_down.at[k, :, 1 - c], rc_down.at[k], sibling))
            for k in range(4)
        ]
        saves = [near(t_down.at[k, :, c], s_down.at[k]) for k in range(4)]
        lines = GradLines(copy, t_gu, SPLITS[1][1], at, (far_a, near_a, far_b, near_b))
        saves_gu = [
            near(t_gu.at[z, :, c, :, pl.ds(0, HID)], gu_a),
            near(t_gu.at[:, xh, c, pl.ds(xl * 64, 64), pl.ds(HID, HID)], gu_b),
        ]
        save_op = near(op, op_out)
        load_cot.wait()

        def hidden_back(j, _):
            load_down(j).wait()
            tile = pl.ds(pl.multiple_of(j * 256, 256), 256)
            gh[:, tile] = dot(cot[...].reshape(count, D), t_down[:, :, :, :, tile].reshape(D, 256))
            return 0

        lax.fori_loop(0, pairs, hidden_back, 0)
        last_down.wait()
        tile = pl.ds(256 * pairs, HID - 256 * pairs)
        gh[:, tile] = dot(cot[...].reshape(count, D), t_down[:, :, :, :, tile].reshape(D, HID - 256 * pairs))
        load_two.wait()

        def hidden(j, _):
            load_gu(j).wait()
            both = pl.ds(pl.multiple_of(j * 256, 256), 256)
            one = pl.ds(pl.multiple_of(j * 128, 128), 128)
            gate_up = dot(two[...].reshape(count, D), t_gu[:, :, :, :, both].reshape(D, 256))
            gate, up = gate_up[:, :128], gate_up[:, 128:]
            back = gh[:, one]
            sigmoid = jax.nn.sigmoid(gate)
            silu = gate * sigmoid
            hid[:, one] = (silu * up).astype(BF16)
            grad_gate = back * up * sigmoid * (1.0 + gate * (1.0 - sigmoid))
            gu[:, both] = jnp.concatenate([grad_gate, back * silu], 1).astype(BF16)
            return 0

        lax.fori_loop(0, tiles_gu, hidden, 0)

        def part_two(k, _):
            cols = pl.ds(pl.multiple_of(k * 512, 512), 512)
            part[:, :, cols] = dot(gu[...], t_gu[k].reshape(512, 2 * HID), NT).astype(BF16).reshape(4, rows, 512)
            return 0

        lax.fori_loop(0, 4, part_two, 0)
        meet(partners)
        ring.start()

        def part_out(k, _):
            cols = pl.ds(pl.multiple_of(k * 512, 512), 512)
            op[:, :, cols] = dot(hid[...], t_down[k].reshape(512, HID), NT).astype(BF16).reshape(4, rows, 512)
            return 0

        def terms_gu(k):
            cols = pl.ds(k * 512, 512)
            turned[...] = jnp.transpose(two[:, :, cols].reshape(count, 512))

            def some(j, _):
                tile = pl.ds(pl.multiple_of(j * 256, 256), 256)
                t_gu[k, :, :, :, tile] = dot(turned[...], gu[:, tile]).astype(BF16).reshape(2, 2, 128, 256)
                return 0

            lax.fori_loop(0, 2 * HID // 256, some, 0)
            cores[k][0].start()

        def terms_down(k):
            cols = pl.ds(k * 512, 512)
            turned[...] = jnp.transpose(cot[:, :, cols].reshape(count, 512))

            def more(j, width=256):
                tile = pl.ds(pl.multiple_of(j * 256, 256), width)
                t_down[k, :, :, :, tile] = dot(turned[...], hid[:, tile]).astype(BF16).reshape(2, 2, 128, width)
                return 0

            lax.fori_loop(0, pairs, lambda j, _: more(j), 0)
            more(pairs, HID - 256 * pairs)
            cores[k][1].start()

        terms_gu(0)
        ring.turn()
        for k in (1, 2, 3):
            terms_gu(k)
        for k in range(4):
            cores[k][0].wait_recv()
            add_up(t_gu.at[k, :, c], rc_gu.at[k])
        lines.start()
        ring.finish()

        def back(r, _):
            rs = pl.ds(r * 32, 32)
            v = mid_ref[rs]
            inv = lax.rsqrt(jnp.mean(v * v, -1, keepdims=True) + EPS)
            v = v * inv
            g = ring.rows(rs)
            value = own_cot[rs].astype(F32) + inv * (g - v * jnp.mean(g * v, -1, keepdims=True))
            gm_ref[rs] = value
            branch[rs] = value.astype(BF16)
            return 0

        lax.fori_loop(0, rows // 32, back, 0)
        gather.start()
        own.start()
        lax.fori_loop(0, 4, part_out, 0)
        save_op.start()
        gather.turn()
        terms_down(0)
        lines.turn()
        for k in (1, 2, 3):
            terms_down(k)
        for k in range(4):
            cores[k][1].wait_recv()
            add_up(t_down.at[k, :, c], rc_down.at[k])
            saves[k].start()
        gather.near()
        gather.far()
        lines.finish()
        for cp in saves_gu:
            cp.start()
        own.wait()
        save_op.wait()
        for cp in saves + saves_gu:
            cp.wait()
        for pair in cores:
            for cp in pair:
                cp.wait_send()
        lines.sent()
        ring.sent()
        gather.sent()

    anywhere, vmem = pl.BlockSpec(memory_space=pl.ANY), pl.BlockSpec(memory_space=pltpu.VMEM)
    copies = 12 + 8 + 12
    return pl.pallas_call(
        kernel,
        out_shape=[
            struct((4, rows, D)),
            struct((rows, D), F32),
            struct((2, 128, HID)),
            struct((4, 64, HID)),
            struct((4, 2, 128, HID)),
            struct((4, rows, D)),
        ],
        in_specs=[anywhere] * 4 + [vmem] * 2,
        out_specs=[anywhere, vmem, anywhere, anywhere, anywhere, anywhere],
        scratch_shapes=[
            pltpu.VMEM((4, rows, D), BF16),
            pltpu.VMEM((2, rows, D // 2), BF16),
            pltpu.VMEM((2, rows, D), BF16),
            pltpu.VMEM((4, rows, D), BF16),
            pltpu.VMEM((count, 2 * HID), BF16),
            pltpu.VMEM((4, rows, D), BF16),
            pltpu.VMEM((count, HID), BF16),
            pltpu.VMEM((count, HID), F32),
            pltpu.VMEM((512, count), BF16),
            pltpu.VMEM((4, 2, 2, 128, 2 * HID), BF16),
            pltpu.VMEM((4, 2, 2, 128, HID), BF16),
            pltpu.VMEM((4, 2, 128, 2 * HID), BF16),
            pltpu.VMEM((4, 2, 128, HID), BF16),
            pltpu.VMEM((rows, D), BF16),
            pltpu.VMEM((4, rows, D), BF16),
            *line_buffers(2 * HID, SPLITS[1][1]),
            pltpu.SemaphoreType.DMA((copies,)),
            pltpu.SemaphoreType.DMA((copies,)),
            pltpu.SemaphoreType.DMA((14,)),
            pltpu.SemaphoreType.DMA((tiles_gu + pairs + 1,)),
        ],
        name="feed_forward",
        compiler_params=pltpu.CompilerParams(
            collective_id=ident, has_side_effects=True, vmem_limit_bytes=VMEM_LIMIT
        ),
    )(seq_two, seq_cot, gu_w, down_w, middle, cotangent)


def shards(tokens, positions, attn_in, attn_out, attn_gain, mlp_in, mlp_down, mlp_gain, cotangent):
    xh, xl, y, z, c = place()
    rows = tokens.shape[0]
    count = 4 * rows
    gain_one = attn_gain.astype(F32)[:, None]
    gain_two = mlp_gain.astype(F32)[:, None]

    in_f = attn_in.astype(F32)
    mlp_f = mlp_in.astype(F32)
    kv = HEAD_DIM * KV_HEADS
    by_y = lambda a: a.reshape(16, TP, -1)
    w_proj = jnp.concatenate(
        [by_y(in_f[:, :D]), by_y(in_f[:, D : D + kv]), by_y(in_f[:, D + kv :])], -1
    )
    w_proj = (w_proj * gain_one[:, :, None]).astype(BF16).transpose(1, 0, 2)
    by_tile = lambda a: a.reshape(16, TP, HID // 128, 1, 128)
    w_gu = jnp.concatenate([by_tile(mlp_f[:, :FF]), by_tile(mlp_f[:, FF:])], 3).reshape(16, TP, 2 * HID)
    w_gu = (w_gu * gain_two[:, :, None]).astype(BF16).transpose(1, 0, 2)
    w_down = by_y(mlp_down).transpose(1, 0, 2)
    spots = jnp.broadcast_to(positions.astype(F32)[None, :], (8, rows))
    lanes = jnp.arange(128)
    inv_freq = ROPE_BASE ** (-2.0 * (lanes % 32).astype(F32) / HEAD_DIM)
    signs = jnp.where(lanes % 64 < 32, -1.0, 1.0)
    freqs = jnp.zeros((8, 128), F32).at[0].set(inv_freq).at[1].set(signs)
    (normed_one_all, cot_all, proj_w, gu_w, down_w, out_w, q_all, kv_all, attended_low, lse, spots_all, middle, two_all) = (
        forward_attention(tokens, cotangent, spots, freqs, w_proj, w_gu, w_down, attn_out, 0)
    )
    branch_all, grad_middle, gu_a, gu_b, sum_down, out_part = feed_forward(
        two_all, cot_all, gu_w, down_w, middle, cotangent, 1
    )
    outputs, input_grad, own_proj, own_gu, own_down, own_out = backward_attention(
        gu_a, gu_b, sum_down, out_part, branch_all, grad_middle, middle, tokens, freqs,
        spots_all, q_all, kv_all.reshape(2 * count, 128), attended_low, lse, normed_one_all, proj_w, out_w, 2,
    )
    own_proj = own_proj.astype(F32).transpose(1, 0, 2)
    cut = lambda a, start, stop: a[:, :, start:stop].reshape(16, -1)
    own_proj = jnp.concatenate(
        [
            cut(own_proj, 0, Q_COLS),
            cut(own_proj, Q_COLS, Q_COLS + HEAD_DIM),
            cut(own_proj, Q_COLS + HEAD_DIM, PROJ),
        ],
        -1,
    )
    own_gu = own_gu.reshape(TP, 16, HID // 128, 2, 128).transpose(1, 3, 0, 2, 4).reshape(16, 2 * FF).astype(F32)
    own_down = own_down.astype(F32).transpose(1, 0, 2).reshape(16, FF)
    return (
        outputs,
        input_grad,
        own_proj * gain_one,
        own_out.astype(F32),
        jnp.sum(own_proj * in_f, -1),
        own_gu * gain_two,
        own_down,
        jnp.sum(own_gu * mlp_f, -1),
    )


def solution(mesh):
    both = ("dp", "ctx")
    wide, flat = P(both, None), P(both)
    in_specs = (wide, flat, wide, wide, flat, wide, wide, flat, wide)
    out_specs = (wide, wide, wide, wide, flat, wide, wide, flat)
    return jax.shard_map(shards, mesh=mesh, in_specs=in_specs, out_specs=out_specs, check_vma=False)
```

```python
import jax
import jax.numpy as jnp
import numpy as np
from jax import lax
from jax.experimental import pallas as pl
from jax.experimental.pallas import tpu as pltpu
from jax.sharding import PartitionSpec as P


D = 2048
HEADS = 32
KV_HEADS = 4
HEAD_DIM = 64
FF = 5632
REPEAT = HEADS // KV_HEADS
TP = 4
Q_COLS = D // TP
PROJ = Q_COLS + 2 * HEAD_DIM
HID = FF // TP

EPS = 1e-05
ROPE_BASE = 10000.0
NEG_FILL = -1e30

MESH = pl.DeviceIdType.MESH
BF16 = jnp.bfloat16
F32 = jnp.float32

SPLITS = ((PROJ, 384), (2 * HID, 13 * 128), (HID, 640))
OUT_SPLIT = 1024
VMEM_LIMIT = 60 << 20

NN = ((1,), (0,))
NT = ((1,), (1,))
TN = ((0,), (0,))


def place():
    dp, ctx = lax.axis_index("dp"), lax.axis_index("ctx")
    return (dp // 2) % 2, ctx // 4, ctx % 4, dp // 4, dp % 2


def device(xh, xl, y, z, c):
    return (z * 4 + xh * 2 + c, xl * 4 + y)


def along_y(d):
    def to(xh, xl, y, z, c):
        return xh, xl, (y + d) % 4, z, c

    return to


def along_x(d):
    def to(xh, xl, y, z, c):
        x = (xh * 2 + xl + d) % 4
        return x // 2, x % 2, y, z, c

    return to


def along_z(d):
    def to(xh, xl, y, z, c):
        return xh, xl, y, (z + d) % 4, c

    return to


def sibling(xh, xl, y, z, c):
    return xh, xl, y, z, 1 - c


def half_partner(xh, xl, y, z, c):
    return xh, 1 - xl, y, z, c


def crossed(xh, xl, y, z, c):
    return xh, xl, z, y, c


def say_hello(routes, cross=False):
    here = place()
    barrier = pltpu.get_barrier_semaphore()
    for back in routes:
        pl.semaphore_signal(barrier, inc=1, device_id=device(*back(*here)), device_id_type=MESH)
    if cross:

        @pl.when(here[2] != here[3])
        def _():
            pl.semaphore_signal(barrier, inc=1, device_id=device(*crossed(*here)), device_id_type=MESH)


def meet(routes, cross=False):
    here = place()
    barrier = pltpu.get_barrier_semaphore()
    if not cross:
        pl.semaphore_wait(barrier, len(routes))
        return
    away = here[2] != here[3]

    @pl.when(away)
    def _():
        pl.semaphore_wait(barrier, len(routes) + 1)

    @pl.when(jnp.logical_not(away))
    def _():
        pl.semaphore_wait(barrier, len(routes))


ALL_LINES = [along(d) for along in (along_y, along_x, along_z) for d in (1, 2, 3)] + [sibling]


class Copies:
    def __init__(self, send, recv):
        self.send, self.recv, self.count = send, recv, 0

    def __call__(self, src, dst, to):
        k, self.count = self.count, self.count + 1
        return pltpu.make_async_remote_copy(
            src_ref=src,
            dst_ref=dst,
            send_sem=self.send.at[k],
            recv_sem=self.recv.at[k],
            device_id=device(*to(*place())),
            device_id_type=MESH,
        )


def comm_call(kernel, name, ident, ins, outs, copies, locals_=0):
    return pl.pallas_call(
        kernel,
        out_shape=outs,
        in_specs=[pl.BlockSpec(memory_space=pl.ANY)] * len(ins),
        out_specs=[pl.BlockSpec(memory_space=pl.ANY)] * len(outs),
        scratch_shapes=[
            pltpu.SemaphoreType.DMA((copies,)),
            pltpu.SemaphoreType.DMA((copies,)),
            pltpu.SemaphoreType.DMA((max(locals_, 1),)),
        ],
        name=name,
        compiler_params=pltpu.CompilerParams(collective_id=ident, has_side_effects=True),
    )(*ins)


def struct(shape, dtype=BF16):
    return jax.ShapeDtypeStruct(shape, dtype)


class RingGather:
    def __init__(self, copy, own, dst, y):
        half = dst.shape[2] // 2
        lo, hi = pl.ds(0, half), pl.ds(half, half)
        back, on = (y + 3) % 4, (y + 1) % 4

        def first(cols, to):
            return copy(own.at[:, cols], dst.at[y, :, cols], to)

        def one(slot, cols, to):
            at = dst.at[slot, :, cols]
            return copy(at, at, to)

        self.first = [first(lo, along_y(1)), first(hi, along_y(3)), first(hi, along_y(1)), first(lo, along_y(3))]
        self.second = [one(back, lo, along_y(1)), one(on, hi, along_y(3))]

    def start(self):
        for cp in self.first:
            cp.start()

    def turn(self):
        for got, cp in zip(self.first, self.second):
            got.wait_recv()
            cp.start()

    def near(self):
        for cp in self.first[2:]:
            cp.wait_recv()

    def far(self):
        for cp in self.second:
            cp.wait_recv()

    def sent(self):
        for cp in self.first + self.second:
            cp.wait_send()


class RingSum:
    def __init__(self, copy, part, halves, whole, y):
        half = part.shape[2] // 2
        lo, hi = pl.ds(0, half), pl.ds(half, half)
        self.part, self.halves, self.whole, self.y = part, halves, whole, y
        self.cols = (lo, hi)
        far, on, back = (y + 2) % 4, (y + 1) % 4, (y + 3) % 4
        self.far = [
            copy(part.at[far, :, lo], halves.at[0], along_y(1)),
            copy(part.at[far, :, hi], halves.at[1], along_y(3)),
        ]
        self.near = [
            copy(part.at[on, :, hi], whole.at[0, :, hi], along_y(1)),
            copy(part.at[back, :, lo], whole.at[1, :, lo], along_y(3)),
        ]
        self.last = [
            copy(part.at[on, :, lo], whole.at[0, :, lo], along_y(1)),
            copy(part.at[back, :, hi], whole.at[1, :, hi], along_y(3)),
        ]
        self.slots = (on, back)

    def start(self):
        for cp in self.far + self.near:
            cp.start()

    def turn(self):
        for k in range(2):
            self.far[k].wait_recv()
            slot, cols = self.slots[k], self.cols[k]

            def body(r, _, slot=slot, cols=cols, k=k):
                rows = pl.ds(r * 32, 32)
                both = self.part[slot, rows, cols].astype(F32) + self.halves[k, rows].astype(F32)
                self.part[slot, rows, cols] = both.astype(BF16)
                return 0

            lax.fori_loop(0, self.part.shape[1] // 32, body, 0)
            self.last[k].start()

    def finish(self):
        for cp in self.near + self.last:
            cp.wait_recv()

    def rows(self, rows):
        own = self.part[self.y, rows].astype(F32)
        return own + self.whole[0, rows].astype(F32) + self.whole[1, rows].astype(F32)

    def sent(self):
        for cp in self.far + self.near + self.last:
            cp.wait_send()


class Gather:
    def __init__(self, copy, out, a, at, rows_only=False):
        xh, xl, y, z, c = at
        cols = out.shape[-1]
        left, right = pl.ds(0, a), pl.ds(a, cols - a)
        def cut(half, n):
            return slice(None) if half is None else pl.ds(half * (n // 2), n // 2)

        if rows_only:
            block = lambda z, x, c, cols: out.at[x[0], c, x[1], z, :, cols]
            z_line = lambda x, c, cols, half: out.at[x[0], c, x[1], cut(half, 4), :, cols]
            x_line = lambda z, c, cols, half: out.at[cut(half, 2), c, :, z, :, cols]
        else:
            block = lambda z, x, c, cols: out.at[z, x[0], c, pl.ds(x[1] * 64, 64), cols]
            z_line = lambda x, c, cols, half: out.at[cut(half, 4), x[0], c, pl.ds(x[1] * 64, 64), cols]
            x_line = lambda z, c, cols, half: out.at[z, cut(half, 2), c, :, cols]

        def same(ref, to):
            return copy(ref, ref, to)

        here = (xh, xl)
        self.first = []
        for d in (1, 3, 2):
            self.first.append(same(block(z, here, c, left), along_x(d)))
            self.first.append(same(block(z, here, c, right), along_z(d)))
        a_lo, a_hi = lambda z: x_line(z, c, left, 0), lambda z: x_line(z, c, left, 1)
        b_lo, b_hi = lambda x: z_line(x, c, right, 0), lambda x: z_line(x, c, right, 1)
        z_at = [(z + d) % 4 for d in range(4)]
        x_at = [along_x(d)(*at)[:2] for d in range(4)]
        self.lines = []
        for lo, hi, spots, along in ((a_lo, a_hi, z_at, along_z), (b_lo, b_hi, x_at, along_x)):
            going = [
                same(lo(spots[0]), along(1)),
                same(hi(spots[0]), along(3)),
                same(hi(spots[0]), along(1)),
                same(lo(spots[0]), along(3)),
            ]
            on = [same(lo(spots[3]), along(1)), same(hi(spots[1]), along(3))]
            self.lines.append((going, on))
        self.core = [same(block(z, here, c, pl.ds(0, cols)), sibling)]
        for d in (1, 3, 2):
            self.core.append(same(block(z, x_at[d], c, left), sibling))
            self.core.append(same(block(z_at[d], here, c, right), sibling))
        self.core_lines = []
        for d in (3, 1, 2):
            self.core_lines.append(
                (same(x_line(z_at[d], c, left, None), sibling), same(z_line(x_at[d], c, right, None), sibling))
            )

    def start(self):
        for cp in self.first:
            cp.start()
        self.core[0].start()

    def turn(self, *which):
        for k in which or (0, 1):
            for cp in self.first[k::2]:
                cp.wait_recv()
            for cp in self.lines[k][0]:
                cp.start()
            for cp in self.core[1 + k :: 2]:
                cp.start()

    def pass_on(self):
        for going, on in self.lines:
            for got, cp in zip(going[:2], on):
                got.wait_recv()
                cp.start()

    def near(self):
        for k, (going, _) in enumerate(self.lines):
            for side in range(2):
                going[2 + side].wait_recv()
                self.core_lines[side][k].start()

    def far(self):
        for k, (_, on) in enumerate(self.lines):
            for cp in on:
                cp.wait_recv()
            self.core_lines[2][k].start()

    def finish(self):
        for cp in self.core + [cp for pair in self.core_lines for cp in pair]:
            cp.wait_recv()

    def sent(self):
        for going, on in self.lines:
            for cp in going + on:
                cp.wait_send()
        for cp in self.first + self.core + [cp for pair in self.core_lines for cp in pair]:
            cp.wait_send()


def dot(left, right, dims=((1,), (0,))):
    return lax.dot_general(left, right, (dims, ((), ())), preferred_element_type=F32)


def swap_halves(v):
    lane = lax.broadcasted_iota(jnp.int32, v.shape, 1)
    return jnp.where(lane % 64 < 32, pltpu.roll(v, 96, 1), pltpu.roll(v, 32, 1))


def forward_attention(tokens, cotangent, positions, freqs, gains, attn_in, mlp_in, mlp_down, out_rows, ident):
    rows = tokens.shape[0]
    count = 4 * rows

    def kernel(
        tok_ref, cot_ref, spot_ref, freq_ref, gain_ref, in_ref, mlp_ref, down_ref, wo,
        normed_out, cot_all, gp, gg, gd, go, q_out, kv_out, att_out, lse_out, spot_out, middle_out, two_all,
        wp, wg, wd, tok, normed, wp_v, wo_v, q_s, kv, vx, bias, att, part, halves, whole, spot_all, own_two, send, recv, local,
    ):
        say_hello(ALL_LINES, True)
        at = place()
        xh, xl, y, z, c = at
        copy = Copies(send, recv)
        slot = pl.ds(xl * 64 + y * 16, 16)
        nlocal = [0]

        def near(src, dst):
            cp = pltpu.make_async_copy(src, dst, local.at[nlocal[0]])
            nlocal[0] += 1
            return cp

        to_y = []
        stay = []
        for i, o in ((wp, gp), (wg, gg), (wd, gd)):
            to_y.append([copy(i.at[(y + d) % 4], o.at[z, xh, c, slot], along_y(d)) for d in (1, 3, 2)])
            stay.append(near(i.at[y], o.at[z, xh, c, slot]))
        over = copy(wo, go.at[xh, c, xl, y], crossed)
        keep = near(wo, go.at[xh, c, xl, z])
        spot_copies = [copy(spot_all.at[y], spot_all.at[y], along_y(d)) for d in (1, 3, 2)]
        tok_ring = RingGather(copy, tok_ref, tok, y)
        cot_ring = RingGather(copy, cot_ref, cot_all, y)
        row_halves = [pl.ds(0, rows // 2), pl.ds(rows // 2, rows // 2)]
        two_rings = [RingGather(copy, own_two.at[r], two_all.at[:, r], y) for r in row_halves]
        branches = [RingSum(copy, part.at[:, r], halves.at[:, r], whole.at[:, r], y) for r in row_halves]
        kv_copy = copy(kv.at[1], kv.at[0], half_partner)
        g_proj = Gather(copy, gp, SPLITS[0][1], at)
        g_gu = Gather(copy, gg, SPLITS[1][1], at)
        g_down = Gather(copy, gd, SPLITS[2][1], at)
        g_out = Gather(copy, go, OUT_SPLIT, at, True)

        cot_own = near(cot_ref, cot_all.at[y])
        tok_own = near(tok_ref, tok.at[y])
        tok_own.start()
        cot_own.start()
        spot_all[y] = jnp.broadcast_to(spot_ref[...].astype(F32), (8, rows))

        gain_one, gain_two = gain_ref[:, 0:1].astype(F32), gain_ref[:, 1:2].astype(F32)
        low_lanes = lax.broadcasted_iota(jnp.int32, (16, 128), 1) < 64
        for k in range(TP):
            qs = pl.ds(k * Q_COLS, Q_COLS)
            wp[k, :, pl.ds(0, Q_COLS)] = (in_ref[:, qs].astype(F32) * gain_one).astype(BF16)
            key = in_ref[:, pl.ds(D + (k // 2) * 128, 128)].astype(F32)
            value = in_ref[:, pl.ds(D + HEAD_DIM * KV_HEADS + (k // 2) * 128, 128)].astype(F32)
            if k % 2 == 0:
                both = jnp.where(low_lanes, key, pltpu.roll(value, 64, 1))
            else:
                both = jnp.where(low_lanes, pltpu.roll(key, 64, 1), value)
            wp[k, :, pl.ds(Q_COLS, 128)] = (both * gain_one).astype(BF16)
        stay[0].start()
        for k in range(TP):
            for j in range(HID // 128):
                for half in range(2):
                    cols = pl.ds(half * FF + k * HID + j * 128, 128)
                    tile = (mlp_ref[:, cols].astype(F32) * gain_two).astype(BF16)
                    wg[k, :, pl.ds(j * 256 + half * 128, 128)] = tile
            wd[k] = down_ref[:, pl.ds(k * HID, HID)]
        for cp in stay[1:]:
            cp.start()
        meet(ALL_LINES, True)
        away = y != z
        for cp in to_y[0]:
            cp.start()

        @pl.when(away)
        def _():
            over.start()

        @pl.when(jnp.logical_not(away))
        def _():
            keep.start()

        for cp in spot_copies + to_y[1] + to_y[2] + tok_ring.first:
            cp.start()

        def norm_block(k):
            def body(r, _):
                rs = pl.ds(r * 32, 32)
                v = tok[k, rs].astype(F32)
                inv = lax.rsqrt(jnp.mean(v * v, -1, keepdims=True) + EPS)
                normed[k, rs] = (v * inv).astype(BF16)
                return 0

            lax.fori_loop(0, rows // 32, body, 0)

        stay[0].wait()
        for cp in to_y[0]:
            cp.wait_recv()
        g_proj.start()

        @pl.when(away)
        def _():
            over.wait()

        @pl.when(jnp.logical_not(away))
        def _():
            keep.wait()

        g_out.start()
        tok_own.wait()
        norm_block(y)
        g_proj.turn()
        stay[1].wait()
        stay[2].wait()
        for cp in to_y[1] + to_y[2]:
            cp.wait_recv()
        g_gu.start()
        g_down.start()
        g_proj.pass_on()
        g_out.turn()
        for cp in spot_copies:
            cp.wait_recv()
        tok_ring.turn()
        g_proj.near()
        g_proj.far()

        cos, sin = [], []
        freq, sign = freq_ref[0:1, :], freq_ref[1:2, :]
        spot_cols = []
        for k in range(4):
            col = jnp.transpose(jnp.broadcast_to(spot_all[k, 0:1, :], (128, 128)))
            spot_out[k] = spot_all[k]
            spot_cols.append(col)
            cos.append(jnp.cos(col * freq))
            sin.append(jnp.sin(col * freq) * sign)
        cos, sin = jnp.concatenate(cos, 0), jnp.concatenate(sin, 0)
        low_half = xl == 0
        reach = jnp.where(low_half, -1.0, 2048.0)
        for k in range(4):
            for j in range(8):
                row = lax.broadcasted_iota(jnp.int32, (128, 128), 0) + k * 128
                col = lax.broadcasted_iota(jnp.int32, (128, 128), 1) + j * 128
                apart = (row - col + 512).astype(F32)
                seen = apart <= spot_cols[k]
                if j < 4:
                    seen = seen & (apart <= reach)
                else:
                    seen = seen & (col - 512 <= row)
                bias[pl.ds(k * 128, 128), pl.ds(j * 128, 128)] = jnp.where(seen, 0.0, NEG_FILL)

        g_proj.finish()
        wp_load = near(gp, wp_v)
        wp_load.start()
        g_out.pass_on()
        tok_ring.near()
        norm_block((y + 3) % 4)
        norm_block((y + 1) % 4)
        g_out.near()
        tok_ring.far()
        cot_ring.start()
        norm_block((y + 2) % 4)
        normed_save = near(normed, normed_out)
        normed_save.start()

        g_gu.turn(0)
        g_down.turn(0)

        wp_load.wait()
        left = normed[...].reshape(count, D)
        lane = lax.broadcasted_iota(jnp.int32, (count, 128), 1)
        upper = lane >= 64
        raw = dot(left, wp_v[:, :, :, :, pl.ds(Q_COLS, 128)].reshape(D, 128))
        turned = raw * jnp.where(upper, 1.0, cos) + swap_halves(raw) * jnp.where(upper, 0.0, sin)
        kv[1] = turned.astype(BF16)
        kv_copy.start()
        g_out.far()
        g_gu.turn(1)
        g_down.turn(1)
        for j in range(2):
            raw2 = dot(left, wp_v[:, :, :, :, pl.ds(j * 256, 256)].reshape(D, 256))
            for e in range(2):
                raw = raw2[:, e * 128 : e * 128 + 128]
                turned = (raw * cos + swap_halves(raw) * sin).astype(BF16).astype(F32) * (HEAD_DIM ** (-0.5))
                pair = j * 2 + e
                q_s[2 * pair] = jnp.where(upper, 0.0, turned).astype(BF16)
                q_s[2 * pair + 1] = jnp.where(upper, 0.0, pltpu.roll(turned, 64, 1)).astype(BF16)
        kv_copy.wait_recv()
        for k in range(2):
            vx[k] = jnp.where(upper, kv[k].astype(F32), 1.0).astype(BF16)
        q_save = near(q_s, q_out)
        q_save.start()
        kv_save = near(kv, kv_out)
        kv_save.start()
        g_out.finish()
        wo_load = near(go, wo_v)
        wo_load.start()

        def attend(pair):
            for b in range(2):
                rs = pl.ds(b * 256, 256)
                seen = 256 * (b + 1)
                lane = lax.broadcasted_iota(jnp.int32, (256, 128), 1) < 64
                found = []
                for e in range(2):
                    q = q_s[2 * pair + e, rs]
                    s0 = dot(q, kv[0], NT) + bias[rs, pl.ds(0, 512)]
                    s1 = dot(q, kv[1, pl.ds(0, seen)], NT) + bias[rs, pl.ds(512, seen)]
                    m = jnp.maximum(jnp.max(s0, -1, keepdims=True), jnp.max(s1, -1, keepdims=True))
                    p0 = jnp.exp(s0 - m).astype(BF16)
                    p1 = jnp.exp(s1 - m).astype(BF16)
                    o = dot(p0, vx[0]) + dot(p1, vx[1, pl.ds(0, seen)])
                    r = pltpu.roll(o, 64, 1)
                    found.append((o, r))
                    log_total = m + jnp.log(jnp.where(lane, o, r))
                    lse_out[2 * pair + e, :, rs] = jnp.transpose(log_total)[0:8]
                (o, r), (o2, r2) = found
                both = jnp.where(lane, r / o, o2 / r2)
                att[rs, pl.ds(pl.multiple_of(pair * 128, 128), 128)] = both.astype(BF16)

        def two_pairs(k):
            def body(i, _):
                attend(2 * k + i)
                return 0

            lax.fori_loop(0, 2, body, 0)

        two_pairs(0)
        cot_ring.turn()
        two_pairs(1)
        att_save = near(att, att_out)
        att_save.start()
        wo_load.wait()

        for j in range(4):
            cols = pl.ds(j * 512, 512)
            w = wo_v[:, :, :, :, :, cols].reshape(Q_COLS, 512)
            part[:, :, cols] = dot(att[...], w).astype(BF16).reshape(4, rows, 512)
        for branch in branches:
            branch.start()
        g_gu.pass_on()
        g_down.pass_on()
        for branch in branches:
            branch.turn()
        g_gu.near()
        g_down.near()
        cot_ring.near()
        cot_ring.far()
        two_own = near(own_two, two_all.at[y])
        for k in range(2):
            branches[k].finish()

            def mid(r, _, k=k):
                rs, half = pl.ds(k * (rows // 2) + r * 32, 32), pl.ds(r * 32, 32)
                v = tok_ref[rs].astype(F32) + branches[k].rows(half)
                middle_out[rs] = v
                inv = lax.rsqrt(jnp.mean(v * v, -1, keepdims=True) + EPS)
                own_two[rs] = (v * inv).astype(BF16)
                return 0

            lax.fori_loop(0, rows // 64, mid, 0)
            two_rings[k].start()
        two_own.start()
        for ring in two_rings:
            ring.turn()
        g_gu.far()
        g_down.far()
        for ring in two_rings:
            ring.near()
            ring.far()
        g_gu.finish()
        g_down.finish()
        for cp in (cot_own, normed_save, q_save, kv_save, att_save, two_own):
            cp.wait()
        for group in to_y:
            for cp in group:
                cp.wait_send()
        for cp in spot_copies + [kv_copy]:
            cp.wait_send()
        for thing in (g_proj, g_out, g_gu, g_down, tok_ring, cot_ring, *two_rings, *branches):
            thing.sent()

    anywhere, vmem = pl.BlockSpec(memory_space=pl.ANY), pl.BlockSpec(memory_space=pltpu.VMEM)
    outs = [
        (struct((4, rows, D)), anywhere),
        (struct((4, rows, D)), anywhere),
        (struct((4, 2, 2, 128, PROJ)), anywhere),
        (struct((4, 2, 2, 128, 2 * HID)), anywhere),
        (struct((4, 2, 2, 128, HID)), anywhere),
        (struct((2, 2, 2, 4, 16, D)), anywhere),
        (struct((REPEAT, count, 128)), anywhere),
        (struct((2, count, 128)), anywhere),
        (struct((count, Q_COLS)), anywhere),
        (struct((REPEAT, 8, count), F32), vmem),
        (struct((4, 8, 128), F32), vmem),
        (struct((rows, D), F32), vmem),
        (struct((4, rows, D)), anywhere),
    ]
    copies = 9 + 1 + 3 + 6 * 6 + 1 + 31 * 4
    return pl.pallas_call(
        kernel,
        out_shape=[o[0] for o in outs],
        in_specs=[vmem] * 9,
        out_specs=[o[1] for o in outs],
        scratch_shapes=[
            pltpu.VMEM((TP, 16, PROJ), BF16),
            pltpu.VMEM((TP, 16, 2 * HID), BF16),
            pltpu.VMEM((TP, 16, HID), BF16),
            pltpu.VMEM((4, rows, D), BF16),
            pltpu.VMEM((4, rows, D), BF16),
            pltpu.VMEM((4, 2, 2, 128, PROJ), BF16),
            pltpu.VMEM((2, 2, 2, 4, 16, D), BF16),
            pltpu.VMEM((REPEAT, count, 128), BF16),
            pltpu.VMEM((2, count, 128), BF16),
            pltpu.VMEM((2, count, 128), BF16),
            pltpu.VMEM((count, 2 * count), F32),
            pltpu.VMEM((count, Q_COLS), BF16),
            pltpu.VMEM((4, rows, D), BF16),
            pltpu.VMEM((2, rows, D // 2), BF16),
            pltpu.VMEM((2, rows, D), BF16),
            pltpu.VMEM((4, 8, 128), F32),
            pltpu.VMEM((rows, D), BF16),
            pltpu.SemaphoreType.DMA((copies,)),
            pltpu.SemaphoreType.DMA((copies,)),
            pltpu.SemaphoreType.DMA((16,)),
        ],
        name="forward_attention",
        compiler_params=pltpu.CompilerParams(
            collective_id=ident, has_side_effects=True, vmem_limit_bytes=VMEM_LIMIT
        ),
    )(tokens, cotangent, positions, freqs, gains, attn_in, mlp_in, mlp_down, out_rows)


def tiles(ref):
    if len(ref.shape) == 2:
        return [ref]
    return [t for k in range(ref.shape[0]) for t in tiles(ref.at[k])]


def add_up(dst, *others):
    for out, *terms in zip(tiles(dst), *[tiles(o) for o in others]):
        rows = out.shape[0]
        step = min(rows, 32)

        def body(r, _, out=out, terms=terms, step=step):
            rs = pl.ds(r * step, step)
            value = out[rs].astype(F32)
            for t in terms:
                value = value + t[rs].astype(F32)
            out[rs] = value.astype(BF16)
            return 0

        lax.fori_loop(0, rows // step, body, 0)


class LineSum:
    def __init__(self, copy, lo, hi, along, far, near):
        self.lo, self.hi, self.far_in, self.near_in = lo, hi, far, near
        self.far = [copy(lo(2), far.at[0], along(1)), copy(hi(2), far.at[1], along(3))]
        self.near = [copy(hi(1), near.at[0, 1], along(1)), copy(lo(3), near.at[1, 0], along(3))]
        self.last = [copy(lo(1), near.at[0, 0], along(1)), copy(hi(3), near.at[1, 1], along(3))]

    def start(self):
        for cp in self.far + self.near:
            cp.start()

    def turn(self):
        self.far[0].wait_recv()
        add_up(self.lo(1), self.far_in.at[0])
        self.last[0].start()
        self.far[1].wait_recv()
        add_up(self.hi(3), self.far_in.at[1])
        self.last[1].start()

    def finish(self):
        for cp in self.near + self.last:
            cp.wait_recv()
        add_up(self.lo(0), self.near_in.at[0, 0], self.near_in.at[1, 0])
        add_up(self.hi(0), self.near_in.at[0, 1], self.near_in.at[1, 1])

    def sent(self):
        for cp in self.far + self.near + self.last:
            cp.wait_send()


class GradLines:
    def __init__(self, copy, terms, a, at, buffers, rows_only=False):
        xh, xl, y, z, c = at
        far_a, near_a, far_b, near_b = buffers
        cols = terms.shape[-1]
        left, right = pl.ds(0, a), pl.ds(a, cols - a)
        x_at = [along_x(d)(*at)[:2] for d in range(4)]
        z_at = [(z + d) % 4 for d in range(4)]
        if rows_only:
            spot = lambda x, z, cols: terms.at[x[0], c, x[1], z, :, cols]
            a_half = lambda h: lambda d: terms.at[h, c, :, z_at[d], :, left]
            b_half = lambda h: lambda d: terms.at[x_at[d][0], c, x_at[d][1], pl.ds(2 * h, 2), :, right]
        else:
            base = (lambda z, xh: (z, xh, c)) if len(terms.shape) == 5 else (lambda z, xh: (z, xh))
            spot = lambda x, z, cols: terms.at[base(z, x[0]) + (pl.ds(x[1] * 64, 64), cols)]
            a_half = lambda h: lambda d: terms.at[base(z_at[d], h) + (slice(None), left)]
            b_half = lambda h: lambda d: terms.at[
                base(pl.ds(2 * h, 2), x_at[d][0]) + (pl.ds(x_at[d][1] * 64, 64), right)
            ]
        self.lines = [
            LineSum(copy, a_half(0), a_half(1), along_z, far_a, near_a),
            LineSum(copy, b_half(0), b_half(1), along_x, far_b, near_b),
        ]
        self.spot_a = lambda x: spot(x, z, left)
        self.spot_b = lambda z: spot(x_at[0], z, right)

    def start(self):
        for line in self.lines:
            line.start()

    def turn(self):
        for line in self.lines:
            line.turn()

    def finish(self):
        for line in self.lines:
            line.finish()

    def sent(self):
        for line in self.lines:
            line.sent()


class GradOwners:
    def __init__(self, copy, local_copy, spot_a, spot_b, out, at, buffers, rows_only=False):
        xh, xl, y, z, c = at
        self.at, self.rows_only = at, rows_only
        got_a, got_b, own = buffers
        a, cols = got_a.shape[-1], own.shape[-1]
        self.second = []
        for d in (1, 3, 2):
            self.second.append(copy(spot_a(along_x(d)(*at)[:2]), got_a.at[d - 1], along_x(d)))
            self.second.append(copy(spot_b((z + d) % 4), got_b.at[d - 1], along_z(d)))
        self.mine = (spot_a((xh, xl)), spot_b(z))
        self.got = (got_a, got_b)
        self.own, self.cuts = own, (pl.ds(0, a), pl.ds(a, cols - a))
        if rows_only:
            self.over = copy(own, out, crossed)
            self.keep = local_copy(own, out)
        else:
            self.to_y = [copy(own.at[(y + d) % 4], out.at[y], along_y(d)) for d in (1, 3, 2)]
            self.keep = local_copy(own.at[y], out.at[y])

    def start(self):
        for cp in self.second:
            cp.start()

    def deliver(self):
        for cp in self.second:
            cp.wait_recv()
        for mine, got, cut in zip(self.mine, self.got, self.cuts):
            value = mine[...].astype(F32)
            for d in range(3):
                value = value + got[d].astype(F32)
            own = self.own
            if self.rows_only:
                own[:, cut] = value.astype(BF16)
            else:
                own[:, :, cut] = value.astype(BF16).reshape(4, 16, value.shape[-1])
        if self.rows_only:
            y, z = self.at[2], self.at[3]

            @pl.when(y != z)
            def _():
                self.over.start()

            @pl.when(y == z)
            def _():
                self.keep.start()

        else:
            for cp in self.to_y:
                cp.start()
            self.keep.start()

    def finish(self):
        if self.rows_only:
            y, z = self.at[2], self.at[3]

            @pl.when(y != z)
            def _():
                self.over.wait()

            @pl.when(y == z)
            def _():
                self.keep.wait()

        else:
            for cp in self.to_y:
                cp.wait()
            self.keep.wait()
        for cp in self.second:
            cp.wait_send()


def line_buffers(cols, a, rows_only=False):
    b = cols - a
    a_half, b_half = ((2, 16), (2, 16)) if rows_only else ((128,), (2, 64))
    return [
        pltpu.VMEM((2,) + a_half + (a,), BF16),
        pltpu.VMEM((2, 2) + a_half + (a,), BF16),
        pltpu.VMEM((2,) + b_half + (b,), BF16),
        pltpu.VMEM((2, 2) + b_half + (b,), BF16),
    ]


def owner_buffers(cols, a, rows_only=False):
    spot, own = (16, (16, cols)) if rows_only else (64, (4, 16, cols))
    return [pltpu.VMEM((3, spot, a), BF16), pltpu.VMEM((3, spot, cols - a), BF16), pltpu.VMEM(own, BF16)]


def rotation(spot_rows, freq_ref):
    cos, sin = [], []
    for k in range(4):
        col = jnp.transpose(jnp.broadcast_to(spot_rows[k, 0:1, :], (128, 128)))
        cos.append(jnp.cos(col * freq_ref[0:1, :]))
        sin.append(jnp.sin(col * freq_ref[0:1, :]) * freq_ref[1:2, :])
    return jnp.concatenate(cos, 0), jnp.concatenate(sin, 0)


def backward_attention(
    gu_a, gu_b, sum_down, out_part, branch_all, grad_middle, middle, tokens, freqs,
    spots, q_all, kv_all, attended, lse, normed_all, proj_w, out_w, ident,
):
    rows = tokens.shape[0]
    count = 4 * rows
    scale = HEAD_DIM ** (-0.5)

    def kernel(
        gu_a_ref, gu_b_ref, s_down, op_ref, br_ref, gm_hbm, mid_hbm, tok_hbm, freq_ref,
        spot_ref, q_ref, kv_ref, att_ref, lse_ref, nm_ref, wp_ref, wo_ref,
        out_ref, ig_ref, o_proj, o_gu, o_down, o_out,
        gm_ref, mid_ref, tok_ref, v_gu_a, v_gu_b, v_down, part, halves, whole, halves2, whole2, br, q_s, do_s, kv, kvt, att, delta, bias, cos_s, sin_s,
        dkv, kv_send, kv_in, gp, normed, wp, wo, t_proj, rc_proj, t_out, rc_out, *rest,
    ):
        bufs, (send, recv, local) = rest[:24], rest[24:]
        say_hello(ALL_LINES, True)
        at = place()
        xh, xl, y, z, c = at
        copy = Copies(send, recv)
        nlocal = [0]

        def near(src, dst):
            cp = pltpu.make_async_copy(src, dst, local.at[nlocal[0]])
            nlocal[0] += 1
            return cp

        load_gu, load_gu_b, load_down = near(gu_a_ref, v_gu_a), near(gu_b_ref, v_gu_b), near(s_down, v_down)
        load_op, load_br, load_wo = near(op_ref, part), near(br_ref, br), near(wo_ref, wo)
        load_att, load_q = near(att_ref, att), near(q_ref, q_s)
        load_kv = near(kv_ref, kv)
        load_nm, load_wp = near(nm_ref, normed), near(wp_ref, wp)
        load_rows = [near(gm_hbm, gm_ref), near(mid_hbm, mid_ref), near(tok_hbm, tok_ref)]
        for cp in (load_br, load_wo, load_gu, load_gu_b, load_op, load_down, load_att, load_q, load_kv, load_nm, load_wp, *load_rows):
            cp.start()
        outs = RingSum(copy, part, halves, whole, y)
        ones = RingSum(copy, part, halves2, whole2, y)
        kv_copy = copy(kv_send, kv_in, half_partner)
        core_proj = copy(t_proj.at[:, :, 1 - c], rc_proj, sibling)
        core_out = copy(t_out.at[:, 1 - c], rc_out, sibling)
        gu_owners = GradOwners(
            copy,
            near,
            lambda x: v_gu_a.at[x[0], pl.ds(x[1] * 64, 64)],
            lambda z: v_gu_b.at[z],
            o_gu,
            at,
            bufs[0:3],
        )
        down_lines = GradLines(copy, v_down, SPLITS[2][1], at, bufs[3:7])
        down_owners = GradOwners(copy, near, down_lines.spot_a, down_lines.spot_b, o_down, at, bufs[7:10])
        proj_lines = GradLines(copy, t_proj, SPLITS[0][1], at, bufs[10:14])
        proj_owners = GradOwners(copy, near, proj_lines.spot_a, proj_lines.spot_b, o_proj, at, bufs[14:17])
        out_lines = GradLines(copy, t_out, OUT_SPLIT, at, bufs[17:21], True)
        out_owners = GradOwners(copy, near, out_lines.spot_a, out_lines.spot_b, o_out, at, bufs[21:24], True)

        cos, sin = rotation(spot_ref, freq_ref)
        cos_s[...] = cos
        sin_s[...] = sin
        reach = jnp.where(xl == 0, -1.0, 2048.0)
        for k in range(4):
            spots_row = spot_ref[k, 0:1, :]
            for j in range(8):
                key = lax.broadcasted_iota(jnp.int32, (128, 128), 0) + j * 128
                row = lax.broadcasted_iota(jnp.int32, (128, 128), 1) + k * 128
                apart = (row - key + 512).astype(F32)
                seen = apart <= spots_row
                if j < 4:
                    seen = seen & (apart <= reach)
                else:
                    seen = seen & (key - 512 <= row)
                bias[pl.ds(j * 128, 128), pl.ds(k * 128, 128)] = jnp.where(seen, 0.0, NEG_FILL)
        dkv[...] = jnp.zeros_like(dkv)

        meet(ALL_LINES, True)
        load_op.wait()
        outs.start()
        load_gu.wait()
        load_gu_b.wait()
        gu_owners.start()
        load_down.wait()
        down_lines.start()

        load_br.wait()
        load_wo.wait()
        load_att.wait()
        lane = lax.broadcasted_iota(jnp.int32, (count, 128), 1)
        for p in range(4):
            if p % 2 == 0:
                both = dot(br[...].reshape(count, D), wo[p // 2].reshape(256, D), NT).astype(BF16).astype(F32)
            low = both[:, p % 2 * 128 : p % 2 * 128 + 128]
            do_s[2 * p] = jnp.where(lane < 64, 0.0, pltpu.roll(low, 64, 1)).astype(BF16)
            do_s[2 * p + 1] = jnp.where(lane < 64, 0.0, low).astype(BF16)
            prod = jnp.transpose(low * att[:, pl.ds(p * 128, 128)].astype(F32))
            for e in range(2):
                total_row = jnp.sum(prod[e * 64 : e * 64 + 64], 0, keepdims=True)
                delta[2 * p + e] = jnp.broadcast_to(total_row, (8, count))
        outs.turn()

        for k in range(4):
            term = dot(att[:, pl.ds(k * 128, 128)], br[...].reshape(count, D), TN)
            t_out[k // 2, k % 2] = term.astype(BF16).reshape(2, 4, 16, D)
        core_out.start()
        load_q.wait()
        load_kv.wait()
        for k in range(2):
            turned = jnp.transpose(kv[pl.ds(k * count, count)].astype(F32)).astype(BF16)
            kvt[:, pl.ds(k * count, count)] = turned

        def backward(pair):
            for b in range(2):
                rs = pl.ds(b * 256, 256)
                seen = pl.ds(0, 512 + 256 * (b + 1))
                found = []
                for e in range(2):
                    h = 2 * pair + e
                    q, do = q_s[h, rs], do_s[h, rs]
                    st = dot(kv[seen], q, NT) + bias[seen, rs] - lse_ref[h, 0:1, rs]
                    p = jnp.exp(st)
                    dp = dot(kv[seen], do, NT)
                    ds = (p * (dp - delta[h, 0:1, rs])).astype(BF16)
                    dkv[seen] += dot(ds, q) + dot(p.astype(BF16), do)
                    found.append(dot(kvt[:, seen], ds)[0:64])
                both = jnp.transpose(jnp.concatenate(found, 0)) * scale
                both = both * cos_s[rs] - swap_halves(both) * sin_s[rs]
                gp[rs, pl.ds(pl.multiple_of(pair * 128, 128), 128)] = both.astype(BF16)

        def two_pairs(k):
            def body(i, _):
                backward(2 * k + i)
                return 0

            lax.fori_loop(0, 2, body, 0)

        two_pairs(0)
        down_lines.turn()
        gu_owners.deliver()
        two_pairs(1)
        kv_send[...] = dkv[pl.ds(0, count)].astype(BF16)
        kv_copy.start()
        core_out.wait_recv()
        add_up(t_out.at[:, c], rc_out)
        out_lines.start()
        down_lines.finish()
        down_owners.start()
        outs.finish()

        for cp in load_rows:
            cp.wait()

        def finish_out(r, _):
            rs = pl.ds(r * 32, 32)
            out_ref[rs] = (mid_ref[rs] + outs.rows(rs)).astype(BF16)
            return 0

        lax.fori_loop(0, rows // 32, finish_out, 0)
        outs.sent()
        kv_copy.wait_recv()
        got = dkv[pl.ds(count, count)] + kv_in[...].astype(F32)
        back = got * cos_s[...] - swap_halves(got) * sin_s[...]
        gp[:, pl.ds(Q_COLS, 128)] = jnp.where(lane < 64, back, got).astype(BF16)

        load_nm.wait()
        for k in range(4):
            left = normed[:, :, pl.ds(k * 512, 512)].reshape(count, 512)
            t_proj[k] = dot(left, gp[...], TN).astype(BF16).reshape(2, 2, 128, PROJ)
        core_proj.start()

        load_wp.wait()
        for j in range(4):
            w = wp[j].reshape(512, PROJ)
            part[:, :, pl.ds(j * 512, 512)] = dot(gp[...], w, NT).astype(BF16).reshape(4, rows, 512)
        ones.start()
        out_lines.turn()
        ones.turn()
        down_owners.deliver()
        core_proj.wait_recv()
        for k in range(4):
            add_up(t_proj.at[k, :, c], rc_proj.at[k])
        proj_lines.start()
        out_lines.finish()
        out_owners.start()
        proj_lines.turn()
        ones.finish()

        def finish_in(r, _):
            rs = pl.ds(r * 32, 32)
            v = tok_ref[rs].astype(F32)
            inv = lax.rsqrt(jnp.mean(v * v, -1, keepdims=True) + EPS)
            v = v * inv
            g = ones.rows(rs)
            ig_ref[rs] = gm_ref[rs] + inv * (g - v * jnp.mean(g * v, -1, keepdims=True))
            return 0

        lax.fori_loop(0, rows // 32, finish_in, 0)
        proj_lines.finish()
        proj_owners.start()
        out_owners.deliver()
        proj_owners.deliver()
        ones.sent()
        for cp in (kv_copy, core_proj, core_out):
            cp.wait_send()
        for owners in (gu_owners, down_owners, out_owners, proj_owners):
            owners.finish()
        for lines in (down_lines, out_lines, proj_lines):
            lines.sent()

    anywhere, vmem = pl.BlockSpec(memory_space=pl.ANY), pl.BlockSpec(memory_space=pltpu.VMEM)
    in_specs = [anywhere] * 8 + [vmem] * 2 + [anywhere] * 3 + [vmem] + [anywhere] * 3
    outs = [
        (struct((rows, D)), vmem),
        (struct((rows, D), F32), vmem),
        (struct((4, 16, PROJ)), anywhere),
        (struct((4, 16, 2 * HID)), anywhere),
        (struct((4, 16, HID)), anywhere),
        (struct((16, D)), anywhere),
    ]
    whole = lambda: [pltpu.VMEM((2, rows, D // 2), BF16), pltpu.VMEM((2, rows, D), BF16)]
    copies = 12 + 3 + 9 + 21 * 2 + 19
    return pl.pallas_call(
        kernel,
        out_shape=[o[0] for o in outs],
        in_specs=in_specs,
        out_specs=[o[1] for o in outs],
        scratch_shapes=[
            pltpu.VMEM((rows, D), F32),
            pltpu.VMEM((rows, D), F32),
            pltpu.VMEM((rows, D), BF16),
            pltpu.VMEM((2, 128, SPLITS[1][1]), BF16),
            pltpu.VMEM((4, 64, 2 * HID - SPLITS[1][1]), BF16),
            pltpu.VMEM((4, 2, 128, HID), BF16),
            pltpu.VMEM((4, rows, D), BF16),
            *whole(),
            *whole(),
            pltpu.VMEM((4, rows, D), BF16),
            pltpu.VMEM((REPEAT, count, 128), BF16),
            pltpu.VMEM((REPEAT, count, 128), BF16),
            pltpu.VMEM((2 * count, 128), BF16),
            pltpu.VMEM((128, 2 * count), BF16),
            pltpu.VMEM((count, Q_COLS), BF16),
            pltpu.VMEM((REPEAT, 8, count), F32),
            pltpu.VMEM((2 * count, count), F32),
            pltpu.VMEM((count, 128), F32),
            pltpu.VMEM((count, 128), F32),
            pltpu.VMEM((2 * count, 128), F32),
            pltpu.VMEM((count, 128), BF16),
            pltpu.VMEM((count, 128), BF16),
            pltpu.VMEM((count, PROJ), BF16),
            pltpu.VMEM((4, rows, D), BF16),
            pltpu.VMEM((4, 2, 2, 128, PROJ), BF16),
            pltpu.VMEM((2, 2, 2, 4, 16, D), BF16),
            pltpu.VMEM((4, 2, 2, 128, PROJ), BF16),
            pltpu.VMEM((4, 2, 128, PROJ), BF16),
            pltpu.VMEM((2, 2, 2, 4, 16, D), BF16),
            pltpu.VMEM((2, 2, 4, 16, D), BF16),
            *owner_buffers(2 * HID, SPLITS[1][1]),
            *line_buffers(HID, SPLITS[2][1]),
            *owner_buffers(HID, SPLITS[2][1]),
            *line_buffers(PROJ, SPLITS[0][1]),
            *owner_buffers(PROJ, SPLITS[0][1]),
            *line_buffers(D, OUT_SPLIT, True),
            *owner_buffers(D, OUT_SPLIT, True),
            pltpu.SemaphoreType.DMA((copies,)),
            pltpu.SemaphoreType.DMA((copies,)),
            pltpu.SemaphoreType.DMA((20,)),
        ],
        name="backward_attention",
        compiler_params=pltpu.CompilerParams(
            collective_id=ident, has_side_effects=True, vmem_limit_bytes=VMEM_LIMIT
        ),
    )(
        gu_a, gu_b, sum_down, out_part, branch_all, grad_middle, middle, tokens, freqs,
        spots, q_all, kv_all, attended, lse, normed_all, proj_w, out_w,
    )


def feed_forward(seq_two, seq_cot, gu_w, down_w, middle, cotangent, ident):
    rows = middle.shape[0]
    count = 4 * rows
    tiles_gu, pairs = HID // 128, HID // 256

    def kernel(
        two_ref, cot_ref, wg_ref, wd_ref, mid_hbm, own_cot_hbm,
        branch_all, gm_ref, gu_a, gu_b, s_down, op_out,
        part, halves, whole, two, gu, cot, hid, gh, turned, t_gu, t_down, rc_gu, rc_down, branch, op,
        mid_ref, own_cot,
        far_a, near_a, far_b, near_b, send, recv, local, weights,
    ):
        partners = [along_y(1), along_y(3), along_x(1), along_x(3), along_z(1), along_z(3), sibling]
        say_hello(partners)
        at = place()
        xh, xl, y, z, c = at
        copy = Copies(send, recv)
        nlocal = [0]

        def near(src, dst):
            cp = pltpu.make_async_copy(src, dst, local.at[nlocal[0]])
            nlocal[0] += 1
            return cp

        def load_gu(j):
            tile = pl.ds(pl.multiple_of(j * 256, 256), 256)
            return pltpu.make_async_copy(wg_ref.at[:, :, :, :, tile], t_gu.at[:, :, :, :, tile], weights.at[j])

        def load_down(j, width=256):
            tile = pl.ds(pl.multiple_of(j * 256, 256), width)
            return pltpu.make_async_copy(
                wd_ref.at[:, :, :, :, tile], t_down.at[:, :, :, :, tile], weights.at[tiles_gu + j]
            )

        load_cot, load_two = near(cot_ref, cot), near(two_ref, two)
        load_rows = [near(mid_hbm, mid_ref), near(own_cot_hbm, own_cot)]
        load_cot.start()
        last_down = load_down(pairs, HID - 256 * pairs)

        def begin_down(j, _):
            load_down(j).start()
            return 0

        def begin_gu(j, _):
            load_gu(j).start()
            return 0

        lax.fori_loop(0, pairs, begin_down, 0)
        last_down.start()
        load_two.start()
        lax.fori_loop(0, tiles_gu, begin_gu, 0)
        for cp in load_rows:
            cp.start()
        row_halves = [pl.ds(0, rows // 2), pl.ds(rows // 2, rows // 2)]
        rings = [RingSum(copy, part.at[:, r], halves.at[:, r], whole.at[:, r], y) for r in row_halves]
        gathers = [RingGather(copy, branch.at[r], branch_all.at[:, r], y) for r in row_halves]
        own = near(branch, branch_all.at[y])
        cores = [
            (copy(t_gu.at[k, :, 1 - c], rc_gu.at[k], sibling), copy(t_down.at[k, :, 1 - c], rc_down.at[k], sibling))
            for k in [(z + d) % 4 for d in range(4)]
        ]
        saves = [near(t_down.at[k, :, c], s_down.at[k]) for k in [(z + d) % 4 for d in range(4)]]
        lines = GradLines(copy, t_gu, SPLITS[1][1], at, (far_a, near_a, far_b, near_b))
        saves_gu = [
            near(t_gu.at[z, :, c, :, pl.ds(0, SPLITS[1][1])], gu_a),
            near(t_gu.at[:, xh, c, pl.ds(xl * 64, 64), pl.ds(SPLITS[1][1], 2 * HID - SPLITS[1][1])], gu_b),
        ]
        save_op = near(op, op_out)
        load_cot.wait()

        def hidden_back(j, _):
            load_down(j).wait()
            tile = pl.ds(pl.multiple_of(j * 256, 256), 256)
            gh[:, tile] = dot(cot[...].reshape(count, D), t_down[:, :, :, :, tile].reshape(D, 256))
            return 0

        lax.fori_loop(0, pairs, hidden_back, 0)
        last_down.wait()
        tile = pl.ds(256 * pairs, HID - 256 * pairs)
        gh[:, tile] = dot(cot[...].reshape(count, D), t_down[:, :, :, :, tile].reshape(D, HID - 256 * pairs))
        load_two.wait()

        def gate_up(j):
            load_gu(j).wait()
            both = pl.ds(pl.multiple_of(j * 256, 256), 256)
            return dot(two[...].reshape(count, D), t_gu[:, :, :, :, both].reshape(D, 256))

        def activate(j, act):
            both = pl.ds(pl.multiple_of(j * 256, 256), 256)
            one = pl.ds(pl.multiple_of(j * 128, 128), 128)
            gate, up = act[:, :128], act[:, 128:]
            back = gh[:, one]
            sigmoid = jax.nn.sigmoid(gate)
            silu = gate * sigmoid
            hid[:, one] = (silu * up).astype(BF16)
            grad_gate = back * up * sigmoid * (1.0 + gate * (1.0 - sigmoid))
            gu[:, both] = jnp.concatenate([grad_gate, back * silu], 1).astype(BF16)

        def hidden(j, _):
            activate(j, gate_up(j))
            return 0

        lax.fori_loop(0, tiles_gu, hidden, 0)

        def part_two(k, _):
            cols = pl.ds(pl.multiple_of(k * 512, 512), 512)
            part[:, :, cols] = dot(gu[...], t_gu[k].reshape(512, 2 * HID), NT).astype(BF16).reshape(4, rows, 512)
            return 0

        lax.fori_loop(0, 4, part_two, 0)
        meet(partners)
        for ring in rings:
            ring.start()

        def part_out(k, _):
            cols = pl.ds(pl.multiple_of(k * 512, 512), 512)
            op[:, :, cols] = dot(hid[...], t_down[k].reshape(512, HID), NT).astype(BF16).reshape(4, rows, 512)
            return 0

        def terms_gu(d):
            k = (z + d) % 4
            cols = pl.ds(pl.multiple_of(k * 512, 512), 512)
            turned[...] = jnp.transpose(two[:, :, cols].reshape(count, 512))

            def some(j, _):
                tile = pl.ds(pl.multiple_of(j * 256, 256), 256)
                t_gu[k, :, :, :, tile] = dot(turned[...], gu[:, tile]).astype(BF16).reshape(2, 2, 128, 256)
                return 0

            lax.fori_loop(0, 2 * HID // 256, some, 0)
            cores[d][0].start()

        def terms_down(d):
            k = (z + d) % 4
            cols = pl.ds(pl.multiple_of(k * 512, 512), 512)
            turned[...] = jnp.transpose(cot[:, :, cols].reshape(count, 512))

            def more(j, width=256):
                tile = pl.ds(pl.multiple_of(j * 256, 256), width)
                t_down[k, :, :, :, tile] = dot(turned[...], hid[:, tile]).astype(BF16).reshape(2, 2, 128, width)
                return 0

            lax.fori_loop(0, pairs, lambda j, _: more(j), 0)
            more(pairs, HID - 256 * pairs)
            cores[d][1].start()

        def add_gu(d):
            k = (z + d) % 4
            cores[d][0].wait_recv()
            add_up(t_gu.at[k, :, c], rc_gu.at[k])

        line_a, line_b = lines.lines
        terms_gu(2)
        terms_gu(1)
        for ring in rings:
            ring.turn()
        add_gu(2)
        for cp in line_a.far:
            cp.start()
        terms_gu(3)
        add_gu(1)
        terms_gu(0)
        add_gu(3)
        for cp in line_a.near:
            cp.start()
        add_gu(0)
        line_b.start()
        for cp in load_rows:
            cp.wait()
        for k in range(2):
            rings[k].finish()

            def back(r, _, k=k):
                rs, half = pl.ds(k * (rows // 2) + r * 32, 32), pl.ds(r * 32, 32)
                v = mid_ref[rs]
                inv = lax.rsqrt(jnp.mean(v * v, -1, keepdims=True) + EPS)
                v = v * inv
                g = rings[k].rows(half)
                value = own_cot[rs].astype(F32) + inv * (g - v * jnp.mean(g * v, -1, keepdims=True))
                gm_ref[rs] = value
                branch[rs] = value.astype(BF16)
                return 0

            lax.fori_loop(0, rows // 64, back, 0)
            gathers[k].start()
        own.start()
        lax.fori_loop(0, 4, part_out, 0)
        save_op.start()
        for gather in gathers:
            gather.turn()
        line_a.turn()
        terms_down(2)
        terms_down(1)
        line_b.turn()
        terms_down(3)
        terms_down(0)
        for d in (2, 1, 3, 0):
            cores[d][1].wait_recv()
            add_up(t_down.at[(z + d) % 4, :, c], rc_down.at[(z + d) % 4])
            saves[d].start()
        for gather in gathers:
            gather.near()
            gather.far()
        lines.finish()
        for cp in saves_gu:
            cp.start()
        own.wait()
        save_op.wait()
        for cp in saves + saves_gu:
            cp.wait()
        for pair in cores:
            for cp in pair:
                cp.wait_send()
        lines.sent()
        for ring in rings + gathers:
            ring.sent()

    anywhere, vmem = pl.BlockSpec(memory_space=pl.ANY), pl.BlockSpec(memory_space=pltpu.VMEM)
    copies = 24 + 8 + 12
    return pl.pallas_call(
        kernel,
        out_shape=[
            struct((4, rows, D)),
            struct((rows, D), F32),
            struct((2, 128, SPLITS[1][1])),
            struct((4, 64, 2 * HID - SPLITS[1][1])),
            struct((4, 2, 128, HID)),
            struct((4, rows, D)),
        ],
        in_specs=[anywhere] * 6,
        out_specs=[anywhere, vmem, anywhere, anywhere, anywhere, anywhere],
        scratch_shapes=[
            pltpu.VMEM((4, rows, D), BF16),
            pltpu.VMEM((2, rows, D // 2), BF16),
            pltpu.VMEM((2, rows, D), BF16),
            pltpu.VMEM((4, rows, D), BF16),
            pltpu.VMEM((count, 2 * HID), BF16),
            pltpu.VMEM((4, rows, D), BF16),
            pltpu.VMEM((count, HID), BF16),
            pltpu.VMEM((count, HID), F32),
            pltpu.VMEM((512, count), BF16),
            pltpu.VMEM((4, 2, 2, 128, 2 * HID), BF16),
            pltpu.VMEM((4, 2, 2, 128, HID), BF16),
            pltpu.VMEM((4, 2, 128, 2 * HID), BF16),
            pltpu.VMEM((4, 2, 128, HID), BF16),
            pltpu.VMEM((rows, D), BF16),
            pltpu.VMEM((4, rows, D), BF16),
            pltpu.VMEM((rows, D), F32),
            pltpu.VMEM((rows, D), BF16),
            *line_buffers(2 * HID, SPLITS[1][1]),
            pltpu.SemaphoreType.DMA((copies,)),
            pltpu.SemaphoreType.DMA((copies,)),
            pltpu.SemaphoreType.DMA((16,)),
            pltpu.SemaphoreType.DMA((tiles_gu + pairs + 1,)),
        ],
        name="feed_forward",
        compiler_params=pltpu.CompilerParams(
            collective_id=ident, has_side_effects=True, vmem_limit_bytes=VMEM_LIMIT
        ),
    )(seq_two, seq_cot, gu_w, down_w, middle, cotangent)


def own_rows(gains, attn_in, mlp_in, proj, gu, down, out):
    def kernel(gain_ref, in_ref, mlp_ref, proj_ref, gu_ref, down_ref, out_ref, g_in, g_mlp, g_down, g_out, g_gain):
        gain_one, gain_two = gain_ref[:, 0:1].astype(F32), gain_ref[:, 1:2].astype(F32)
        lane = lax.broadcasted_iota(jnp.int32, (16, 128), 1)
        low = lane < 64

        def put(dst, weights, at, value, gain, total):
            cols = pl.ds(at, 128)
            dst[:, cols] = value * gain
            return total + value * weights[:, cols].astype(F32)

        first = jnp.zeros((16, 128), F32)
        for k in range(TP):
            for j in range(Q_COLS // 128):
                value = proj_ref[k, :, pl.ds(j * 128, 128)].astype(F32)
                first = put(g_in, in_ref, k * Q_COLS + j * 128, value, gain_one, first)
        for k in range(0, TP, 2):
            even = proj_ref[k, :, pl.ds(Q_COLS, 128)].astype(F32)
            odd = proj_ref[k + 1, :, pl.ds(Q_COLS, 128)].astype(F32)
            key = jnp.where(low, even, pltpu.roll(odd, 64, 1))
            value = jnp.where(low, pltpu.roll(even, 64, 1), odd)
            first = put(g_in, in_ref, D + k * 64, key, gain_one, first)
            first = put(g_in, in_ref, D + HEAD_DIM * KV_HEADS + k * 64, value, gain_one, first)
        second = jnp.zeros((16, 128), F32)
        for k in range(TP):
            for j in range(HID // 128):
                for half in range(2):
                    value = gu_ref[k, :, pl.ds(j * 256 + half * 128, 128)].astype(F32)
                    second = put(g_mlp, mlp_ref, half * FF + k * HID + j * 128, value, gain_two, second)
            g_down[:, pl.ds(k * HID, HID)] = down_ref[k].astype(F32)
        g_out[...] = out_ref[...].astype(F32)
        sums = jnp.sum(first, -1, keepdims=True), jnp.sum(second, -1, keepdims=True)
        g_gain[...] = jnp.transpose(jnp.where(lane == 0, sums[0], sums[1]))[0:8]

    shapes = [(16, attn_in.shape[1]), (16, 2 * FF), (16, FF), (16, D), (8, 16)]
    return pl.pallas_call(
        kernel,
        out_shape=[struct(shape, F32) for shape in shapes],
        in_specs=[pl.BlockSpec(memory_space=pltpu.VMEM)] * 7,
        out_specs=[pl.BlockSpec(memory_space=pltpu.VMEM)] * 5,
        name="own_rows",
        compiler_params=pltpu.CompilerParams(vmem_limit_bytes=VMEM_LIMIT),
    )(gains, attn_in, mlp_in, proj, gu, down, out)


def shards(tokens, positions, attn_in, attn_out, attn_gain, mlp_in, mlp_down, mlp_gain, cotangent):
    rows = tokens.shape[0]
    count = 4 * rows
    gains = jnp.stack([attn_gain, mlp_gain], 1)
    lanes = np.arange(128)
    freqs = np.zeros((8, 128), np.float32)
    freqs[0] = np.float32(ROPE_BASE) ** (-2.0 * (lanes % 32).astype(np.float32) / HEAD_DIM)
    freqs[1] = np.where(lanes % 64 < 32, -1.0, 1.0)
    (normed_one_all, cot_all, proj_w, gu_w, down_w, out_w, q_all, kv_all, attended_low, lse, spots_all, middle, two_all) = (
        forward_attention(tokens, cotangent, positions[None], freqs, gains, attn_in, mlp_in, mlp_down, attn_out, 0)
    )
    branch_all, grad_middle, gu_a, gu_b, sum_down, out_part = feed_forward(
        two_all, cot_all, gu_w, down_w, middle, cotangent, 1
    )
    outputs, input_grad, own_proj, own_gu, own_down, own_out = backward_attention(
        gu_a, gu_b, sum_down, out_part, branch_all, grad_middle, middle, tokens, freqs,
        spots_all, q_all, kv_all.reshape(2 * count, 128), attended_low, lse, normed_one_all, proj_w, out_w, 2,
    )
    grad_in, grad_mlp, grad_down, grad_out, grad_gains = own_rows(
        gains, attn_in, mlp_in, own_proj, own_gu, own_down, own_out
    )
    return outputs, input_grad, grad_in, grad_out, grad_gains[0], grad_mlp, grad_down, grad_gains[1]


def solution(mesh):
    both = ("dp", "ctx")
    wide, flat = P(both, None), P(both)
    in_specs = (wide, flat, wide, wide, flat, wide, wide, flat, wide)
    out_specs = (wide, wide, wide, wide, flat, wide, wide, flat)
    return jax.shard_map(shards, mesh=mesh, in_specs=in_specs, out_specs=out_specs, check_vma=False)
```

```python
import jax
import jax.numpy as jnp
import numpy as np
from jax import lax
from jax.experimental import pallas as pl
from jax.experimental.pallas import tpu as pltpu
from jax.sharding import PartitionSpec as P


D = 2048
HEADS = 32
KV_HEADS = 4
HEAD_DIM = 64
FF = 5632
REPEAT = HEADS // KV_HEADS
TP = 4
Q_COLS = D // TP
PROJ = Q_COLS + 2 * HEAD_DIM
HID = FF // TP

EPS = 1e-05
ROPE_BASE = 10000.0
NEG_FILL = -1e30

MESH = pl.DeviceIdType.MESH
BF16 = jnp.bfloat16
F32 = jnp.float32

SPLITS = ((PROJ, 384), (2 * HID, 13 * 128), (HID, 640))
OUT_SPLIT = 1024
VMEM_LIMIT = 60 << 20

NN = ((1,), (0,))
NT = ((1,), (1,))
TN = ((0,), (0,))


def place():
    dp, ctx = lax.axis_index("dp"), lax.axis_index("ctx")
    return (dp // 2) % 2, ctx // 4, ctx % 4, dp // 4, dp % 2


def device(xh, xl, y, z, c):
    return (z * 4 + xh * 2 + c, xl * 4 + y)


def along_y(d):
    def to(xh, xl, y, z, c):
        return xh, xl, (y + d) % 4, z, c

    return to


def along_x(d):
    def to(xh, xl, y, z, c):
        x = (xh * 2 + xl + d) % 4
        return x // 2, x % 2, y, z, c

    return to


def along_z(d):
    def to(xh, xl, y, z, c):
        return xh, xl, y, (z + d) % 4, c

    return to


def sibling(xh, xl, y, z, c):
    return xh, xl, y, z, 1 - c


def half_partner(xh, xl, y, z, c):
    return xh, 1 - xl, y, z, c


def crossed(xh, xl, y, z, c):
    return xh, xl, z, y, c


def say_hello(routes, cross=False):
    here = place()
    barrier = pltpu.get_barrier_semaphore()
    for back in routes:
        pl.semaphore_signal(barrier, inc=1, device_id=device(*back(*here)), device_id_type=MESH)
    if cross:

        @pl.when(here[2] != here[3])
        def _():
            pl.semaphore_signal(barrier, inc=1, device_id=device(*crossed(*here)), device_id_type=MESH)


def meet(routes, cross=False):
    here = place()
    barrier = pltpu.get_barrier_semaphore()
    if not cross:
        pl.semaphore_wait(barrier, len(routes))
        return
    away = here[2] != here[3]

    @pl.when(away)
    def _():
        pl.semaphore_wait(barrier, len(routes) + 1)

    @pl.when(jnp.logical_not(away))
    def _():
        pl.semaphore_wait(barrier, len(routes))


ALL_LINES = [along(d) for along in (along_y, along_x, along_z) for d in (1, 2, 3)] + [sibling]


class Copies:
    def __init__(self, send, recv):
        self.send, self.recv, self.count = send, recv, 0

    def __call__(self, src, dst, to):
        k, self.count = self.count, self.count + 1
        return pltpu.make_async_remote_copy(
            src_ref=src,
            dst_ref=dst,
            send_sem=self.send.at[k],
            recv_sem=self.recv.at[k],
            device_id=device(*to(*place())),
            device_id_type=MESH,
        )


def comm_call(kernel, name, ident, ins, outs, copies, locals_=0):
    return pl.pallas_call(
        kernel,
        out_shape=outs,
        in_specs=[pl.BlockSpec(memory_space=pl.ANY)] * len(ins),
        out_specs=[pl.BlockSpec(memory_space=pl.ANY)] * len(outs),
        scratch_shapes=[
            pltpu.SemaphoreType.DMA((copies,)),
            pltpu.SemaphoreType.DMA((copies,)),
            pltpu.SemaphoreType.DMA((max(locals_, 1),)),
        ],
        name=name,
        compiler_params=pltpu.CompilerParams(collective_id=ident, has_side_effects=True),
    )(*ins)


def struct(shape, dtype=BF16):
    return jax.ShapeDtypeStruct(shape, dtype)


class RingGather:
    def __init__(self, copy, own, dst, y):
        half = dst.shape[2] // 2
        lo, hi = pl.ds(0, half), pl.ds(half, half)
        back, on = (y + 3) % 4, (y + 1) % 4

        def first(cols, to):
            return copy(own.at[:, cols], dst.at[y, :, cols], to)

        def one(slot, cols, to):
            at = dst.at[slot, :, cols]
            return copy(at, at, to)

        self.first = [first(lo, along_y(1)), first(hi, along_y(3)), first(hi, along_y(1)), first(lo, along_y(3))]
        self.second = [one(back, lo, along_y(1)), one(on, hi, along_y(3))]

    def start(self):
        for cp in self.first:
            cp.start()

    def turn(self):
        for got, cp in zip(self.first, self.second):
            got.wait_recv()
            cp.start()

    def near(self):
        for cp in self.first[2:]:
            cp.wait_recv()

    def far(self):
        for cp in self.second:
            cp.wait_recv()

    def sent(self):
        for cp in self.first + self.second:
            cp.wait_send()


class RingSum:
    def __init__(self, copy, part, halves, whole, y):
        half = part.shape[2] // 2
        lo, hi = pl.ds(0, half), pl.ds(half, half)
        self.part, self.halves, self.whole, self.y = part, halves, whole, y
        self.cols = (lo, hi)
        far, on, back = (y + 2) % 4, (y + 1) % 4, (y + 3) % 4
        self.far = [
            copy(part.at[far, :, lo], halves.at[0], along_y(1)),
            copy(part.at[far, :, hi], halves.at[1], along_y(3)),
        ]
        self.near = [
            copy(part.at[on, :, hi], whole.at[0, :, hi], along_y(1)),
            copy(part.at[back, :, lo], whole.at[1, :, lo], along_y(3)),
        ]
        self.last = [
            copy(part.at[on, :, lo], whole.at[0, :, lo], along_y(1)),
            copy(part.at[back, :, hi], whole.at[1, :, hi], along_y(3)),
        ]
        self.slots = (on, back)

    def start(self):
        for cp in self.far + self.near:
            cp.start()

    def turn(self):
        for k in range(2):
            self.far[k].wait_recv()
            slot, cols = self.slots[k], self.cols[k]

            def body(r, _, slot=slot, cols=cols, k=k):
                rows = pl.ds(r * 32, 32)
                both = self.part[slot, rows, cols].astype(F32) + self.halves[k, rows].astype(F32)
                self.part[slot, rows, cols] = both.astype(BF16)
                return 0

            lax.fori_loop(0, self.part.shape[1] // 32, body, 0)
            self.last[k].start()

    def finish(self):
        for cp in self.near + self.last:
            cp.wait_recv()

    def rows(self, rows):
        own = self.part[self.y, rows].astype(F32)
        return own + self.whole[0, rows].astype(F32) + self.whole[1, rows].astype(F32)

    def sent(self):
        for cp in self.far + self.near + self.last:
            cp.wait_send()


class Gather:
    def __init__(self, copy, out, a, at, rows_only=False):
        xh, xl, y, z, c = at
        cols = out.shape[-1]
        left, right = pl.ds(0, a), pl.ds(a, cols - a)
        def cut(half, n):
            return slice(None) if half is None else pl.ds(half * (n // 2), n // 2)

        if rows_only:
            block = lambda z, x, c, cols: out.at[x[0], c, x[1], z, :, cols]
            z_line = lambda x, c, cols, half: out.at[x[0], c, x[1], cut(half, 4), :, cols]
            x_line = lambda z, c, cols, half: out.at[cut(half, 2), c, :, z, :, cols]
        else:
            block = lambda z, x, c, cols: out.at[z, x[0], c, pl.ds(x[1] * 64, 64), cols]
            z_line = lambda x, c, cols, half: out.at[cut(half, 4), x[0], c, pl.ds(x[1] * 64, 64), cols]
            x_line = lambda z, c, cols, half: out.at[z, cut(half, 2), c, :, cols]

        def same(ref, to):
            return copy(ref, ref, to)

        here = (xh, xl)
        self.first = []
        for d in (1, 3, 2):
            self.first.append(same(block(z, here, c, left), along_x(d)))
            self.first.append(same(block(z, here, c, right), along_z(d)))
        a_lo, a_hi = lambda z: x_line(z, c, left, 0), lambda z: x_line(z, c, left, 1)
        b_lo, b_hi = lambda x: z_line(x, c, right, 0), lambda x: z_line(x, c, right, 1)
        z_at = [(z + d) % 4 for d in range(4)]
        x_at = [along_x(d)(*at)[:2] for d in range(4)]
        self.lines = []
        for lo, hi, spots, along in ((a_lo, a_hi, z_at, along_z), (b_lo, b_hi, x_at, along_x)):
            going = [
                same(lo(spots[0]), along(1)),
                same(hi(spots[0]), along(3)),
                same(hi(spots[0]), along(1)),
                same(lo(spots[0]), along(3)),
            ]
            on = [same(lo(spots[3]), along(1)), same(hi(spots[1]), along(3))]
            self.lines.append((going, on))
        self.core = [same(block(z, here, c, pl.ds(0, cols)), sibling)]
        for d in (1, 3, 2):
            self.core.append(same(block(z, x_at[d], c, left), sibling))
            self.core.append(same(block(z_at[d], here, c, right), sibling))
        self.core_lines = []
        for d in (3, 1, 2):
            self.core_lines.append(
                (same(x_line(z_at[d], c, left, None), sibling), same(z_line(x_at[d], c, right, None), sibling))
            )

    def start(self):
        for cp in self.first:
            cp.start()
        self.core[0].start()

    def turn(self, *which):
        for k in which or (0, 1):
            for cp in self.first[k::2]:
                cp.wait_recv()
            for cp in self.lines[k][0]:
                cp.start()
            for cp in self.core[1 + k :: 2]:
                cp.start()

    def pass_on(self):
        for going, on in self.lines:
            for got, cp in zip(going[:2], on):
                got.wait_recv()
                cp.start()

    def near(self):
        for k, (going, _) in enumerate(self.lines):
            for side in range(2):
                going[2 + side].wait_recv()
                self.core_lines[side][k].start()

    def far(self):
        for k, (_, on) in enumerate(self.lines):
            for cp in on:
                cp.wait_recv()
            self.core_lines[2][k].start()

    def finish(self):
        for cp in self.core + [cp for pair in self.core_lines for cp in pair]:
            cp.wait_recv()

    def sent(self):
        for going, on in self.lines:
            for cp in going + on:
                cp.wait_send()
        for cp in self.first + self.core + [cp for pair in self.core_lines for cp in pair]:
            cp.wait_send()


def dot(left, right, dims=((1,), (0,))):
    return lax.dot_general(left, right, (dims, ((), ())), preferred_element_type=F32)


def swap_halves(v):
    lane = lax.broadcasted_iota(jnp.int32, v.shape, 1)
    return jnp.where(lane % 64 < 32, pltpu.roll(v, 96, 1), pltpu.roll(v, 32, 1))


def forward_attention(tokens, cotangent, positions, freqs, gains, attn_in, mlp_in, mlp_down, out_rows, ident):
    rows = tokens.shape[0]
    count = 4 * rows

    def kernel(
        tok_ref, cot_ref, spot_ref, freq_ref, gain_ref, in_ref, mlp_ref, down_ref, wo,
        normed_out, cot_all, gp, gg, gd, go, q_out, kv_out, att_out, lse_out, cos_out, sin_out, bias_out, middle_out, two_all,
        wp, wg, wd, tok, normed, wp_v, wo_v, q_s, kv, vx, bias, att, part, halves, whole, spot_all, own_two, cos_s, sin_s, bias_t, send, recv, local,
    ):
        say_hello(ALL_LINES, True)
        at = place()
        xh, xl, y, z, c = at
        copy = Copies(send, recv)
        slot = pl.ds(xl * 64 + y * 16, 16)
        nlocal = [0]

        def near(src, dst):
            cp = pltpu.make_async_copy(src, dst, local.at[nlocal[0]])
            nlocal[0] += 1
            return cp

        to_y = []
        stay = []
        for i, o in ((wp, gp), (wg, gg), (wd, gd)):
            to_y.append([copy(i.at[(y + d) % 4], o.at[z, xh, c, slot], along_y(d)) for d in (1, 3, 2)])
            stay.append(near(i.at[y], o.at[z, xh, c, slot]))
        over = copy(wo, go.at[xh, c, xl, y], crossed)
        keep = near(wo, go.at[xh, c, xl, z])
        spot_copies = [copy(spot_all.at[y], spot_all.at[y], along_y(d)) for d in (1, 3, 2)]
        tok_ring = RingGather(copy, tok_ref, tok, y)
        cot_ring = RingGather(copy, cot_ref, cot_all, y)
        row_halves = [pl.ds(0, rows // 2), pl.ds(rows // 2, rows // 2)]
        two_rings = [RingGather(copy, own_two.at[r], two_all.at[:, r], y) for r in row_halves]
        branches = [RingSum(copy, part.at[:, r], halves.at[:, r], whole.at[:, r], y) for r in row_halves]
        kv_copy = copy(kv.at[1], kv.at[0], half_partner)
        g_proj = Gather(copy, gp, SPLITS[0][1], at)
        g_gu = Gather(copy, gg, SPLITS[1][1], at)
        g_down = Gather(copy, gd, SPLITS[2][1], at)
        g_out = Gather(copy, go, OUT_SPLIT, at, True)

        cot_own = near(cot_ref, cot_all.at[y])
        tok_own = near(tok_ref, tok.at[y])
        tok_own.start()
        cot_own.start()
        spot_all[y] = jnp.broadcast_to(spot_ref[...].astype(F32), (8, rows))

        gain_one, gain_two = gain_ref[:, 0:1].astype(F32), gain_ref[:, 1:2].astype(F32)
        low_lanes = lax.broadcasted_iota(jnp.int32, (16, 128), 1) < 64
        for k in range(TP):
            qs = pl.ds(k * Q_COLS, Q_COLS)
            wp[k, :, pl.ds(0, Q_COLS)] = (in_ref[:, qs].astype(F32) * gain_one).astype(BF16)
            key = in_ref[:, pl.ds(D + (k // 2) * 128, 128)].astype(F32)
            value = in_ref[:, pl.ds(D + HEAD_DIM * KV_HEADS + (k // 2) * 128, 128)].astype(F32)
            if k % 2 == 0:
                both = jnp.where(low_lanes, key, pltpu.roll(value, 64, 1))
            else:
                both = jnp.where(low_lanes, pltpu.roll(key, 64, 1), value)
            wp[k, :, pl.ds(Q_COLS, 128)] = (both * gain_one).astype(BF16)
        stay[0].start()
        for k in range(TP):
            for j in range(HID // 128):
                for half in range(2):
                    cols = pl.ds(half * FF + k * HID + j * 128, 128)
                    tile = (mlp_ref[:, cols].astype(F32) * gain_two).astype(BF16)
                    wg[k, :, pl.ds(j * 256 + half * 128, 128)] = tile
            wd[k] = down_ref[:, pl.ds(k * HID, HID)]
        for cp in stay[1:]:
            cp.start()
        meet(ALL_LINES, True)
        away = y != z
        for cp in to_y[0]:
            cp.start()

        @pl.when(away)
        def _():
            over.start()

        @pl.when(jnp.logical_not(away))
        def _():
            keep.start()

        for cp in spot_copies + to_y[1] + to_y[2] + tok_ring.first:
            cp.start()

        def norm_block(k):
            def body(r, _):
                rs = pl.ds(r * 32, 32)
                v = tok[k, rs].astype(F32)
                inv = lax.rsqrt(jnp.mean(v * v, -1, keepdims=True) + EPS)
                normed[k, rs] = (v * inv).astype(BF16)
                return 0

            lax.fori_loop(0, rows // 32, body, 0)

        stay[0].wait()
        for cp in to_y[0]:
            cp.wait_recv()
        g_proj.start()

        @pl.when(away)
        def _():
            over.wait()

        @pl.when(jnp.logical_not(away))
        def _():
            keep.wait()

        g_out.start()
        tok_own.wait()
        norm_block(y)
        g_proj.turn()
        stay[1].wait()
        for cp in to_y[1]:
            cp.wait_recv()
        g_gu.start()
        g_proj.pass_on()
        stay[2].wait()
        for cp in to_y[2]:
            cp.wait_recv()
        g_down.start()
        g_out.turn()
        for cp in spot_copies:
            cp.wait_recv()
        tok_ring.turn()
        g_proj.near()
        g_proj.far()

        cos, sin = [], []
        freq, sign = freq_ref[0:1, :], freq_ref[1:2, :]
        spot_cols = []
        for k in range(4):
            col = jnp.transpose(jnp.broadcast_to(spot_all[k, 0:1, :], (128, 128)))
            spot_cols.append(col)
            cos.append(jnp.cos(col * freq))
            sin.append(jnp.sin(col * freq) * sign)
        cos, sin = jnp.concatenate(cos, 0), jnp.concatenate(sin, 0)
        cos_s[...] = cos
        sin_s[...] = sin
        turn_saves = [near(cos_s, cos_out), near(sin_s, sin_out)]
        for cp in turn_saves:
            cp.start()
        low_half = xl == 0
        reach = jnp.where(low_half, -1.0, 2048.0)
        for k in range(4):
            for j in range(8):
                row = lax.broadcasted_iota(jnp.int32, (128, 128), 0) + k * 128
                col = lax.broadcasted_iota(jnp.int32, (128, 128), 1) + j * 128
                apart = (row - col + 512).astype(F32)
                seen = apart <= spot_cols[k]
                if j < 4:
                    seen = seen & (apart <= reach)
                else:
                    seen = seen & (col - 512 <= row)
                bias[pl.ds(k * 128, 128), pl.ds(j * 128, 128)] = jnp.where(seen, 0.0, NEG_FILL)

        g_proj.finish()
        wp_load = near(gp, wp_v)
        wp_load.start()
        g_out.pass_on()
        tok_ring.near()
        norm_block((y + 3) % 4)
        norm_block((y + 1) % 4)
        g_out.near()
        tok_ring.far()
        cot_ring.start()
        norm_block((y + 2) % 4)
        normed_save = near(normed, normed_out)
        normed_save.start()

        g_gu.turn(0)
        g_down.turn(0)

        wp_load.wait()
        left = normed[...].reshape(count, D)
        lane = lax.broadcasted_iota(jnp.int32, (count, 128), 1)
        upper = lane >= 64
        raw = dot(left, wp_v[:, :, :, :, pl.ds(Q_COLS, 128)].reshape(D, 128))
        turned = raw * jnp.where(upper, 1.0, cos) + swap_halves(raw) * jnp.where(upper, 0.0, sin)
        kv[1] = turned.astype(BF16)
        kv_copy.start()
        g_out.far()
        g_gu.turn(1)
        g_down.turn(1)
        for j in range(2):
            raw2 = dot(left, wp_v[:, :, :, :, pl.ds(j * 256, 256)].reshape(D, 256))
            for e in range(2):
                raw = raw2[:, e * 128 : e * 128 + 128]
                turned = (raw * cos + swap_halves(raw) * sin).astype(BF16).astype(F32) * (HEAD_DIM ** (-0.5))
                pair = j * 2 + e
                q_s[2 * pair] = jnp.where(upper, 0.0, turned).astype(BF16)
                q_s[2 * pair + 1] = jnp.where(upper, 0.0, pltpu.roll(turned, 64, 1)).astype(BF16)
        kv_copy.wait_recv()
        for k in range(2):
            vx[k] = jnp.where(upper, kv[k].astype(F32), 1.0).astype(BF16)
        q_save = near(q_s, q_out)
        q_save.start()
        kv_save = near(kv, kv_out)
        kv_save.start()
        g_out.finish()
        wo_load = near(go, wo_v)
        wo_load.start()

        def attend(pair):
            for b in range(2):
                rs = pl.ds(b * 256, 256)
                seen = 256 * (b + 1)
                lane = lax.broadcasted_iota(jnp.int32, (256, 128), 1) < 64
                found = []
                for e in range(2):
                    q = q_s[2 * pair + e, rs]
                    s0 = dot(q, kv[0], NT) + bias[rs, pl.ds(0, 512)]
                    s1 = dot(q, kv[1, pl.ds(0, seen)], NT) + bias[rs, pl.ds(512, seen)]
                    m = jnp.maximum(jnp.max(s0, -1, keepdims=True), jnp.max(s1, -1, keepdims=True))
                    p0 = jnp.exp(s0 - m).astype(BF16)
                    p1 = jnp.exp(s1 - m).astype(BF16)
                    o = dot(p0, vx[0]) + dot(p1, vx[1, pl.ds(0, seen)])
                    r = pltpu.roll(o, 64, 1)
                    found.append((o, r))
                    log_total = m + jnp.log(jnp.where(lane, o, r))
                    lse_out[2 * pair + e, :, rs] = jnp.transpose(log_total)[0:8]
                (o, r), (o2, r2) = found
                both = jnp.where(lane, r / o, o2 / r2)
                att[rs, pl.ds(pl.multiple_of(pair * 128, 128), 128)] = both.astype(BF16)

        def two_pairs(k):
            def body(i, _):
                attend(2 * k + i)
                return 0

            lax.fori_loop(0, 2, body, 0)

        two_pairs(0)
        cot_ring.turn()
        two_pairs(1)
        att_save = near(att, att_out)
        att_save.start()
        wo_load.wait()

        for j in range(4):
            cols = pl.ds(j * 512, 512)
            w = wo_v[:, :, :, :, :, cols].reshape(Q_COLS, 512)
            part[:, :, cols] = dot(att[...], w).astype(BF16).reshape(4, rows, 512)
        for branch in branches:
            branch.start()

        for k in range(4):
            for j in range(8):
                key = lax.broadcasted_iota(jnp.int32, (128, 128), 0) + j * 128
                row = lax.broadcasted_iota(jnp.int32, (128, 128), 1) + k * 128
                apart = (row - key + 512).astype(F32)
                seen = apart <= spot_all[k, 0:1, :]
                if j < 4:
                    seen = seen & (apart <= reach)
                else:
                    seen = seen & (key - 512 <= row)
                bias_t[pl.ds(j * 128, 128), pl.ds(k * 128, 128)] = jnp.where(seen, 0.0, NEG_FILL)
        bias_save = near(bias_t, bias_out)
        bias_save.start()
        g_gu.pass_on()
        g_down.pass_on()
        for branch in branches:
            branch.turn()
        g_gu.near()
        g_down.near()
        cot_ring.near()
        cot_ring.far()
        two_own = near(own_two, two_all.at[y])
        for k in range(2):
            branches[k].finish()

            def mid(r, _, k=k):
                rs, half = pl.ds(k * (rows // 2) + r * 32, 32), pl.ds(r * 32, 32)
                v = tok_ref[rs].astype(F32) + branches[k].rows(half)
                middle_out[rs] = v
                inv = lax.rsqrt(jnp.mean(v * v, -1, keepdims=True) + EPS)
                own_two[rs] = (v * inv).astype(BF16)
                return 0

            lax.fori_loop(0, rows // 64, mid, 0)
            two_rings[k].start()
        two_own.start()
        for ring in two_rings:
            ring.turn()
        g_gu.far()
        g_down.far()
        for ring in two_rings:
            ring.near()
            ring.far()
        g_gu.finish()
        g_down.finish()
        for cp in (cot_own, normed_save, q_save, kv_save, att_save, two_own, bias_save, *turn_saves):
            cp.wait()
        for group in to_y:
            for cp in group:
                cp.wait_send()
        for cp in spot_copies + [kv_copy]:
            cp.wait_send()
        for thing in (g_proj, g_out, g_gu, g_down, tok_ring, cot_ring, *two_rings, *branches):
            thing.sent()

    anywhere, vmem = pl.BlockSpec(memory_space=pl.ANY), pl.BlockSpec(memory_space=pltpu.VMEM)
    outs = [
        (struct((4, rows, D)), anywhere),
        (struct((4, rows, D)), anywhere),
        (struct((4, 2, 2, 128, PROJ)), anywhere),
        (struct((4, 2, 2, 128, 2 * HID)), anywhere),
        (struct((4, 2, 2, 128, HID)), anywhere),
        (struct((2, 2, 2, 4, 16, D)), anywhere),
        (struct((REPEAT, count, 128)), anywhere),
        (struct((2, count, 128)), anywhere),
        (struct((count, Q_COLS)), anywhere),
        (struct((REPEAT, 8, count), F32), vmem),
        (struct((count, 128), F32), anywhere),
        (struct((count, 128), F32), anywhere),
        (struct((2 * count, count), F32), anywhere),
        (struct((rows, D), F32), vmem),
        (struct((4, rows, D)), anywhere),
    ]
    copies = 9 + 1 + 3 + 6 * 6 + 1 + 31 * 4
    return pl.pallas_call(
        kernel,
        out_shape=[o[0] for o in outs],
        in_specs=[vmem] * 9,
        out_specs=[o[1] for o in outs],
        scratch_shapes=[
            pltpu.VMEM((TP, 16, PROJ), BF16),
            pltpu.VMEM((TP, 16, 2 * HID), BF16),
            pltpu.VMEM((TP, 16, HID), BF16),
            pltpu.VMEM((4, rows, D), BF16),
            pltpu.VMEM((4, rows, D), BF16),
            pltpu.VMEM((4, 2, 2, 128, PROJ), BF16),
            pltpu.VMEM((2, 2, 2, 4, 16, D), BF16),
            pltpu.VMEM((REPEAT, count, 128), BF16),
            pltpu.VMEM((2, count, 128), BF16),
            pltpu.VMEM((2, count, 128), BF16),
            pltpu.VMEM((count, 2 * count), F32),
            pltpu.VMEM((count, Q_COLS), BF16),
            pltpu.VMEM((4, rows, D), BF16),
            pltpu.VMEM((2, rows, D // 2), BF16),
            pltpu.VMEM((2, rows, D), BF16),
            pltpu.VMEM((4, 8, 128), F32),
            pltpu.VMEM((rows, D), BF16),
            pltpu.VMEM((count, 128), F32),
            pltpu.VMEM((count, 128), F32),
            pltpu.VMEM((2 * count, count), F32),
            pltpu.SemaphoreType.DMA((copies,)),
            pltpu.SemaphoreType.DMA((copies,)),
            pltpu.SemaphoreType.DMA((20,)),
        ],
        name="forward_attention",
        compiler_params=pltpu.CompilerParams(
            collective_id=ident, has_side_effects=True, vmem_limit_bytes=VMEM_LIMIT
        ),
    )(tokens, cotangent, positions, freqs, gains, attn_in, mlp_in, mlp_down, out_rows)


def tiles(ref):
    if len(ref.shape) == 2:
        return [ref]
    return [t for k in range(ref.shape[0]) for t in tiles(ref.at[k])]


def add_up(dst, *others):
    for out, *terms in zip(tiles(dst), *[tiles(o) for o in others]):
        rows = out.shape[0]
        step = min(rows, 32)

        def body(r, _, out=out, terms=terms, step=step):
            rs = pl.ds(r * step, step)
            value = out[rs].astype(F32)
            for t in terms:
                value = value + t[rs].astype(F32)
            out[rs] = value.astype(BF16)
            return 0

        lax.fori_loop(0, rows // step, body, 0)


class LineSum:
    def __init__(self, copy, lo, hi, along, far, near):
        self.lo, self.hi, self.far_in, self.near_in = lo, hi, far, near
        self.far = [copy(lo(2), far.at[0], along(1)), copy(hi(2), far.at[1], along(3))]
        self.near = [copy(hi(1), near.at[0, 1], along(1)), copy(lo(3), near.at[1, 0], along(3))]
        self.last = [copy(lo(1), near.at[0, 0], along(1)), copy(hi(3), near.at[1, 1], along(3))]

    def start(self):
        for cp in self.far + self.near:
            cp.start()

    def turn(self):
        self.far[0].wait_recv()
        add_up(self.lo(1), self.far_in.at[0])
        self.last[0].start()
        self.far[1].wait_recv()
        add_up(self.hi(3), self.far_in.at[1])
        self.last[1].start()

    def finish(self):
        for cp in self.near + self.last:
            cp.wait_recv()
        add_up(self.lo(0), self.near_in.at[0, 0], self.near_in.at[1, 0])
        add_up(self.hi(0), self.near_in.at[0, 1], self.near_in.at[1, 1])

    def sent(self):
        for cp in self.far + self.near + self.last:
            cp.wait_send()


class GradLines:
    def __init__(self, copy, terms, a, at, buffers, rows_only=False):
        xh, xl, y, z, c = at
        far_a, near_a, far_b, near_b = buffers
        cols = terms.shape[-1]
        left, right = pl.ds(0, a), pl.ds(a, cols - a)
        x_at = [along_x(d)(*at)[:2] for d in range(4)]
        z_at = [(z + d) % 4 for d in range(4)]
        if rows_only:
            spot = lambda x, z, cols: terms.at[x[0], c, x[1], z, :, cols]
            a_half = lambda h: lambda d: terms.at[h, c, :, z_at[d], :, left]
            b_half = lambda h: lambda d: terms.at[x_at[d][0], c, x_at[d][1], pl.ds(2 * h, 2), :, right]
        else:
            base = (lambda z, xh: (z, xh, c)) if len(terms.shape) == 5 else (lambda z, xh: (z, xh))
            spot = lambda x, z, cols: terms.at[base(z, x[0]) + (pl.ds(x[1] * 64, 64), cols)]
            a_half = lambda h: lambda d: terms.at[base(z_at[d], h) + (slice(None), left)]
            b_half = lambda h: lambda d: terms.at[
                base(pl.ds(2 * h, 2), x_at[d][0]) + (pl.ds(x_at[d][1] * 64, 64), right)
            ]
        self.lines = [
            LineSum(copy, a_half(0), a_half(1), along_z, far_a, near_a),
            LineSum(copy, b_half(0), b_half(1), along_x, far_b, near_b),
        ]
        self.spot_a = lambda x: spot(x, z, left)
        self.spot_b = lambda z: spot(x_at[0], z, right)

    def start(self):
        for line in self.lines:
            line.start()

    def turn(self):
        for line in self.lines:
            line.turn()

    def finish(self):
        for line in self.lines:
            line.finish()

    def sent(self):
        for line in self.lines:
            line.sent()


class GradOwners:
    def __init__(self, copy, local_copy, spot_a, spot_b, out, at, buffers, rows_only=False):
        xh, xl, y, z, c = at
        self.at, self.rows_only = at, rows_only
        got_a, got_b, own = buffers
        a, cols = got_a.shape[-1], own.shape[-1]
        self.second = []
        for d in (1, 3, 2):
            self.second.append(copy(spot_a(along_x(d)(*at)[:2]), got_a.at[d - 1], along_x(d)))
            self.second.append(copy(spot_b((z + d) % 4), got_b.at[d - 1], along_z(d)))
        self.mine = (spot_a((xh, xl)), spot_b(z))
        self.got = (got_a, got_b)
        self.own, self.cuts = own, (pl.ds(0, a), pl.ds(a, cols - a))
        if rows_only:
            self.over = copy(own, out, crossed)
            self.keep = local_copy(own, out)
        else:
            self.to_y = [copy(own.at[(y + d) % 4], out.at[y], along_y(d)) for d in (1, 3, 2)]
            self.keep = local_copy(own.at[y], out.at[y])

    def start(self):
        for cp in self.second:
            cp.start()

    def deliver(self):
        for cp in self.second:
            cp.wait_recv()
        for mine, got, cut in zip(self.mine, self.got, self.cuts):
            value = mine[...].astype(F32)
            for d in range(3):
                value = value + got[d].astype(F32)
            own = self.own
            if self.rows_only:
                own[:, cut] = value.astype(BF16)
            else:
                own[:, :, cut] = value.astype(BF16).reshape(4, 16, value.shape[-1])
        if self.rows_only:
            y, z = self.at[2], self.at[3]

            @pl.when(y != z)
            def _():
                self.over.start()

            @pl.when(y == z)
            def _():
                self.keep.start()

        else:
            for cp in self.to_y:
                cp.start()
            self.keep.start()

    def finish(self):
        if self.rows_only:
            y, z = self.at[2], self.at[3]

            @pl.when(y != z)
            def _():
                self.over.wait()

            @pl.when(y == z)
            def _():
                self.keep.wait()

        else:
            for cp in self.to_y:
                cp.wait()
            self.keep.wait()
        for cp in self.second:
            cp.wait_send()


def line_buffers(cols, a, rows_only=False):
    b = cols - a
    a_half, b_half = ((2, 16), (2, 16)) if rows_only else ((128,), (2, 64))
    return [
        pltpu.VMEM((2,) + a_half + (a,), BF16),
        pltpu.VMEM((2, 2) + a_half + (a,), BF16),
        pltpu.VMEM((2,) + b_half + (b,), BF16),
        pltpu.VMEM((2, 2) + b_half + (b,), BF16),
    ]


def owner_buffers(cols, a, rows_only=False):
    spot, own = (16, (16, cols)) if rows_only else (64, (4, 16, cols))
    return [pltpu.VMEM((3, spot, a), BF16), pltpu.VMEM((3, spot, cols - a), BF16), pltpu.VMEM(own, BF16)]


def backward_attention(
    gu_a, gu_b, sum_down, out_part, branch_all, grad_middle, middle, tokens,
    cosines, sines, bias_all, q_all, kv_all, attended, lse, normed_all, proj_w, out_w, ident,
):
    rows = tokens.shape[0]
    count = 4 * rows
    scale = HEAD_DIM ** (-0.5)

    def kernel(
        gu_a_ref, gu_b_ref, s_down, op_ref, br_ref, gm_hbm, mid_hbm, tok_hbm,
        cos_ref, sin_ref, bias_ref, q_ref, kv_ref, att_ref, lse_ref, nm_ref, wp_ref, wo_ref,
        out_ref, ig_ref, o_proj, o_gu, o_down, o_out,
        gm_ref, mid_ref, tok_ref, v_gu_a, v_gu_b, v_down, part, part_in, halves, whole, halves2, whole2, br, q_s, do_s, kv, kvt, att, delta, bias, cos_s, sin_s,
        dkv, kv_send, kv_in, gp, normed, wp, wo, t_proj, rc_proj, t_out, rc_out, *rest,
    ):
        bufs, (send, recv, local) = rest[:24], rest[24:]
        say_hello(ALL_LINES, True)
        at = place()
        xh, xl, y, z, c = at
        copy = Copies(send, recv)
        nlocal = [0]

        def near(src, dst):
            cp = pltpu.make_async_copy(src, dst, local.at[nlocal[0]])
            nlocal[0] += 1
            return cp

        load_gu, load_gu_b, load_down = near(gu_a_ref, v_gu_a), near(gu_b_ref, v_gu_b), near(s_down, v_down)
        load_op, load_br, load_wo = near(op_ref, part), near(br_ref, br), near(wo_ref, wo)
        load_att, load_q = near(att_ref, att), near(q_ref, q_s)
        load_kv = near(kv_ref, kv)
        load_turns = [near(cos_ref, cos_s), near(sin_ref, sin_s), near(bias_ref, bias)]
        load_nm, load_wp = near(nm_ref, normed), near(wp_ref, wp)
        load_rows = [near(gm_hbm, gm_ref), near(mid_hbm, mid_ref), near(tok_hbm, tok_ref)]
        for cp in (load_br, load_wo, load_gu, load_gu_b, load_op, load_down, load_att, load_q, load_kv, *load_turns, load_nm, load_wp, *load_rows):
            cp.start()
        outs = RingSum(copy, part, halves, whole, y)
        ones = RingSum(copy, part_in, halves2, whole2, y)
        kv_copy = copy(kv_send, kv_in, half_partner)
        core_proj = [
            copy(t_proj.at[:, :, 1 - c, :, cols], rc_proj.at[:, :, :, cols], sibling)
            for cols in (pl.ds(0, Q_COLS), pl.ds(Q_COLS, 128))
        ]
        core_out = copy(t_out.at[:, 1 - c], rc_out, sibling)
        gu_owners = GradOwners(
            copy,
            near,
            lambda x: v_gu_a.at[x[0], pl.ds(x[1] * 64, 64)],
            lambda z: v_gu_b.at[z],
            o_gu,
            at,
            bufs[0:3],
        )
        down_lines = GradLines(copy, v_down, SPLITS[2][1], at, bufs[3:7])
        down_owners = GradOwners(copy, near, down_lines.spot_a, down_lines.spot_b, o_down, at, bufs[7:10])
        proj_lines = GradLines(copy, t_proj, SPLITS[0][1], at, bufs[10:14])
        proj_owners = GradOwners(copy, near, proj_lines.spot_a, proj_lines.spot_b, o_proj, at, bufs[14:17])
        out_lines = GradLines(copy, t_out, OUT_SPLIT, at, bufs[17:21], True)
        out_owners = GradOwners(copy, near, out_lines.spot_a, out_lines.spot_b, o_out, at, bufs[21:24], True)

        dkv[...] = jnp.zeros_like(dkv)

        meet(ALL_LINES, True)
        load_op.wait()
        outs.start()
        load_gu.wait()
        load_gu_b.wait()
        gu_owners.start()
        load_down.wait()
        down_lines.start()

        load_br.wait()
        load_wo.wait()
        load_att.wait()
        lane = lax.broadcasted_iota(jnp.int32, (count, 128), 1)
        for p in range(4):
            if p % 2 == 0:
                both = dot(br[...].reshape(count, D), wo[p // 2].reshape(256, D), NT).astype(BF16).astype(F32)
            low = both[:, p % 2 * 128 : p % 2 * 128 + 128]
            do_s[2 * p] = jnp.where(lane < 64, 0.0, pltpu.roll(low, 64, 1)).astype(BF16)
            do_s[2 * p + 1] = jnp.where(lane < 64, 0.0, low).astype(BF16)
            prod = jnp.transpose(low * att[:, pl.ds(p * 128, 128)].astype(F32))
            for e in range(2):
                total_row = jnp.sum(prod[e * 64 : e * 64 + 64], 0, keepdims=True)
                delta[2 * p + e] = jnp.broadcast_to(total_row, (8, count))
        outs.turn()

        for k in range(4):
            term = dot(att[:, pl.ds(k * 128, 128)], br[...].reshape(count, D), TN)
            t_out[k // 2, k % 2] = term.astype(BF16).reshape(2, 4, 16, D)
        core_out.start()
        load_q.wait()
        load_kv.wait()
        for k in range(2):
            turned = jnp.transpose(kv[pl.ds(k * count, count)].astype(F32)).astype(BF16)
            kvt[:, pl.ds(k * count, count)] = turned

        def backward(pair):
            for b in range(2):
                rs = pl.ds(b * 256, 256)
                seen = pl.ds(0, 512 + 256 * (b + 1))
                found = []
                for e in range(2):
                    h = 2 * pair + e
                    q, do = q_s[h, rs], do_s[h, rs]
                    st = dot(kv[seen], q, NT) + bias[seen, rs] - lse_ref[h, 0:1, rs]
                    p = jnp.exp(st)
                    dp = dot(kv[seen], do, NT)
                    ds = (p * (dp - delta[h, 0:1, rs])).astype(BF16)
                    dkv[seen] += dot(ds, q) + dot(p.astype(BF16), do)
                    found.append(dot(kvt[:, seen], ds)[0:64])
                both = jnp.transpose(jnp.concatenate(found, 0)) * scale
                both = both * cos_s[rs] - swap_halves(both) * sin_s[rs]
                gp[rs, pl.ds(pl.multiple_of(pair * 128, 128), 128)] = both.astype(BF16)

        def two_pairs(k):
            def body(i, _):
                backward(2 * k + i)
                return 0

            lax.fori_loop(0, 2, body, 0)

        for cp in load_turns:
            cp.wait()
        two_pairs(0)
        down_lines.turn()
        gu_owners.deliver()
        two_pairs(1)
        kv_send[...] = dkv[pl.ds(0, count)].astype(BF16)
        kv_copy.start()
        core_out.wait_recv()
        add_up(t_out.at[:, c], rc_out)
        out_lines.start()
        load_nm.wait()
        for k in range(4):
            left = normed[:, :, pl.ds(k * 512, 512)].reshape(count, 512)
            term = dot(left, gp[:, pl.ds(0, Q_COLS)], TN)
            t_proj[k, :, :, :, pl.ds(0, Q_COLS)] = term.astype(BF16).reshape(2, 2, 128, Q_COLS)
        core_proj[0].start()
        kv_copy.wait_recv()
        got = dkv[pl.ds(count, count)] + kv_in[...].astype(F32)
        back = got * cos_s[...] - swap_halves(got) * sin_s[...]
        gp[:, pl.ds(Q_COLS, 128)] = jnp.where(lane < 64, back, got).astype(BF16)
        for k in range(4):
            left = normed[:, :, pl.ds(k * 512, 512)].reshape(count, 512)
            term = dot(left, gp[:, pl.ds(Q_COLS, 128)], TN)
            t_proj[k, :, :, :, pl.ds(Q_COLS, 128)] = term.astype(BF16).reshape(2, 2, 128, 128)
        core_proj[1].start()

        load_wp.wait()
        for j in range(4):
            w = wp[j].reshape(512, PROJ)
            part_in[:, :, pl.ds(j * 512, 512)] = dot(gp[...], w, NT).astype(BF16).reshape(4, rows, 512)
        ones.start()
        down_lines.finish()
        down_owners.start()
        outs.finish()

        for cp in load_rows:
            cp.wait()

        def finish_out(r, _):
            rs = pl.ds(r * 32, 32)
            out_ref[rs] = (mid_ref[rs] + outs.rows(rs)).astype(BF16)
            return 0

        lax.fori_loop(0, rows // 32, finish_out, 0)
        outs.sent()
        out_lines.turn()
        ones.turn()
        down_owners.deliver()
        for cp in core_proj:
            cp.wait_recv()
        for k in range(4):
            add_up(t_proj.at[k, :, c], rc_proj.at[k])
        proj_lines.start()
        out_lines.finish()
        out_owners.start()
        proj_lines.turn()
        ones.finish()

        def finish_in(r, _):
            rs = pl.ds(r * 32, 32)
            v = tok_ref[rs].astype(F32)
            inv = lax.rsqrt(jnp.mean(v * v, -1, keepdims=True) + EPS)
            v = v * inv
            g = ones.rows(rs)
            ig_ref[rs] = gm_ref[rs] + inv * (g - v * jnp.mean(g * v, -1, keepdims=True))
            return 0

        lax.fori_loop(0, rows // 32, finish_in, 0)
        proj_lines.finish()
        proj_owners.start()
        out_owners.deliver()
        proj_owners.deliver()
        ones.sent()
        for cp in (kv_copy, *core_proj, core_out):
            cp.wait_send()
        for owners in (gu_owners, down_owners, out_owners, proj_owners):
            owners.finish()
        for lines in (down_lines, out_lines, proj_lines):
            lines.sent()

    anywhere, vmem = pl.BlockSpec(memory_space=pl.ANY), pl.BlockSpec(memory_space=pltpu.VMEM)
    in_specs = [anywhere] * 14 + [vmem] + [anywhere] * 3
    outs = [
        (struct((rows, D)), vmem),
        (struct((rows, D), F32), vmem),
        (struct((4, 16, PROJ)), anywhere),
        (struct((4, 16, 2 * HID)), anywhere),
        (struct((4, 16, HID)), anywhere),
        (struct((16, D)), anywhere),
    ]
    whole = lambda: [pltpu.VMEM((2, rows, D // 2), BF16), pltpu.VMEM((2, rows, D), BF16)]
    copies = 12 + 4 + 9 + 21 * 2 + 19
    return pl.pallas_call(
        kernel,
        out_shape=[o[0] for o in outs],
        in_specs=in_specs,
        out_specs=[o[1] for o in outs],
        scratch_shapes=[
            pltpu.VMEM((rows, D), F32),
            pltpu.VMEM((rows, D), F32),
            pltpu.VMEM((rows, D), BF16),
            pltpu.VMEM((2, 128, SPLITS[1][1]), BF16),
            pltpu.VMEM((4, 64, 2 * HID - SPLITS[1][1]), BF16),
            pltpu.VMEM((4, 2, 128, HID), BF16),
            pltpu.VMEM((4, rows, D), BF16),
            pltpu.VMEM((4, rows, D), BF16),
            *whole(),
            *whole(),
            pltpu.VMEM((4, rows, D), BF16),
            pltpu.VMEM((REPEAT, count, 128), BF16),
            pltpu.VMEM((REPEAT, count, 128), BF16),
            pltpu.VMEM((2 * count, 128), BF16),
            pltpu.VMEM((128, 2 * count), BF16),
            pltpu.VMEM((count, Q_COLS), BF16),
            pltpu.VMEM((REPEAT, 8, count), F32),
            pltpu.VMEM((2 * count, count), F32),
            pltpu.VMEM((count, 128), F32),
            pltpu.VMEM((count, 128), F32),
            pltpu.VMEM((2 * count, 128), F32),
            pltpu.VMEM((count, 128), BF16),
            pltpu.VMEM((count, 128), BF16),
            pltpu.VMEM((count, PROJ), BF16),
            pltpu.VMEM((4, rows, D), BF16),
            pltpu.VMEM((4, 2, 2, 128, PROJ), BF16),
            pltpu.VMEM((2, 2, 2, 4, 16, D), BF16),
            pltpu.VMEM((4, 2, 2, 128, PROJ), BF16),
            pltpu.VMEM((4, 2, 128, PROJ), BF16),
            pltpu.VMEM((2, 2, 2, 4, 16, D), BF16),
            pltpu.VMEM((2, 2, 4, 16, D), BF16),
            *owner_buffers(2 * HID, SPLITS[1][1]),
            *line_buffers(HID, SPLITS[2][1]),
            *owner_buffers(HID, SPLITS[2][1]),
            *line_buffers(PROJ, SPLITS[0][1]),
            *owner_buffers(PROJ, SPLITS[0][1]),
            *line_buffers(D, OUT_SPLIT, True),
            *owner_buffers(D, OUT_SPLIT, True),
            pltpu.SemaphoreType.DMA((copies,)),
            pltpu.SemaphoreType.DMA((copies,)),
            pltpu.SemaphoreType.DMA((24,)),
        ],
        name="backward_attention",
        compiler_params=pltpu.CompilerParams(
            collective_id=ident, has_side_effects=True, vmem_limit_bytes=VMEM_LIMIT
        ),
    )(
        gu_a, gu_b, sum_down, out_part, branch_all, grad_middle, middle, tokens,
        cosines, sines, bias_all, q_all, kv_all, attended, lse, normed_all, proj_w, out_w,
    )


def feed_forward(seq_two, seq_cot, gu_w, down_w, middle, cotangent, ident):
    rows = middle.shape[0]
    count = 4 * rows
    tiles_gu, pairs = HID // 128, HID // 256

    def kernel(
        two_ref, cot_ref, wg_ref, wd_ref, mid_hbm, own_cot_hbm,
        branch_all, gm_ref, gu_a, gu_b, s_down, op_out,
        part, halves, whole, two, gu, cot, hid, gh, turned, t_gu, t_down, rc_gu, rc_down, branch, op,
        mid_ref, own_cot,
        far_a, near_a, far_b, near_b, send, recv, local, weights,
    ):
        partners = [along_y(1), along_y(3), along_x(1), along_x(3), along_z(1), along_z(3), sibling]
        say_hello(partners)
        at = place()
        xh, xl, y, z, c = at
        copy = Copies(send, recv)
        nlocal = [0]

        def near(src, dst):
            cp = pltpu.make_async_copy(src, dst, local.at[nlocal[0]])
            nlocal[0] += 1
            return cp

        def load_gu(j):
            tile = pl.ds(pl.multiple_of(j * 256, 256), 256)
            return pltpu.make_async_copy(wg_ref.at[:, :, :, :, tile], t_gu.at[:, :, :, :, tile], weights.at[j])

        def load_down(j, width=256):
            tile = pl.ds(pl.multiple_of(j * 256, 256), width)
            return pltpu.make_async_copy(
                wd_ref.at[:, :, :, :, tile], t_down.at[:, :, :, :, tile], weights.at[tiles_gu + j]
            )

        load_cot, load_two = near(cot_ref, cot), near(two_ref, two)
        load_rows = [near(mid_hbm, mid_ref), near(own_cot_hbm, own_cot)]
        load_cot.start()
        last_down = load_down(pairs, HID - 256 * pairs)

        def begin_down(j, _):
            load_down(j).start()
            return 0

        def begin_gu(j, _):
            load_gu(j).start()
            return 0

        lax.fori_loop(0, pairs, begin_down, 0)
        last_down.start()
        load_two.start()
        lax.fori_loop(0, tiles_gu, begin_gu, 0)
        for cp in load_rows:
            cp.start()
        row_halves = [pl.ds(0, rows // 2), pl.ds(rows // 2, rows // 2)]
        rings = [RingSum(copy, part.at[:, r], halves.at[:, r], whole.at[:, r], y) for r in row_halves]
        gathers = [RingGather(copy, branch.at[r], branch_all.at[:, r], y) for r in row_halves]
        own = near(branch, branch_all.at[y])
        cores = [
            (copy(t_gu.at[k, :, 1 - c], rc_gu.at[k], sibling), copy(t_down.at[k, :, 1 - c], rc_down.at[k], sibling))
            for k in [(z + d) % 4 for d in range(4)]
        ]
        saves = [near(t_down.at[k, :, c], s_down.at[k]) for k in [(z + d) % 4 for d in range(4)]]
        lines = GradLines(copy, t_gu, SPLITS[1][1], at, (far_a, near_a, far_b, near_b))
        saves_gu = [
            near(t_gu.at[z, :, c, :, pl.ds(0, SPLITS[1][1])], gu_a),
            near(t_gu.at[:, xh, c, pl.ds(xl * 64, 64), pl.ds(SPLITS[1][1], 2 * HID - SPLITS[1][1])], gu_b),
        ]
        save_op = near(op, op_out)
        load_cot.wait()

        def hidden_back(j, _):
            load_down(j).wait()
            tile = pl.ds(pl.multiple_of(j * 256, 256), 256)
            gh[:, tile] = dot(cot[...].reshape(count, D), t_down[:, :, :, :, tile].reshape(D, 256))
            return 0

        lax.fori_loop(0, pairs, hidden_back, 0)
        last_down.wait()
        tile = pl.ds(256 * pairs, HID - 256 * pairs)
        gh[:, tile] = dot(cot[...].reshape(count, D), t_down[:, :, :, :, tile].reshape(D, HID - 256 * pairs))
        load_two.wait()

        def gate_up(j):
            load_gu(j).wait()
            both = pl.ds(pl.multiple_of(j * 256, 256), 256)
            return dot(two[...].reshape(count, D), t_gu[:, :, :, :, both].reshape(D, 256))

        def activate(j, act):
            both = pl.ds(pl.multiple_of(j * 256, 256), 256)
            one = pl.ds(pl.multiple_of(j * 128, 128), 128)
            gate, up = act[:, :128], act[:, 128:]
            back = gh[:, one]
            sigmoid = jax.nn.sigmoid(gate)
            silu = gate * sigmoid
            hid[:, one] = (silu * up).astype(BF16)
            grad_gate = back * up * sigmoid * (1.0 + gate * (1.0 - sigmoid))
            gu[:, both] = jnp.concatenate([grad_gate, back * silu], 1).astype(BF16)

        def hidden(j, _):
            activate(j, gate_up(j))
            return 0

        lax.fori_loop(0, tiles_gu, hidden, 0)

        def part_two(k, _):
            cols = pl.ds(pl.multiple_of(k * 512, 512), 512)
            part[:, :, cols] = dot(gu[...], t_gu[k].reshape(512, 2 * HID), NT).astype(BF16).reshape(4, rows, 512)
            return 0

        lax.fori_loop(0, 4, part_two, 0)
        meet(partners)
        for ring in rings:
            ring.start()

        def part_out(k, _):
            cols = pl.ds(pl.multiple_of(k * 512, 512), 512)
            op[:, :, cols] = dot(hid[...], t_down[k].reshape(512, HID), NT).astype(BF16).reshape(4, rows, 512)
            return 0

        def terms_gu(d):
            k = (z + d) % 4
            cols = pl.ds(pl.multiple_of(k * 512, 512), 512)
            turned[...] = jnp.transpose(two[:, :, cols].reshape(count, 512))

            def some(j, _):
                tile = pl.ds(pl.multiple_of(j * 256, 256), 256)
                t_gu[k, :, :, :, tile] = dot(turned[...], gu[:, tile]).astype(BF16).reshape(2, 2, 128, 256)
                return 0

            lax.fori_loop(0, 2 * HID // 256, some, 0)
            cores[d][0].start()

        def terms_down(d):
            k = (z + d) % 4
            cols = pl.ds(pl.multiple_of(k * 512, 512), 512)
            turned[...] = jnp.transpose(cot[:, :, cols].reshape(count, 512))

            def more(j, width=256):
                tile = pl.ds(pl.multiple_of(j * 256, 256), width)
                t_down[k, :, :, :, tile] = dot(turned[...], hid[:, tile]).astype(BF16).reshape(2, 2, 128, width)
                return 0

            lax.fori_loop(0, pairs, lambda j, _: more(j), 0)
            more(pairs, HID - 256 * pairs)
            cores[d][1].start()

        def add_gu(d):
            k = (z + d) % 4
            cores[d][0].wait_recv()
            add_up(t_gu.at[k, :, c], rc_gu.at[k])

        line_a, line_b = lines.lines
        terms_gu(2)
        terms_gu(1)
        for ring in rings:
            ring.turn()
        add_gu(2)
        for cp in line_a.far:
            cp.start()
        terms_gu(3)
        add_gu(1)
        terms_gu(0)
        add_gu(3)
        for cp in line_a.near:
            cp.start()
        add_gu(0)
        line_b.start()
        for cp in load_rows:
            cp.wait()
        for k in range(2):
            rings[k].finish()

            def back(r, _, k=k):
                rs, half = pl.ds(k * (rows // 2) + r * 32, 32), pl.ds(r * 32, 32)
                v = mid_ref[rs]
                inv = lax.rsqrt(jnp.mean(v * v, -1, keepdims=True) + EPS)
                v = v * inv
                g = rings[k].rows(half)
                value = own_cot[rs].astype(F32) + inv * (g - v * jnp.mean(g * v, -1, keepdims=True))
                gm_ref[rs] = value
                branch[rs] = value.astype(BF16)
                return 0

            lax.fori_loop(0, rows // 64, back, 0)
            gathers[k].start()
        own.start()
        lax.fori_loop(0, 4, part_out, 0)
        save_op.start()
        for gather in gathers:
            gather.turn()
        line_a.turn()
        terms_down(2)
        terms_down(1)
        line_b.turn()
        terms_down(3)
        terms_down(0)
        for d in (2, 1, 3, 0):
            cores[d][1].wait_recv()
            add_up(t_down.at[(z + d) % 4, :, c], rc_down.at[(z + d) % 4])
            saves[d].start()
        for gather in gathers:
            gather.near()
            gather.far()
        lines.finish()
        for cp in saves_gu:
            cp.start()
        own.wait()
        save_op.wait()
        for cp in saves + saves_gu:
            cp.wait()
        for pair in cores:
            for cp in pair:
                cp.wait_send()
        lines.sent()
        for ring in rings + gathers:
            ring.sent()

    anywhere, vmem = pl.BlockSpec(memory_space=pl.ANY), pl.BlockSpec(memory_space=pltpu.VMEM)
    copies = 24 + 8 + 12
    return pl.pallas_call(
        kernel,
        out_shape=[
            struct((4, rows, D)),
            struct((rows, D), F32),
            struct((2, 128, SPLITS[1][1])),
            struct((4, 64, 2 * HID - SPLITS[1][1])),
            struct((4, 2, 128, HID)),
            struct((4, rows, D)),
        ],
        in_specs=[anywhere] * 6,
        out_specs=[anywhere, vmem, anywhere, anywhere, anywhere, anywhere],
        scratch_shapes=[
            pltpu.VMEM((4, rows, D), BF16),
            pltpu.VMEM((2, rows, D // 2), BF16),
            pltpu.VMEM((2, rows, D), BF16),
            pltpu.VMEM((4, rows, D), BF16),
            pltpu.VMEM((count, 2 * HID), BF16),
            pltpu.VMEM((4, rows, D), BF16),
            pltpu.VMEM((count, HID), BF16),
            pltpu.VMEM((count, HID), F32),
            pltpu.VMEM((512, count), BF16),
            pltpu.VMEM((4, 2, 2, 128, 2 * HID), BF16),
            pltpu.VMEM((4, 2, 2, 128, HID), BF16),
            pltpu.VMEM((4, 2, 128, 2 * HID), BF16),
            pltpu.VMEM((4, 2, 128, HID), BF16),
            pltpu.VMEM((rows, D), BF16),
            pltpu.VMEM((4, rows, D), BF16),
            pltpu.VMEM((rows, D), F32),
            pltpu.VMEM((rows, D), BF16),
            *line_buffers(2 * HID, SPLITS[1][1]),
            pltpu.SemaphoreType.DMA((copies,)),
            pltpu.SemaphoreType.DMA((copies,)),
            pltpu.SemaphoreType.DMA((16,)),
            pltpu.SemaphoreType.DMA((tiles_gu + pairs + 1,)),
        ],
        name="feed_forward",
        compiler_params=pltpu.CompilerParams(
            collective_id=ident, has_side_effects=True, vmem_limit_bytes=VMEM_LIMIT
        ),
    )(seq_two, seq_cot, gu_w, down_w, middle, cotangent)


def own_rows(gains, attn_in, mlp_in, proj, gu, down, out):
    def kernel(gain_ref, in_ref, mlp_ref, proj_ref, gu_ref, down_ref, out_ref, g_in, g_mlp, g_down, g_out, g_gain):
        gain_one, gain_two = gain_ref[:, 0:1].astype(F32), gain_ref[:, 1:2].astype(F32)
        lane = lax.broadcasted_iota(jnp.int32, (16, 128), 1)
        low = lane < 64

        def put(dst, weights, at, value, gain, total):
            cols = pl.ds(at, 128)
            dst[:, cols] = value * gain
            return total + value * weights[:, cols].astype(F32)

        first = jnp.zeros((16, 128), F32)
        for k in range(TP):
            for j in range(Q_COLS // 128):
                value = proj_ref[k, :, pl.ds(j * 128, 128)].astype(F32)
                first = put(g_in, in_ref, k * Q_COLS + j * 128, value, gain_one, first)
        for k in range(0, TP, 2):
            even = proj_ref[k, :, pl.ds(Q_COLS, 128)].astype(F32)
            odd = proj_ref[k + 1, :, pl.ds(Q_COLS, 128)].astype(F32)
            key = jnp.where(low, even, pltpu.roll(odd, 64, 1))
            value = jnp.where(low, pltpu.roll(even, 64, 1), odd)
            first = put(g_in, in_ref, D + k * 64, key, gain_one, first)
            first = put(g_in, in_ref, D + HEAD_DIM * KV_HEADS + k * 64, value, gain_one, first)
        second = jnp.zeros((16, 128), F32)
        for k in range(TP):
            for j in range(HID // 128):
                for half in range(2):
                    value = gu_ref[k, :, pl.ds(j * 256 + half * 128, 128)].astype(F32)
                    second = put(g_mlp, mlp_ref, half * FF + k * HID + j * 128, value, gain_two, second)
            g_down[:, pl.ds(k * HID, HID)] = down_ref[k].astype(F32)
        g_out[...] = out_ref[...].astype(F32)
        sums = jnp.sum(first, -1, keepdims=True), jnp.sum(second, -1, keepdims=True)
        g_gain[...] = jnp.transpose(jnp.where(lane == 0, sums[0], sums[1]))[0:8]

    shapes = [(16, attn_in.shape[1]), (16, 2 * FF), (16, FF), (16, D), (8, 16)]
    return pl.pallas_call(
        kernel,
        out_shape=[struct(shape, F32) for shape in shapes],
        in_specs=[pl.BlockSpec(memory_space=pltpu.VMEM)] * 7,
        out_specs=[pl.BlockSpec(memory_space=pltpu.VMEM)] * 5,
        name="own_rows",
        compiler_params=pltpu.CompilerParams(vmem_limit_bytes=VMEM_LIMIT),
    )(gains, attn_in, mlp_in, proj, gu, down, out)


def shards(tokens, positions, attn_in, attn_out, attn_gain, mlp_in, mlp_down, mlp_gain, cotangent):
    rows = tokens.shape[0]
    count = 4 * rows
    gains = jnp.stack([attn_gain, mlp_gain], 1)
    lanes = np.arange(128)
    freqs = np.zeros((8, 128), np.float32)
    freqs[0] = np.float32(ROPE_BASE) ** (-2.0 * (lanes % 32).astype(np.float32) / HEAD_DIM)
    freqs[1] = np.where(lanes % 64 < 32, -1.0, 1.0)
    (normed_one_all, cot_all, proj_w, gu_w, down_w, out_w, q_all, kv_all, attended_low, lse, cosines, sines, bias_all, middle, two_all) = (
        forward_attention(tokens, cotangent, positions[None], freqs, gains, attn_in, mlp_in, mlp_down, attn_out, 0)
    )
    branch_all, grad_middle, gu_a, gu_b, sum_down, out_part = feed_forward(
        two_all, cot_all, gu_w, down_w, middle, cotangent, 1
    )
    outputs, input_grad, own_proj, own_gu, own_down, own_out = backward_attention(
        gu_a, gu_b, sum_down, out_part, branch_all, grad_middle, middle, tokens,
        cosines, sines, bias_all, q_all, kv_all.reshape(2 * count, 128), attended_low, lse, normed_one_all, proj_w, out_w, 2,
    )
    grad_in, grad_mlp, grad_down, grad_out, grad_gains = own_rows(
        gains, attn_in, mlp_in, own_proj, own_gu, own_down, own_out
    )
    return outputs, input_grad, grad_in, grad_out, grad_gains[0], grad_mlp, grad_down, grad_gains[1]


def solution(mesh):
    both = ("dp", "ctx")
    wide, flat = P(both, None), P(both)
    in_specs = (wide, flat, wide, wide, flat, wide, wide, flat, wide)
    out_specs = (wide, wide, wide, wide, flat, wide, wide, flat)
    return jax.shard_map(shards, mesh=mesh, in_specs=in_specs, out_specs=out_specs, check_vma=False)
```

```python
import jax
import jax.numpy as jnp
import numpy as np
from jax import lax
from jax.experimental import pallas as pl
from jax.experimental.pallas import tpu as pltpu
from jax.sharding import PartitionSpec as P


D = 2048
HEADS = 32
KV_HEADS = 4
HEAD_DIM = 64
FF = 5632
REPEAT = HEADS // KV_HEADS
TP = 4
Q_COLS = D // TP
PROJ = Q_COLS + 2 * HEAD_DIM
HID = FF // TP

EPS = 1e-05
ROPE_BASE = 10000.0
NEG_FILL = -1e30

MESH = pl.DeviceIdType.MESH
BF16 = jnp.bfloat16
F32 = jnp.float32

SPLITS = ((PROJ, 384), (2 * HID, 13 * 128), (HID, 640))
OUT_SPLIT = 1024
VMEM_LIMIT = 60 << 20

NN = ((1,), (0,))
NT = ((1,), (1,))
TN = ((0,), (0,))


def place():
    dp, ctx = lax.axis_index("dp"), lax.axis_index("ctx")
    return (dp // 2) % 2, ctx // 4, ctx % 4, dp // 4, dp % 2


def device(xh, xl, y, z, c):
    return (z * 4 + xh * 2 + c, xl * 4 + y)


def along_y(d):
    def to(xh, xl, y, z, c):
        return xh, xl, (y + d) % 4, z, c

    return to


def along_x(d):
    def to(xh, xl, y, z, c):
        x = (xh * 2 + xl + d) % 4
        return x // 2, x % 2, y, z, c

    return to


def along_z(d):
    def to(xh, xl, y, z, c):
        return xh, xl, y, (z + d) % 4, c

    return to


def sibling(xh, xl, y, z, c):
    return xh, xl, y, z, 1 - c


def half_partner(xh, xl, y, z, c):
    return xh, 1 - xl, y, z, c


def crossed(xh, xl, y, z, c):
    return xh, xl, z, y, c


def say_hello(routes, cross=False):
    here = place()
    barrier = pltpu.get_barrier_semaphore()
    for back in routes:
        pl.semaphore_signal(barrier, inc=1, device_id=device(*back(*here)), device_id_type=MESH)
    if cross:

        @pl.when(here[2] != here[3])
        def _():
            pl.semaphore_signal(barrier, inc=1, device_id=device(*crossed(*here)), device_id_type=MESH)


def meet(routes, cross=False):
    here = place()
    barrier = pltpu.get_barrier_semaphore()
    if not cross:
        pl.semaphore_wait(barrier, len(routes))
        return
    away = here[2] != here[3]

    @pl.when(away)
    def _():
        pl.semaphore_wait(barrier, len(routes) + 1)

    @pl.when(jnp.logical_not(away))
    def _():
        pl.semaphore_wait(barrier, len(routes))


ALL_LINES = [along(d) for along in (along_y, along_x, along_z) for d in (1, 2, 3)] + [sibling]


class Copies:
    def __init__(self, send, recv):
        self.send, self.recv, self.count = send, recv, 0

    def __call__(self, src, dst, to):
        k, self.count = self.count, self.count + 1
        return pltpu.make_async_remote_copy(
            src_ref=src,
            dst_ref=dst,
            send_sem=self.send.at[k],
            recv_sem=self.recv.at[k],
            device_id=device(*to(*place())),
            device_id_type=MESH,
        )


def comm_call(kernel, name, ident, ins, outs, copies, locals_=0):
    return pl.pallas_call(
        kernel,
        out_shape=outs,
        in_specs=[pl.BlockSpec(memory_space=pl.ANY)] * len(ins),
        out_specs=[pl.BlockSpec(memory_space=pl.ANY)] * len(outs),
        scratch_shapes=[
            pltpu.SemaphoreType.DMA((copies,)),
            pltpu.SemaphoreType.DMA((copies,)),
            pltpu.SemaphoreType.DMA((max(locals_, 1),)),
        ],
        name=name,
        compiler_params=pltpu.CompilerParams(collective_id=ident, has_side_effects=True),
    )(*ins)


def struct(shape, dtype=BF16):
    return jax.ShapeDtypeStruct(shape, dtype)


class RingGather:
    def __init__(self, copy, own, dst, y):
        half = dst.shape[2] // 2
        lo, hi = pl.ds(0, half), pl.ds(half, half)
        back, on = (y + 3) % 4, (y + 1) % 4

        def first(cols, to):
            return copy(own.at[:, cols], dst.at[y, :, cols], to)

        def one(slot, cols, to):
            at = dst.at[slot, :, cols]
            return copy(at, at, to)

        self.first = [first(lo, along_y(1)), first(hi, along_y(3)), first(hi, along_y(1)), first(lo, along_y(3))]
        self.second = [one(back, lo, along_y(1)), one(on, hi, along_y(3))]

    def start(self):
        for cp in self.first:
            cp.start()

    def turn(self):
        for got, cp in zip(self.first, self.second):
            got.wait_recv()
            cp.start()

    def near(self):
        for cp in self.first[2:]:
            cp.wait_recv()

    def far(self):
        for cp in self.second:
            cp.wait_recv()

    def sent(self):
        for cp in self.first + self.second:
            cp.wait_send()


class RingSum:
    def __init__(self, copy, part, halves, whole, y):
        half = part.shape[2] // 2
        lo, hi = pl.ds(0, half), pl.ds(half, half)
        self.part, self.halves, self.whole, self.y = part, halves, whole, y
        self.cols = (lo, hi)
        far, on, back = (y + 2) % 4, (y + 1) % 4, (y + 3) % 4
        self.far = [
            copy(part.at[far, :, lo], halves.at[0], along_y(1)),
            copy(part.at[far, :, hi], halves.at[1], along_y(3)),
        ]
        self.near = [
            copy(part.at[on, :, hi], whole.at[0, :, hi], along_y(1)),
            copy(part.at[back, :, lo], whole.at[1, :, lo], along_y(3)),
        ]
        self.last = [
            copy(part.at[on, :, lo], whole.at[0, :, lo], along_y(1)),
            copy(part.at[back, :, hi], whole.at[1, :, hi], along_y(3)),
        ]
        self.slots = (on, back)

    def start(self):
        for cp in self.far + self.near:
            cp.start()

    def turn(self):
        for k in range(2):
            self.far[k].wait_recv()
            slot, cols = self.slots[k], self.cols[k]

            def body(r, _, slot=slot, cols=cols, k=k):
                rows = pl.ds(r * 32, 32)
                both = self.part[slot, rows, cols].astype(F32) + self.halves[k, rows].astype(F32)
                self.part[slot, rows, cols] = both.astype(BF16)
                return 0

            lax.fori_loop(0, self.part.shape[1] // 32, body, 0)
            self.last[k].start()

    def finish(self):
        for cp in self.near + self.last:
            cp.wait_recv()

    def rows(self, rows):
        own = self.part[self.y, rows].astype(F32)
        return own + self.whole[0, rows].astype(F32) + self.whole[1, rows].astype(F32)

    def sent(self):
        for cp in self.far + self.near + self.last:
            cp.wait_send()


class Gather:
    def __init__(self, copy, out, a, at, rows_only=False):
        xh, xl, y, z, c = at
        cols = out.shape[-1]
        left, right = pl.ds(0, a), pl.ds(a, cols - a)
        def cut(half, n):
            return slice(None) if half is None else pl.ds(half * (n // 2), n // 2)

        if rows_only:
            block = lambda z, x, c, cols: out.at[x[0], c, x[1], z, :, cols]
            z_line = lambda x, c, cols, half: out.at[x[0], c, x[1], cut(half, 4), :, cols]
            x_line = lambda z, c, cols, half: out.at[cut(half, 2), c, :, z, :, cols]
        else:
            block = lambda z, x, c, cols: out.at[z, x[0], c, pl.ds(x[1] * 64, 64), cols]
            z_line = lambda x, c, cols, half: out.at[cut(half, 4), x[0], c, pl.ds(x[1] * 64, 64), cols]
            x_line = lambda z, c, cols, half: out.at[z, cut(half, 2), c, :, cols]

        def same(ref, to):
            return copy(ref, ref, to)

        here = (xh, xl)
        self.first = []
        for d in (1, 3, 2):
            self.first.append(same(block(z, here, c, left), along_x(d)))
            self.first.append(same(block(z, here, c, right), along_z(d)))
        a_lo, a_hi = lambda z: x_line(z, c, left, 0), lambda z: x_line(z, c, left, 1)
        b_lo, b_hi = lambda x: z_line(x, c, right, 0), lambda x: z_line(x, c, right, 1)
        z_at = [(z + d) % 4 for d in range(4)]
        x_at = [along_x(d)(*at)[:2] for d in range(4)]
        self.lines = []
        for lo, hi, spots, along in ((a_lo, a_hi, z_at, along_z), (b_lo, b_hi, x_at, along_x)):
            going = [
                same(lo(spots[0]), along(1)),
                same(hi(spots[0]), along(3)),
                same(hi(spots[0]), along(1)),
                same(lo(spots[0]), along(3)),
            ]
            on = [same(lo(spots[3]), along(1)), same(hi(spots[1]), along(3))]
            self.lines.append((going, on))
        self.core = [same(block(z, here, c, pl.ds(0, cols)), sibling)]
        for d in (1, 3, 2):
            self.core.append(same(block(z, x_at[d], c, left), sibling))
            self.core.append(same(block(z_at[d], here, c, right), sibling))
        self.core_lines = []
        for d in (3, 1, 2):
            self.core_lines.append(
                (same(x_line(z_at[d], c, left, None), sibling), same(z_line(x_at[d], c, right, None), sibling))
            )

    def start(self):
        for cp in self.first:
            cp.start()
        self.core[0].start()

    def turn(self, *which):
        for k in which or (0, 1):
            for cp in self.first[k::2]:
                cp.wait_recv()
            for cp in self.lines[k][0]:
                cp.start()
            for cp in self.core[1 + k :: 2]:
                cp.start()

    def pass_on(self):
        for going, on in self.lines:
            for got, cp in zip(going[:2], on):
                got.wait_recv()
                cp.start()

    def near(self):
        for k, (going, _) in enumerate(self.lines):
            for side in range(2):
                going[2 + side].wait_recv()
                self.core_lines[side][k].start()

    def far(self):
        for k, (_, on) in enumerate(self.lines):
            for cp in on:
                cp.wait_recv()
            self.core_lines[2][k].start()

    def finish(self):
        for cp in self.core + [cp for pair in self.core_lines for cp in pair]:
            cp.wait_recv()

    def sent(self):
        for going, on in self.lines:
            for cp in going + on:
                cp.wait_send()
        for cp in self.first + self.core + [cp for pair in self.core_lines for cp in pair]:
            cp.wait_send()


def dot(left, right, dims=((1,), (0,))):
    return lax.dot_general(left, right, (dims, ((), ())), preferred_element_type=F32)


def column(row_ref):
    row = jnp.broadcast_to(row_ref[...].astype(F32), (16, 16))
    diagonal = lax.broadcasted_iota(jnp.int32, (16, 16), 0) == lax.broadcasted_iota(jnp.int32, (16, 16), 1)
    return jnp.sum(jnp.where(diagonal, row, 0.0), 1, keepdims=True)


def swap_halves(v):
    lane = lax.broadcasted_iota(jnp.int32, v.shape, 1)
    return jnp.where(lane % 64 < 32, pltpu.roll(v, 96, 1), pltpu.roll(v, 32, 1))


def forward_attention(tokens, cotangent, positions, freqs, attn_gain, mlp_gain, attn_in, mlp_in, mlp_down, out_rows, ident):
    rows = tokens.shape[0]
    count = 4 * rows

    def kernel(
        tok_ref, cot_ref, spot_ref, freq_ref, one_ref, two_ref, in_ref, mlp_ref, down_ref, wo,
        normed_out, cot_all, gp, gg, gd, go, q_out, kv_out, att_out, lse_out, cos_out, sin_out, bias_out, middle_out, two_all,
        wp, wg, wd, tok, normed, wp_v, wo_v, q_s, kv, vx, bias, att, part, halves, whole, spot_all, own_two, cos_s, sin_s, bias_t, send, recv, local,
    ):
        say_hello(ALL_LINES, True)
        at = place()
        xh, xl, y, z, c = at
        copy = Copies(send, recv)
        slot = pl.ds(xl * 64 + y * 16, 16)
        nlocal = [0]

        def near(src, dst):
            cp = pltpu.make_async_copy(src, dst, local.at[nlocal[0]])
            nlocal[0] += 1
            return cp

        to_y = []
        stay = []
        for i, o in ((wp, gp), (wg, gg), (wd, gd)):
            to_y.append([copy(i.at[(y + d) % 4], o.at[z, xh, c, slot], along_y(d)) for d in (1, 3, 2)])
            stay.append(near(i.at[y], o.at[z, xh, c, slot]))
        over = copy(wo, go.at[xh, c, xl, y], crossed)
        keep = near(wo, go.at[xh, c, xl, z])
        spot_copies = [copy(spot_all.at[y], spot_all.at[y], along_y(d)) for d in (1, 3, 2)]
        tok_ring = RingGather(copy, tok_ref, tok, y)
        cot_ring = RingGather(copy, cot_ref, cot_all, y)
        row_halves = [pl.ds(0, rows // 2), pl.ds(rows // 2, rows // 2)]
        two_rings = [RingGather(copy, own_two.at[r], two_all.at[:, r], y) for r in row_halves]
        branches = [RingSum(copy, part.at[:, r], halves.at[:, r], whole.at[:, r], y) for r in row_halves]
        kv_copy = copy(kv.at[1], kv.at[0], half_partner)
        g_proj = Gather(copy, gp, SPLITS[0][1], at)
        g_gu = Gather(copy, gg, SPLITS[1][1], at)
        g_down = Gather(copy, gd, SPLITS[2][1], at)
        g_out = Gather(copy, go, OUT_SPLIT, at, True)

        cot_own = near(cot_ref, cot_all.at[y])
        tok_own = near(tok_ref, tok.at[y])
        tok_own.start()
        cot_own.start()
        spot_all[y] = jnp.broadcast_to(spot_ref[...].astype(F32), (8, rows))

        gain_one, gain_two = column(one_ref), column(two_ref)
        low_lanes = lax.broadcasted_iota(jnp.int32, (16, 128), 1) < 64
        for k in range(TP):
            qs = pl.ds(k * Q_COLS, Q_COLS)
            wp[k, :, pl.ds(0, Q_COLS)] = (in_ref[:, qs].astype(F32) * gain_one).astype(BF16)
            key = in_ref[:, pl.ds(D + (k // 2) * 128, 128)].astype(F32)
            value = in_ref[:, pl.ds(D + HEAD_DIM * KV_HEADS + (k // 2) * 128, 128)].astype(F32)
            if k % 2 == 0:
                both = jnp.where(low_lanes, key, pltpu.roll(value, 64, 1))
            else:
                both = jnp.where(low_lanes, pltpu.roll(key, 64, 1), value)
            wp[k, :, pl.ds(Q_COLS, 128)] = (both * gain_one).astype(BF16)
        stay[0].start()
        for k in range(TP):
            for j in range(HID // 128):
                for half in range(2):
                    cols = pl.ds(half * FF + k * HID + j * 128, 128)
                    tile = (mlp_ref[:, cols].astype(F32) * gain_two).astype(BF16)
                    wg[k, :, pl.ds(j * 256 + half * 128, 128)] = tile
            wd[k] = down_ref[:, pl.ds(k * HID, HID)]
        for cp in stay[1:]:
            cp.start()
        meet(ALL_LINES, True)
        away = y != z
        for cp in to_y[0]:
            cp.start()

        @pl.when(away)
        def _():
            over.start()

        @pl.when(jnp.logical_not(away))
        def _():
            keep.start()

        for cp in spot_copies + to_y[1] + to_y[2] + tok_ring.first:
            cp.start()

        def norm_block(k):
            def body(r, _):
                rs = pl.ds(r * 32, 32)
                v = tok[k, rs].astype(F32)
                inv = lax.rsqrt(jnp.mean(v * v, -1, keepdims=True) + EPS)
                normed[k, rs] = (v * inv).astype(BF16)
                return 0

            lax.fori_loop(0, rows // 32, body, 0)

        stay[0].wait()
        for cp in to_y[0]:
            cp.wait_recv()
        g_proj.start()

        @pl.when(away)
        def _():
            over.wait()

        @pl.when(jnp.logical_not(away))
        def _():
            keep.wait()

        g_out.start()
        tok_own.wait()
        norm_block(y)
        g_proj.turn()
        stay[1].wait()
        for cp in to_y[1]:
            cp.wait_recv()
        g_gu.start()
        g_proj.pass_on()
        stay[2].wait()
        for cp in to_y[2]:
            cp.wait_recv()
        g_down.start()
        g_out.turn()
        for cp in spot_copies:
            cp.wait_recv()
        tok_ring.turn()
        g_proj.near()
        g_proj.far()

        cos, sin = [], []
        freq, sign = freq_ref[0:1, :], freq_ref[1:2, :]
        spot_cols = []
        for k in range(4):
            col = jnp.transpose(jnp.broadcast_to(spot_all[k, 0:1, :], (128, 128)))
            spot_cols.append(col)
            cos.append(jnp.cos(col * freq))
            sin.append(jnp.sin(col * freq) * sign)
        cos, sin = jnp.concatenate(cos, 0), jnp.concatenate(sin, 0)
        cos_s[...] = cos
        sin_s[...] = sin
        turn_saves = [near(cos_s, cos_out), near(sin_s, sin_out)]
        for cp in turn_saves:
            cp.start()
        low_half = xl == 0
        reach = jnp.where(low_half, -1.0, 2048.0)
        for k in range(4):
            for j in range(8):
                row = lax.broadcasted_iota(jnp.int32, (128, 128), 0) + k * 128
                col = lax.broadcasted_iota(jnp.int32, (128, 128), 1) + j * 128
                apart = (row - col + 512).astype(F32)
                seen = apart <= spot_cols[k]
                if j < 4:
                    seen = seen & (apart <= reach)
                else:
                    seen = seen & (col - 512 <= row)
                bias[pl.ds(k * 128, 128), pl.ds(j * 128, 128)] = jnp.where(seen, 0.0, NEG_FILL)

        g_proj.finish()
        wp_load = near(gp, wp_v)
        wp_load.start()
        g_out.pass_on()
        tok_ring.near()
        norm_block((y + 3) % 4)
        norm_block((y + 1) % 4)
        g_out.near()
        tok_ring.far()
        cot_ring.start()
        norm_block((y + 2) % 4)
        normed_save = near(normed, normed_out)
        normed_save.start()

        g_gu.turn(0)
        g_down.turn(0)

        wp_load.wait()
        left = normed[...].reshape(count, D)
        lane = lax.broadcasted_iota(jnp.int32, (count, 128), 1)
        upper = lane >= 64
        raw = dot(left, wp_v[:, :, :, :, pl.ds(Q_COLS, 128)].reshape(D, 128))
        turned = raw * jnp.where(upper, 1.0, cos) + swap_halves(raw) * jnp.where(upper, 0.0, sin)
        kv[1] = turned.astype(BF16)
        kv_copy.start()
        g_out.far()
        g_gu.turn(1)
        g_down.turn(1)
        for j in range(2):
            raw2 = dot(left, wp_v[:, :, :, :, pl.ds(j * 256, 256)].reshape(D, 256))
            for e in range(2):
                raw = raw2[:, e * 128 : e * 128 + 128]
                turned = (raw * cos + swap_halves(raw) * sin).astype(BF16).astype(F32) * (HEAD_DIM ** (-0.5))
                pair = j * 2 + e
                q_s[2 * pair] = jnp.where(upper, 0.0, turned).astype(BF16)
                q_s[2 * pair + 1] = jnp.where(upper, 0.0, pltpu.roll(turned, 64, 1)).astype(BF16)
        kv_copy.wait_recv()
        for k in range(2):
            vx[k] = jnp.where(upper, kv[k].astype(F32), 1.0).astype(BF16)
        q_save = near(q_s, q_out)
        q_save.start()
        kv_save = near(kv, kv_out)
        kv_save.start()
        g_out.finish()
        wo_load = near(go, wo_v)
        wo_load.start()

        def attend(pair):
            for b in range(2):
                rs = pl.ds(b * 256, 256)
                seen = 256 * (b + 1)
                lane = lax.broadcasted_iota(jnp.int32, (256, 128), 1) < 64
                found = []
                for e in range(2):
                    q = q_s[2 * pair + e, rs]
                    s0 = dot(q, kv[0], NT) + bias[rs, pl.ds(0, 512)]
                    s1 = dot(q, kv[1, pl.ds(0, seen)], NT) + bias[rs, pl.ds(512, seen)]
                    m = jnp.maximum(jnp.max(s0, -1, keepdims=True), jnp.max(s1, -1, keepdims=True))
                    p0 = jnp.exp(s0 - m).astype(BF16)
                    p1 = jnp.exp(s1 - m).astype(BF16)
                    o = dot(p0, vx[0]) + dot(p1, vx[1, pl.ds(0, seen)])
                    r = pltpu.roll(o, 64, 1)
                    found.append((o, r))
                    log_total = m + jnp.log(jnp.where(lane, o, r))
                    lse_out[2 * pair + e, :, rs] = jnp.transpose(log_total)[0:8]
                (o, r), (o2, r2) = found
                both = jnp.where(lane, r / o, o2 / r2)
                att[rs, pl.ds(pl.multiple_of(pair * 128, 128), 128)] = both.astype(BF16)

        def two_pairs(k):
            def body(i, _):
                attend(2 * k + i)
                return 0

            lax.fori_loop(0, 2, body, 0)

        two_pairs(0)
        cot_ring.turn()
        two_pairs(1)
        att_save = near(att, att_out)
        att_save.start()
        wo_load.wait()

        for j in range(4):
            cols = pl.ds(j * 512, 512)
            w = wo_v[:, :, :, :, :, cols].reshape(Q_COLS, 512)
            part[:, :, cols] = dot(att[...], w).astype(BF16).reshape(4, rows, 512)
        for branch in branches:
            branch.start()

        for k in range(4):
            for j in range(8):
                key = lax.broadcasted_iota(jnp.int32, (128, 128), 0) + j * 128
                row = lax.broadcasted_iota(jnp.int32, (128, 128), 1) + k * 128
                apart = (row - key + 512).astype(F32)
                seen = apart <= spot_all[k, 0:1, :]
                if j < 4:
                    seen = seen & (apart <= reach)
                else:
                    seen = seen & (key - 512 <= row)
                bias_t[pl.ds(j * 128, 128), pl.ds(k * 128, 128)] = jnp.where(seen, 0.0, NEG_FILL)
        bias_save = near(bias_t, bias_out)
        bias_save.start()
        g_gu.pass_on()
        g_down.pass_on()
        for branch in branches:
            branch.turn()
        g_gu.near()
        g_down.near()
        cot_ring.near()
        cot_ring.far()
        two_own = near(own_two, two_all.at[y])
        for k in range(2):
            branches[k].finish()

            def mid(r, _, k=k):
                rs, half = pl.ds(k * (rows // 2) + r * 32, 32), pl.ds(r * 32, 32)
                v = tok_ref[rs].astype(F32) + branches[k].rows(half)
                middle_out[rs] = v
                inv = lax.rsqrt(jnp.mean(v * v, -1, keepdims=True) + EPS)
                own_two[rs] = (v * inv).astype(BF16)
                return 0

            lax.fori_loop(0, rows // 64, mid, 0)
            two_rings[k].start()
        two_own.start()
        for ring in two_rings:
            ring.turn()
        g_gu.far()
        g_down.far()
        for ring in two_rings:
            ring.near()
            ring.far()
        g_gu.finish()
        g_down.finish()
        for cp in (cot_own, normed_save, q_save, kv_save, att_save, two_own, bias_save, *turn_saves):
            cp.wait()
        for group in to_y:
            for cp in group:
                cp.wait_send()
        for cp in spot_copies + [kv_copy]:
            cp.wait_send()
        for thing in (g_proj, g_out, g_gu, g_down, tok_ring, cot_ring, *two_rings, *branches):
            thing.sent()

    anywhere, vmem = pl.BlockSpec(memory_space=pl.ANY), pl.BlockSpec(memory_space=pltpu.VMEM)
    outs = [
        (struct((4, rows, D)), anywhere),
        (struct((4, rows, D)), anywhere),
        (struct((4, 2, 2, 128, PROJ)), anywhere),
        (struct((4, 2, 2, 128, 2 * HID)), anywhere),
        (struct((4, 2, 2, 128, HID)), anywhere),
        (struct((2, 2, 2, 4, 16, D)), anywhere),
        (struct((REPEAT, count, 128)), anywhere),
        (struct((2, count, 128)), anywhere),
        (struct((count, Q_COLS)), anywhere),
        (struct((REPEAT, 8, count), F32), vmem),
        (struct((count, 128), F32), anywhere),
        (struct((count, 128), F32), anywhere),
        (struct((2 * count, count), F32), anywhere),
        (struct((rows, D), F32), vmem),
        (struct((4, rows, D)), anywhere),
    ]
    copies = 9 + 1 + 3 + 6 * 6 + 1 + 31 * 4
    return pl.pallas_call(
        kernel,
        out_shape=[o[0] for o in outs],
        in_specs=[vmem] * 10,
        out_specs=[o[1] for o in outs],
        scratch_shapes=[
            pltpu.VMEM((TP, 16, PROJ), BF16),
            pltpu.VMEM((TP, 16, 2 * HID), BF16),
            pltpu.VMEM((TP, 16, HID), BF16),
            pltpu.VMEM((4, rows, D), BF16),
            pltpu.VMEM((4, rows, D), BF16),
            pltpu.VMEM((4, 2, 2, 128, PROJ), BF16),
            pltpu.VMEM((2, 2, 2, 4, 16, D), BF16),
            pltpu.VMEM((REPEAT, count, 128), BF16),
            pltpu.VMEM((2, count, 128), BF16),
            pltpu.VMEM((2, count, 128), BF16),
            pltpu.VMEM((count, 2 * count), F32),
            pltpu.VMEM((count, Q_COLS), BF16),
            pltpu.VMEM((4, rows, D), BF16),
            pltpu.VMEM((2, rows, D // 2), BF16),
            pltpu.VMEM((2, rows, D), BF16),
            pltpu.VMEM((4, 8, 128), F32),
            pltpu.VMEM((rows, D), BF16),
            pltpu.VMEM((count, 128), F32),
            pltpu.VMEM((count, 128), F32),
            pltpu.VMEM((2 * count, count), F32),
            pltpu.SemaphoreType.DMA((copies,)),
            pltpu.SemaphoreType.DMA((copies,)),
            pltpu.SemaphoreType.DMA((20,)),
        ],
        name="forward_attention",
        compiler_params=pltpu.CompilerParams(
            collective_id=ident, has_side_effects=True, vmem_limit_bytes=VMEM_LIMIT
        ),
    )(tokens, cotangent, positions, freqs, attn_gain, mlp_gain, attn_in, mlp_in, mlp_down, out_rows)


def tiles(ref):
    if len(ref.shape) == 2:
        return [ref]
    return [t for k in range(ref.shape[0]) for t in tiles(ref.at[k])]


def add_up(dst, *others):
    for out, *terms in zip(tiles(dst), *[tiles(o) for o in others]):
        rows = out.shape[0]
        step = min(rows, 32)

        def body(r, _, out=out, terms=terms, step=step):
            rs = pl.ds(r * step, step)
            value = out[rs].astype(F32)
            for t in terms:
                value = value + t[rs].astype(F32)
            out[rs] = value.astype(BF16)
            return 0

        lax.fori_loop(0, rows // step, body, 0)


class LineSum:
    def __init__(self, copy, lo, hi, along, far, near):
        self.lo, self.hi, self.far_in, self.near_in = lo, hi, far, near
        self.far = [copy(lo(2), far.at[0], along(1)), copy(hi(2), far.at[1], along(3))]
        self.near = [copy(hi(1), near.at[0, 1], along(1)), copy(lo(3), near.at[1, 0], along(3))]
        self.last = [copy(lo(1), near.at[0, 0], along(1)), copy(hi(3), near.at[1, 1], along(3))]

    def start(self):
        for cp in self.far + self.near:
            cp.start()

    def turn(self):
        self.far[0].wait_recv()
        add_up(self.lo(1), self.far_in.at[0])
        self.last[0].start()
        self.far[1].wait_recv()
        add_up(self.hi(3), self.far_in.at[1])
        self.last[1].start()

    def finish(self):
        for cp in self.near + self.last:
            cp.wait_recv()
        add_up(self.lo(0), self.near_in.at[0, 0], self.near_in.at[1, 0])
        add_up(self.hi(0), self.near_in.at[0, 1], self.near_in.at[1, 1])

    def sent(self):
        for cp in self.far + self.near + self.last:
            cp.wait_send()


class GradLines:
    def __init__(self, copy, terms, a, at, buffers, rows_only=False):
        xh, xl, y, z, c = at
        far_a, near_a, far_b, near_b = buffers
        cols = terms.shape[-1]
        left, right = pl.ds(0, a), pl.ds(a, cols - a)
        x_at = [along_x(d)(*at)[:2] for d in range(4)]
        z_at = [(z + d) % 4 for d in range(4)]
        if rows_only:
            spot = lambda x, z, cols: terms.at[x[0], c, x[1], z, :, cols]
            a_half = lambda h: lambda d: terms.at[h, c, :, z_at[d], :, left]
            b_half = lambda h: lambda d: terms.at[x_at[d][0], c, x_at[d][1], pl.ds(2 * h, 2), :, right]
        else:
            base = (lambda z, xh: (z, xh, c)) if len(terms.shape) == 5 else (lambda z, xh: (z, xh))
            spot = lambda x, z, cols: terms.at[base(z, x[0]) + (pl.ds(x[1] * 64, 64), cols)]
            a_half = lambda h: lambda d: terms.at[base(z_at[d], h) + (slice(None), left)]
            b_half = lambda h: lambda d: terms.at[
                base(pl.ds(2 * h, 2), x_at[d][0]) + (pl.ds(x_at[d][1] * 64, 64), right)
            ]
        self.lines = [
            LineSum(copy, a_half(0), a_half(1), along_z, far_a, near_a),
            LineSum(copy, b_half(0), b_half(1), along_x, far_b, near_b),
        ]
        self.spot_a = lambda x: spot(x, z, left)
        self.spot_b = lambda z: spot(x_at[0], z, right)

    def start(self):
        for line in self.lines:
            line.start()

    def turn(self):
        for line in self.lines:
            line.turn()

    def finish(self):
        for line in self.lines:
            line.finish()

    def sent(self):
        for line in self.lines:
            line.sent()


class GradOwners:
    def __init__(self, copy, local_copy, spot_a, spot_b, out, at, buffers, rows_only=False):
        xh, xl, y, z, c = at
        self.at, self.rows_only = at, rows_only
        got_a, got_b, own = buffers
        a, cols = got_a.shape[-1], own.shape[-1]
        self.second = []
        for d in (1, 3, 2):
            self.second.append(copy(spot_a(along_x(d)(*at)[:2]), got_a.at[d - 1], along_x(d)))
            self.second.append(copy(spot_b((z + d) % 4), got_b.at[d - 1], along_z(d)))
        self.mine = (spot_a((xh, xl)), spot_b(z))
        self.got = (got_a, got_b)
        self.own, self.cuts = own, (pl.ds(0, a), pl.ds(a, cols - a))
        if rows_only:
            self.over = copy(own, out, crossed)
            self.keep = local_copy(own, out)
        else:
            self.to_y = [copy(own.at[(y + d) % 4], out.at[y], along_y(d)) for d in (1, 3, 2)]
            self.keep = local_copy(own.at[y], out.at[y])

    def start(self):
        for cp in self.second:
            cp.start()

    def deliver(self):
        for cp in self.second:
            cp.wait_recv()
        for mine, got, cut in zip(self.mine, self.got, self.cuts):
            value = mine[...].astype(F32)
            for d in range(3):
                value = value + got[d].astype(F32)
            own = self.own
            if self.rows_only:
                own[:, cut] = value.astype(BF16)
            else:
                own[:, :, cut] = value.astype(BF16).reshape(4, 16, value.shape[-1])
        if self.rows_only:
            y, z = self.at[2], self.at[3]

            @pl.when(y != z)
            def _():
                self.over.start()

            @pl.when(y == z)
            def _():
                self.keep.start()

        else:
            for cp in self.to_y:
                cp.start()
            self.keep.start()

    def finish(self):
        if self.rows_only:
            y, z = self.at[2], self.at[3]

            @pl.when(y != z)
            def _():
                self.over.wait()

            @pl.when(y == z)
            def _():
                self.keep.wait()

        else:
            for cp in self.to_y:
                cp.wait()
            self.keep.wait()
        for cp in self.second:
            cp.wait_send()


def line_buffers(cols, a, rows_only=False):
    b = cols - a
    a_half, b_half = ((2, 16), (2, 16)) if rows_only else ((128,), (2, 64))
    return [
        pltpu.VMEM((2,) + a_half + (a,), BF16),
        pltpu.VMEM((2, 2) + a_half + (a,), BF16),
        pltpu.VMEM((2,) + b_half + (b,), BF16),
        pltpu.VMEM((2, 2) + b_half + (b,), BF16),
    ]


def owner_buffers(cols, a, rows_only=False):
    spot, own = (16, (16, cols)) if rows_only else (64, (4, 16, cols))
    return [pltpu.VMEM((3, spot, a), BF16), pltpu.VMEM((3, spot, cols - a), BF16), pltpu.VMEM(own, BF16)]


def backward_attention(
    gu_a, gu_b, sum_down, out_part, branch_all, grad_middle, middle, tokens,
    cosines, sines, bias_all, q_all, kv_all, attended, lse, normed_all, proj_w, out_w, ident,
):
    rows = tokens.shape[0]
    count = 4 * rows
    scale = HEAD_DIM ** (-0.5)

    def kernel(
        gu_a_ref, gu_b_ref, s_down, op_ref, br_ref, gm_hbm, mid_hbm, tok_hbm,
        cos_ref, sin_ref, bias_ref, q_ref, kv_ref, att_ref, lse_ref, nm_ref, wp_ref, wo_ref,
        out_ref, ig_ref, o_proj, o_gu, o_down, o_out,
        gm_ref, mid_ref, tok_ref, v_gu_a, v_gu_b, v_down, part, part_in, halves, whole, halves2, whole2, br, q_s, do_s, kv, kvt, att, delta, bias, cos_s, sin_s,
        dkv, kv_send, kv_in, gp, normed, wp, wo, t_proj, rc_proj, t_out, rc_out, *rest,
    ):
        bufs, (send, recv, local) = rest[:24], rest[24:]
        say_hello(ALL_LINES, True)
        at = place()
        xh, xl, y, z, c = at
        copy = Copies(send, recv)
        nlocal = [0]

        def near(src, dst):
            cp = pltpu.make_async_copy(src, dst, local.at[nlocal[0]])
            nlocal[0] += 1
            return cp

        load_gu, load_gu_b, load_down = near(gu_a_ref, v_gu_a), near(gu_b_ref, v_gu_b), near(s_down, v_down)
        load_op, load_br, load_wo = near(op_ref, part), near(br_ref, br), near(wo_ref, wo)
        load_att, load_q = near(att_ref, att), near(q_ref, q_s)
        load_kv = near(kv_ref, kv)
        load_turns = [near(cos_ref, cos_s), near(sin_ref, sin_s), near(bias_ref, bias)]
        load_nm, load_wp = near(nm_ref, normed), near(wp_ref, wp)
        load_rows = [near(gm_hbm, gm_ref), near(mid_hbm, mid_ref), near(tok_hbm, tok_ref)]
        for cp in (load_br, load_wo, load_gu, load_gu_b, load_op, load_down, load_att, load_q, load_kv, *load_turns, load_nm, load_wp, *load_rows):
            cp.start()
        outs = RingSum(copy, part, halves, whole, y)
        ones = RingSum(copy, part_in, halves2, whole2, y)
        kv_copy = copy(kv_send, kv_in, half_partner)
        core_proj = [
            copy(t_proj.at[:, :, 1 - c, :, cols], rc_proj.at[:, :, :, cols], sibling)
            for cols in (pl.ds(0, Q_COLS), pl.ds(Q_COLS, 128))
        ]
        core_out = copy(t_out.at[:, 1 - c], rc_out, sibling)
        gu_owners = GradOwners(
            copy,
            near,
            lambda x: v_gu_a.at[x[0], pl.ds(x[1] * 64, 64)],
            lambda z: v_gu_b.at[z],
            o_gu,
            at,
            bufs[0:3],
        )
        down_lines = GradLines(copy, v_down, SPLITS[2][1], at, bufs[3:7])
        down_owners = GradOwners(copy, near, down_lines.spot_a, down_lines.spot_b, o_down, at, bufs[7:10])
        proj_lines = GradLines(copy, t_proj, SPLITS[0][1], at, bufs[10:14])
        proj_owners = GradOwners(copy, near, proj_lines.spot_a, proj_lines.spot_b, o_proj, at, bufs[14:17])
        out_lines = GradLines(copy, t_out, OUT_SPLIT, at, bufs[17:21], True)
        out_owners = GradOwners(copy, near, out_lines.spot_a, out_lines.spot_b, o_out, at, bufs[21:24], True)

        dkv[...] = jnp.zeros_like(dkv)

        meet(ALL_LINES, True)
        load_op.wait()
        outs.start()
        load_gu.wait()
        load_gu_b.wait()
        gu_owners.start()
        load_down.wait()
        down_lines.start()

        load_br.wait()
        load_wo.wait()
        load_att.wait()
        lane = lax.broadcasted_iota(jnp.int32, (count, 128), 1)
        for p in range(4):
            if p % 2 == 0:
                both = dot(br[...].reshape(count, D), wo[p // 2].reshape(256, D), NT).astype(BF16).astype(F32)
            low = both[:, p % 2 * 128 : p % 2 * 128 + 128]
            do_s[2 * p] = jnp.where(lane < 64, 0.0, pltpu.roll(low, 64, 1)).astype(BF16)
            do_s[2 * p + 1] = jnp.where(lane < 64, 0.0, low).astype(BF16)
            prod = jnp.transpose(low * att[:, pl.ds(p * 128, 128)].astype(F32))
            for e in range(2):
                total_row = jnp.sum(prod[e * 64 : e * 64 + 64], 0, keepdims=True)
                delta[2 * p + e] = jnp.broadcast_to(total_row, (8, count))
        outs.turn()

        for k in range(4):
            term = dot(att[:, pl.ds(k * 128, 128)], br[...].reshape(count, D), TN)
            t_out[k // 2, k % 2] = term.astype(BF16).reshape(2, 4, 16, D)
        core_out.start()
        load_q.wait()
        load_kv.wait()
        for k in range(2):
            turned = jnp.transpose(kv[pl.ds(k * count, count)].astype(F32)).astype(BF16)
            kvt[:, pl.ds(k * count, count)] = turned

        def backward(pair):
            for b in range(2):
                rs = pl.ds(b * 256, 256)
                seen = pl.ds(0, 512 + 256 * (b + 1))
                found = []
                for e in range(2):
                    h = 2 * pair + e
                    q, do = q_s[h, rs], do_s[h, rs]
                    st = dot(kv[seen], q, NT) + bias[seen, rs] - lse_ref[h, 0:1, rs]
                    p = jnp.exp(st)
                    dp = dot(kv[seen], do, NT)
                    ds = (p * (dp - delta[h, 0:1, rs])).astype(BF16)
                    dkv[seen] += dot(ds, q) + dot(p.astype(BF16), do)
                    found.append(dot(kvt[:, seen], ds)[0:64])
                both = jnp.transpose(jnp.concatenate(found, 0)) * scale
                both = both * cos_s[rs] - swap_halves(both) * sin_s[rs]
                gp[rs, pl.ds(pl.multiple_of(pair * 128, 128), 128)] = both.astype(BF16)

        def two_pairs(k):
            def body(i, _):
                backward(2 * k + i)
                return 0

            lax.fori_loop(0, 2, body, 0)

        for cp in load_turns:
            cp.wait()
        two_pairs(0)
        down_lines.turn()
        gu_owners.deliver()
        two_pairs(1)
        kv_send[...] = dkv[pl.ds(0, count)].astype(BF16)
        kv_copy.start()
        core_out.wait_recv()
        add_up(t_out.at[:, c], rc_out)
        out_lines.start()
        load_nm.wait()
        for k in range(4):
            left = normed[:, :, pl.ds(k * 512, 512)].reshape(count, 512)
            term = dot(left, gp[:, pl.ds(0, Q_COLS)], TN)
            t_proj[k, :, :, :, pl.ds(0, Q_COLS)] = term.astype(BF16).reshape(2, 2, 128, Q_COLS)
        core_proj[0].start()
        kv_copy.wait_recv()
        got = dkv[pl.ds(count, count)] + kv_in[...].astype(F32)
        back = got * cos_s[...] - swap_halves(got) * sin_s[...]
        gp[:, pl.ds(Q_COLS, 128)] = jnp.where(lane < 64, back, got).astype(BF16)
        for k in range(4):
            left = normed[:, :, pl.ds(k * 512, 512)].reshape(count, 512)
            term = dot(left, gp[:, pl.ds(Q_COLS, 128)], TN)
            t_proj[k, :, :, :, pl.ds(Q_COLS, 128)] = term.astype(BF16).reshape(2, 2, 128, 128)
        core_proj[1].start()

        load_wp.wait()
        for j in range(4):
            w = wp[j].reshape(512, PROJ)
            part_in[:, :, pl.ds(j * 512, 512)] = dot(gp[...], w, NT).astype(BF16).reshape(4, rows, 512)
        ones.start()
        for cp in core_proj:
            cp.wait_recv()
        for k in range(4):
            add_up(t_proj.at[k, :, c], rc_proj.at[k])
        proj_lines.start()
        out_lines.turn()
        ones.turn()
        proj_lines.turn()
        down_lines.finish()
        down_owners.start()
        out_lines.finish()
        out_owners.start()
        proj_lines.finish()
        proj_owners.start()
        down_owners.deliver()
        out_owners.deliver()
        proj_owners.deliver()
        outs.finish()

        for cp in load_rows:
            cp.wait()

        def finish_out(r, _):
            rs = pl.ds(r * 32, 32)
            out_ref[rs] = (mid_ref[rs] + outs.rows(rs)).astype(BF16)
            return 0

        lax.fori_loop(0, rows // 32, finish_out, 0)
        outs.sent()
        ones.finish()

        def finish_in(r, _):
            rs = pl.ds(r * 32, 32)
            v = tok_ref[rs].astype(F32)
            inv = lax.rsqrt(jnp.mean(v * v, -1, keepdims=True) + EPS)
            v = v * inv
            g = ones.rows(rs)
            ig_ref[rs] = gm_ref[rs] + inv * (g - v * jnp.mean(g * v, -1, keepdims=True))
            return 0

        lax.fori_loop(0, rows // 32, finish_in, 0)
        ones.sent()
        for cp in (kv_copy, *core_proj, core_out):
            cp.wait_send()
        for owners in (gu_owners, down_owners, out_owners, proj_owners):
            owners.finish()
        for lines in (down_lines, out_lines, proj_lines):
            lines.sent()

    anywhere, vmem = pl.BlockSpec(memory_space=pl.ANY), pl.BlockSpec(memory_space=pltpu.VMEM)
    in_specs = [anywhere] * 14 + [vmem] + [anywhere] * 3
    outs = [
        (struct((rows, D)), vmem),
        (struct((rows, D), F32), vmem),
        (struct((4, 16, PROJ)), anywhere),
        (struct((4, 16, 2 * HID)), anywhere),
        (struct((4, 16, HID)), anywhere),
        (struct((16, D)), anywhere),
    ]
    whole = lambda: [pltpu.VMEM((2, rows, D // 2), BF16), pltpu.VMEM((2, rows, D), BF16)]
    copies = 12 + 4 + 9 + 21 * 2 + 19
    return pl.pallas_call(
        kernel,
        out_shape=[o[0] for o in outs],
        in_specs=in_specs,
        out_specs=[o[1] for o in outs],
        scratch_shapes=[
            pltpu.VMEM((rows, D), F32),
            pltpu.VMEM((rows, D), F32),
            pltpu.VMEM((rows, D), BF16),
            pltpu.VMEM((2, 128, SPLITS[1][1]), BF16),
            pltpu.VMEM((4, 64, 2 * HID - SPLITS[1][1]), BF16),
            pltpu.VMEM((4, 2, 128, HID), BF16),
            pltpu.VMEM((4, rows, D), BF16),
            pltpu.VMEM((4, rows, D), BF16),
            *whole(),
            *whole(),
            pltpu.VMEM((4, rows, D), BF16),
            pltpu.VMEM((REPEAT, count, 128), BF16),
            pltpu.VMEM((REPEAT, count, 128), BF16),
            pltpu.VMEM((2 * count, 128), BF16),
            pltpu.VMEM((128, 2 * count), BF16),
            pltpu.VMEM((count, Q_COLS), BF16),
            pltpu.VMEM((REPEAT, 8, count), F32),
            pltpu.VMEM((2 * count, count), F32),
            pltpu.VMEM((count, 128), F32),
            pltpu.VMEM((count, 128), F32),
            pltpu.VMEM((2 * count, 128), F32),
            pltpu.VMEM((count, 128), BF16),
            pltpu.VMEM((count, 128), BF16),
            pltpu.VMEM((count, PROJ), BF16),
            pltpu.VMEM((4, rows, D), BF16),
            pltpu.VMEM((4, 2, 2, 128, PROJ), BF16),
            pltpu.VMEM((2, 2, 2, 4, 16, D), BF16),
            pltpu.VMEM((4, 2, 2, 128, PROJ), BF16),
            pltpu.VMEM((4, 2, 128, PROJ), BF16),
            pltpu.VMEM((2, 2, 2, 4, 16, D), BF16),
            pltpu.VMEM((2, 2, 4, 16, D), BF16),
            *owner_buffers(2 * HID, SPLITS[1][1]),
            *line_buffers(HID, SPLITS[2][1]),
            *owner_buffers(HID, SPLITS[2][1]),
            *line_buffers(PROJ, SPLITS[0][1]),
            *owner_buffers(PROJ, SPLITS[0][1]),
            *line_buffers(D, OUT_SPLIT, True),
            *owner_buffers(D, OUT_SPLIT, True),
            pltpu.SemaphoreType.DMA((copies,)),
            pltpu.SemaphoreType.DMA((copies,)),
            pltpu.SemaphoreType.DMA((24,)),
        ],
        name="backward_attention",
        compiler_params=pltpu.CompilerParams(
            collective_id=ident, has_side_effects=True, vmem_limit_bytes=VMEM_LIMIT
        ),
    )(
        gu_a, gu_b, sum_down, out_part, branch_all, grad_middle, middle, tokens,
        cosines, sines, bias_all, q_all, kv_all, attended, lse, normed_all, proj_w, out_w,
    )


def feed_forward(seq_two, seq_cot, gu_w, down_w, middle, cotangent, ident):
    rows = middle.shape[0]
    count = 4 * rows
    tiles_gu, pairs = HID // 128, HID // 256

    def kernel(
        two_ref, cot_ref, wg_ref, wd_ref, mid_hbm, own_cot_hbm,
        branch_all, gm_ref, gu_a, gu_b, s_down, op_out,
        part, halves, whole, two, gu, cot, hid, gh, turned, t_gu, t_down, rc_gu, rc_down, branch, op,
        mid_ref, own_cot,
        far_a, near_a, far_b, near_b, send, recv, local, weights,
    ):
        partners = [along_y(1), along_y(3), along_x(1), along_x(3), along_z(1), along_z(3), sibling]
        say_hello(partners)
        at = place()
        xh, xl, y, z, c = at
        copy = Copies(send, recv)
        nlocal = [0]

        def near(src, dst):
            cp = pltpu.make_async_copy(src, dst, local.at[nlocal[0]])
            nlocal[0] += 1
            return cp

        def load_gu(j):
            tile = pl.ds(pl.multiple_of(j * 256, 256), 256)
            return pltpu.make_async_copy(wg_ref.at[:, :, :, :, tile], t_gu.at[:, :, :, :, tile], weights.at[j])

        def load_down(j, width=256):
            tile = pl.ds(pl.multiple_of(j * 256, 256), width)
            return pltpu.make_async_copy(
                wd_ref.at[:, :, :, :, tile], t_down.at[:, :, :, :, tile], weights.at[tiles_gu + j]
            )

        load_cot, load_two = near(cot_ref, cot), near(two_ref, two)
        load_rows = [near(mid_hbm, mid_ref), near(own_cot_hbm, own_cot)]
        load_cot.start()
        last_down = load_down(pairs, HID - 256 * pairs)

        def begin_down(j, _):
            load_down(j).start()
            return 0

        def begin_gu(j, _):
            load_gu(j).start()
            return 0

        lax.fori_loop(0, pairs, begin_down, 0)
        last_down.start()
        load_two.start()
        lax.fori_loop(0, tiles_gu, begin_gu, 0)
        for cp in load_rows:
            cp.start()
        row_halves = [pl.ds(0, rows // 2), pl.ds(rows // 2, rows // 2)]
        rings = [RingSum(copy, part.at[:, r], halves.at[:, r], whole.at[:, r], y) for r in row_halves]
        gathers = [RingGather(copy, branch.at[r], branch_all.at[:, r], y) for r in row_halves]
        own = near(branch, branch_all.at[y])
        cores = [
            (copy(t_gu.at[k, :, 1 - c], rc_gu.at[k], sibling), copy(t_down.at[k, :, 1 - c], rc_down.at[k], sibling))
            for k in [(z + d) % 4 for d in range(4)]
        ]
        saves = [near(t_down.at[k, :, c], s_down.at[k]) for k in [(z + d) % 4 for d in range(4)]]
        lines = GradLines(copy, t_gu, SPLITS[1][1], at, (far_a, near_a, far_b, near_b))
        saves_gu = [
            near(t_gu.at[z, :, c, :, pl.ds(0, SPLITS[1][1])], gu_a),
            near(t_gu.at[:, xh, c, pl.ds(xl * 64, 64), pl.ds(SPLITS[1][1], 2 * HID - SPLITS[1][1])], gu_b),
        ]
        save_op = near(op, op_out)
        load_cot.wait()

        def hidden_back(j, _):
            load_down(j).wait()
            tile = pl.ds(pl.multiple_of(j * 256, 256), 256)
            gh[:, tile] = dot(cot[...].reshape(count, D), t_down[:, :, :, :, tile].reshape(D, 256))
            return 0

        lax.fori_loop(0, pairs, hidden_back, 0)
        last_down.wait()
        tile = pl.ds(256 * pairs, HID - 256 * pairs)
        gh[:, tile] = dot(cot[...].reshape(count, D), t_down[:, :, :, :, tile].reshape(D, HID - 256 * pairs))
        load_two.wait()

        def gate_up(j):
            load_gu(j).wait()
            both = pl.ds(pl.multiple_of(j * 256, 256), 256)
            return dot(two[...].reshape(count, D), t_gu[:, :, :, :, both].reshape(D, 256))

        def activate(j, act):
            both = pl.ds(pl.multiple_of(j * 256, 256), 256)
            one = pl.ds(pl.multiple_of(j * 128, 128), 128)
            gate, up = act[:, :128], act[:, 128:]
            back = gh[:, one]
            sigmoid = jax.nn.sigmoid(gate)
            silu = gate * sigmoid
            hid[:, one] = (silu * up).astype(BF16)
            grad_gate = back * up * sigmoid * (1.0 + gate * (1.0 - sigmoid))
            gu[:, both] = jnp.concatenate([grad_gate, back * silu], 1).astype(BF16)

        def hidden(j, _):
            activate(j, gate_up(j))
            return 0

        lax.fori_loop(0, tiles_gu, hidden, 0)

        def part_two(k, _):
            cols = pl.ds(pl.multiple_of(k * 512, 512), 512)
            part[:, :, cols] = dot(gu[...], t_gu[k].reshape(512, 2 * HID), NT).astype(BF16).reshape(4, rows, 512)
            return 0

        lax.fori_loop(0, 4, part_two, 0)
        meet(partners)
        for ring in rings:
            ring.start()

        def part_out(k, _):
            cols = pl.ds(pl.multiple_of(k * 512, 512), 512)
            op[:, :, cols] = dot(hid[...], t_down[k].reshape(512, HID), NT).astype(BF16).reshape(4, rows, 512)
            return 0

        def terms_gu(d):
            k = (z + d) % 4
            cols = pl.ds(pl.multiple_of(k * 512, 512), 512)
            turned[...] = jnp.transpose(two[:, :, cols].reshape(count, 512))

            def some(j, _):
                tile = pl.ds(pl.multiple_of(j * 256, 256), 256)
                t_gu[k, :, :, :, tile] = dot(turned[...], gu[:, tile]).astype(BF16).reshape(2, 2, 128, 256)
                return 0

            lax.fori_loop(0, 2 * HID // 256, some, 0)
            cores[d][0].start()

        def terms_down(d):
            k = (z + d) % 4
            cols = pl.ds(pl.multiple_of(k * 512, 512), 512)
            turned[...] = jnp.transpose(cot[:, :, cols].reshape(count, 512))

            def more(j, width=256):
                tile = pl.ds(pl.multiple_of(j * 256, 256), width)
                t_down[k, :, :, :, tile] = dot(turned[...], hid[:, tile]).astype(BF16).reshape(2, 2, 128, width)
                return 0

            lax.fori_loop(0, pairs, lambda j, _: more(j), 0)
            more(pairs, HID - 256 * pairs)
            cores[d][1].start()

        def add_gu(d):
            k = (z + d) % 4
            cores[d][0].wait_recv()
            add_up(t_gu.at[k, :, c], rc_gu.at[k])

        line_a, line_b = lines.lines
        terms_gu(2)
        terms_gu(1)
        for ring in rings:
            ring.turn()
        add_gu(2)
        for cp in line_a.far:
            cp.start()
        terms_gu(3)
        add_gu(1)
        terms_gu(0)
        add_gu(3)
        for cp in line_a.near:
            cp.start()
        add_gu(0)
        line_b.start()
        for cp in load_rows:
            cp.wait()
        for k in range(2):
            rings[k].finish()

            def back(r, _, k=k):
                rs, half = pl.ds(k * (rows // 2) + r * 32, 32), pl.ds(r * 32, 32)
                v = mid_ref[rs]
                inv = lax.rsqrt(jnp.mean(v * v, -1, keepdims=True) + EPS)
                v = v * inv
                g = rings[k].rows(half)
                value = own_cot[rs].astype(F32) + inv * (g - v * jnp.mean(g * v, -1, keepdims=True))
                gm_ref[rs] = value
                branch[rs] = value.astype(BF16)
                return 0

            lax.fori_loop(0, rows // 64, back, 0)
            gathers[k].start()
        own.start()
        lax.fori_loop(0, 4, part_out, 0)
        save_op.start()
        for gather in gathers:
            gather.turn()
        line_a.turn()
        terms_down(2)
        terms_down(1)
        line_b.turn()
        terms_down(3)
        terms_down(0)
        for d in (2, 1, 3, 0):
            cores[d][1].wait_recv()
            add_up(t_down.at[(z + d) % 4, :, c], rc_down.at[(z + d) % 4])
            saves[d].start()
        for gather in gathers:
            gather.near()
            gather.far()
        lines.finish()
        for cp in saves_gu:
            cp.start()
        own.wait()
        save_op.wait()
        for cp in saves + saves_gu:
            cp.wait()
        for pair in cores:
            for cp in pair:
                cp.wait_send()
        lines.sent()
        for ring in rings + gathers:
            ring.sent()

    anywhere, vmem = pl.BlockSpec(memory_space=pl.ANY), pl.BlockSpec(memory_space=pltpu.VMEM)
    copies = 24 + 8 + 12
    return pl.pallas_call(
        kernel,
        out_shape=[
            struct((4, rows, D)),
            struct((rows, D), F32),
            struct((2, 128, SPLITS[1][1])),
            struct((4, 64, 2 * HID - SPLITS[1][1])),
            struct((4, 2, 128, HID)),
            struct((4, rows, D)),
        ],
        in_specs=[anywhere] * 6,
        out_specs=[anywhere, vmem, anywhere, anywhere, anywhere, anywhere],
        scratch_shapes=[
            pltpu.VMEM((4, rows, D), BF16),
            pltpu.VMEM((2, rows, D // 2), BF16),
            pltpu.VMEM((2, rows, D), BF16),
            pltpu.VMEM((4, rows, D), BF16),
            pltpu.VMEM((count, 2 * HID), BF16),
            pltpu.VMEM((4, rows, D), BF16),
            pltpu.VMEM((count, HID), BF16),
            pltpu.VMEM((count, HID), F32),
            pltpu.VMEM((512, count), BF16),
            pltpu.VMEM((4, 2, 2, 128, 2 * HID), BF16),
            pltpu.VMEM((4, 2, 2, 128, HID), BF16),
            pltpu.VMEM((4, 2, 128, 2 * HID), BF16),
            pltpu.VMEM((4, 2, 128, HID), BF16),
            pltpu.VMEM((rows, D), BF16),
            pltpu.VMEM((4, rows, D), BF16),
            pltpu.VMEM((rows, D), F32),
            pltpu.VMEM((rows, D), BF16),
            *line_buffers(2 * HID, SPLITS[1][1]),
            pltpu.SemaphoreType.DMA((copies,)),
            pltpu.SemaphoreType.DMA((copies,)),
            pltpu.SemaphoreType.DMA((16,)),
            pltpu.SemaphoreType.DMA((tiles_gu + pairs + 1,)),
        ],
        name="feed_forward",
        compiler_params=pltpu.CompilerParams(
            collective_id=ident, has_side_effects=True, vmem_limit_bytes=VMEM_LIMIT
        ),
    )(seq_two, seq_cot, gu_w, down_w, middle, cotangent)


def own_rows(attn_gain, mlp_gain, attn_in, mlp_in, proj, gu, down, out):
    def kernel(one_ref, two_ref, in_ref, mlp_ref, proj_ref, gu_ref, down_ref, out_ref, g_in, g_mlp, g_down, g_out, g_gain):
        gain_one, gain_two = column(one_ref), column(two_ref)
        lane = lax.broadcasted_iota(jnp.int32, (16, 128), 1)
        low = lane < 64

        def put(dst, weights, at, value, gain, total):
            cols = pl.ds(at, 128)
            dst[:, cols] = value * gain
            return total + value * weights[:, cols].astype(F32)

        first = jnp.zeros((16, 128), F32)
        for k in range(TP):
            for j in range(Q_COLS // 128):
                value = proj_ref[k, :, pl.ds(j * 128, 128)].astype(F32)
                first = put(g_in, in_ref, k * Q_COLS + j * 128, value, gain_one, first)
        for k in range(0, TP, 2):
            even = proj_ref[k, :, pl.ds(Q_COLS, 128)].astype(F32)
            odd = proj_ref[k + 1, :, pl.ds(Q_COLS, 128)].astype(F32)
            key = jnp.where(low, even, pltpu.roll(odd, 64, 1))
            value = jnp.where(low, pltpu.roll(even, 64, 1), odd)
            first = put(g_in, in_ref, D + k * 64, key, gain_one, first)
            first = put(g_in, in_ref, D + HEAD_DIM * KV_HEADS + k * 64, value, gain_one, first)
        second = jnp.zeros((16, 128), F32)
        for k in range(TP):
            for j in range(HID // 128):
                for half in range(2):
                    value = gu_ref[k, :, pl.ds(j * 256 + half * 128, 128)].astype(F32)
                    second = put(g_mlp, mlp_ref, half * FF + k * HID + j * 128, value, gain_two, second)
            g_down[:, pl.ds(k * HID, HID)] = down_ref[k].astype(F32)
        g_out[...] = out_ref[...].astype(F32)
        sums = jnp.sum(first, -1, keepdims=True), jnp.sum(second, -1, keepdims=True)
        g_gain[...] = jnp.transpose(jnp.where(lane == 0, sums[0], sums[1]))[0:8]

    shapes = [(16, attn_in.shape[1]), (16, 2 * FF), (16, FF), (16, D), (8, 16)]
    return pl.pallas_call(
        kernel,
        out_shape=[struct(shape, F32) for shape in shapes],
        in_specs=[pl.BlockSpec(memory_space=pltpu.VMEM)] * 8,
        out_specs=[pl.BlockSpec(memory_space=pltpu.VMEM)] * 5,
        name="own_rows",
        compiler_params=pltpu.CompilerParams(vmem_limit_bytes=VMEM_LIMIT),
    )(attn_gain, mlp_gain, attn_in, mlp_in, proj, gu, down, out)


def shards(tokens, positions, attn_in, attn_out, attn_gain, mlp_in, mlp_down, mlp_gain, cotangent):
    rows = tokens.shape[0]
    count = 4 * rows
    attn_gain, mlp_gain = attn_gain[None], mlp_gain[None]
    lanes = np.arange(128)
    freqs = np.zeros((8, 128), np.float32)
    freqs[0] = np.float32(ROPE_BASE) ** (-2.0 * (lanes % 32).astype(np.float32) / HEAD_DIM)
    freqs[1] = np.where(lanes % 64 < 32, -1.0, 1.0)
    (normed_one_all, cot_all, proj_w, gu_w, down_w, out_w, q_all, kv_all, attended_low, lse, cosines, sines, bias_all, middle, two_all) = (
        forward_attention(tokens, cotangent, positions[None], freqs, attn_gain, mlp_gain, attn_in, mlp_in, mlp_down, attn_out, 0)
    )
    branch_all, grad_middle, gu_a, gu_b, sum_down, out_part = feed_forward(
        two_all, cot_all, gu_w, down_w, middle, cotangent, 1
    )
    outputs, input_grad, own_proj, own_gu, own_down, own_out = backward_attention(
        gu_a, gu_b, sum_down, out_part, branch_all, grad_middle, middle, tokens,
        cosines, sines, bias_all, q_all, kv_all.reshape(2 * count, 128), attended_low, lse, normed_one_all, proj_w, out_w, 2,
    )
    grad_in, grad_mlp, grad_down, grad_out, grad_gains = own_rows(
        attn_gain, mlp_gain, attn_in, mlp_in, own_proj, own_gu, own_down, own_out
    )
    return outputs, input_grad, grad_in, grad_out, grad_gains[0], grad_mlp, grad_down, grad_gains[1]


def solution(mesh):
    both = ("dp", "ctx")
    wide, flat = P(both, None), P(both)
    in_specs = (wide, flat, wide, wide, flat, wide, wide, flat, wide)
    out_specs = (wide, wide, wide, wide, flat, wide, wide, flat)
    return jax.shard_map(shards, mesh=mesh, in_specs=in_specs, out_specs=out_specs, check_vma=False)
```

```python
import jax
import jax.numpy as jnp
import numpy as np
from jax import lax
from jax.experimental import pallas as pl
from jax.experimental.pallas import tpu as pltpu
from jax.sharding import PartitionSpec as P


D = 2048
HEADS = 32
KV_HEADS = 4
HEAD_DIM = 64
FF = 5632
REPEAT = HEADS // KV_HEADS
TP = 4
Q_COLS = D // TP
PROJ = Q_COLS + 2 * HEAD_DIM
HID = FF // TP

EPS = 1e-05
ROPE_BASE = 10000.0
NEG_FILL = -1e30

MESH = pl.DeviceIdType.MESH
BF16 = jnp.bfloat16
F32 = jnp.float32

SPLITS = ((PROJ, 384), (2 * HID, 13 * 128), (HID, 640))
OUT_SPLIT = 1024
VMEM_LIMIT = 60 << 20

NN = ((1,), (0,))
NT = ((1,), (1,))
TN = ((0,), (0,))


def place():
    dp, ctx = lax.axis_index("dp"), lax.axis_index("ctx")
    return (dp // 2) % 2, ctx // 4, ctx % 4, dp // 4, dp % 2


def device(xh, xl, y, z, c):
    return (z * 4 + xh * 2 + c, xl * 4 + y)


def along_y(d):
    def to(xh, xl, y, z, c):
        return xh, xl, (y + d) % 4, z, c

    return to


def along_x(d):
    def to(xh, xl, y, z, c):
        x = (xh * 2 + xl + d) % 4
        return x // 2, x % 2, y, z, c

    return to


def along_z(d):
    def to(xh, xl, y, z, c):
        return xh, xl, y, (z + d) % 4, c

    return to


def sibling(xh, xl, y, z, c):
    return xh, xl, y, z, 1 - c


def half_partner(xh, xl, y, z, c):
    return xh, 1 - xl, y, z, c


def crossed(xh, xl, y, z, c):
    return xh, xl, z, y, c


def say_hello(routes, cross=False):
    here = place()
    barrier = pltpu.get_barrier_semaphore()
    for back in routes:
        pl.semaphore_signal(barrier, inc=1, device_id=device(*back(*here)), device_id_type=MESH)
    if cross:

        @pl.when(here[2] != here[3])
        def _():
            pl.semaphore_signal(barrier, inc=1, device_id=device(*crossed(*here)), device_id_type=MESH)


def meet(routes, cross=False):
    here = place()
    barrier = pltpu.get_barrier_semaphore()
    if not cross:
        pl.semaphore_wait(barrier, len(routes))
        return
    away = here[2] != here[3]

    @pl.when(away)
    def _():
        pl.semaphore_wait(barrier, len(routes) + 1)

    @pl.when(jnp.logical_not(away))
    def _():
        pl.semaphore_wait(barrier, len(routes))


ALL_LINES = [along(d) for along in (along_y, along_x, along_z) for d in (1, 2, 3)] + [sibling]


class Copies:
    def __init__(self, send, recv):
        self.send, self.recv, self.count = send, recv, 0

    def __call__(self, src, dst, to):
        k, self.count = self.count, self.count + 1
        return pltpu.make_async_remote_copy(
            src_ref=src,
            dst_ref=dst,
            send_sem=self.send.at[k],
            recv_sem=self.recv.at[k],
            device_id=device(*to(*place())),
            device_id_type=MESH,
        )


def comm_call(kernel, name, ident, ins, outs, copies, locals_=0):
    return pl.pallas_call(
        kernel,
        out_shape=outs,
        in_specs=[pl.BlockSpec(memory_space=pl.ANY)] * len(ins),
        out_specs=[pl.BlockSpec(memory_space=pl.ANY)] * len(outs),
        scratch_shapes=[
            pltpu.SemaphoreType.DMA((copies,)),
            pltpu.SemaphoreType.DMA((copies,)),
            pltpu.SemaphoreType.DMA((max(locals_, 1),)),
        ],
        name=name,
        compiler_params=pltpu.CompilerParams(collective_id=ident, has_side_effects=True),
    )(*ins)


def struct(shape, dtype=BF16):
    return jax.ShapeDtypeStruct(shape, dtype)


class RingGather:
    def __init__(self, copy, own, dst, y):
        half = dst.shape[2] // 2
        lo, hi = pl.ds(0, half), pl.ds(half, half)
        back, on = (y + 3) % 4, (y + 1) % 4

        def first(cols, to):
            return copy(own.at[:, cols], dst.at[y, :, cols], to)

        def one(slot, cols, to):
            at = dst.at[slot, :, cols]
            return copy(at, at, to)

        self.first = [first(lo, along_y(1)), first(hi, along_y(3)), first(hi, along_y(1)), first(lo, along_y(3))]
        self.second = [one(back, lo, along_y(1)), one(on, hi, along_y(3))]

    def start(self):
        for cp in self.first:
            cp.start()

    def turn(self):
        for got, cp in zip(self.first, self.second):
            got.wait_recv()
            cp.start()

    def near(self):
        for cp in self.first[2:]:
            cp.wait_recv()

    def far(self):
        for cp in self.second:
            cp.wait_recv()

    def sent(self):
        for cp in self.first + self.second:
            cp.wait_send()


class RingSum:
    def __init__(self, copy, part, halves, whole, y):
        half = part.shape[2] // 2
        lo, hi = pl.ds(0, half), pl.ds(half, half)
        self.part, self.halves, self.whole, self.y = part, halves, whole, y
        self.cols = (lo, hi)
        far, on, back = (y + 2) % 4, (y + 1) % 4, (y + 3) % 4
        self.far = [
            copy(part.at[far, :, lo], halves.at[0], along_y(1)),
            copy(part.at[far, :, hi], halves.at[1], along_y(3)),
        ]
        self.near = [
            copy(part.at[on, :, hi], whole.at[0, :, hi], along_y(1)),
            copy(part.at[back, :, lo], whole.at[1, :, lo], along_y(3)),
        ]
        self.last = [
            copy(part.at[on, :, lo], whole.at[0, :, lo], along_y(1)),
            copy(part.at[back, :, hi], whole.at[1, :, hi], along_y(3)),
        ]
        self.slots = (on, back)

    def start(self):
        for cp in self.far + self.near:
            cp.start()

    def turn(self):
        for k in range(2):
            self.far[k].wait_recv()
            slot, cols = self.slots[k], self.cols[k]

            def body(r, _, slot=slot, cols=cols, k=k):
                rows = pl.ds(r * 32, 32)
                both = self.part[slot, rows, cols].astype(F32) + self.halves[k, rows].astype(F32)
                self.part[slot, rows, cols] = both.astype(BF16)
                return 0

            lax.fori_loop(0, self.part.shape[1] // 32, body, 0)
            self.last[k].start()

    def finish(self):
        for cp in self.near + self.last:
            cp.wait_recv()

    def rows(self, rows):
        own = self.part[self.y, rows].astype(F32)
        return own + self.whole[0, rows].astype(F32) + self.whole[1, rows].astype(F32)

    def sent(self):
        for cp in self.far + self.near + self.last:
            cp.wait_send()


class Gather:
    def __init__(self, copy, out, a, at, rows_only=False):
        xh, xl, y, z, c = at
        cols = out.shape[-1]
        left, right = pl.ds(0, a), pl.ds(a, cols - a)
        def cut(half, n):
            return slice(None) if half is None else pl.ds(half * (n // 2), n // 2)

        if rows_only:
            block = lambda z, x, c, cols: out.at[x[0], c, x[1], z, :, cols]
            z_line = lambda x, c, cols, half: out.at[x[0], c, x[1], cut(half, 4), :, cols]
            x_line = lambda z, c, cols, half: out.at[cut(half, 2), c, :, z, :, cols]
        else:
            block = lambda z, x, c, cols: out.at[z, x[0], c, pl.ds(x[1] * 64, 64), cols]
            z_line = lambda x, c, cols, half: out.at[cut(half, 4), x[0], c, pl.ds(x[1] * 64, 64), cols]
            x_line = lambda z, c, cols, half: out.at[z, cut(half, 2), c, :, cols]

        def same(ref, to):
            return copy(ref, ref, to)

        here = (xh, xl)
        self.first = []
        for d in (1, 3, 2):
            self.first.append(same(block(z, here, c, left), along_x(d)))
            self.first.append(same(block(z, here, c, right), along_z(d)))
        a_lo, a_hi = lambda z: x_line(z, c, left, 0), lambda z: x_line(z, c, left, 1)
        b_lo, b_hi = lambda x: z_line(x, c, right, 0), lambda x: z_line(x, c, right, 1)
        z_at = [(z + d) % 4 for d in range(4)]
        x_at = [along_x(d)(*at)[:2] for d in range(4)]
        self.lines = []
        for lo, hi, spots, along in ((a_lo, a_hi, z_at, along_z), (b_lo, b_hi, x_at, along_x)):
            going = [
                same(lo(spots[0]), along(1)),
                same(hi(spots[0]), along(3)),
                same(hi(spots[0]), along(1)),
                same(lo(spots[0]), along(3)),
            ]
            on = [same(lo(spots[3]), along(1)), same(hi(spots[1]), along(3))]
            self.lines.append((going, on))
        self.core = [same(block(z, here, c, pl.ds(0, cols)), sibling)]
        for d in (1, 3, 2):
            self.core.append(same(block(z, x_at[d], c, left), sibling))
            self.core.append(same(block(z_at[d], here, c, right), sibling))
        self.core_lines = []
        for d in (3, 1, 2):
            self.core_lines.append(
                (same(x_line(z_at[d], c, left, None), sibling), same(z_line(x_at[d], c, right, None), sibling))
            )

    def start(self):
        for cp in self.first:
            cp.start()
        self.core[0].start()

    def turn(self, *which):
        for k in which or (0, 1):
            for cp in self.first[k::2]:
                cp.wait_recv()
            for cp in self.lines[k][0]:
                cp.start()
            for cp in self.core[1 + k :: 2]:
                cp.start()

    def pass_on(self):
        for going, on in self.lines:
            for got, cp in zip(going[:2], on):
                got.wait_recv()
                cp.start()

    def near(self):
        for k, (going, _) in enumerate(self.lines):
            for side in range(2):
                going[2 + side].wait_recv()
                self.core_lines[side][k].start()

    def far(self):
        for k, (_, on) in enumerate(self.lines):
            for cp in on:
                cp.wait_recv()
            self.core_lines[2][k].start()

    def finish(self):
        for cp in self.core + [cp for pair in self.core_lines for cp in pair]:
            cp.wait_recv()

    def sent(self):
        for going, on in self.lines:
            for cp in going + on:
                cp.wait_send()
        for cp in self.first + self.core + [cp for pair in self.core_lines for cp in pair]:
            cp.wait_send()


def dot(left, right, dims=((1,), (0,))):
    return lax.dot_general(left, right, (dims, ((), ())), preferred_element_type=F32)


def column(row_ref):
    row = jnp.broadcast_to(row_ref[...].astype(F32), (16, 16))
    diagonal = lax.broadcasted_iota(jnp.int32, (16, 16), 0) == lax.broadcasted_iota(jnp.int32, (16, 16), 1)
    return jnp.sum(jnp.where(diagonal, row, 0.0), 1, keepdims=True)


def swap_halves(v):
    lane = lax.broadcasted_iota(jnp.int32, v.shape, 1)
    return jnp.where(lane % 64 < 32, pltpu.roll(v, 96, 1), pltpu.roll(v, 32, 1))


def forward_attention(tokens, cotangent, positions, freqs, attn_gain, mlp_gain, attn_in, mlp_in, mlp_down, out_rows, ident):
    rows = tokens.shape[0]
    count = 4 * rows

    def kernel(
        tok_ref, cot_ref, spot_ref, freq_ref, one_ref, two_ref, in_ref, mlp_ref, down_ref, wo,
        normed_out, cot_all, gp, gg, gd, go, q_out, kv_out, att_out, lse_out, cos_out, sin_out, bias_out, middle_hbm, two_all,
        wp, wg, wd, tok, normed, wp_v, wo_v, q_s, kv, vx, bias, att, part, halves, whole, spot_all, own_two, middle_out, cos_s, sin_s, bias_t, send, recv, local,
    ):
        say_hello(ALL_LINES, True)
        at = place()
        xh, xl, y, z, c = at
        copy = Copies(send, recv)
        slot = pl.ds(xl * 64 + y * 16, 16)
        nlocal = [0]

        def near(src, dst):
            cp = pltpu.make_async_copy(src, dst, local.at[nlocal[0]])
            nlocal[0] += 1
            return cp

        to_y = []
        stay = []
        for i, o in ((wp, gp), (wg, gg), (wd, gd)):
            to_y.append([copy(i.at[(y + d) % 4], o.at[z, xh, c, slot], along_y(d)) for d in (1, 3, 2)])
            stay.append(near(i.at[y], o.at[z, xh, c, slot]))
        over = copy(wo, go.at[xh, c, xl, y], crossed)
        keep = near(wo, go.at[xh, c, xl, z])
        spot_copies = [copy(spot_all.at[y], spot_all.at[y], along_y(d)) for d in (1, 3, 2)]
        tok_ring = RingGather(copy, tok_ref, tok, y)
        cot_ring = RingGather(copy, cot_ref, cot_all, y)
        row_halves = [pl.ds(0, rows // 2), pl.ds(rows // 2, rows // 2)]
        two_rings = [RingGather(copy, own_two.at[r], two_all.at[:, r], y) for r in row_halves]
        branches = [RingSum(copy, part.at[:, r], halves.at[:, r], whole.at[:, r], y) for r in row_halves]
        kv_copy = copy(kv.at[1], kv.at[0], half_partner)
        g_proj = Gather(copy, gp, SPLITS[0][1], at)
        g_gu = Gather(copy, gg, SPLITS[1][1], at)
        g_down = Gather(copy, gd, SPLITS[2][1], at)
        g_out = Gather(copy, go, OUT_SPLIT, at, True)

        cot_own = near(cot_ref, cot_all.at[y])
        tok_own = near(tok_ref, tok.at[y])
        tok_own.start()
        cot_own.start()
        spot_all[y] = jnp.broadcast_to(spot_ref[...].astype(F32), (8, rows))

        gain_one, gain_two = column(one_ref), column(two_ref)
        low_lanes = lax.broadcasted_iota(jnp.int32, (16, 128), 1) < 64
        for k in range(TP):
            qs = pl.ds(k * Q_COLS, Q_COLS)
            wp[k, :, pl.ds(0, Q_COLS)] = (in_ref[:, qs].astype(F32) * gain_one).astype(BF16)
            key = in_ref[:, pl.ds(D + (k // 2) * 128, 128)].astype(F32)
            value = in_ref[:, pl.ds(D + HEAD_DIM * KV_HEADS + (k // 2) * 128, 128)].astype(F32)
            if k % 2 == 0:
                both = jnp.where(low_lanes, key, pltpu.roll(value, 64, 1))
            else:
                both = jnp.where(low_lanes, pltpu.roll(key, 64, 1), value)
            wp[k, :, pl.ds(Q_COLS, 128)] = (both * gain_one).astype(BF16)
        stay[0].start()
        for k in range(TP):
            for j in range(HID // 128):
                for half in range(2):
                    cols = pl.ds(half * FF + k * HID + j * 128, 128)
                    tile = (mlp_ref[:, cols].astype(F32) * gain_two).astype(BF16)
                    wg[k, :, pl.ds(j * 256 + half * 128, 128)] = tile
            wd[k] = down_ref[:, pl.ds(k * HID, HID)]
        for cp in stay[1:]:
            cp.start()
        meet(ALL_LINES, True)
        away = y != z
        for cp in to_y[0]:
            cp.start()

        @pl.when(away)
        def _():
            over.start()

        @pl.when(jnp.logical_not(away))
        def _():
            keep.start()

        for cp in spot_copies + to_y[1] + to_y[2] + tok_ring.first:
            cp.start()

        def norm_block(k):
            def body(r, _):
                rs = pl.ds(r * 32, 32)
                v = tok[k, rs].astype(F32)
                inv = lax.rsqrt(jnp.mean(v * v, -1, keepdims=True) + EPS)
                normed[k, rs] = (v * inv).astype(BF16)
                return 0

            lax.fori_loop(0, rows // 32, body, 0)

        stay[0].wait()
        for cp in to_y[0]:
            cp.wait_recv()
        g_proj.start()

        @pl.when(away)
        def _():
            over.wait()

        @pl.when(jnp.logical_not(away))
        def _():
            keep.wait()

        g_out.start()
        tok_own.wait()
        norm_block(y)
        g_proj.turn()
        stay[1].wait()
        for cp in to_y[1]:
            cp.wait_recv()
        g_gu.start()
        g_proj.pass_on()
        stay[2].wait()
        for cp in to_y[2]:
            cp.wait_recv()
        g_down.start()
        g_out.turn()
        for cp in spot_copies:
            cp.wait_recv()
        tok_ring.turn()
        g_proj.near()
        g_proj.far()

        cos, sin = [], []
        freq, sign = freq_ref[0:1, :], freq_ref[1:2, :]
        spot_cols = []
        for k in range(4):
            col = jnp.transpose(jnp.broadcast_to(spot_all[k, 0:1, :], (128, 128)))
            spot_cols.append(col)
            cos.append(jnp.cos(col * freq))
            sin.append(jnp.sin(col * freq) * sign)
        cos, sin = jnp.concatenate(cos, 0), jnp.concatenate(sin, 0)
        cos_s[...] = cos
        sin_s[...] = sin
        turn_saves = [near(cos_s, cos_out), near(sin_s, sin_out)]
        for cp in turn_saves:
            cp.start()
        low_half = xl == 0
        reach = jnp.where(low_half, -1.0, 2048.0)
        for k in range(4):
            for j in range(8):
                row = lax.broadcasted_iota(jnp.int32, (128, 128), 0) + k * 128
                col = lax.broadcasted_iota(jnp.int32, (128, 128), 1) + j * 128
                apart = (row - col + 512).astype(F32)
                seen = apart <= spot_cols[k]
                if j < 4:
                    seen = seen & (apart <= reach)
                else:
                    seen = seen & (col - 512 <= row)
                bias[pl.ds(k * 128, 128), pl.ds(j * 128, 128)] = jnp.where(seen, 0.0, NEG_FILL)

        g_proj.finish()
        wp_load = near(gp, wp_v)
        wp_load.start()
        g_out.pass_on()
        tok_ring.near()
        norm_block((y + 3) % 4)
        norm_block((y + 1) % 4)
        g_out.near()
        tok_ring.far()
        cot_ring.start()
        norm_block((y + 2) % 4)
        normed_save = near(normed, normed_out)
        normed_save.start()

        g_gu.turn(0)
        g_down.turn(0)

        wp_load.wait()
        left = normed[...].reshape(count, D)
        lane = lax.broadcasted_iota(jnp.int32, (count, 128), 1)
        upper = lane >= 64
        raw = dot(left, wp_v[:, :, :, :, pl.ds(Q_COLS, 128)].reshape(D, 128))
        turned = raw * jnp.where(upper, 1.0, cos) + swap_halves(raw) * jnp.where(upper, 0.0, sin)
        kv[1] = turned.astype(BF16)
        kv_copy.start()
        g_out.far()
        g_gu.turn(1)
        g_down.turn(1)
        for j in range(2):
            raw2 = dot(left, wp_v[:, :, :, :, pl.ds(j * 256, 256)].reshape(D, 256))
            for e in range(2):
                raw = raw2[:, e * 128 : e * 128 + 128]
                turned = (raw * cos + swap_halves(raw) * sin).astype(BF16).astype(F32) * (HEAD_DIM ** (-0.5))
                pair = j * 2 + e
                q_s[2 * pair] = jnp.where(upper, 0.0, turned).astype(BF16)
                q_s[2 * pair + 1] = jnp.where(upper, 0.0, pltpu.roll(turned, 64, 1)).astype(BF16)
        kv_copy.wait_recv()
        for k in range(2):
            vx[k] = jnp.where(upper, kv[k].astype(F32), 1.0).astype(BF16)
        q_save = near(q_s, q_out)
        q_save.start()
        kv_save = near(kv, kv_out)
        kv_save.start()
        g_out.finish()
        wo_load = near(go, wo_v)
        wo_load.start()

        def attend(pair):
            for b in range(2):
                rs = pl.ds(b * 256, 256)
                seen = 256 * (b + 1)
                lane = lax.broadcasted_iota(jnp.int32, (256, 128), 1) < 64
                found = []
                for e in range(2):
                    q = q_s[2 * pair + e, rs]
                    s0 = dot(q, kv[0], NT) + bias[rs, pl.ds(0, 512)]
                    s1 = dot(q, kv[1, pl.ds(0, seen)], NT) + bias[rs, pl.ds(512, seen)]
                    m = jnp.maximum(jnp.max(s0, -1, keepdims=True), jnp.max(s1, -1, keepdims=True))
                    p0 = jnp.exp(s0 - m).astype(BF16)
                    p1 = jnp.exp(s1 - m).astype(BF16)
                    o = dot(p0, vx[0]) + dot(p1, vx[1, pl.ds(0, seen)])
                    r = pltpu.roll(o, 64, 1)
                    found.append((o, r))
                    log_total = m + jnp.log(jnp.where(lane, o, r))
                    lse_out[2 * pair + e, :, rs] = jnp.transpose(log_total)[0:8]
                (o, r), (o2, r2) = found
                both = jnp.where(lane, r / o, o2 / r2)
                att[rs, pl.ds(pl.multiple_of(pair * 128, 128), 128)] = both.astype(BF16)

        def two_pairs(k):
            def body(i, _):
                attend(2 * k + i)
                return 0

            lax.fori_loop(0, 2, body, 0)

        two_pairs(0)
        cot_ring.turn()
        two_pairs(1)
        att_save = near(att, att_out)
        att_save.start()
        wo_load.wait()

        for j in range(4):
            cols = pl.ds(j * 512, 512)
            w = wo_v[:, :, :, :, :, cols].reshape(Q_COLS, 512)
            part[:, :, cols] = dot(att[...], w).astype(BF16).reshape(4, rows, 512)
        for branch in branches:
            branch.start()

        for k in range(4):
            for j in range(8):
                key = lax.broadcasted_iota(jnp.int32, (128, 128), 0) + j * 128
                row = lax.broadcasted_iota(jnp.int32, (128, 128), 1) + k * 128
                apart = (row - key + 512).astype(F32)
                seen = apart <= spot_all[k, 0:1, :]
                if j < 4:
                    seen = seen & (apart <= reach)
                else:
                    seen = seen & (key - 512 <= row)
                bias_t[pl.ds(j * 128, 128), pl.ds(k * 128, 128)] = jnp.where(seen, 0.0, NEG_FILL)
        bias_save = near(bias_t, bias_out)
        bias_save.start()
        g_gu.pass_on()
        g_down.pass_on()
        for branch in branches:
            branch.turn()
        g_gu.near()
        g_down.near()
        cot_ring.near()
        cot_ring.far()
        two_own = near(own_two, two_all.at[y])
        for k in range(2):
            branches[k].finish()

            def mid(r, _, k=k):
                rs, half = pl.ds(k * (rows // 2) + r * 32, 32), pl.ds(r * 32, 32)
                v = tok_ref[rs].astype(F32) + branches[k].rows(half)
                middle_out[rs] = v
                inv = lax.rsqrt(jnp.mean(v * v, -1, keepdims=True) + EPS)
                own_two[rs] = (v * inv).astype(BF16)
                return 0

            lax.fori_loop(0, rows // 64, mid, 0)
            two_rings[k].start()
        two_own.start()
        middle_save = near(middle_out, middle_hbm)
        middle_save.start()
        for ring in two_rings:
            ring.turn()
        g_gu.far()
        g_down.far()
        for ring in two_rings:
            ring.near()
            ring.far()
        g_gu.finish()
        g_down.finish()
        for cp in (cot_own, normed_save, q_save, kv_save, att_save, two_own, middle_save, bias_save, *turn_saves):
            cp.wait()
        for group in to_y:
            for cp in group:
                cp.wait_send()
        for cp in spot_copies + [kv_copy]:
            cp.wait_send()
        for thing in (g_proj, g_out, g_gu, g_down, tok_ring, cot_ring, *two_rings, *branches):
            thing.sent()

    anywhere, vmem = pl.BlockSpec(memory_space=pl.ANY), pl.BlockSpec(memory_space=pltpu.VMEM)
    outs = [
        (struct((4, rows, D)), anywhere),
        (struct((4, rows, D)), anywhere),
        (struct((4, 2, 2, 128, PROJ)), anywhere),
        (struct((4, 2, 2, 128, 2 * HID)), anywhere),
        (struct((4, 2, 2, 128, HID)), anywhere),
        (struct((2, 2, 2, 4, 16, D)), anywhere),
        (struct((REPEAT, count, 128)), anywhere),
        (struct((2, count, 128)), anywhere),
        (struct((count, Q_COLS)), anywhere),
        (struct((REPEAT, 8, count), F32), vmem),
        (struct((count, 128), F32), anywhere),
        (struct((count, 128), F32), anywhere),
        (struct((2 * count, count), F32), anywhere),
        (struct((rows, D), F32), anywhere),
        (struct((4, rows, D)), anywhere),
    ]
    copies = 9 + 1 + 3 + 6 * 6 + 1 + 31 * 4
    return pl.pallas_call(
        kernel,
        out_shape=[o[0] for o in outs],
        in_specs=[vmem] * 10,
        out_specs=[o[1] for o in outs],
        scratch_shapes=[
            pltpu.VMEM((TP, 16, PROJ), BF16),
            pltpu.VMEM((TP, 16, 2 * HID), BF16),
            pltpu.VMEM((TP, 16, HID), BF16),
            pltpu.VMEM((4, rows, D), BF16),
            pltpu.VMEM((4, rows, D), BF16),
            pltpu.VMEM((4, 2, 2, 128, PROJ), BF16),
            pltpu.VMEM((2, 2, 2, 4, 16, D), BF16),
            pltpu.VMEM((REPEAT, count, 128), BF16),
            pltpu.VMEM((2, count, 128), BF16),
            pltpu.VMEM((2, count, 128), BF16),
            pltpu.VMEM((count, 2 * count), F32),
            pltpu.VMEM((count, Q_COLS), BF16),
            pltpu.VMEM((4, rows, D), BF16),
            pltpu.VMEM((2, rows, D // 2), BF16),
            pltpu.VMEM((2, rows, D), BF16),
            pltpu.VMEM((4, 8, 128), F32),
            pltpu.VMEM((rows, D), BF16),
            pltpu.VMEM((rows, D), F32),
            pltpu.VMEM((count, 128), F32),
            pltpu.VMEM((count, 128), F32),
            pltpu.VMEM((2 * count, count), F32),
            pltpu.SemaphoreType.DMA((copies,)),
            pltpu.SemaphoreType.DMA((copies,)),
            pltpu.SemaphoreType.DMA((22,)),
        ],
        name="forward_attention",
        compiler_params=pltpu.CompilerParams(
            collective_id=ident, has_side_effects=True, vmem_limit_bytes=VMEM_LIMIT
        ),
    )(tokens, cotangent, positions, freqs, attn_gain, mlp_gain, attn_in, mlp_in, mlp_down, out_rows)


def tiles(ref):
    if len(ref.shape) == 2:
        return [ref]
    return [t for k in range(ref.shape[0]) for t in tiles(ref.at[k])]


def add_up(dst, *others):
    for out, *terms in zip(tiles(dst), *[tiles(o) for o in others]):
        rows = out.shape[0]
        step = min(rows, 32)

        def body(r, _, out=out, terms=terms, step=step):
            rs = pl.ds(r * step, step)
            value = out[rs].astype(F32)
            for t in terms:
                value = value + t[rs].astype(F32)
            out[rs] = value.astype(BF16)
            return 0

        lax.fori_loop(0, rows // step, body, 0)


class LineSum:
    def __init__(self, copy, lo, hi, along, far, near):
        self.lo, self.hi, self.far_in, self.near_in = lo, hi, far, near
        self.far = [copy(lo(2), far.at[0], along(1)), copy(hi(2), far.at[1], along(3))]
        self.near = [copy(hi(1), near.at[0, 1], along(1)), copy(lo(3), near.at[1, 0], along(3))]
        self.last = [copy(lo(1), near.at[0, 0], along(1)), copy(hi(3), near.at[1, 1], along(3))]

    def start(self):
        for cp in self.far + self.near:
            cp.start()

    def turn(self):
        self.far[0].wait_recv()
        add_up(self.lo(1), self.far_in.at[0])
        self.last[0].start()
        self.far[1].wait_recv()
        add_up(self.hi(3), self.far_in.at[1])
        self.last[1].start()

    def finish(self):
        for cp in self.near + self.last:
            cp.wait_recv()
        add_up(self.lo(0), self.near_in.at[0, 0], self.near_in.at[1, 0])
        add_up(self.hi(0), self.near_in.at[0, 1], self.near_in.at[1, 1])

    def sent(self):
        for cp in self.far + self.near + self.last:
            cp.wait_send()


class GradLines:
    def __init__(self, copy, terms, a, at, buffers, rows_only=False):
        xh, xl, y, z, c = at
        far_a, near_a, far_b, near_b = buffers
        cols = terms.shape[-1]
        left, right = pl.ds(0, a), pl.ds(a, cols - a)
        x_at = [along_x(d)(*at)[:2] for d in range(4)]
        z_at = [(z + d) % 4 for d in range(4)]
        if rows_only:
            spot = lambda x, z, cols: terms.at[x[0], c, x[1], z, :, cols]
            a_half = lambda h: lambda d: terms.at[h, c, :, z_at[d], :, left]
            b_half = lambda h: lambda d: terms.at[x_at[d][0], c, x_at[d][1], pl.ds(2 * h, 2), :, right]
        else:
            base = (lambda z, xh: (z, xh, c)) if len(terms.shape) == 5 else (lambda z, xh: (z, xh))
            spot = lambda x, z, cols: terms.at[base(z, x[0]) + (pl.ds(x[1] * 64, 64), cols)]
            a_half = lambda h: lambda d: terms.at[base(z_at[d], h) + (slice(None), left)]
            b_half = lambda h: lambda d: terms.at[
                base(pl.ds(2 * h, 2), x_at[d][0]) + (pl.ds(x_at[d][1] * 64, 64), right)
            ]
        self.lines = [
            LineSum(copy, a_half(0), a_half(1), along_z, far_a, near_a),
            LineSum(copy, b_half(0), b_half(1), along_x, far_b, near_b),
        ]
        self.spot_a = lambda x: spot(x, z, left)
        self.spot_b = lambda z: spot(x_at[0], z, right)

    def start(self):
        for line in self.lines:
            line.start()

    def turn(self):
        for line in self.lines:
            line.turn()

    def finish(self):
        for line in self.lines:
            line.finish()

    def sent(self):
        for line in self.lines:
            line.sent()


class GradOwners:
    def __init__(self, copy, local_copy, spot_a, spot_b, out, at, buffers, rows_only=False):
        xh, xl, y, z, c = at
        self.at, self.rows_only = at, rows_only
        got_a, got_b, own = buffers
        a, cols = got_a.shape[-1], own.shape[-1]
        self.second = []
        for d in (1, 3, 2):
            self.second.append(copy(spot_a(along_x(d)(*at)[:2]), got_a.at[d - 1], along_x(d)))
            self.second.append(copy(spot_b((z + d) % 4), got_b.at[d - 1], along_z(d)))
        self.mine = (spot_a((xh, xl)), spot_b(z))
        self.got = (got_a, got_b)
        self.own, self.cuts = own, (pl.ds(0, a), pl.ds(a, cols - a))
        if rows_only:
            self.over = copy(own, out, crossed)
            self.keep = local_copy(own, out)
        else:
            self.to_y = [copy(own.at[(y + d) % 4], out.at[y], along_y(d)) for d in (1, 3, 2)]
            self.keep = local_copy(own.at[y], out.at[y])

    def start(self):
        for cp in self.second:
            cp.start()

    def deliver(self):
        for cp in self.second:
            cp.wait_recv()
        for mine, got, cut in zip(self.mine, self.got, self.cuts):
            value = mine[...].astype(F32)
            for d in range(3):
                value = value + got[d].astype(F32)
            own = self.own
            if self.rows_only:
                own[:, cut] = value.astype(BF16)
            else:
                own[:, :, cut] = value.astype(BF16).reshape(4, 16, value.shape[-1])
        if self.rows_only:
            y, z = self.at[2], self.at[3]

            @pl.when(y != z)
            def _():
                self.over.start()

            @pl.when(y == z)
            def _():
                self.keep.start()

        else:
            for cp in self.to_y:
                cp.start()
            self.keep.start()

    def finish(self):
        if self.rows_only:
            y, z = self.at[2], self.at[3]

            @pl.when(y != z)
            def _():
                self.over.wait()

            @pl.when(y == z)
            def _():
                self.keep.wait()

        else:
            for cp in self.to_y:
                cp.wait()
            self.keep.wait()
        for cp in self.second:
            cp.wait_send()


def line_buffers(cols, a, rows_only=False):
    b = cols - a
    a_half, b_half = ((2, 16), (2, 16)) if rows_only else ((128,), (2, 64))
    return [
        pltpu.VMEM((2,) + a_half + (a,), BF16),
        pltpu.VMEM((2, 2) + a_half + (a,), BF16),
        pltpu.VMEM((2,) + b_half + (b,), BF16),
        pltpu.VMEM((2, 2) + b_half + (b,), BF16),
    ]


def owner_buffers(cols, a, rows_only=False):
    spot, own = (16, (16, cols)) if rows_only else (64, (4, 16, cols))
    return [pltpu.VMEM((3, spot, a), BF16), pltpu.VMEM((3, spot, cols - a), BF16), pltpu.VMEM(own, BF16)]


def backward_attention(
    gu_a, gu_b, sum_down, out_part, branch_all, grad_middle, middle, tokens,
    cosines, sines, bias_all, q_all, kv_all, attended, lse, normed_all, proj_w, out_w, ident,
):
    rows = tokens.shape[0]
    count = 4 * rows
    scale = HEAD_DIM ** (-0.5)

    def kernel(
        gu_a_ref, gu_b_ref, s_down, op_ref, br_ref, gm_hbm, mid_hbm, tok_hbm,
        cos_ref, sin_ref, bias_ref, q_ref, kv_ref, att_ref, lse_ref, nm_ref, wp_ref, wo_ref,
        out_ref, ig_ref, o_proj, o_gu, o_down, o_out,
        gm_ref, mid_ref, tok_ref, v_gu_a, v_gu_b, v_down, part, part_in, halves, whole, halves2, whole2, br, q_s, do_s, kv, kvt, att, delta, bias, cos_s, sin_s,
        dkv, kv_send, kv_in, gp, normed, wp, wo, t_proj, rc_proj, t_out, rc_out, *rest,
    ):
        bufs, (send, recv, local) = rest[:24], rest[24:]
        say_hello(ALL_LINES, True)
        at = place()
        xh, xl, y, z, c = at
        copy = Copies(send, recv)
        nlocal = [0]

        def near(src, dst):
            cp = pltpu.make_async_copy(src, dst, local.at[nlocal[0]])
            nlocal[0] += 1
            return cp

        load_gu, load_gu_b, load_down = near(gu_a_ref, v_gu_a), near(gu_b_ref, v_gu_b), near(s_down, v_down)
        load_op, load_br, load_wo = near(op_ref, part), near(br_ref, br), near(wo_ref, wo)
        load_att, load_q = near(att_ref, att), near(q_ref, q_s)
        load_kv = near(kv_ref, kv)
        load_turns = [near(cos_ref, cos_s), near(sin_ref, sin_s), near(bias_ref, bias)]
        load_nm, load_wp = near(nm_ref, normed), near(wp_ref, wp)
        load_rows = [near(gm_hbm, gm_ref), near(mid_hbm, mid_ref), near(tok_hbm, tok_ref)]
        for cp in (load_br, load_wo, load_gu, load_gu_b, load_op, load_down, load_att, load_q, load_kv, *load_turns, load_nm, load_wp, *load_rows):
            cp.start()
        outs = RingSum(copy, part, halves, whole, y)
        ones = RingSum(copy, part_in, halves2, whole2, y)
        kv_copy = copy(kv_send, kv_in, half_partner)
        core_proj = [
            copy(t_proj.at[:, :, 1 - c, :, cols], rc_proj.at[:, :, :, cols], sibling)
            for cols in (pl.ds(0, Q_COLS), pl.ds(Q_COLS, 128))
        ]
        core_out = copy(t_out.at[:, 1 - c], rc_out, sibling)
        gu_owners = GradOwners(
            copy,
            near,
            lambda x: v_gu_a.at[x[0], pl.ds(x[1] * 64, 64)],
            lambda z: v_gu_b.at[z],
            o_gu,
            at,
            bufs[0:3],
        )
        down_lines = GradLines(copy, v_down, SPLITS[2][1], at, bufs[3:7])
        down_owners = GradOwners(copy, near, down_lines.spot_a, down_lines.spot_b, o_down, at, bufs[7:10])
        proj_lines = GradLines(copy, t_proj, SPLITS[0][1], at, bufs[10:14])
        proj_owners = GradOwners(copy, near, proj_lines.spot_a, proj_lines.spot_b, o_proj, at, bufs[14:17])
        out_lines = GradLines(copy, t_out, OUT_SPLIT, at, bufs[17:21], True)
        out_owners = GradOwners(copy, near, out_lines.spot_a, out_lines.spot_b, o_out, at, bufs[21:24], True)

        dkv[...] = jnp.zeros_like(dkv)

        meet(ALL_LINES, True)
        load_op.wait()
        outs.start()
        load_gu.wait()
        load_gu_b.wait()
        gu_owners.start()
        load_down.wait()
        down_lines.start()

        load_br.wait()
        load_wo.wait()
        load_att.wait()
        lane = lax.broadcasted_iota(jnp.int32, (count, 128), 1)
        for p in range(4):
            if p % 2 == 0:
                both = dot(br[...].reshape(count, D), wo[p // 2].reshape(256, D), NT).astype(BF16).astype(F32)
            low = both[:, p % 2 * 128 : p % 2 * 128 + 128]
            do_s[2 * p] = jnp.where(lane < 64, 0.0, pltpu.roll(low, 64, 1)).astype(BF16)
            do_s[2 * p + 1] = jnp.where(lane < 64, 0.0, low).astype(BF16)
            prod = jnp.transpose(low * att[:, pl.ds(p * 128, 128)].astype(F32))
            for e in range(2):
                total_row = jnp.sum(prod[e * 64 : e * 64 + 64], 0, keepdims=True)
                delta[2 * p + e] = jnp.broadcast_to(total_row, (8, count))
        outs.turn()

        for k in range(4):
            term = dot(att[:, pl.ds(k * 128, 128)], br[...].reshape(count, D), TN)
            t_out[k // 2, k % 2] = term.astype(BF16).reshape(2, 4, 16, D)
        core_out.start()
        load_q.wait()
        load_kv.wait()
        for k in range(2):
            turned = jnp.transpose(kv[pl.ds(k * count, count)].astype(F32)).astype(BF16)
            kvt[:, pl.ds(k * count, count)] = turned

        def backward(pair):
            for b in range(2):
                rs = pl.ds(b * 256, 256)
                seen = pl.ds(0, 512 + 256 * (b + 1))
                found = []
                for e in range(2):
                    h = 2 * pair + e
                    q, do = q_s[h, rs], do_s[h, rs]
                    st = dot(kv[seen], q, NT) + bias[seen, rs] - lse_ref[h, 0:1, rs]
                    p = jnp.exp(st)
                    dp = dot(kv[seen], do, NT)
                    ds = (p * (dp - delta[h, 0:1, rs])).astype(BF16)
                    dkv[seen] += dot(ds, q) + dot(p.astype(BF16), do)
                    found.append(dot(kvt[:, seen], ds)[0:64])
                both = jnp.transpose(jnp.concatenate(found, 0)) * scale
                both = both * cos_s[rs] - swap_halves(both) * sin_s[rs]
                gp[rs, pl.ds(pl.multiple_of(pair * 128, 128), 128)] = both.astype(BF16)

        def two_pairs(k):
            def body(i, _):
                backward(2 * k + i)
                return 0

            lax.fori_loop(0, 2, body, 0)

        for cp in load_turns:
            cp.wait()
        two_pairs(0)
        down_lines.turn()
        gu_owners.deliver()
        two_pairs(1)
        kv_send[...] = dkv[pl.ds(0, count)].astype(BF16)
        kv_copy.start()
        core_out.wait_recv()
        add_up(t_out.at[:, c], rc_out)
        out_lines.start()
        load_nm.wait()
        for k in range(4):
            left = normed[:, :, pl.ds(k * 512, 512)].reshape(count, 512)
            term = dot(left, gp[:, pl.ds(0, Q_COLS)], TN)
            t_proj[k, :, :, :, pl.ds(0, Q_COLS)] = term.astype(BF16).reshape(2, 2, 128, Q_COLS)
        core_proj[0].start()
        kv_copy.wait_recv()
        got = dkv[pl.ds(count, count)] + kv_in[...].astype(F32)
        back = got * cos_s[...] - swap_halves(got) * sin_s[...]
        gp[:, pl.ds(Q_COLS, 128)] = jnp.where(lane < 64, back, got).astype(BF16)
        for k in range(4):
            left = normed[:, :, pl.ds(k * 512, 512)].reshape(count, 512)
            term = dot(left, gp[:, pl.ds(Q_COLS, 128)], TN)
            t_proj[k, :, :, :, pl.ds(Q_COLS, 128)] = term.astype(BF16).reshape(2, 2, 128, 128)
        core_proj[1].start()

        load_wp.wait()
        for j in range(4):
            w = wp[j].reshape(512, PROJ)
            part_in[:, :, pl.ds(j * 512, 512)] = dot(gp[...], w, NT).astype(BF16).reshape(4, rows, 512)
        ones.start()
        for cp in core_proj:
            cp.wait_recv()
        for k in range(4):
            add_up(t_proj.at[k, :, c], rc_proj.at[k])
        proj_lines.start()
        out_lines.turn()
        ones.turn()
        proj_lines.turn()
        down_lines.finish()
        down_owners.start()
        out_lines.finish()
        out_owners.start()
        proj_lines.finish()
        proj_owners.start()
        down_owners.deliver()
        out_owners.deliver()
        proj_owners.deliver()
        outs.finish()

        for cp in load_rows:
            cp.wait()

        def finish_out(r, _):
            rs = pl.ds(r * 32, 32)
            out_ref[rs] = (mid_ref[rs] + outs.rows(rs)).astype(BF16)
            return 0

        lax.fori_loop(0, rows // 32, finish_out, 0)
        outs.sent()
        ones.finish()

        def finish_in(r, _):
            rs = pl.ds(r * 32, 32)
            v = tok_ref[rs].astype(F32)
            inv = lax.rsqrt(jnp.mean(v * v, -1, keepdims=True) + EPS)
            v = v * inv
            g = ones.rows(rs)
            ig_ref[rs] = gm_ref[rs] + inv * (g - v * jnp.mean(g * v, -1, keepdims=True))
            return 0

        lax.fori_loop(0, rows // 32, finish_in, 0)
        ones.sent()
        for cp in (kv_copy, *core_proj, core_out):
            cp.wait_send()
        for owners in (gu_owners, down_owners, out_owners, proj_owners):
            owners.finish()
        for lines in (down_lines, out_lines, proj_lines):
            lines.sent()

    anywhere, vmem = pl.BlockSpec(memory_space=pl.ANY), pl.BlockSpec(memory_space=pltpu.VMEM)
    in_specs = [anywhere] * 14 + [vmem] + [anywhere] * 3
    outs = [
        (struct((rows, D)), vmem),
        (struct((rows, D), F32), vmem),
        (struct((4, 16, PROJ)), anywhere),
        (struct((4, 16, 2 * HID)), anywhere),
        (struct((4, 16, HID)), anywhere),
        (struct((16, D)), anywhere),
    ]
    whole = lambda: [pltpu.VMEM((2, rows, D // 2), BF16), pltpu.VMEM((2, rows, D), BF16)]
    copies = 12 + 4 + 9 + 21 * 2 + 19
    return pl.pallas_call(
        kernel,
        out_shape=[o[0] for o in outs],
        in_specs=in_specs,
        out_specs=[o[1] for o in outs],
        scratch_shapes=[
            pltpu.VMEM((rows, D), F32),
            pltpu.VMEM((rows, D), F32),
            pltpu.VMEM((rows, D), BF16),
            pltpu.VMEM((2, 128, SPLITS[1][1]), BF16),
            pltpu.VMEM((4, 64, 2 * HID - SPLITS[1][1]), BF16),
            pltpu.VMEM((4, 2, 128, HID), BF16),
            pltpu.VMEM((4, rows, D), BF16),
            pltpu.VMEM((4, rows, D), BF16),
            *whole(),
            *whole(),
            pltpu.VMEM((4, rows, D), BF16),
            pltpu.VMEM((REPEAT, count, 128), BF16),
            pltpu.VMEM((REPEAT, count, 128), BF16),
            pltpu.VMEM((2 * count, 128), BF16),
            pltpu.VMEM((128, 2 * count), BF16),
            pltpu.VMEM((count, Q_COLS), BF16),
            pltpu.VMEM((REPEAT, 8, count), F32),
            pltpu.VMEM((2 * count, count), F32),
            pltpu.VMEM((count, 128), F32),
            pltpu.VMEM((count, 128), F32),
            pltpu.VMEM((2 * count, 128), F32),
            pltpu.VMEM((count, 128), BF16),
            pltpu.VMEM((count, 128), BF16),
            pltpu.VMEM((count, PROJ), BF16),
            pltpu.VMEM((4, rows, D), BF16),
            pltpu.VMEM((4, 2, 2, 128, PROJ), BF16),
            pltpu.VMEM((2, 2, 2, 4, 16, D), BF16),
            pltpu.VMEM((4, 2, 2, 128, PROJ), BF16),
            pltpu.VMEM((4, 2, 128, PROJ), BF16),
            pltpu.VMEM((2, 2, 2, 4, 16, D), BF16),
            pltpu.VMEM((2, 2, 4, 16, D), BF16),
            *owner_buffers(2 * HID, SPLITS[1][1]),
            *line_buffers(HID, SPLITS[2][1]),
            *owner_buffers(HID, SPLITS[2][1]),
            *line_buffers(PROJ, SPLITS[0][1]),
            *owner_buffers(PROJ, SPLITS[0][1]),
            *line_buffers(D, OUT_SPLIT, True),
            *owner_buffers(D, OUT_SPLIT, True),
            pltpu.SemaphoreType.DMA((copies,)),
            pltpu.SemaphoreType.DMA((copies,)),
            pltpu.SemaphoreType.DMA((24,)),
        ],
        name="backward_attention",
        compiler_params=pltpu.CompilerParams(
            collective_id=ident, has_side_effects=True, vmem_limit_bytes=VMEM_LIMIT
        ),
    )(
        gu_a, gu_b, sum_down, out_part, branch_all, grad_middle, middle, tokens,
        cosines, sines, bias_all, q_all, kv_all, attended, lse, normed_all, proj_w, out_w,
    )


def feed_forward(seq_two, seq_cot, gu_w, down_w, middle, cotangent, ident):
    rows = middle.shape[0]
    count = 4 * rows
    tiles_gu, pairs = HID // 128, HID // 256

    def kernel(
        two_ref, cot_ref, wg_ref, wd_ref, mid_hbm, own_cot_hbm,
        branch_all, gm_hbm, gu_a, gu_b, s_down, op_out,
        part, halves, whole, two, gu, cot, hid, gh, turned, t_gu, t_down, rc_gu, rc_down, branch, op,
        mid_ref, own_cot, gm_ref,
        far_a, near_a, far_b, near_b, send, recv, local, weights,
    ):
        partners = [along_y(1), along_y(3), along_x(1), along_x(3), along_z(1), along_z(3), sibling]
        say_hello(partners)
        at = place()
        xh, xl, y, z, c = at
        copy = Copies(send, recv)
        nlocal = [0]

        def near(src, dst):
            cp = pltpu.make_async_copy(src, dst, local.at[nlocal[0]])
            nlocal[0] += 1
            return cp

        def load_gu(j):
            tile = pl.ds(pl.multiple_of(j * 256, 256), 256)
            return pltpu.make_async_copy(wg_ref.at[:, :, :, :, tile], t_gu.at[:, :, :, :, tile], weights.at[j])

        def load_down(j, width=256):
            tile = pl.ds(pl.multiple_of(j * 256, 256), width)
            return pltpu.make_async_copy(
                wd_ref.at[:, :, :, :, tile], t_down.at[:, :, :, :, tile], weights.at[tiles_gu + j]
            )

        load_cot, load_two = near(cot_ref, cot), near(two_ref, two)
        load_rows = [near(mid_hbm, mid_ref), near(own_cot_hbm, own_cot)]
        load_cot.start()
        last_down = load_down(pairs, HID - 256 * pairs)

        def begin_down(j, _):
            load_down(j).start()
            return 0

        def begin_gu(j, _):
            load_gu(j).start()
            return 0

        lax.fori_loop(0, pairs, begin_down, 0)
        last_down.start()
        load_two.start()
        lax.fori_loop(0, tiles_gu, begin_gu, 0)
        for cp in load_rows:
            cp.start()
        row_halves = [pl.ds(0, rows // 2), pl.ds(rows // 2, rows // 2)]
        rings = [RingSum(copy, part.at[:, r], halves.at[:, r], whole.at[:, r], y) for r in row_halves]
        gathers = [RingGather(copy, branch.at[r], branch_all.at[:, r], y) for r in row_halves]
        own = near(branch, branch_all.at[y])
        cores = [
            (copy(t_gu.at[k, :, 1 - c], rc_gu.at[k], sibling), copy(t_down.at[k, :, 1 - c], rc_down.at[k], sibling))
            for k in [(z + d) % 4 for d in range(4)]
        ]
        saves = [near(t_down.at[k, :, c], s_down.at[k]) for k in [(z + d) % 4 for d in range(4)]]
        lines = GradLines(copy, t_gu, SPLITS[1][1], at, (far_a, near_a, far_b, near_b))
        saves_gu = [
            near(t_gu.at[z, :, c, :, pl.ds(0, SPLITS[1][1])], gu_a),
            near(t_gu.at[:, xh, c, pl.ds(xl * 64, 64), pl.ds(SPLITS[1][1], 2 * HID - SPLITS[1][1])], gu_b),
        ]
        save_op = near(op, op_out)
        load_cot.wait()

        def hidden_back(j, _):
            load_down(j).wait()
            tile = pl.ds(pl.multiple_of(j * 256, 256), 256)
            gh[:, tile] = dot(cot[...].reshape(count, D), t_down[:, :, :, :, tile].reshape(D, 256))
            return 0

        lax.fori_loop(0, pairs, hidden_back, 0)
        last_down.wait()
        tile = pl.ds(256 * pairs, HID - 256 * pairs)
        gh[:, tile] = dot(cot[...].reshape(count, D), t_down[:, :, :, :, tile].reshape(D, HID - 256 * pairs))
        load_two.wait()

        def gate_up(j):
            load_gu(j).wait()
            both = pl.ds(pl.multiple_of(j * 256, 256), 256)
            return dot(two[...].reshape(count, D), t_gu[:, :, :, :, both].reshape(D, 256))

        def activate(j, act):
            both = pl.ds(pl.multiple_of(j * 256, 256), 256)
            one = pl.ds(pl.multiple_of(j * 128, 128), 128)
            gate, up = act[:, :128], act[:, 128:]
            back = gh[:, one]
            sigmoid = jax.nn.sigmoid(gate)
            silu = gate * sigmoid
            hid[:, one] = (silu * up).astype(BF16)
            grad_gate = back * up * sigmoid * (1.0 + gate * (1.0 - sigmoid))
            gu[:, both] = jnp.concatenate([grad_gate, back * silu], 1).astype(BF16)

        def hidden(j, _):
            activate(j, gate_up(j))
            return 0

        lax.fori_loop(0, tiles_gu, hidden, 0)

        def part_two(k, _):
            cols = pl.ds(pl.multiple_of(k * 512, 512), 512)
            part[:, :, cols] = dot(gu[...], t_gu[k].reshape(512, 2 * HID), NT).astype(BF16).reshape(4, rows, 512)
            return 0

        lax.fori_loop(0, 4, part_two, 0)
        meet(partners)
        for ring in rings:
            ring.start()

        def part_out(k, _):
            cols = pl.ds(pl.multiple_of(k * 512, 512), 512)
            op[:, :, cols] = dot(hid[...], t_down[k].reshape(512, HID), NT).astype(BF16).reshape(4, rows, 512)
            return 0

        def terms_gu(d):
            k = (z + d) % 4
            cols = pl.ds(pl.multiple_of(k * 512, 512), 512)
            turned[...] = jnp.transpose(two[:, :, cols].reshape(count, 512))

            def some(j, _):
                tile = pl.ds(pl.multiple_of(j * 256, 256), 256)
                t_gu[k, :, :, :, tile] = dot(turned[...], gu[:, tile]).astype(BF16).reshape(2, 2, 128, 256)
                return 0

            lax.fori_loop(0, 2 * HID // 256, some, 0)
            cores[d][0].start()

        def terms_down(d):
            k = (z + d) % 4
            cols = pl.ds(pl.multiple_of(k * 512, 512), 512)
            turned[...] = jnp.transpose(cot[:, :, cols].reshape(count, 512))

            def more(j, width=256):
                tile = pl.ds(pl.multiple_of(j * 256, 256), width)
                t_down[k, :, :, :, tile] = dot(turned[...], hid[:, tile]).astype(BF16).reshape(2, 2, 128, width)
                return 0

            lax.fori_loop(0, pairs, lambda j, _: more(j), 0)
            more(pairs, HID - 256 * pairs)
            cores[d][1].start()

        def add_gu(d):
            k = (z + d) % 4
            cores[d][0].wait_recv()
            add_up(t_gu.at[k, :, c], rc_gu.at[k])

        line_a, line_b = lines.lines
        terms_gu(2)
        terms_gu(1)
        for ring in rings:
            ring.turn()
        add_gu(2)
        for cp in line_a.far:
            cp.start()
        terms_gu(3)
        add_gu(1)
        terms_gu(0)
        add_gu(3)
        for cp in line_a.near:
            cp.start()
        add_gu(0)
        line_b.start()
        for cp in load_rows:
            cp.wait()
        for k in range(2):
            rings[k].finish()

            def back(r, _, k=k):
                rs, half = pl.ds(k * (rows // 2) + r * 32, 32), pl.ds(r * 32, 32)
                v = mid_ref[rs]
                inv = lax.rsqrt(jnp.mean(v * v, -1, keepdims=True) + EPS)
                v = v * inv
                g = rings[k].rows(half)
                value = own_cot[rs].astype(F32) + inv * (g - v * jnp.mean(g * v, -1, keepdims=True))
                gm_ref[rs] = value
                branch[rs] = value.astype(BF16)
                return 0

            lax.fori_loop(0, rows // 64, back, 0)
            gathers[k].start()
        own.start()
        save_gm = near(gm_ref, gm_hbm)
        save_gm.start()
        lax.fori_loop(0, 4, part_out, 0)
        save_op.start()
        for gather in gathers:
            gather.turn()
        line_a.turn()
        terms_down(2)
        terms_down(1)
        line_b.turn()
        terms_down(3)
        terms_down(0)
        for d in (2, 1, 3, 0):
            cores[d][1].wait_recv()
            add_up(t_down.at[(z + d) % 4, :, c], rc_down.at[(z + d) % 4])
            saves[d].start()
        for gather in gathers:
            gather.near()
            gather.far()
        lines.finish()
        for cp in saves_gu:
            cp.start()
        own.wait()
        save_gm.wait()
        save_op.wait()
        for cp in saves + saves_gu:
            cp.wait()
        for pair in cores:
            for cp in pair:
                cp.wait_send()
        lines.sent()
        for ring in rings + gathers:
            ring.sent()

    anywhere, vmem = pl.BlockSpec(memory_space=pl.ANY), pl.BlockSpec(memory_space=pltpu.VMEM)
    copies = 24 + 8 + 12
    return pl.pallas_call(
        kernel,
        out_shape=[
            struct((4, rows, D)),
            struct((rows, D), F32),
            struct((2, 128, SPLITS[1][1])),
            struct((4, 64, 2 * HID - SPLITS[1][1])),
            struct((4, 2, 128, HID)),
            struct((4, rows, D)),
        ],
        in_specs=[anywhere] * 6,
        out_specs=[anywhere] * 6,
        scratch_shapes=[
            pltpu.VMEM((4, rows, D), BF16),
            pltpu.VMEM((2, rows, D // 2), BF16),
            pltpu.VMEM((2, rows, D), BF16),
            pltpu.VMEM((4, rows, D), BF16),
            pltpu.VMEM((count, 2 * HID), BF16),
            pltpu.VMEM((4, rows, D), BF16),
            pltpu.VMEM((count, HID), BF16),
            pltpu.VMEM((count, HID), F32),
            pltpu.VMEM((512, count), BF16),
            pltpu.VMEM((4, 2, 2, 128, 2 * HID), BF16),
            pltpu.VMEM((4, 2, 2, 128, HID), BF16),
            pltpu.VMEM((4, 2, 128, 2 * HID), BF16),
            pltpu.VMEM((4, 2, 128, HID), BF16),
            pltpu.VMEM((rows, D), BF16),
            pltpu.VMEM((4, rows, D), BF16),
            pltpu.VMEM((rows, D), F32),
            pltpu.VMEM((rows, D), BF16),
            pltpu.VMEM((rows, D), F32),
            *line_buffers(2 * HID, SPLITS[1][1]),
            pltpu.SemaphoreType.DMA((copies,)),
            pltpu.SemaphoreType.DMA((copies,)),
            pltpu.SemaphoreType.DMA((18,)),
            pltpu.SemaphoreType.DMA((tiles_gu + pairs + 1,)),
        ],
        name="feed_forward",
        compiler_params=pltpu.CompilerParams(
            collective_id=ident, has_side_effects=True, vmem_limit_bytes=VMEM_LIMIT
        ),
    )(seq_two, seq_cot, gu_w, down_w, middle, cotangent)


def own_rows(attn_gain, mlp_gain, attn_in, mlp_in, proj, gu, down, out):
    def kernel(one_ref, two_ref, in_ref, mlp_ref, proj_ref, gu_ref, down_ref, out_ref, g_in, g_mlp, g_down, g_out, g_gain):
        gain_one, gain_two = column(one_ref), column(two_ref)
        lane = lax.broadcasted_iota(jnp.int32, (16, 128), 1)
        low = lane < 64

        def put(dst, weights, at, value, gain, total):
            cols = pl.ds(at, 128)
            dst[:, cols] = value * gain
            return total + value * weights[:, cols].astype(F32)

        first = jnp.zeros((16, 128), F32)
        for k in range(TP):
            for j in range(Q_COLS // 128):
                value = proj_ref[k, :, pl.ds(j * 128, 128)].astype(F32)
                first = put(g_in, in_ref, k * Q_COLS + j * 128, value, gain_one, first)
        for k in range(0, TP, 2):
            even = proj_ref[k, :, pl.ds(Q_COLS, 128)].astype(F32)
            odd = proj_ref[k + 1, :, pl.ds(Q_COLS, 128)].astype(F32)
            key = jnp.where(low, even, pltpu.roll(odd, 64, 1))
            value = jnp.where(low, pltpu.roll(even, 64, 1), odd)
            first = put(g_in, in_ref, D + k * 64, key, gain_one, first)
            first = put(g_in, in_ref, D + HEAD_DIM * KV_HEADS + k * 64, value, gain_one, first)
        second = jnp.zeros((16, 128), F32)
        for k in range(TP):
            for j in range(HID // 128):
                for half in range(2):
                    value = gu_ref[k, :, pl.ds(j * 256 + half * 128, 128)].astype(F32)
                    second = put(g_mlp, mlp_ref, half * FF + k * HID + j * 128, value, gain_two, second)
            g_down[:, pl.ds(k * HID, HID)] = down_ref[k].astype(F32)
        g_out[...] = out_ref[...].astype(F32)
        sums = jnp.sum(first, -1, keepdims=True), jnp.sum(second, -1, keepdims=True)
        g_gain[...] = jnp.transpose(jnp.where(lane == 0, sums[0], sums[1]))[0:8]

    shapes = [(16, attn_in.shape[1]), (16, 2 * FF), (16, FF), (16, D), (8, 16)]
    return pl.pallas_call(
        kernel,
        out_shape=[struct(shape, F32) for shape in shapes],
        in_specs=[pl.BlockSpec(memory_space=pltpu.VMEM)] * 8,
        out_specs=[pl.BlockSpec(memory_space=pltpu.VMEM)] * 5,
        name="own_rows",
        compiler_params=pltpu.CompilerParams(vmem_limit_bytes=VMEM_LIMIT),
    )(attn_gain, mlp_gain, attn_in, mlp_in, proj, gu, down, out)


def shards(tokens, positions, attn_in, attn_out, attn_gain, mlp_in, mlp_down, mlp_gain, cotangent):
    rows = tokens.shape[0]
    count = 4 * rows
    attn_gain, mlp_gain = attn_gain[None], mlp_gain[None]
    lanes = np.arange(128)
    freqs = np.zeros((8, 128), np.float32)
    freqs[0] = np.float32(ROPE_BASE) ** (-2.0 * (lanes % 32).astype(np.float32) / HEAD_DIM)
    freqs[1] = np.where(lanes % 64 < 32, -1.0, 1.0)
    (normed_one_all, cot_all, proj_w, gu_w, down_w, out_w, q_all, kv_all, attended_low, lse, cosines, sines, bias_all, middle, two_all) = (
        forward_attention(tokens, cotangent, positions[None], freqs, attn_gain, mlp_gain, attn_in, mlp_in, mlp_down, attn_out, 0)
    )
    branch_all, grad_middle, gu_a, gu_b, sum_down, out_part = feed_forward(
        two_all, cot_all, gu_w, down_w, middle, cotangent, 1
    )
    outputs, input_grad, own_proj, own_gu, own_down, own_out = backward_attention(
        gu_a, gu_b, sum_down, out_part, branch_all, grad_middle, middle, tokens,
        cosines, sines, bias_all, q_all, kv_all.reshape(2 * count, 128), attended_low, lse, normed_one_all, proj_w, out_w, 2,
    )
    grad_in, grad_mlp, grad_down, grad_out, grad_gains = own_rows(
        attn_gain, mlp_gain, attn_in, mlp_in, own_proj, own_gu, own_down, own_out
    )
    return outputs, input_grad, grad_in, grad_out, grad_gains[0], grad_mlp, grad_down, grad_gains[1]


def solution(mesh):
    both = ("dp", "ctx")
    wide, flat = P(both, None), P(both)
    in_specs = (wide, flat, wide, wide, flat, wide, wide, flat, wide)
    out_specs = (wide, wide, wide, wide, flat, wide, wide, flat)
    return jax.shard_map(shards, mesh=mesh, in_specs=in_specs, out_specs=out_specs, check_vma=False)
```

```python
import jax
import jax.numpy as jnp
import numpy as np
from jax import lax
from jax.experimental import pallas as pl
from jax.experimental.pallas import tpu as pltpu
from jax.sharding import PartitionSpec as P


D = 2048
HEADS = 32
KV_HEADS = 4
HEAD_DIM = 64
FF = 5632
REPEAT = HEADS // KV_HEADS
TP = 4
Q_COLS = D // TP
PROJ = Q_COLS + 2 * HEAD_DIM
HID = FF // TP

EPS = 1e-05
ROPE_BASE = 10000.0
NEG_FILL = -1e30

MESH = pl.DeviceIdType.MESH
BF16 = jnp.bfloat16
F32 = jnp.float32

SPLITS = ((PROJ, 384), (2 * HID, 13 * 128), (HID, 640))
OUT_SPLIT = 1024
VMEM_LIMIT = 60 << 20

NN = ((1,), (0,))
NT = ((1,), (1,))
TN = ((0,), (0,))


def place():
    dp, ctx = lax.axis_index("dp"), lax.axis_index("ctx")
    return (dp // 2) % 2, ctx // 4, ctx % 4, dp // 4, dp % 2


def device(xh, xl, y, z, c):
    return (z * 4 + xh * 2 + c, xl * 4 + y)


def along_y(d):
    def to(xh, xl, y, z, c):
        return xh, xl, (y + d) % 4, z, c

    return to


def along_x(d):
    def to(xh, xl, y, z, c):
        x = (xh * 2 + xl + d) % 4
        return x // 2, x % 2, y, z, c

    return to


def along_z(d):
    def to(xh, xl, y, z, c):
        return xh, xl, y, (z + d) % 4, c

    return to


def sibling(xh, xl, y, z, c):
    return xh, xl, y, z, 1 - c


def half_partner(xh, xl, y, z, c):
    return xh, 1 - xl, y, z, c


def crossed(xh, xl, y, z, c):
    return xh, xl, z, y, c


def say_hello(routes, cross=False):
    here = place()
    barrier = pltpu.get_barrier_semaphore()
    for back in routes:
        pl.semaphore_signal(barrier, inc=1, device_id=device(*back(*here)), device_id_type=MESH)
    if cross:

        @pl.when(here[2] != here[3])
        def _():
            pl.semaphore_signal(barrier, inc=1, device_id=device(*crossed(*here)), device_id_type=MESH)


def meet(routes, cross=False):
    here = place()
    barrier = pltpu.get_barrier_semaphore()
    if not cross:
        pl.semaphore_wait(barrier, len(routes))
        return
    away = here[2] != here[3]

    @pl.when(away)
    def _():
        pl.semaphore_wait(barrier, len(routes) + 1)

    @pl.when(jnp.logical_not(away))
    def _():
        pl.semaphore_wait(barrier, len(routes))


ALL_LINES = [along(d) for along in (along_y, along_x, along_z) for d in (1, 2, 3)] + [sibling]


class Copies:
    def __init__(self, send, recv):
        self.send, self.recv, self.count = send, recv, 0

    def __call__(self, src, dst, to):
        k, self.count = self.count, self.count + 1
        return pltpu.make_async_remote_copy(
            src_ref=src,
            dst_ref=dst,
            send_sem=self.send.at[k],
            recv_sem=self.recv.at[k],
            device_id=device(*to(*place())),
            device_id_type=MESH,
        )


def comm_call(kernel, name, ident, ins, outs, copies, locals_=0):
    return pl.pallas_call(
        kernel,
        out_shape=outs,
        in_specs=[pl.BlockSpec(memory_space=pl.ANY)] * len(ins),
        out_specs=[pl.BlockSpec(memory_space=pl.ANY)] * len(outs),
        scratch_shapes=[
            pltpu.SemaphoreType.DMA((copies,)),
            pltpu.SemaphoreType.DMA((copies,)),
            pltpu.SemaphoreType.DMA((max(locals_, 1),)),
        ],
        name=name,
        compiler_params=pltpu.CompilerParams(collective_id=ident, has_side_effects=True),
    )(*ins)


def struct(shape, dtype=BF16):
    return jax.ShapeDtypeStruct(shape, dtype)


class RingGather:
    def __init__(self, copy, own, dst, y):
        half = dst.shape[2] // 2
        lo, hi = pl.ds(0, half), pl.ds(half, half)
        back, on = (y + 3) % 4, (y + 1) % 4

        def first(cols, to):
            return copy(own.at[:, cols], dst.at[y, :, cols], to)

        def one(slot, cols, to):
            at = dst.at[slot, :, cols]
            return copy(at, at, to)

        self.first = [first(lo, along_y(1)), first(hi, along_y(3)), first(hi, along_y(1)), first(lo, along_y(3))]
        self.second = [one(back, lo, along_y(1)), one(on, hi, along_y(3))]

    def start(self):
        for cp in self.first:
            cp.start()

    def turn(self):
        for got, cp in zip(self.first, self.second):
            got.wait_recv()
            cp.start()

    def near(self):
        for cp in self.first[2:]:
            cp.wait_recv()

    def far(self):
        for cp in self.second:
            cp.wait_recv()

    def sent(self):
        for cp in self.first + self.second:
            cp.wait_send()


class RingSum:
    def __init__(self, copy, part, halves, whole, y):
        half = part.shape[2] // 2
        lo, hi = pl.ds(0, half), pl.ds(half, half)
        self.part, self.halves, self.whole, self.y = part, halves, whole, y
        self.cols = (lo, hi)
        far, on, back = (y + 2) % 4, (y + 1) % 4, (y + 3) % 4
        self.far = [
            copy(part.at[far, :, lo], halves.at[0], along_y(1)),
            copy(part.at[far, :, hi], halves.at[1], along_y(3)),
        ]
        self.near = [
            copy(part.at[on, :, hi], whole.at[0, :, hi], along_y(1)),
            copy(part.at[back, :, lo], whole.at[1, :, lo], along_y(3)),
        ]
        self.last = [
            copy(part.at[on, :, lo], whole.at[0, :, lo], along_y(1)),
            copy(part.at[back, :, hi], whole.at[1, :, hi], along_y(3)),
        ]
        self.slots = (on, back)

    def start(self):
        for cp in self.far + self.near:
            cp.start()

    def turn(self):
        for k in range(2):
            self.far[k].wait_recv()
            slot, cols = self.slots[k], self.cols[k]

            def body(r, _, slot=slot, cols=cols, k=k):
                rows = pl.ds(r * 32, 32)
                both = self.part[slot, rows, cols].astype(F32) + self.halves[k, rows].astype(F32)
                self.part[slot, rows, cols] = both.astype(BF16)
                return 0

            lax.fori_loop(0, self.part.shape[1] // 32, body, 0)
            self.last[k].start()

    def finish(self):
        for cp in self.near + self.last:
            cp.wait_recv()

    def rows(self, rows):
        own = self.part[self.y, rows].astype(F32)
        return own + self.whole[0, rows].astype(F32) + self.whole[1, rows].astype(F32)

    def sent(self):
        for cp in self.far + self.near + self.last:
            cp.wait_send()


class Gather:
    def __init__(self, copy, out, a, at, rows_only=False):
        xh, xl, y, z, c = at
        cols = out.shape[-1]
        left, right = pl.ds(0, a), pl.ds(a, cols - a)
        def cut(half, n):
            return slice(None) if half is None else pl.ds(half * (n // 2), n // 2)

        if rows_only:
            block = lambda z, x, c, cols: out.at[x[0], c, x[1], z, :, cols]
            z_line = lambda x, c, cols, half: out.at[x[0], c, x[1], cut(half, 4), :, cols]
            x_line = lambda z, c, cols, half: out.at[cut(half, 2), c, :, z, :, cols]
        else:
            block = lambda z, x, c, cols: out.at[z, x[0], c, pl.ds(x[1] * 64, 64), cols]
            z_line = lambda x, c, cols, half: out.at[cut(half, 4), x[0], c, pl.ds(x[1] * 64, 64), cols]
            x_line = lambda z, c, cols, half: out.at[z, cut(half, 2), c, :, cols]

        def same(ref, to):
            return copy(ref, ref, to)

        here = (xh, xl)
        self.first = []
        for d in (1, 3, 2):
            self.first.append(same(block(z, here, c, left), along_x(d)))
            self.first.append(same(block(z, here, c, right), along_z(d)))
        a_lo, a_hi = lambda z: x_line(z, c, left, 0), lambda z: x_line(z, c, left, 1)
        b_lo, b_hi = lambda x: z_line(x, c, right, 0), lambda x: z_line(x, c, right, 1)
        z_at = [(z + d) % 4 for d in range(4)]
        x_at = [along_x(d)(*at)[:2] for d in range(4)]
        self.lines = []
        for lo, hi, spots, along in ((a_lo, a_hi, z_at, along_z), (b_lo, b_hi, x_at, along_x)):
            going = [
                same(lo(spots[0]), along(1)),
                same(hi(spots[0]), along(3)),
                same(hi(spots[0]), along(1)),
                same(lo(spots[0]), along(3)),
            ]
            on = [same(lo(spots[3]), along(1)), same(hi(spots[1]), along(3))]
            self.lines.append((going, on))
        self.core = [same(block(z, here, c, pl.ds(0, cols)), sibling)]
        for d in (1, 3, 2):
            self.core.append(same(block(z, x_at[d], c, left), sibling))
            self.core.append(same(block(z_at[d], here, c, right), sibling))
        self.core_lines = []
        for d in (3, 1, 2):
            self.core_lines.append(
                (same(x_line(z_at[d], c, left, None), sibling), same(z_line(x_at[d], c, right, None), sibling))
            )

    def start(self):
        for cp in self.first:
            cp.start()
        self.core[0].start()

    def turn(self, *which):
        for k in which or (0, 1):
            for cp in self.first[k::2]:
                cp.wait_recv()
            for cp in self.lines[k][0]:
                cp.start()
            for cp in self.core[1 + k :: 2]:
                cp.start()

    def pass_on(self):
        for going, on in self.lines:
            for got, cp in zip(going[:2], on):
                got.wait_recv()
                cp.start()

    def near(self):
        for k, (going, _) in enumerate(self.lines):
            for side in range(2):
                going[2 + side].wait_recv()
                self.core_lines[side][k].start()

    def far(self):
        for k, (_, on) in enumerate(self.lines):
            for cp in on:
                cp.wait_recv()
            self.core_lines[2][k].start()

    def finish(self):
        for cp in self.core + [cp for pair in self.core_lines for cp in pair]:
            cp.wait_recv()

    def sent(self):
        for going, on in self.lines:
            for cp in going + on:
                cp.wait_send()
        for cp in self.first + self.core + [cp for pair in self.core_lines for cp in pair]:
            cp.wait_send()


def dot(left, right, dims=((1,), (0,))):
    return lax.dot_general(left, right, (dims, ((), ())), preferred_element_type=F32)


def column(row_ref):
    row = jnp.broadcast_to(row_ref[...].astype(F32), (16, 16))
    diagonal = lax.broadcasted_iota(jnp.int32, (16, 16), 0) == lax.broadcasted_iota(jnp.int32, (16, 16), 1)
    return jnp.sum(jnp.where(diagonal, row, 0.0), 1, keepdims=True)


def swap_halves(v):
    lane = lax.broadcasted_iota(jnp.int32, v.shape, 1)
    return jnp.where(lane % 64 < 32, pltpu.roll(v, 96, 1), pltpu.roll(v, 32, 1))


def forward_attention(tokens, cotangent, positions, freqs, attn_gain, mlp_gain, attn_in, mlp_in, mlp_down, out_rows, ident):
    rows = tokens.shape[0]
    count = 4 * rows

    def kernel(
        tok_ref, cot_ref, spot_ref, freq_ref, one_ref, two_ref, in_ref, mlp_ref, down_ref, wo,
        normed_out, cot_all, gp, gg, gd, go, q_out, kv_out, att_out, lse_out, cos_out, sin_out, bias_out, middle_hbm, two_all,
        wp, wg, wd, tok, normed, wp_v, wo_v, q_s, kv, vx, bias, att, part, halves, whole, spot_all, own_two, middle_out, cos_s, sin_s, bias_t, send, recv, local,
    ):
        say_hello(ALL_LINES, True)
        at = place()
        xh, xl, y, z, c = at
        copy = Copies(send, recv)
        slot = pl.ds(xl * 64 + y * 16, 16)
        nlocal = [0]

        def near(src, dst):
            cp = pltpu.make_async_copy(src, dst, local.at[nlocal[0]])
            nlocal[0] += 1
            return cp

        to_y = []
        stay = []
        for i, o in ((wp, gp), (wg, gg), (wd, gd)):
            to_y.append([copy(i.at[(y + d) % 4], o.at[z, xh, c, slot], along_y(d)) for d in (1, 3, 2)])
            stay.append(near(i.at[y], o.at[z, xh, c, slot]))
        over = copy(wo, go.at[xh, c, xl, y], crossed)
        keep = near(wo, go.at[xh, c, xl, z])
        spot_copies = [copy(spot_all.at[y], spot_all.at[y], along_y(d)) for d in (1, 3, 2)]
        tok_ring = RingGather(copy, tok_ref, tok, y)
        cot_ring = RingGather(copy, cot_ref, cot_all, y)
        row_halves = [pl.ds(0, rows // 2), pl.ds(rows // 2, rows // 2)]
        two_rings = [RingGather(copy, own_two.at[r], two_all.at[:, r], y) for r in row_halves]
        branches = [RingSum(copy, part.at[:, r], halves.at[:, r], whole.at[:, r], y) for r in row_halves]
        kv_copy = copy(kv.at[1], kv.at[0], half_partner)
        g_proj = Gather(copy, gp, SPLITS[0][1], at)
        g_gu = Gather(copy, gg, SPLITS[1][1], at)
        g_down = Gather(copy, gd, SPLITS[2][1], at)
        g_out = Gather(copy, go, OUT_SPLIT, at, True)

        cot_own = near(cot_ref, cot_all.at[y])
        tok_own = near(tok_ref, tok.at[y])
        tok_own.start()
        cot_own.start()
        spot_all[y] = jnp.broadcast_to(spot_ref[...].astype(F32), (8, rows))

        gain_one, gain_two = column(one_ref), column(two_ref)
        low_lanes = lax.broadcasted_iota(jnp.int32, (16, 128), 1) < 64
        for k in range(TP):
            qs = pl.ds(k * Q_COLS, Q_COLS)
            wp[k, :, pl.ds(0, Q_COLS)] = (in_ref[:, qs].astype(F32) * gain_one).astype(BF16)
            key = in_ref[:, pl.ds(D + (k // 2) * 128, 128)].astype(F32)
            value = in_ref[:, pl.ds(D + HEAD_DIM * KV_HEADS + (k // 2) * 128, 128)].astype(F32)
            if k % 2 == 0:
                both = jnp.where(low_lanes, key, pltpu.roll(value, 64, 1))
            else:
                both = jnp.where(low_lanes, pltpu.roll(key, 64, 1), value)
            wp[k, :, pl.ds(Q_COLS, 128)] = (both * gain_one).astype(BF16)
        stay[0].start()
        for k in range(TP):
            for j in range(HID // 128):
                for half in range(2):
                    cols = pl.ds(half * FF + k * HID + j * 128, 128)
                    tile = (mlp_ref[:, cols].astype(F32) * gain_two).astype(BF16)
                    wg[k, :, pl.ds(j * 256 + half * 128, 128)] = tile
            wd[k] = down_ref[:, pl.ds(k * HID, HID)]
        for cp in stay[1:]:
            cp.start()
        meet(ALL_LINES, True)
        away = y != z
        for cp in to_y[0]:
            cp.start()

        @pl.when(away)
        def _():
            over.start()

        @pl.when(jnp.logical_not(away))
        def _():
            keep.start()

        for cp in spot_copies + to_y[1] + to_y[2] + tok_ring.first:
            cp.start()

        def norm_block(k):
            def body(r, _):
                rs = pl.ds(r * 32, 32)
                v = tok[k, rs].astype(F32)
                inv = lax.rsqrt(jnp.mean(v * v, -1, keepdims=True) + EPS)
                normed[k, rs] = (v * inv).astype(BF16)
                return 0

            lax.fori_loop(0, rows // 32, body, 0)

        stay[0].wait()
        for cp in to_y[0]:
            cp.wait_recv()
        g_proj.start()

        @pl.when(away)
        def _():
            over.wait()

        @pl.when(jnp.logical_not(away))
        def _():
            keep.wait()

        g_out.start()
        tok_own.wait()
        norm_block(y)
        g_proj.turn()
        stay[1].wait()
        for cp in to_y[1]:
            cp.wait_recv()
        g_gu.start()
        g_proj.pass_on()
        stay[2].wait()
        for cp in to_y[2]:
            cp.wait_recv()
        g_down.start()
        g_out.turn()
        for cp in spot_copies:
            cp.wait_recv()
        tok_ring.turn()
        g_proj.near()
        g_proj.far()

        cos, sin = [], []
        freq, sign = freq_ref[0:1, :], freq_ref[1:2, :]
        spot_cols = []
        for k in range(4):
            col = jnp.transpose(jnp.broadcast_to(spot_all[k, 0:1, :], (128, 128)))
            spot_cols.append(col)
            cos.append(jnp.cos(col * freq))
            sin.append(jnp.sin(col * freq) * sign)
        cos, sin = jnp.concatenate(cos, 0), jnp.concatenate(sin, 0)
        cos_s[...] = cos
        sin_s[...] = sin
        turn_saves = [near(cos_s, cos_out), near(sin_s, sin_out)]
        for cp in turn_saves:
            cp.start()
        low_half = xl == 0
        reach = jnp.where(low_half, -1.0, 2048.0)
        for k in range(4):
            for j in range(8):
                row = lax.broadcasted_iota(jnp.int32, (128, 128), 0) + k * 128
                col = lax.broadcasted_iota(jnp.int32, (128, 128), 1) + j * 128
                apart = (row - col + 512).astype(F32)
                seen = apart <= spot_cols[k]
                if j < 4:
                    seen = seen & (apart <= reach)
                else:
                    seen = seen & (col - 512 <= row)
                bias[pl.ds(k * 128, 128), pl.ds(j * 128, 128)] = jnp.where(seen, 0.0, NEG_FILL)

        g_proj.finish()
        wp_load = near(gp, wp_v)
        wp_load.start()
        g_out.pass_on()
        tok_ring.near()
        norm_block((y + 3) % 4)
        norm_block((y + 1) % 4)
        g_out.near()
        tok_ring.far()
        cot_ring.start()
        norm_block((y + 2) % 4)
        normed_save = near(normed, normed_out)
        normed_save.start()

        g_gu.turn(0)
        g_down.turn(0)

        wp_load.wait()
        left = normed[...].reshape(count, D)
        lane = lax.broadcasted_iota(jnp.int32, (count, 128), 1)
        upper = lane >= 64
        raw = dot(left, wp_v[:, :, :, :, pl.ds(Q_COLS, 128)].reshape(D, 128))
        turned = raw * jnp.where(upper, 1.0, cos) + swap_halves(raw) * jnp.where(upper, 0.0, sin)
        kv[1] = turned.astype(BF16)
        kv_copy.start()
        g_out.far()
        g_gu.turn(1)
        g_down.turn(1)
        for j in range(2):
            raw2 = dot(left, wp_v[:, :, :, :, pl.ds(j * 256, 256)].reshape(D, 256))
            for e in range(2):
                raw = raw2[:, e * 128 : e * 128 + 128]
                turned = (raw * cos + swap_halves(raw) * sin).astype(BF16).astype(F32) * (HEAD_DIM ** (-0.5))
                pair = j * 2 + e
                q_s[2 * pair] = jnp.where(upper, 0.0, turned).astype(BF16)
                q_s[2 * pair + 1] = jnp.where(upper, 0.0, pltpu.roll(turned, 64, 1)).astype(BF16)
        kv_copy.wait_recv()
        for k in range(2):
            vx[k] = jnp.where(upper, kv[k].astype(F32), 1.0).astype(BF16)
        q_save = near(q_s, q_out)
        q_save.start()
        kv_save = near(kv, kv_out)
        kv_save.start()
        g_out.finish()
        wo_load = near(go, wo_v)
        wo_load.start()

        def attend(pair):
            for b in range(2):
                rs = pl.ds(b * 256, 256)
                seen = 256 * (b + 1)
                lane = lax.broadcasted_iota(jnp.int32, (256, 128), 1) < 64
                found = []
                for e in range(2):
                    q = q_s[2 * pair + e, rs]
                    s0 = dot(q, kv[0], NT) + bias[rs, pl.ds(0, 512)]
                    s1 = dot(q, kv[1, pl.ds(0, seen)], NT) + bias[rs, pl.ds(512, seen)]
                    m = jnp.maximum(jnp.max(s0, -1, keepdims=True), jnp.max(s1, -1, keepdims=True))
                    p0 = jnp.exp(s0 - m).astype(BF16)
                    p1 = jnp.exp(s1 - m).astype(BF16)
                    o = dot(p0, vx[0]) + dot(p1, vx[1, pl.ds(0, seen)])
                    r = pltpu.roll(o, 64, 1)
                    found.append((o, r))
                    log_total = m + jnp.log(jnp.where(lane, o, r))
                    lse_out[2 * pair + e, :, rs] = jnp.transpose(log_total)[0:8]
                (o, r), (o2, r2) = found
                both = jnp.where(lane, r / o, o2 / r2)
                att[rs, pl.ds(pl.multiple_of(pair * 128, 128), 128)] = both.astype(BF16)

        def two_pairs(k):
            def body(i, _):
                attend(2 * k + i)
                return 0

            lax.fori_loop(0, 2, body, 0)

        two_pairs(0)
        cot_ring.turn()
        two_pairs(1)
        att_save = near(att, att_out)
        att_save.start()
        wo_load.wait()

        for j in range(4):
            cols = pl.ds(j * 512, 512)
            w = wo_v[:, :, :, :, :, cols].reshape(Q_COLS, 512)
            part[:, :, cols] = dot(att[...], w).astype(BF16).reshape(4, rows, 512)
        for branch in branches:
            branch.start()

        for k in range(4):
            for j in range(8):
                key = lax.broadcasted_iota(jnp.int32, (128, 128), 0) + j * 128
                row = lax.broadcasted_iota(jnp.int32, (128, 128), 1) + k * 128
                apart = (row - key + 512).astype(F32)
                seen = apart <= spot_all[k, 0:1, :]
                if j < 4:
                    seen = seen & (apart <= reach)
                else:
                    seen = seen & (key - 512 <= row)
                bias_t[pl.ds(j * 128, 128), pl.ds(k * 128, 128)] = jnp.where(seen, 0.0, NEG_FILL)
        bias_save = near(bias_t, bias_out)
        bias_save.start()
        g_gu.pass_on()
        g_down.pass_on()
        for branch in branches:
            branch.turn()
        g_gu.near()
        g_down.near()
        cot_ring.near()
        cot_ring.far()
        two_own = near(own_two, two_all.at[y])
        for k in range(2):
            branches[k].finish()

            def mid(r, _, k=k):
                rs, half = pl.ds(k * (rows // 2) + r * 32, 32), pl.ds(r * 32, 32)
                v = tok_ref[rs].astype(F32) + branches[k].rows(half)
                middle_out[rs] = v
                inv = lax.rsqrt(jnp.mean(v * v, -1, keepdims=True) + EPS)
                own_two[rs] = (v * inv).astype(BF16)
                return 0

            lax.fori_loop(0, rows // 64, mid, 0)
            two_rings[k].start()
        two_own.start()
        middle_save = near(middle_out, middle_hbm)
        middle_save.start()
        for ring in two_rings:
            ring.turn()
        g_gu.far()
        g_down.far()
        for ring in two_rings:
            ring.near()
            ring.far()
        g_gu.finish()
        g_down.finish()
        for cp in (cot_own, normed_save, q_save, kv_save, att_save, two_own, middle_save, bias_save, *turn_saves):
            cp.wait()
        for group in to_y:
            for cp in group:
                cp.wait_send()
        for cp in spot_copies + [kv_copy]:
            cp.wait_send()
        for thing in (g_proj, g_out, g_gu, g_down, tok_ring, cot_ring, *two_rings, *branches):
            thing.sent()

    anywhere, vmem = pl.BlockSpec(memory_space=pl.ANY), pl.BlockSpec(memory_space=pltpu.VMEM)
    outs = [
        (struct((4, rows, D)), anywhere),
        (struct((4, rows, D)), anywhere),
        (struct((4, 2, 2, 128, PROJ)), anywhere),
        (struct((4, 2, 2, 128, 2 * HID)), anywhere),
        (struct((4, 2, 2, 128, HID)), anywhere),
        (struct((2, 2, 2, 4, 16, D)), anywhere),
        (struct((REPEAT, count, 128)), anywhere),
        (struct((2, count, 128)), anywhere),
        (struct((count, Q_COLS)), anywhere),
        (struct((REPEAT, 8, count), F32), vmem),
        (struct((count, 128), F32), anywhere),
        (struct((count, 128), F32), anywhere),
        (struct((2 * count, count), F32), anywhere),
        (struct((rows, D), F32), anywhere),
        (struct((4, rows, D)), anywhere),
    ]
    copies = 9 + 1 + 3 + 6 * 6 + 1 + 31 * 4
    return pl.pallas_call(
        kernel,
        out_shape=[o[0] for o in outs],
        in_specs=[vmem] * 10,
        out_specs=[o[1] for o in outs],
        scratch_shapes=[
            pltpu.VMEM((TP, 16, PROJ), BF16),
            pltpu.VMEM((TP, 16, 2 * HID), BF16),
            pltpu.VMEM((TP, 16, HID), BF16),
            pltpu.VMEM((4, rows, D), BF16),
            pltpu.VMEM((4, rows, D), BF16),
            pltpu.VMEM((4, 2, 2, 128, PROJ), BF16),
            pltpu.VMEM((2, 2, 2, 4, 16, D), BF16),
            pltpu.VMEM((REPEAT, count, 128), BF16),
            pltpu.VMEM((2, count, 128), BF16),
            pltpu.VMEM((2, count, 128), BF16),
            pltpu.VMEM((count, 2 * count), F32),
            pltpu.VMEM((count, Q_COLS), BF16),
            pltpu.VMEM((4, rows, D), BF16),
            pltpu.VMEM((2, rows, D // 2), BF16),
            pltpu.VMEM((2, rows, D), BF16),
            pltpu.VMEM((4, 8, 128), F32),
            pltpu.VMEM((rows, D), BF16),
            pltpu.VMEM((rows, D), F32),
            pltpu.VMEM((count, 128), F32),
            pltpu.VMEM((count, 128), F32),
            pltpu.VMEM((2 * count, count), F32),
            pltpu.SemaphoreType.DMA((copies,)),
            pltpu.SemaphoreType.DMA((copies,)),
            pltpu.SemaphoreType.DMA((22,)),
        ],
        name="forward_attention",
        compiler_params=pltpu.CompilerParams(
            collective_id=ident, has_side_effects=True, vmem_limit_bytes=VMEM_LIMIT
        ),
    )(tokens, cotangent, positions, freqs, attn_gain, mlp_gain, attn_in, mlp_in, mlp_down, out_rows)


def tiles(ref):
    if len(ref.shape) == 2:
        return [ref]
    return [t for k in range(ref.shape[0]) for t in tiles(ref.at[k])]


def add_up(dst, *others):
    for out, *terms in zip(tiles(dst), *[tiles(o) for o in others]):
        rows = out.shape[0]
        step = min(rows, 32)

        def body(r, _, out=out, terms=terms, step=step):
            rs = pl.ds(r * step, step)
            value = out[rs].astype(F32)
            for t in terms:
                value = value + t[rs].astype(F32)
            out[rs] = value.astype(BF16)
            return 0

        lax.fori_loop(0, rows // step, body, 0)


class LineSum:
    def __init__(self, copy, lo, hi, along, far, near):
        self.lo, self.hi, self.far_in, self.near_in = lo, hi, far, near
        self.far = [copy(lo(2), far.at[0], along(1)), copy(hi(2), far.at[1], along(3))]
        self.near = [copy(hi(1), near.at[0, 1], along(1)), copy(lo(3), near.at[1, 0], along(3))]
        self.last = [copy(lo(1), near.at[0, 0], along(1)), copy(hi(3), near.at[1, 1], along(3))]

    def start(self):
        for cp in self.far + self.near:
            cp.start()

    def turn(self):
        self.far[0].wait_recv()
        add_up(self.lo(1), self.far_in.at[0])
        self.last[0].start()
        self.far[1].wait_recv()
        add_up(self.hi(3), self.far_in.at[1])
        self.last[1].start()

    def finish(self):
        for cp in self.near + self.last:
            cp.wait_recv()
        add_up(self.lo(0), self.near_in.at[0, 0], self.near_in.at[1, 0])
        add_up(self.hi(0), self.near_in.at[0, 1], self.near_in.at[1, 1])

    def sent(self):
        for cp in self.far + self.near + self.last:
            cp.wait_send()


class GradLines:
    def __init__(self, copy, terms, a, at, buffers, rows_only=False):
        xh, xl, y, z, c = at
        far_a, near_a, far_b, near_b = buffers
        cols = terms.shape[-1]
        left, right = pl.ds(0, a), pl.ds(a, cols - a)
        x_at = [along_x(d)(*at)[:2] for d in range(4)]
        z_at = [(z + d) % 4 for d in range(4)]
        if rows_only:
            spot = lambda x, z, cols: terms.at[x[0], c, x[1], z, :, cols]
            a_half = lambda h: lambda d: terms.at[h, c, :, z_at[d], :, left]
            b_half = lambda h: lambda d: terms.at[x_at[d][0], c, x_at[d][1], pl.ds(2 * h, 2), :, right]
        else:
            base = (lambda z, xh: (z, xh, c)) if len(terms.shape) == 5 else (lambda z, xh: (z, xh))
            spot = lambda x, z, cols: terms.at[base(z, x[0]) + (pl.ds(x[1] * 64, 64), cols)]
            a_half = lambda h: lambda d: terms.at[base(z_at[d], h) + (slice(None), left)]
            b_half = lambda h: lambda d: terms.at[
                base(pl.ds(2 * h, 2), x_at[d][0]) + (pl.ds(x_at[d][1] * 64, 64), right)
            ]
        self.lines = [
            LineSum(copy, a_half(0), a_half(1), along_z, far_a, near_a),
            LineSum(copy, b_half(0), b_half(1), along_x, far_b, near_b),
        ]
        self.spot_a = lambda x: spot(x, z, left)
        self.spot_b = lambda z: spot(x_at[0], z, right)

    def start(self):
        for line in self.lines:
            line.start()

    def turn(self):
        for line in self.lines:
            line.turn()

    def finish(self):
        for line in self.lines:
            line.finish()

    def sent(self):
        for line in self.lines:
            line.sent()


class GradOwners:
    def __init__(self, copy, local_copy, spot_a, spot_b, out, at, buffers, rows_only=False):
        xh, xl, y, z, c = at
        self.at, self.rows_only = at, rows_only
        got_a, got_b, own = buffers
        a, cols = got_a.shape[-1], own.shape[-1]
        self.second = []
        for d in (1, 3, 2):
            self.second.append(copy(spot_a(along_x(d)(*at)[:2]), got_a.at[d - 1], along_x(d)))
            self.second.append(copy(spot_b((z + d) % 4), got_b.at[d - 1], along_z(d)))
        self.mine = (spot_a((xh, xl)), spot_b(z))
        self.got = (got_a, got_b)
        self.own, self.cuts = own, (pl.ds(0, a), pl.ds(a, cols - a))
        if rows_only:
            self.over = copy(own, out, crossed)
            self.keep = local_copy(own, out)
        else:
            self.to_y = [copy(own.at[(y + d) % 4], out.at[y], along_y(d)) for d in (1, 3, 2)]
            self.keep = local_copy(own.at[y], out.at[y])

    def start(self):
        for cp in self.second:
            cp.start()

    def deliver(self):
        for cp in self.second:
            cp.wait_recv()
        for mine, got, cut in zip(self.mine, self.got, self.cuts):
            value = mine[...].astype(F32)
            for d in range(3):
                value = value + got[d].astype(F32)
            own = self.own
            if self.rows_only:
                own[:, cut] = value.astype(BF16)
            else:
                own[:, :, cut] = value.astype(BF16).reshape(4, 16, value.shape[-1])
        if self.rows_only:
            y, z = self.at[2], self.at[3]

            @pl.when(y != z)
            def _():
                self.over.start()

            @pl.when(y == z)
            def _():
                self.keep.start()

        else:
            for cp in self.to_y:
                cp.start()
            self.keep.start()

    def finish(self):
        if self.rows_only:
            y, z = self.at[2], self.at[3]

            @pl.when(y != z)
            def _():
                self.over.wait()

            @pl.when(y == z)
            def _():
                self.keep.wait()

        else:
            for cp in self.to_y:
                cp.wait()
            self.keep.wait()
        for cp in self.second:
            cp.wait_send()


def line_buffers(cols, a, rows_only=False):
    b = cols - a
    a_half, b_half = ((2, 16), (2, 16)) if rows_only else ((128,), (2, 64))
    return [
        pltpu.VMEM((2,) + a_half + (a,), BF16),
        pltpu.VMEM((2, 2) + a_half + (a,), BF16),
        pltpu.VMEM((2,) + b_half + (b,), BF16),
        pltpu.VMEM((2, 2) + b_half + (b,), BF16),
    ]


def owner_buffers(cols, a, rows_only=False):
    spot, own = (16, (16, cols)) if rows_only else (64, (4, 16, cols))
    return [pltpu.VMEM((3, spot, a), BF16), pltpu.VMEM((3, spot, cols - a), BF16), pltpu.VMEM(own, BF16)]


def backward_attention(
    gu_a, gu_b, sum_down, out_part, branch_all, grad_middle, middle, tokens,
    cosines, sines, bias_all, q_all, kv_all, attended, lse, normed_all, proj_w, out_w, ident,
):
    rows = tokens.shape[0]
    count = 4 * rows
    scale = HEAD_DIM ** (-0.5)

    def kernel(
        gu_a_ref, gu_b_ref, s_down, op_ref, br_ref, gm_hbm, mid_hbm, tok_hbm,
        cos_ref, sin_ref, bias_ref, q_ref, kv_ref, att_ref, lse_ref, nm_ref, wp_ref, wo_ref,
        out_ref, ig_ref, o_proj, o_gu, o_down, o_out,
        gm_ref, mid_ref, tok_ref, v_gu_a, v_gu_b, v_down, part, part_in, halves, whole, halves2, whole2, br, q_s, do_s, kv, kvt, att, delta, bias, cos_s, sin_s,
        dkv, kv_send, kv_in, gp, normed, wp, wo, t_proj, rc_proj, t_out, rc_out, *rest,
    ):
        bufs, (send, recv, local) = rest[:24], rest[24:]
        say_hello(ALL_LINES, True)
        at = place()
        xh, xl, y, z, c = at
        copy = Copies(send, recv)
        nlocal = [0]

        def near(src, dst):
            cp = pltpu.make_async_copy(src, dst, local.at[nlocal[0]])
            nlocal[0] += 1
            return cp

        load_gu, load_gu_b, load_down = near(gu_a_ref, v_gu_a), near(gu_b_ref, v_gu_b), near(s_down, v_down)
        load_op, load_br, load_wo = near(op_ref, part), near(br_ref, br), near(wo_ref, wo)
        load_att, load_q = near(att_ref, att), near(q_ref, q_s)
        load_kv = near(kv_ref, kv)
        load_turns = [near(cos_ref, cos_s), near(sin_ref, sin_s), near(bias_ref, bias)]
        load_nm, load_wp = near(nm_ref, normed), near(wp_ref, wp)
        load_rows = [near(gm_hbm, gm_ref), near(mid_hbm, mid_ref), near(tok_hbm, tok_ref)]
        for cp in (load_br, load_wo, load_gu, load_gu_b, load_op, load_down, load_att, load_q, load_kv, *load_turns, load_nm, load_wp, *load_rows):
            cp.start()
        outs = RingSum(copy, part, halves, whole, y)
        ones = RingSum(copy, part_in, halves2, whole2, y)
        kv_copy = copy(kv_send, kv_in, half_partner)
        core_proj = [
            copy(t_proj.at[:, :, 1 - c, :, cols], rc_proj.at[:, :, :, cols], sibling)
            for cols in (pl.ds(0, Q_COLS), pl.ds(Q_COLS, 128))
        ]
        core_out = copy(t_out.at[:, 1 - c], rc_out, sibling)
        gu_owners = GradOwners(
            copy,
            near,
            lambda x: v_gu_a.at[x[0], pl.ds(x[1] * 64, 64)],
            lambda z: v_gu_b.at[z],
            o_gu,
            at,
            bufs[0:3],
        )
        down_lines = GradLines(copy, v_down, SPLITS[2][1], at, bufs[3:7])
        down_owners = GradOwners(copy, near, down_lines.spot_a, down_lines.spot_b, o_down, at, bufs[7:10])
        proj_lines = GradLines(copy, t_proj, SPLITS[0][1], at, bufs[10:14])
        proj_owners = GradOwners(copy, near, proj_lines.spot_a, proj_lines.spot_b, o_proj, at, bufs[14:17])
        out_lines = GradLines(copy, t_out, OUT_SPLIT, at, bufs[17:21], True)
        out_owners = GradOwners(copy, near, out_lines.spot_a, out_lines.spot_b, o_out, at, bufs[21:24], True)

        dkv[...] = jnp.zeros_like(dkv)

        meet(ALL_LINES, True)
        load_op.wait()
        outs.start()
        load_gu.wait()
        load_gu_b.wait()
        gu_owners.start()
        load_down.wait()
        down_lines.start()

        load_br.wait()
        load_wo.wait()
        load_att.wait()
        lane = lax.broadcasted_iota(jnp.int32, (count, 128), 1)
        for p in range(4):
            if p % 2 == 0:
                both = dot(br[...].reshape(count, D), wo[p // 2].reshape(256, D), NT).astype(BF16).astype(F32)
            low = both[:, p % 2 * 128 : p % 2 * 128 + 128]
            do_s[2 * p] = jnp.where(lane < 64, 0.0, pltpu.roll(low, 64, 1)).astype(BF16)
            do_s[2 * p + 1] = jnp.where(lane < 64, 0.0, low).astype(BF16)
            prod = jnp.transpose(low * att[:, pl.ds(p * 128, 128)].astype(F32))
            for e in range(2):
                total_row = jnp.sum(prod[e * 64 : e * 64 + 64], 0, keepdims=True)
                delta[2 * p + e] = jnp.broadcast_to(total_row, (8, count))
        outs.turn()

        for k in range(4):
            term = dot(att[:, pl.ds(k * 128, 128)], br[...].reshape(count, D), TN)
            t_out[k // 2, k % 2] = term.astype(BF16).reshape(2, 4, 16, D)
        core_out.start()
        load_q.wait()
        load_kv.wait()
        for k in range(2):
            turned = jnp.transpose(kv[pl.ds(k * count, count)].astype(F32)).astype(BF16)
            kvt[:, pl.ds(k * count, count)] = turned

        def backward(pair):
            for b in range(2):
                rs = pl.ds(b * 256, 256)
                seen = pl.ds(0, 512 + 256 * (b + 1))
                found = []
                for e in range(2):
                    h = 2 * pair + e
                    q, do = q_s[h, rs], do_s[h, rs]
                    st = dot(kv[seen], q, NT) + bias[seen, rs] - lse_ref[h, 0:1, rs]
                    p = jnp.exp(st)
                    dp = dot(kv[seen], do, NT)
                    ds = (p * (dp - delta[h, 0:1, rs])).astype(BF16)
                    dkv[seen] += dot(ds, q) + dot(p.astype(BF16), do)
                    found.append(dot(kvt[:, seen], ds)[0:64])
                both = jnp.transpose(jnp.concatenate(found, 0)) * scale
                both = both * cos_s[rs] - swap_halves(both) * sin_s[rs]
                gp[rs, pl.ds(pl.multiple_of(pair * 128, 128), 128)] = both.astype(BF16)

        def two_pairs(k):
            def body(i, _):
                backward(2 * k + i)
                return 0

            lax.fori_loop(0, 2, body, 0)

        for cp in load_turns:
            cp.wait()
        two_pairs(0)
        down_lines.turn()
        gu_owners.deliver()
        two_pairs(1)
        kv_send[...] = dkv[pl.ds(0, count)].astype(BF16)
        kv_copy.start()
        core_out.wait_recv()
        add_up(t_out.at[:, c], rc_out)
        out_lines.start()
        load_nm.wait()
        for k in range(4):
            left = normed[:, :, pl.ds(k * 512, 512)].reshape(count, 512)
            term = dot(left, gp[:, pl.ds(0, Q_COLS)], TN)
            t_proj[k, :, :, :, pl.ds(0, Q_COLS)] = term.astype(BF16).reshape(2, 2, 128, Q_COLS)
        core_proj[0].start()
        kv_copy.wait_recv()
        got = dkv[pl.ds(count, count)] + kv_in[...].astype(F32)
        back = got * cos_s[...] - swap_halves(got) * sin_s[...]
        gp[:, pl.ds(Q_COLS, 128)] = jnp.where(lane < 64, back, got).astype(BF16)
        for k in range(4):
            left = normed[:, :, pl.ds(k * 512, 512)].reshape(count, 512)
            term = dot(left, gp[:, pl.ds(Q_COLS, 128)], TN)
            t_proj[k, :, :, :, pl.ds(Q_COLS, 128)] = term.astype(BF16).reshape(2, 2, 128, 128)
        core_proj[1].start()

        load_wp.wait()
        for j in range(4):
            w = wp[j].reshape(512, PROJ)
            part_in[:, :, pl.ds(j * 512, 512)] = dot(gp[...], w, NT).astype(BF16).reshape(4, rows, 512)
        ones.start()
        for cp in core_proj:
            cp.wait_recv()
        for k in range(4):
            add_up(t_proj.at[k, :, c], rc_proj.at[k])
        proj_lines.start()
        out_lines.turn()
        ones.turn()
        proj_lines.turn()
        down_lines.finish()
        down_owners.start()
        out_lines.finish()
        out_owners.start()
        proj_lines.finish()
        proj_owners.start()
        down_owners.deliver()
        out_owners.deliver()
        proj_owners.deliver()
        outs.finish()

        for cp in load_rows:
            cp.wait()

        def finish_out(r, _):
            rs = pl.ds(r * 32, 32)
            out_ref[rs] = (mid_ref[rs] + outs.rows(rs)).astype(BF16)
            return 0

        lax.fori_loop(0, rows // 32, finish_out, 0)
        outs.sent()
        ones.finish()

        def finish_in(r, _):
            rs = pl.ds(r * 32, 32)
            v = tok_ref[rs].astype(F32)
            inv = lax.rsqrt(jnp.mean(v * v, -1, keepdims=True) + EPS)
            v = v * inv
            g = ones.rows(rs)
            ig_ref[rs] = gm_ref[rs] + inv * (g - v * jnp.mean(g * v, -1, keepdims=True))
            return 0

        lax.fori_loop(0, rows // 32, finish_in, 0)
        ones.sent()
        for cp in (kv_copy, *core_proj, core_out):
            cp.wait_send()
        for owners in (gu_owners, down_owners, out_owners, proj_owners):
            owners.finish()
        for lines in (down_lines, out_lines, proj_lines):
            lines.sent()

    anywhere, vmem = pl.BlockSpec(memory_space=pl.ANY), pl.BlockSpec(memory_space=pltpu.VMEM)
    in_specs = [anywhere] * 14 + [vmem] + [anywhere] * 3
    outs = [
        (struct((rows, D)), vmem),
        (struct((rows, D), F32), vmem),
        (struct((4, 16, PROJ)), anywhere),
        (struct((4, 16, 2 * HID)), anywhere),
        (struct((4, 16, HID)), anywhere),
        (struct((16, D)), anywhere),
    ]
    whole = lambda: [pltpu.VMEM((2, rows, D // 2), BF16), pltpu.VMEM((2, rows, D), BF16)]
    copies = 12 + 4 + 9 + 21 * 2 + 19
    return pl.pallas_call(
        kernel,
        out_shape=[o[0] for o in outs],
        in_specs=in_specs,
        out_specs=[o[1] for o in outs],
        scratch_shapes=[
            pltpu.VMEM((rows, D), F32),
            pltpu.VMEM((rows, D), F32),
            pltpu.VMEM((rows, D), BF16),
            pltpu.VMEM((2, 128, SPLITS[1][1]), BF16),
            pltpu.VMEM((4, 64, 2 * HID - SPLITS[1][1]), BF16),
            pltpu.VMEM((4, 2, 128, HID), BF16),
            pltpu.VMEM((4, rows, D), BF16),
            pltpu.VMEM((4, rows, D), BF16),
            *whole(),
            *whole(),
            pltpu.VMEM((4, rows, D), BF16),
            pltpu.VMEM((REPEAT, count, 128), BF16),
            pltpu.VMEM((REPEAT, count, 128), BF16),
            pltpu.VMEM((2 * count, 128), BF16),
            pltpu.VMEM((128, 2 * count), BF16),
            pltpu.VMEM((count, Q_COLS), BF16),
            pltpu.VMEM((REPEAT, 8, count), F32),
            pltpu.VMEM((2 * count, count), F32),
            pltpu.VMEM((count, 128), F32),
            pltpu.VMEM((count, 128), F32),
            pltpu.VMEM((2 * count, 128), F32),
            pltpu.VMEM((count, 128), BF16),
            pltpu.VMEM((count, 128), BF16),
            pltpu.VMEM((count, PROJ), BF16),
            pltpu.VMEM((4, rows, D), BF16),
            pltpu.VMEM((4, 2, 2, 128, PROJ), BF16),
            pltpu.VMEM((2, 2, 2, 4, 16, D), BF16),
            pltpu.VMEM((4, 2, 2, 128, PROJ), BF16),
            pltpu.VMEM((4, 2, 128, PROJ), BF16),
            pltpu.VMEM((2, 2, 2, 4, 16, D), BF16),
            pltpu.VMEM((2, 2, 4, 16, D), BF16),
            *owner_buffers(2 * HID, SPLITS[1][1]),
            *line_buffers(HID, SPLITS[2][1]),
            *owner_buffers(HID, SPLITS[2][1]),
            *line_buffers(PROJ, SPLITS[0][1]),
            *owner_buffers(PROJ, SPLITS[0][1]),
            *line_buffers(D, OUT_SPLIT, True),
            *owner_buffers(D, OUT_SPLIT, True),
            pltpu.SemaphoreType.DMA((copies,)),
            pltpu.SemaphoreType.DMA((copies,)),
            pltpu.SemaphoreType.DMA((24,)),
        ],
        name="backward_attention",
        compiler_params=pltpu.CompilerParams(
            collective_id=ident, has_side_effects=True, vmem_limit_bytes=VMEM_LIMIT
        ),
    )(
        gu_a, gu_b, sum_down, out_part, branch_all, grad_middle, middle, tokens,
        cosines, sines, bias_all, q_all, kv_all, attended, lse, normed_all, proj_w, out_w,
    )


def feed_forward(seq_two, seq_cot, gu_w, down_w, middle, cotangent, ident):
    rows = middle.shape[0]
    count = 4 * rows
    tiles_gu, pairs = HID // 128, HID // 256

    def kernel(
        two_ref, cot_ref, wg_ref, wd_ref, mid_hbm, own_cot_hbm,
        branch_all, gm_hbm, gu_a, gu_b, s_down, op_out,
        part, halves, whole, two, gu, cot, hid, gh, turned, t_gu, t_down, rc_gu, rc_down, branch, op,
        mid_ref, own_cot, gm_ref,
        far_a, near_a, far_b, near_b, send, recv, local, weights,
    ):
        partners = [along_y(1), along_y(3), along_x(1), along_x(3), along_z(1), along_z(3), sibling]
        say_hello(partners)
        at = place()
        xh, xl, y, z, c = at
        copy = Copies(send, recv)
        nlocal = [0]

        def near(src, dst):
            cp = pltpu.make_async_copy(src, dst, local.at[nlocal[0]])
            nlocal[0] += 1
            return cp

        def load_gu(j):
            tile = pl.ds(pl.multiple_of(j * 256, 256), 256)
            return pltpu.make_async_copy(wg_ref.at[:, :, :, :, tile], t_gu.at[:, :, :, :, tile], weights.at[j])

        def load_down(j, width=256):
            tile = pl.ds(pl.multiple_of(j * 256, 256), width)
            return pltpu.make_async_copy(
                wd_ref.at[:, :, :, :, tile], t_down.at[:, :, :, :, tile], weights.at[tiles_gu + j]
            )

        load_cot, load_two = near(cot_ref, cot), near(two_ref, two)
        load_rows = [near(mid_hbm, mid_ref), near(own_cot_hbm, own_cot)]
        load_cot.start()
        last_down = load_down(pairs, HID - 256 * pairs)

        def begin_down(j, _):
            load_down(j).start()
            return 0

        def begin_gu(j, _):
            load_gu(j).start()
            return 0

        lax.fori_loop(0, pairs, begin_down, 0)
        last_down.start()
        load_two.start()
        lax.fori_loop(0, tiles_gu, begin_gu, 0)
        for cp in load_rows:
            cp.start()
        row_halves = [pl.ds(0, rows // 2), pl.ds(rows // 2, rows // 2)]
        rings = [RingSum(copy, part.at[:, r], halves.at[:, r], whole.at[:, r], y) for r in row_halves]
        gathers = [RingGather(copy, branch.at[r], branch_all.at[:, r], y) for r in row_halves]
        own = near(branch, branch_all.at[y])
        cores = [
            (copy(t_gu.at[k, :, 1 - c], rc_gu.at[k], sibling), copy(t_down.at[k, :, 1 - c], rc_down.at[k], sibling))
            for k in [(z + d) % 4 for d in range(4)]
        ]
        saves = [near(t_down.at[k, :, c], s_down.at[k]) for k in [(z + d) % 4 for d in range(4)]]
        lines = GradLines(copy, t_gu, SPLITS[1][1], at, (far_a, near_a, far_b, near_b))
        saves_gu = [
            near(t_gu.at[z, :, c, :, pl.ds(0, SPLITS[1][1])], gu_a),
            near(t_gu.at[:, xh, c, pl.ds(xl * 64, 64), pl.ds(SPLITS[1][1], 2 * HID - SPLITS[1][1])], gu_b),
        ]
        save_op = near(op, op_out)
        load_cot.wait()

        def hidden_back(j, _):
            load_down(j).wait()
            tile = pl.ds(pl.multiple_of(j * 256, 256), 256)
            gh[:, tile] = dot(cot[...].reshape(count, D), t_down[:, :, :, :, tile].reshape(D, 256))
            return 0

        lax.fori_loop(0, pairs, hidden_back, 0)
        last_down.wait()
        tile = pl.ds(256 * pairs, HID - 256 * pairs)
        gh[:, tile] = dot(cot[...].reshape(count, D), t_down[:, :, :, :, tile].reshape(D, HID - 256 * pairs))
        load_two.wait()

        def gate_up(j):
            load_gu(j).wait()
            both = pl.ds(pl.multiple_of(j * 256, 256), 256)
            return dot(two[...].reshape(count, D), t_gu[:, :, :, :, both].reshape(D, 256))

        def activate(j, act):
            both = pl.ds(pl.multiple_of(j * 256, 256), 256)
            one = pl.ds(pl.multiple_of(j * 128, 128), 128)
            gate, up = act[:, :128], act[:, 128:]
            back = gh[:, one]
            sigmoid = jax.nn.sigmoid(gate)
            silu = gate * sigmoid
            hid[:, one] = (silu * up).astype(BF16)
            grad_gate = back * up * sigmoid * (1.0 + gate * (1.0 - sigmoid))
            gu[:, both] = jnp.concatenate([grad_gate, back * silu], 1).astype(BF16)

        def hidden(j, _):
            activate(j, gate_up(j))
            return 0

        lax.fori_loop(0, tiles_gu, hidden, 0)

        def part_two(k, _):
            cols = pl.ds(pl.multiple_of(k * 512, 512), 512)
            part[:, :, cols] = dot(gu[...], t_gu[k].reshape(512, 2 * HID), NT).astype(BF16).reshape(4, rows, 512)
            return 0

        lax.fori_loop(0, 4, part_two, 0)
        meet(partners)
        for ring in rings:
            ring.start()

        def part_out(k, _):
            cols = pl.ds(pl.multiple_of(k * 512, 512), 512)
            op[:, :, cols] = dot(hid[...], t_down[k].reshape(512, HID), NT).astype(BF16).reshape(4, rows, 512)
            return 0

        def terms_gu(d):
            k = (z + d) % 4
            cols = pl.ds(pl.multiple_of(k * 512, 512), 512)
            turned[...] = jnp.transpose(two[:, :, cols].reshape(count, 512))

            def some(j, _):
                tile = pl.ds(pl.multiple_of(j * 256, 256), 256)
                t_gu[k, :, :, :, tile] = dot(turned[...], gu[:, tile]).astype(BF16).reshape(2, 2, 128, 256)
                return 0

            lax.fori_loop(0, 2 * HID // 256, some, 0)
            cores[d][0].start()

        def terms_down(d):
            k = (z + d) % 4
            cols = pl.ds(pl.multiple_of(k * 512, 512), 512)
            turned[...] = jnp.transpose(cot[:, :, cols].reshape(count, 512))

            def more(j, width=256):
                tile = pl.ds(pl.multiple_of(j * 256, 256), width)
                t_down[k, :, :, :, tile] = dot(turned[...], hid[:, tile]).astype(BF16).reshape(2, 2, 128, width)
                return 0

            lax.fori_loop(0, pairs, lambda j, _: more(j), 0)
            more(pairs, HID - 256 * pairs)
            cores[d][1].start()

        def add_gu(d):
            k = (z + d) % 4
            cores[d][0].wait_recv()
            add_up(t_gu.at[k, :, c], rc_gu.at[k])

        line_a, line_b = lines.lines
        terms_gu(2)
        terms_gu(1)
        for ring in rings:
            ring.turn()
        add_gu(2)
        for cp in line_a.far:
            cp.start()
        terms_gu(3)
        add_gu(1)
        terms_gu(0)
        add_gu(3)
        for cp in line_a.near:
            cp.start()
        add_gu(0)
        line_b.start()
        for cp in load_rows:
            cp.wait()
        for k in range(2):
            rings[k].finish()

            def back(r, _, k=k):
                rs, half = pl.ds(k * (rows // 2) + r * 32, 32), pl.ds(r * 32, 32)
                v = mid_ref[rs]
                inv = lax.rsqrt(jnp.mean(v * v, -1, keepdims=True) + EPS)
                v = v * inv
                g = rings[k].rows(half)
                value = own_cot[rs].astype(F32) + inv * (g - v * jnp.mean(g * v, -1, keepdims=True))
                gm_ref[rs] = value
                branch[rs] = value.astype(BF16)
                return 0

            lax.fori_loop(0, rows // 64, back, 0)
            gathers[k].start()
        own.start()
        save_gm = near(gm_ref, gm_hbm)
        save_gm.start()
        lax.fori_loop(0, 4, part_out, 0)
        save_op.start()
        for gather in gathers:
            gather.turn()
        line_a.turn()
        terms_down(2)
        terms_down(1)
        line_b.turn()
        terms_down(3)
        terms_down(0)
        for d in (2, 1, 3, 0):
            cores[d][1].wait_recv()
            add_up(t_down.at[(z + d) % 4, :, c], rc_down.at[(z + d) % 4])
            saves[d].start()
        for gather in gathers:
            gather.near()
            gather.far()
        lines.finish()
        for cp in saves_gu:
            cp.start()
        own.wait()
        save_gm.wait()
        save_op.wait()
        for cp in saves + saves_gu:
            cp.wait()
        for pair in cores:
            for cp in pair:
                cp.wait_send()
        lines.sent()
        for ring in rings + gathers:
            ring.sent()

    anywhere, vmem = pl.BlockSpec(memory_space=pl.ANY), pl.BlockSpec(memory_space=pltpu.VMEM)
    copies = 24 + 8 + 12
    return pl.pallas_call(
        kernel,
        out_shape=[
            struct((4, rows, D)),
            struct((rows, D), F32),
            struct((2, 128, SPLITS[1][1])),
            struct((4, 64, 2 * HID - SPLITS[1][1])),
            struct((4, 2, 128, HID)),
            struct((4, rows, D)),
        ],
        in_specs=[anywhere] * 6,
        out_specs=[anywhere] * 6,
        scratch_shapes=[
            pltpu.VMEM((4, rows, D), BF16),
            pltpu.VMEM((2, rows, D // 2), BF16),
            pltpu.VMEM((2, rows, D), BF16),
            pltpu.VMEM((4, rows, D), BF16),
            pltpu.VMEM((count, 2 * HID), BF16),
            pltpu.VMEM((4, rows, D), BF16),
            pltpu.VMEM((count, HID), BF16),
            pltpu.VMEM((count, HID), F32),
            pltpu.VMEM((512, count), BF16),
            pltpu.VMEM((4, 2, 2, 128, 2 * HID), BF16),
            pltpu.VMEM((4, 2, 2, 128, HID), BF16),
            pltpu.VMEM((4, 2, 128, 2 * HID), BF16),
            pltpu.VMEM((4, 2, 128, HID), BF16),
            pltpu.VMEM((rows, D), BF16),
            pltpu.VMEM((4, rows, D), BF16),
            pltpu.VMEM((rows, D), F32),
            pltpu.VMEM((rows, D), BF16),
            pltpu.VMEM((rows, D), F32),
            *line_buffers(2 * HID, SPLITS[1][1]),
            pltpu.SemaphoreType.DMA((copies,)),
            pltpu.SemaphoreType.DMA((copies,)),
            pltpu.SemaphoreType.DMA((18,)),
            pltpu.SemaphoreType.DMA((tiles_gu + pairs + 1,)),
        ],
        name="feed_forward",
        compiler_params=pltpu.CompilerParams(
            collective_id=ident, has_side_effects=True, vmem_limit_bytes=VMEM_LIMIT
        ),
    )(seq_two, seq_cot, gu_w, down_w, middle, cotangent)


def own_rows(attn_gain, mlp_gain, attn_in, mlp_in, proj, gu, down, out):
    def kernel(one_ref, two_ref, in_ref, mlp_ref, proj_ref, gu_ref, down_ref, out_ref, g_in, g_mlp, g_down, g_out, g_one, g_two):
        gain_one, gain_two = column(one_ref), column(two_ref)
        lane = lax.broadcasted_iota(jnp.int32, (16, 128), 1)
        low = lane < 64

        def put(dst, weights, at, value, gain, total):
            cols = pl.ds(at, 128)
            dst[:, cols] = value * gain
            return total + value * weights[:, cols].astype(F32)

        first = jnp.zeros((16, 128), F32)
        for k in range(TP):
            for j in range(Q_COLS // 128):
                value = proj_ref[k, :, pl.ds(j * 128, 128)].astype(F32)
                first = put(g_in, in_ref, k * Q_COLS + j * 128, value, gain_one, first)
        for k in range(0, TP, 2):
            even = proj_ref[k, :, pl.ds(Q_COLS, 128)].astype(F32)
            odd = proj_ref[k + 1, :, pl.ds(Q_COLS, 128)].astype(F32)
            key = jnp.where(low, even, pltpu.roll(odd, 64, 1))
            value = jnp.where(low, pltpu.roll(even, 64, 1), odd)
            first = put(g_in, in_ref, D + k * 64, key, gain_one, first)
            first = put(g_in, in_ref, D + HEAD_DIM * KV_HEADS + k * 64, value, gain_one, first)
        second = jnp.zeros((16, 128), F32)
        for k in range(TP):
            for j in range(HID // 128):
                for half in range(2):
                    value = gu_ref[k, :, pl.ds(j * 256 + half * 128, 128)].astype(F32)
                    second = put(g_mlp, mlp_ref, half * FF + k * HID + j * 128, value, gain_two, second)
            g_down[:, pl.ds(k * HID, HID)] = down_ref[k].astype(F32)
        g_out[...] = out_ref[...].astype(F32)
        sums = jnp.sum(first, -1, keepdims=True), jnp.sum(second, -1, keepdims=True)
        turned = jnp.transpose(jnp.where(lane == 0, sums[0], sums[1]))
        g_one[...], g_two[...] = turned[0:1], turned[1:2]

    shapes = [(16, attn_in.shape[1]), (16, 2 * FF), (16, FF), (16, D), (1, 16), (1, 16)]
    return pl.pallas_call(
        kernel,
        out_shape=[struct(shape, F32) for shape in shapes],
        in_specs=[pl.BlockSpec(memory_space=pltpu.VMEM)] * 8,
        out_specs=[pl.BlockSpec(memory_space=pltpu.VMEM)] * 6,
        name="own_rows",
        compiler_params=pltpu.CompilerParams(vmem_limit_bytes=VMEM_LIMIT),
    )(attn_gain, mlp_gain, attn_in, mlp_in, proj, gu, down, out)


def shards(tokens, positions, attn_in, attn_out, attn_gain, mlp_in, mlp_down, mlp_gain, cotangent):
    rows = tokens.shape[0]
    count = 4 * rows
    attn_gain, mlp_gain = attn_gain[None], mlp_gain[None]
    lanes = np.arange(128)
    freqs = np.zeros((8, 128), np.float32)
    freqs[0] = np.float32(ROPE_BASE) ** (-2.0 * (lanes % 32).astype(np.float32) / HEAD_DIM)
    freqs[1] = np.where(lanes % 64 < 32, -1.0, 1.0)
    (normed_one_all, cot_all, proj_w, gu_w, down_w, out_w, q_all, kv_all, attended_low, lse, cosines, sines, bias_all, middle, two_all) = (
        forward_attention(tokens, cotangent, positions[None], freqs, attn_gain, mlp_gain, attn_in, mlp_in, mlp_down, attn_out, 0)
    )
    branch_all, grad_middle, gu_a, gu_b, sum_down, out_part = feed_forward(
        two_all, cot_all, gu_w, down_w, middle, cotangent, 1
    )
    outputs, input_grad, own_proj, own_gu, own_down, own_out = backward_attention(
        gu_a, gu_b, sum_down, out_part, branch_all, grad_middle, middle, tokens,
        cosines, sines, bias_all, q_all, kv_all.reshape(2 * count, 128), attended_low, lse, normed_one_all, proj_w, out_w, 2,
    )
    grad_in, grad_mlp, grad_down, grad_out, grad_one, grad_two = own_rows(
        attn_gain, mlp_gain, attn_in, mlp_in, own_proj, own_gu, own_down, own_out
    )
    return outputs, input_grad, grad_in, grad_out, grad_one[0], grad_mlp, grad_down, grad_two[0]


def solution(mesh):
    both = ("dp", "ctx")
    wide, flat = P(both, None), P(both)
    in_specs = (wide, flat, wide, wide, flat, wide, wide, flat, wide)
    out_specs = (wide, wide, wide, wide, flat, wide, wide, flat)
    return jax.shard_map(shards, mesh=mesh, in_specs=in_specs, out_specs=out_specs, check_vma=False)
```
